32 devices in a mesh: dp: 4 (over z), expert: 2 (over x), tensor: 4 (over y, core).
Axes of the slice: x: 2, y: 2, z: 4, core: 2. Of those that a mesh axis runs over, the one named last changes fastest.
Arguments:
- tokens: bfloat16 [8, 512, 1536], P('dp', 'expert'), may hold values from -6 to 6
- cotangent: bfloat16 [8, 512, 1536], P('dp', 'expert'), may hold values from -6 to 6
- seg_start: int32 [8, 9], P('dp'), may hold values from 0 to 511, as said below
- seg_parent: int32 [8, 9], P('dp'), may hold values from 0 to 4, as said below
- routes: int32 [8, 512, 4], P('dp', 'expert'), may hold values from 0 to 7, all different within a row; in each aligned block of 256 rows (0 to 255, 256 to 511, ..., all dimensions but the last counted through in order) at most 256 rows name the same one
- attn_gain: bfloat16 [1536], P('dp'), may hold values from 0.5 to 1.5
- w_query: bfloat16 [1536, 1536], P('dp', 'tensor'), may hold values from -0.15625 to 0.15625
- key_projection_weight: bfloat16 [1536, 256], P('dp'), may hold values from -0.15625 to 0.15625
- value_projection_weight: bfloat16 [1536, 256], P('dp'), may hold values from -0.15625 to 0.15625
- w_output: bfloat16 [1536, 1536], P('tensor', 'dp'), may hold values from -0.625 to 0.625
- moe_gain: bfloat16 [1536], P('dp'), may hold values from 0.5 to 1.5
- w_router: bfloat16 [1536, 8], P('dp'), may hold values from -0.078125 to 0.078125
- w_gate: bfloat16 [8, 1536, 768], P('expert', 'dp', 'tensor'), may hold values from -0.15625 to 0.15625
- w_up: bfloat16 [8, 1536, 768], P('expert', 'dp', 'tensor'), may hold values from -0.15625 to 0.15625
- w_down: bfloat16 [8, 768, 1536], P('expert', 'tensor', 'dp'), may hold values from -0.625 to 0.625
Outputs:
- mixed_out: bfloat16 [8, 512, 1536], P('dp', 'expert')
- d_tokens: float32 [8, 512, 1536], P('dp', 'expert')
- d_attn_gain: float32 [1536], P(('dp', 'expert'))
- d_query: float32 [1536, 1536], P(('dp', 'expert'), 'tensor')
- d_key: float32 [1536, 256], P(('dp', 'expert', 'tensor'))
- d_value: float32 [1536, 256], P(('dp', 'expert', 'tensor'))
- d_output: float32 [1536, 1536], P('tensor', ('dp', 'expert'))
- d_moe_gain: float32 [1536], P(('dp', 'expert'))
- d_router: float32 [1536, 8], P(('dp', 'expert'))
- d_gate: float32 [8, 1536, 768], P('expert', 'dp', 'tensor')
- d_up: float32 [8, 1536, 768], P('expert', 'dp', 'tensor')
- d_down: float32 [8, 768, 1536], P('expert', 'tensor', 'dp')
The draws below stay inside these ranges and needn't reach their ends.
Inputs may be any that keep to these rules, and one draw needn't show every extreme that they name: `seg_start`: for each tree: entry 0 is 0, entry 1 is 512/2 (the trunk ends there); entries 2 to 8 are the starts of the other segments, rising strictly, each segment one token or more. `seg_parent`: entries 0 to 4 are 0 (trunk and branches hang from the trunk); entry 5 + i is the branch (1 to 4) of leaf i, each branch exactly once. `routes`: each token names 4 different experts; among the 256 tokens of one device of one tree (aligned blocks), no expert is named more than 256 times.
All inputs are finite; a program needn't handle non-finite values.
Results may differ from the reference program's by a relative error of at most 0.029.
Values may be sent and summed in bfloat16 or wider, within the bound.
A program may use at most 256 MiB of HBM per device.

```python
import math
import jax
import jax.numpy as jnp
import numpy as np
from jax import lax

MODEL_WIDTH = 1536
QUERY_HEADS = 12
KEY_VALUE_HEADS = 2
HEAD_SIZE = 128
FF = 768
TOP = 4
TOK_DEV = 256
BRANCHES = 4
EXPERTS = 8
TREE_LEN = 512
TREES = 8
CAP = 256
N_TENSOR = 4


def draw_seg_start(key, part):
    key = jax.random.fold_in(key, 11)
    trunk_len = TREE_LEN // 2
    cut_count = 2 * BRANCHES - 1

    def one_tree(tree_key):
        picked = jax.random.permutation(tree_key, trunk_len - 1)[:cut_count].astype(jnp.int32) + 1 + trunk_len
        return jnp.concatenate([jnp.zeros((1,), jnp.int32), jnp.full((1,), trunk_len, jnp.int32), jnp.sort(picked).astype(jnp.int32)])
    return jax.vmap(one_tree)(jax.random.split(key, TREES))


def draw_seg_parent(key, part):
    key = jax.random.fold_in(key, 12)

    def one_tree(tree_key):
        leaf_parent = jax.random.permutation(tree_key, BRANCHES).astype(jnp.int32) + 1
        return jnp.concatenate([jnp.zeros((BRANCHES + 1,), jnp.int32), leaf_parent])
    return jax.vmap(one_tree)(jax.random.split(key, TREES))


def shard_levels(stream_key, extent, cuts, low, high):
    def one(axis_at, shards_of):
        draws = jax.random.uniform(jax.random.fold_in(jax.random.fold_in(stream_key, 6), axis_at), (shards_of,), jnp.float32, low / len(cuts), high / len(cuts))
        return jnp.repeat(jnp.exp(draws), extent[axis_at] // shards_of).reshape((-1,) + (1,) * (len(extent) - axis_at - 1))

    level = one(*cuts[0])
    for cut in cuts[1:]:
        level = level * one(*cut)
    return level


def shared_out(own_key, own, number, rows, amount, top, bound, skew):
    sequence = jax.random.permutation(own_key, amount)
    crowded, common = shares(amount, rows * top, bound, skew, True), shares(amount, rows * top, bound, skew, False)
    places = jnp.arange(amount)

    def named(lengths, rotation):
        used = int((lengths > 0).sum())
        fixed = max(1, used // 4)
        moved = fixed + (places - fixed + rotation * (used - fixed)) % max(1, amount - fixed)
        return jnp.zeros((amount,), jnp.int32).at[sequence[jnp.where(places < fixed, places, moved)]].set(jnp.asarray(lengths, jnp.int32))

    lengths = jnp.where(number % 4 == 0, named(crowded, number // 4), named(common, number - number // 4 - 1))
    mixed = jax.random.permutation(jax.random.fold_in(own, 3), amount)
    donor, taker = mixed[0:amount // 2 * 2:2], mixed[1:amount // 2 * 2:2]
    room = jnp.minimum(lengths[donor] - 1, bound - lengths[taker]) // 2
    room = jnp.where((donor == sequence[0]) | (taker == sequence[0]) | (lengths[taker] == 0), 0, jnp.maximum(room, 0))
    moved = jax.random.randint(jax.random.fold_in(own, 4), (amount // 2,), 0, 1 << 20) % (room + 1)
    lengths = lengths.at[donor].add(-moved).at[taker].add(moved)
    items = jnp.searchsorted(jnp.cumsum(lengths), jnp.arange(rows * top), side="right").astype(jnp.int32)
    listing = items.reshape(top, rows).T
    listing = listing[jax.random.permutation(jax.random.fold_in(own, 1), rows)]
    rotation = jax.random.randint(jax.random.fold_in(own, 2), (rows, 1), 0, top)
    return jnp.take_along_axis(listing, (jnp.arange(top)[None, :] + rotation) % top, axis=1)


def shares(amount, total, limit, lean, full):
    portions = [(1 << 20) // math.isqrt(standing ** lean) + 1 for standing in range(1, amount + 1)]
    largest = limit if full else min(limit, max(-(-total // amount), total * portions[0] // sum(portions)))
    least = 1 if total - largest >= amount - 1 else 0
    counts, spare = [largest] + [least] * (amount - 1), total - largest - least * (amount - 1)
    while spare > 0:
        free = [i for i in range(1, amount) if counts[i] < largest] or [i for i in range(1, amount) if counts[i] < limit]
        whole, budget = sum([portions[i] for i in free]), spare
        for i in free:
            more = min(limit - counts[i], max(1, budget * portions[i] // whole), spare)
            counts[i] = counts[i] + more
            spare = spare - more
    return np.array(counts)


def centred(stream_key, shape, deviation, limit, cuts=(), kind=jnp.bfloat16):
    drawn = jax.random.normal(stream_key, shape, jnp.float32) * deviation
    if len(cuts) > 0:
        drawn = shard_levels(stream_key, shape, cuts, -0.22, 0.18) * drawn
    return jnp.clip(drawn, min=-limit, max=limit).astype(kind)


def setup_inputs(seed: int = 0) -> dict:
    seeds = jax.random.split(jax.random.key(seed), 16)
    tokens = centred(seeds[0], (TREES, TREE_LEN, MODEL_WIDTH), 1.0, 6.0, ((0, 4), (1, 2)))
    cotangent = centred(seeds[1], (TREES, TREE_LEN, MODEL_WIDTH), 1.0, 6.0, ((0, 4), (1, 2)))
    seg_start = draw_seg_start(jax.random.fold_in(seeds[15], 71), 0)
    seg_parent = draw_seg_parent(jax.random.fold_in(seeds[15], 71), 0)
    routes_keys = jax.random.split(jax.random.fold_in(seeds[4], 1), TREES * TREE_LEN // TOK_DEV)
    routes_turns = jax.random.permutation(jax.random.fold_in(seeds[4], 3), TREES * TREE_LEN // TOK_DEV)
    routes = jax.vmap(lambda own, number: shared_out(jax.random.fold_in(seeds[4], 2), own, number, TOK_DEV, EXPERTS, TOP, CAP, 2))(routes_keys, routes_turns).reshape((TREES, TREE_LEN, TOP))
    attn_gain = jnp.clip(1.0 + 0.1 * jax.random.normal(seeds[5], (MODEL_WIDTH,), jnp.float32), 0.5, 1.5).astype(jnp.bfloat16)
    w_query = centred(seeds[6], (MODEL_WIDTH, QUERY_HEADS * HEAD_SIZE), MODEL_WIDTH ** -0.5, 0.15625, ((0, 4), (1, 4)))
    key_projection_weight = centred(seeds[7], (MODEL_WIDTH, KEY_VALUE_HEADS * HEAD_SIZE), MODEL_WIDTH ** -0.5, 0.15625, ((0, 4),))
    value_projection_weight = centred(seeds[8], (MODEL_WIDTH, KEY_VALUE_HEADS * HEAD_SIZE), MODEL_WIDTH ** -0.5, 0.15625, ((0, 4),))
    w_output = centred(seeds[9], (QUERY_HEADS * HEAD_SIZE, MODEL_WIDTH), (QUERY_HEADS * HEAD_SIZE // 16) ** -0.5, 0.625, ((0, 4), (1, 4)))
    moe_gain = jnp.clip(1.0 + 0.1 * jax.random.normal(seeds[10], (MODEL_WIDTH,), jnp.float32), 0.5, 1.5).astype(jnp.bfloat16)
    w_router = centred(seeds[11], (MODEL_WIDTH, EXPERTS), (4 * MODEL_WIDTH) ** -0.5, 0.078125, ((0, 4),))
    w_gate = centred(seeds[12], (EXPERTS, MODEL_WIDTH, FF), MODEL_WIDTH ** -0.5, 0.15625, ((0, 2), (1, 4), (2, 4)))
    w_up = centred(seeds[13], (EXPERTS, MODEL_WIDTH, FF), MODEL_WIDTH ** -0.5, 0.15625, ((0, 2), (1, 4), (2, 4)))
    w_down = centred(seeds[14], (EXPERTS, FF, MODEL_WIDTH), (FF // 8) ** -0.5, 0.625, ((0, 2), (1, 4), (2, 4)))
    return dict(tokens=tokens, cotangent=cotangent, seg_start=seg_start, seg_parent=seg_parent, routes=routes, attn_gain=attn_gain, w_query=w_query, key_projection_weight=key_projection_weight, value_projection_weight=value_projection_weight, w_output=w_output, moe_gain=moe_gain, w_router=w_router, w_gate=w_gate, w_up=w_up, w_down=w_down)


EPS = 1e-05
ROPE_BASE = 10000.0
NEG = -1e+30
HIGH = lax.Precision.HIGHEST

@jax.custom_vjp
def reduced_precision(v):
    return lax.optimization_barrier(v.astype(jnp.bfloat16)).astype(jnp.float32)

@jax.custom_vjp
def reduced_backward(v):
    return v

def low_keep(v):
    return (reduced_precision(v), None)

def low_pass(kept, grad):
    return (grad,)

def back_keep(v):
    return (v, None)

def back_low(kept, grad):
    return (reduced_precision(grad),)
reduced_precision.defvjp(low_keep, low_pass)
reduced_backward.defvjp(back_keep, back_low)

def matrix_product(left, right):
    return jnp.dot(left, right, precision=HIGH, preferred_element_type=jnp.float32)

def normed(value_matrix, gain):
    return value_matrix * lax.rsqrt(lax.optimization_barrier(jnp.mean(value_matrix * value_matrix, -1, keepdims=True)) + EPS) * gain

def layout(starts, parents, places, sequence_length):
    labels = jnp.arange(starts.shape[0], dtype=jnp.int32)
    segment = lax.optimization_barrier(jnp.sum((starts[None, :] <= places[:, None]).astype(jnp.int32), 1, dtype=jnp.int32)) - 1
    hot_own = segment[:, None] == labels[None, :]
    parent_one = lax.optimization_barrier(jnp.sum(jnp.where(hot_own, parents[None, :], 0), 1, dtype=jnp.int32))
    hot_above = parent_one[:, None] == labels[None, :]
    parent_two = lax.optimization_barrier(jnp.sum(jnp.where(hot_above, parents[None, :], 0), 1, dtype=jnp.int32))
    hot_further = parent_two[:, None] == labels[None, :]
    seg_ends = jnp.concatenate([starts[1:], jnp.full((1,), sequence_length, jnp.int32)])
    seg_lengths = seg_ends - starts
    own_start = lax.optimization_barrier(jnp.sum(jnp.where(hot_own, starts[None, :], 0), 1, dtype=jnp.int32))
    above_len = lax.optimization_barrier(jnp.sum(jnp.where(hot_above, seg_lengths[None, :], 0), 1, dtype=jnp.int32))
    further_len = lax.optimization_barrier(jnp.sum(jnp.where(hot_further, seg_lengths[None, :], 0), 1, dtype=jnp.int32))
    depths = places - own_start + jnp.where(segment != 0, above_len, 0) + jnp.where(parent_one != 0, further_len, 0)
    return (segment, parent_one, parent_two, depths.astype(jnp.int32))

def angles(depths, feature):
    half_width = feature // 2
    frequency = ROPE_BASE ** (-2.0 * jnp.arange(half_width, dtype=jnp.float32) / feature)
    turning = depths.astype(jnp.float32)[:, None] * frequency[None, :]
    return (jnp.cos(turning), jnp.sin(turning))

def rotated_input(value_matrix, cosine_table, sine_lookup, sign):
    half_width = value_matrix.shape[-1] // 2
    front = value_matrix[..., :half_width]
    back_half = value_matrix[..., half_width:]
    cos_rows = cosine_table[:, None, :]
    sin_rows = sign * sine_lookup[:, None, :]
    return jnp.concatenate([front * cos_rows - back_half * sin_rows, back_half * cos_rows + front * sin_rows], -1)

def visible_mask(key_segment, key_places, segment, parent_one, parent_two, places):
    linked = (key_segment[None, :] == segment[:, None]) | (key_segment[None, :] == parent_one[:, None]) | (key_segment[None, :] == parent_two[:, None])
    return linked & (key_places[None, :] <= places[:, None])

def tree_forward(tokens_tree, params, starts, parents, routed):
    attn_gain, w_query, key_projection_weight, value_projection_weight, w_output, moe_gain, w_router, w_gate, w_up, w_down = params
    sequence_length = tokens_tree.shape[0]
    group_width = QUERY_HEADS // KEY_VALUE_HEADS
    places = jnp.arange(sequence_length, dtype=jnp.int32)
    segment, parent_one, parent_two, depths = layout(starts, parents, places, sequence_length)
    cosine_table, sine_lookup = angles(depths, HEAD_SIZE)
    hidden_first = reduced_precision(normed(tokens_tree, attn_gain))
    query_matrix = reduced_backward(matrix_product(hidden_first, reduced_precision(w_query))).reshape(sequence_length, QUERY_HEADS, HEAD_SIZE)
    key_matrix = reduced_backward(matrix_product(hidden_first, reduced_precision(key_projection_weight))).reshape(sequence_length, KEY_VALUE_HEADS, HEAD_SIZE)
    value_matrix = reduced_precision(reduced_backward(matrix_product(hidden_first, reduced_precision(value_projection_weight)))).reshape(sequence_length, KEY_VALUE_HEADS, HEAD_SIZE)
    query_matrix = reduced_precision(rotated_input(query_matrix, cosine_table, sine_lookup, 1.0)).reshape(sequence_length, KEY_VALUE_HEADS, group_width, HEAD_SIZE)
    key_matrix = reduced_precision(rotated_input(key_matrix, cosine_table, sine_lookup, 1.0))
    block_rows = min(512, sequence_length)

    def attend(number):
        first_row = number * block_rows
        query_rows = lax.dynamic_slice_in_dim(query_matrix, first_row, block_rows, 0)
        window = [lax.dynamic_slice_in_dim(source, first_row, block_rows, 0) for source in (segment, parent_one, parent_two, places)]
        visible = visible_mask(segment, places, window[0], window[1], window[2], window[3])
        scores = reduced_backward(jnp.einsum('qcgd,kcd->cgqk', query_rows, key_matrix, precision=HIGH) * HEAD_SIZE ** (-0.5))
        scores = jnp.where(visible[None, None], scores, NEG)
        row_max = lax.optimization_barrier(jnp.max(scores, -1, keepdims=True))
        exponent = jnp.exp(scores - row_max)
        attend_probs = reduced_precision(exponent / lax.optimization_barrier(jnp.sum(exponent, -1, keepdims=True)))
        return jnp.einsum('cgqk,kcd->qcgd', attend_probs, value_matrix, precision=HIGH)
    head_out = lax.map(jax.checkpoint(attend), jnp.arange(sequence_length // block_rows, dtype=jnp.int32))
    context = reduced_precision(reduced_backward(head_out.reshape(sequence_length, QUERY_HEADS * HEAD_SIZE)))
    after_attn = tokens_tree + reduced_backward(matrix_product(context, reduced_precision(w_output)))
    hidden_two = reduced_precision(normed(after_attn, moe_gain))
    logits = reduced_backward(matrix_product(hidden_two, reduced_precision(w_router)))
    chosen = routed[:, :, None] == jnp.arange(EXPERTS, dtype=jnp.int32)[None, None, :]
    picked = lax.optimization_barrier(jnp.sum(jnp.where(chosen, logits[:, None, :], 0.0), -1))
    gate_mix = jax.nn.softmax(picked, -1)
    mixing = lax.optimization_barrier(jnp.sum(jnp.where(chosen, gate_mix[:, :, None], 0.0), 1))
    quarter = FF // N_TENSOR
    gate_parts = reduced_precision(w_gate).reshape(EXPERTS, MODEL_WIDTH, N_TENSOR, quarter).transpose(0, 2, 1, 3)
    up_parts = reduced_precision(w_up).reshape(EXPERTS, MODEL_WIDTH, N_TENSOR, quarter).transpose(0, 2, 1, 3)
    down_parts = reduced_precision(w_down).reshape(EXPERTS, N_TENSOR, quarter, MODEL_WIDTH)

    def expert(running, inputs):
        gate_w, up_w, down_w, share_col = inputs
        spread_rows = reduced_backward(jnp.broadcast_to(hidden_two, (N_TENSOR, sequence_length, MODEL_WIDTH)))
        pre_gate = reduced_backward(jnp.einsum('tld,tdf->tlf', spread_rows, gate_w, precision=HIGH))
        pre_up = reduced_backward(jnp.einsum('tld,tdf->tlf', spread_rows, up_w, precision=HIGH))
        hidden = reduced_precision(jax.nn.gelu(pre_gate) * pre_up)
        produced = reduced_backward(reduced_precision(jnp.einsum('tlf,tfd->tld', hidden, down_w, precision=HIGH)))
        return (running + share_col[:, None] * lax.optimization_barrier(jnp.sum(produced, 0)), None)
    moe_out, unused = lax.scan(jax.checkpoint(expert), jnp.zeros_like(tokens_tree), (gate_parts, up_parts, down_parts, mixing.T))
    return after_attn + moe_out

def reference(tokens, cotangent, seg_start, seg_parent, routes, attn_gain, w_query, key_projection_weight, value_projection_weight, w_output, moe_gain, w_router, w_gate, w_up, w_down):
    params = (attn_gain.astype(jnp.float32), w_query.astype(jnp.float32), key_projection_weight.astype(jnp.float32), value_projection_weight.astype(jnp.float32), w_output.astype(jnp.float32), moe_gain.astype(jnp.float32), w_router.astype(jnp.float32), w_gate.astype(jnp.float32), w_up.astype(jnp.float32), w_down.astype(jnp.float32))

    def one_tree(running, inputs):
        tokens_tree, upstream, starts, parents, routed = inputs

        def forward(tree_in, weights):
            return tree_forward(tree_in, weights, starts, parents, routed)
        result, pullback = jax.vjp(forward, tokens_tree.astype(jnp.float32), params)
        tree_grad, weight_grads = pullback(upstream.astype(jnp.float32))
        running = jax.tree.map(jnp.add, running, weight_grads)
        return (running, (result.astype(jnp.bfloat16), tree_grad))
    zeros = jax.tree.map(jnp.zeros_like, params)
    grads_all, (mixed_out, d_tokens) = lax.scan(one_tree, zeros, (tokens, cotangent, seg_start, seg_parent, routes))
    return (mixed_out, d_tokens, grads_all[0], grads_all[1], grads_all[2], grads_all[3], grads_all[4], grads_all[5], grads_all[6], grads_all[7], grads_all[8], grads_all[9])
```

```python
import jax
import jax.numpy as jnp
from jax import lax
from jax.sharding import PartitionSpec as P

QUERY_HEADS = 12
KEY_VALUE_HEADS = 2
HEAD_SIZE = 128
GROUP = QUERY_HEADS // KEY_VALUE_HEADS
EPS = 1e-05
ROPE_BASE = 10000.0
NEG = -1e30
F32 = jnp.float32
BF16 = jnp.bfloat16


def dot(left, right, dims):
    return lax.dot_general(left, right, (dims, ((), ())), preferred_element_type=F32)


def norm_factor(rows):
    return lax.rsqrt(jnp.mean(rows * rows, -1, keepdims=True) + EPS)


def norm_back(rows, factor, gain, upstream):
    scaled = upstream * gain
    gain_grad = jnp.sum(upstream * rows * factor, 0)
    inner = jnp.mean(scaled * rows, -1, keepdims=True)
    return factor * scaled - rows * (factor * factor * factor * inner), gain_grad


def layout(starts, parents, places, length):
    labels = jnp.arange(starts.shape[1], dtype=jnp.int32)

    def pick(table, at):
        hot = at[:, :, None] == labels[None, None, :]
        return jnp.sum(jnp.where(hot, table[:, None, :], 0), 2, dtype=jnp.int32)

    segment = jnp.sum((starts[:, None, :] <= places[None, :, None]).astype(jnp.int32), 2) - 1
    above = pick(parents, segment)
    further = pick(parents, above)
    ends = jnp.concatenate(
        [starts[:, 1:], jnp.full((starts.shape[0], 1), length, jnp.int32)], 1
    )
    lengths = ends - starts
    depths = (
        places[None, :]
        - pick(starts, segment)
        + jnp.where(segment != 0, pick(lengths, above), 0)
        + jnp.where(above != 0, pick(lengths, further), 0)
    )
    return segment, above, further, depths


def angles(depths):
    half = HEAD_SIZE // 2
    frequency = ROPE_BASE ** (-2.0 * jnp.arange(half, dtype=F32) / HEAD_SIZE)
    turning = depths.astype(F32)[..., None] * frequency
    return jnp.cos(turning), jnp.sin(turning)


def rotate(heads, cosine, sine):
    half = HEAD_SIZE // 2
    front, back = heads[..., :half], heads[..., half:]
    return jnp.concatenate([front * cosine - back * sine, back * cosine + front * sine], -1)


def shards(
    tokens,
    cotangent,
    seg_start,
    seg_parent,
    routes,
    attn_gain,
    w_query,
    w_key,
    w_value,
    w_output,
    moe_gain,
    w_router,
    w_gate,
    w_up,
    w_down,
):
    trees, rows, width = tokens.shape
    expert_count = lax.axis_size("expert")
    tensor_count = lax.axis_size("tensor")
    tensor_at = lax.axis_index("tensor")
    expert_at = lax.axis_index("expert")
    length = rows * expert_count
    heads = w_query.shape[1] // HEAD_SIZE
    kv_head = tensor_at * heads // GROUP
    inv_root = HEAD_SIZE ** (-0.5)
    own_experts = w_gate.shape[0]
    quarter = w_gate.shape[2]
    all_experts = w_router.shape[1]

    def over_dp(array, axis):
        return lax.all_gather(array, "dp", axis=axis, tiled=True)

    w_query = over_dp(w_query, 0)
    w_output = over_dp(w_output, 1)
    gate_t = over_dp(jnp.swapaxes(w_gate, 1, 2), 2)
    up_t = over_dp(jnp.swapaxes(w_up, 1, 2), 2)
    down = over_dp(w_down, 2)
    small = over_dp(
        jnp.concatenate(
            [
                lax.dynamic_slice_in_dim(w_key, kv_head * HEAD_SIZE, HEAD_SIZE, 1),
                lax.dynamic_slice_in_dim(w_value, kv_head * HEAD_SIZE, HEAD_SIZE, 1),
                w_router,
                attn_gain[:, None],
                moe_gain[:, None],
            ],
            1,
        ),
        0,
    )
    w_kv = small[:, : 2 * HEAD_SIZE]
    w_router = small[:, 2 * HEAD_SIZE : 2 * HEAD_SIZE + all_experts]
    attn_gain = small[:, -2].astype(F32)
    moe_gain = small[:, -1].astype(F32)

    all_places = jnp.arange(length, dtype=jnp.int32)
    places = expert_at * rows + jnp.arange(rows, dtype=jnp.int32)
    segment, above, further, depths = layout(seg_start, seg_parent, places, length)
    key_segment = layout(seg_start, seg_parent, all_places, length)[0]
    cosine, sine = angles(depths)
    of_key = key_segment[:, None, :]
    visible = (
        (of_key == segment[:, :, None])
        | (of_key == above[:, :, None])
        | (of_key == further[:, :, None])
    ) & (all_places[None, None, :] <= places[None, :, None])

    residual = tokens.astype(F32).reshape(trees * rows, width)
    factor_one = norm_factor(residual)
    hidden_one = (residual * factor_one * attn_gain).astype(BF16)
    query_pre = dot(hidden_one, w_query, ((1,), (0,))).reshape(trees, rows, heads, HEAD_SIZE)
    kv_pre = dot(hidden_one, w_kv, ((1,), (0,))).reshape(trees, rows, 2 * HEAD_SIZE)
    queries = rotate(query_pre, cosine[:, :, None, :], sine[:, :, None, :]).astype(BF16)
    own_keys = rotate(kv_pre[..., :HEAD_SIZE], cosine, sine).astype(BF16)
    own_kv = jnp.concatenate([own_keys, kv_pre[..., HEAD_SIZE:].astype(BF16)], -1)
    keys_values = lax.all_gather(own_kv, "expert", axis=1, tiled=True)
    keys, values = keys_values[..., :HEAD_SIZE], keys_values[..., HEAD_SIZE:]
    scores = jnp.einsum("bqhd,bkd->bhqk", queries, keys, preferred_element_type=F32) * inv_root
    scores = jnp.where(visible[:, None], scores, NEG)
    row_max = jnp.max(scores, -1, keepdims=True)
    exponent = jnp.exp(scores - row_max)
    probs = exponent / jnp.sum(exponent, -1, keepdims=True)
    probs_low = probs.astype(BF16)
    context = jnp.einsum("bhqk,bkd->bqhd", probs_low, values, preferred_element_type=F32)
    context_low = context.reshape(trees * rows, heads * HEAD_SIZE).astype(BF16)
    attn_out = dot(context_low, w_output, ((1,), (0,))).astype(BF16)
    after_attn = residual + lax.psum(attn_out, "tensor").astype(F32)

    factor_two = norm_factor(after_attn)
    hidden_two = (after_attn * factor_two * moe_gain).astype(BF16)
    logits = dot(hidden_two, w_router, ((1,), (0,)))
    chosen = jnp.any(
        routes.reshape(trees * rows, -1)[:, :, None]
        == jnp.arange(all_experts, dtype=jnp.int32)[None, None, :],
        1,
    )
    masked = jnp.where(chosen, logits, NEG)
    raised = jnp.where(chosen, jnp.exp(masked - jnp.max(masked, -1, keepdims=True)), 0.0)
    mixing = raised / jnp.sum(raised, -1, keepdims=True)

    def over_expert(array):
        full = lax.all_gather(
            array.reshape(trees, rows, array.shape[-1]), "expert", axis=1, tiled=True
        )
        return full.reshape(trees * length, array.shape[-1])

    every_hidden = over_expert(hidden_two)
    every_up = over_expert(cotangent)
    every_mix = lax.dynamic_slice_in_dim(
        over_expert(mixing), expert_at * own_experts, own_experts, 1
    )
    count = trees * length
    pre_gate = dot(every_hidden, gate_t.reshape(-1, width), ((1,), (1,)))
    pre_up = dot(every_hidden, up_t.reshape(-1, width), ((1,), (1,)))
    down_rows = down.reshape(-1, width)
    down_back = dot(every_up, down_rows, ((1,), (1,)))
    wide_mix = jnp.repeat(every_mix, quarter, axis=1)
    activated, pull = jax.vjp(jax.nn.gelu, pre_gate)
    hidden = activated * pre_up
    mixed_hidden = (hidden * wide_mix).astype(BF16)
    moe_part = dot(mixed_hidden, down_rows, ((1,), (0,))).astype(BF16)
    gate_part = jnp.sum((hidden * down_back).reshape(count, own_experts, quarter), -1)
    hidden_grad = wide_mix * down_back
    gate_pre = pull(hidden_grad * pre_up)[0].astype(BF16)
    up_pre = (hidden_grad * activated).astype(BF16)
    two_part = (
        dot(gate_pre, gate_t.reshape(-1, width), ((1,), (0,)))
        + dot(up_pre, up_t.reshape(-1, width), ((1,), (0,)))
    ).astype(BF16)
    d_down = dot(mixed_hidden, every_up, ((0,), (0,)))
    d_gate = dot(gate_pre, every_hidden, ((0,), (0,)))
    d_up = dot(up_pre, every_hidden, ((0,), (0,)))

    def to_owner(array):
        array = array.reshape(trees, length, array.shape[-1])
        part = lax.psum_scatter(array, "expert", scatter_dimension=1, tiled=True)
        return lax.psum(part, "tensor").reshape(trees * rows, -1)

    spread = jnp.arange(all_experts) // own_experts == expert_at
    gate_wide = jnp.where(
        spread[None, :], jnp.tile(gate_part, (1, all_experts // own_experts)), 0.0
    )
    two_grad = to_owner(two_part).astype(F32)
    mix_grad = to_owner(gate_wide)
    mixed_out = (after_attn + to_owner(moe_part).astype(F32)).astype(BF16)

    picked_grad = mixing * (mix_grad - jnp.sum(mixing * mix_grad, -1, keepdims=True))
    logit_grad = picked_grad.astype(BF16)
    two_grad = two_grad + dot(logit_grad, w_router, ((1,), (1,)))
    d_router = dot(hidden_two, logit_grad, ((0,), (0,)))
    norm_two, d_moe_gain = norm_back(after_attn, factor_two, moe_gain, two_grad)
    attn_grad = cotangent.astype(F32).reshape(trees * rows, width) + norm_two
    attn_low = attn_grad.astype(BF16)

    d_output = dot(context_low, attn_low, ((0,), (0,)))
    context_grad = (
        dot(attn_low, w_output, ((1,), (1,)))
        .astype(BF16)
        .reshape(trees, rows, heads, HEAD_SIZE)
    )
    prob_grad = jnp.einsum("bqhd,bkd->bhqk", context_grad, values, preferred_element_type=F32)
    score_grad = probs * (prob_grad - jnp.sum(probs * prob_grad, -1, keepdims=True))
    score_grad = score_grad.astype(BF16)
    query_grad = (
        jnp.einsum("bhqk,bkd->bqhd", score_grad, keys, preferred_element_type=F32) * inv_root
    )
    key_grad = (
        jnp.einsum("bhqk,bqhd->bkd", score_grad, queries, preferred_element_type=F32) * inv_root
    )
    value_grad = jnp.einsum("bhqk,bqhd->bkd", probs_low, context_grad, preferred_element_type=F32)
    kv_part = jnp.concatenate([key_grad, value_grad], -1).astype(BF16)
    kv_sum = lax.psum_scatter(kv_part, "expert", scatter_dimension=1, tiled=True)
    sharing = GROUP // heads
    own_rows = rows // sharing
    place = tensor_at % sharing
    kv_rows = kv_sum.reshape(trees, sharing, own_rows, 2 * HEAD_SIZE)
    mine = lax.dynamic_index_in_dim(kv_rows, place, 1, False).astype(F32)
    for step in range(1, sharing):
        order = [
            (at, at // sharing * sharing + (at + step) % sharing) for at in range(tensor_count)
        ]
        away = lax.dynamic_index_in_dim(kv_rows, (place + step) % sharing, 1, False)
        mine = mine + lax.ppermute(away, "tensor", order).astype(F32)

    def own(array):
        return lax.dynamic_slice_in_dim(array, place * own_rows, own_rows, 1)

    key_low = rotate(mine[..., :HEAD_SIZE], own(cosine), -own(sine)).astype(BF16)
    kv_low = jnp.concatenate([key_low, mine[..., HEAD_SIZE:].astype(BF16)], -1)
    kv_low = kv_low.reshape(trees * own_rows, 2 * HEAD_SIZE)
    hidden_own = own(hidden_one.reshape(trees, rows, width)).reshape(trees * own_rows, width)
    d_kv = dot(hidden_own, kv_low, ((0,), (0,)))
    kv_back = dot(kv_low, w_kv, ((1,), (1,))).reshape(trees, own_rows, width)
    query_low = rotate(query_grad, cosine[:, :, None, :], -sine[:, :, None, :])
    query_low = query_low.astype(BF16).reshape(trees * rows, heads * HEAD_SIZE)
    d_query = dot(hidden_one, query_low, ((0,), (0,)))
    one_part = dot(query_low, w_query, ((1,), (1,))).reshape(trees, rows, width)
    one_part = lax.dynamic_update_slice_in_dim(
        one_part, own(one_part) + kv_back, place * own_rows, 1
    ).reshape(trees * rows, width)
    one_grad = lax.psum(one_part.astype(BF16), "tensor").astype(F32)
    norm_one, d_attn_gain = norm_back(residual, factor_one, attn_gain, one_grad)
    d_tokens = (attn_grad + norm_one).reshape(trees, rows, width)

    def scatter_dp(array, axis):
        return lax.psum_scatter(array, "dp", scatter_dimension=axis, tiled=True)

    def scatter_expert(array, axis):
        return lax.psum_scatter(array, "expert", scatter_dimension=axis, tiled=True)

    def experts_home(array):
        return scatter_dp(array.astype(BF16), 1).astype(F32).reshape(own_experts, quarter, -1)

    d_gate, d_up, d_down = experts_home(d_gate), experts_home(d_up), experts_home(d_down)
    d_query = scatter_expert(scatter_dp(d_query.astype(BF16), 0), 0).astype(F32)
    d_output = scatter_expert(scatter_dp(d_output.astype(BF16), 1), 1).astype(F32)
    flat = jnp.concatenate([d_attn_gain[:, None], d_moe_gain[:, None], d_router], 1)
    flat = scatter_expert(scatter_dp(flat, 0), 0)
    of_head = (jnp.arange(KEY_VALUE_HEADS) == kv_head).astype(F32)[None, None, :, None]
    d_kv = scatter_expert(scatter_dp(d_kv, 0), 0).reshape(-1, 2, 1, HEAD_SIZE) * of_head
    d_kv = d_kv.reshape(-1, 2 * KEY_VALUE_HEADS * HEAD_SIZE)
    d_kv = lax.psum_scatter(d_kv, "tensor", scatter_dimension=0, tiled=True)
    return (
        mixed_out.reshape(trees, rows, width),
        d_tokens,
        flat[:, 0],
        d_query,
        d_kv[:, : KEY_VALUE_HEADS * HEAD_SIZE],
        d_kv[:, KEY_VALUE_HEADS * HEAD_SIZE :],
        d_output,
        flat[:, 1],
        flat[:, 2:],
        jnp.swapaxes(d_gate, 1, 2),
        jnp.swapaxes(d_up, 1, 2),
        d_down,
    )


def solution(mesh):
    placed = (
        P("dp", "expert", None),
        P("dp", "expert", None),
        P("dp", None),
        P("dp", None),
        P("dp", "expert", None),
        P("dp"),
        P("dp", "tensor"),
        P("dp", None),
        P("dp", None),
        P("tensor", "dp"),
        P("dp"),
        P("dp", None),
        P("expert", "dp", "tensor"),
        P("expert", "dp", "tensor"),
        P("expert", "tensor", "dp"),
    )
    return jax.shard_map(
        shards,
        mesh=mesh,
        in_specs=placed,
        out_specs=(
            P("dp", "expert", None),
            P("dp", "expert", None),
            P(("dp", "expert")),
            P(("dp", "expert"), "tensor"),
            P(("dp", "expert", "tensor"), None),
            P(("dp", "expert", "tensor"), None),
            P("tensor", ("dp", "expert")),
            P(("dp", "expert")),
            P(("dp", "expert"), None),
            P("expert", "dp", "tensor"),
            P("expert", "dp", "tensor"),
            P("expert", "tensor", "dp"),
        ),
        check_vma=False,
    )
```

```python
import functools
import math

import jax
import jax.numpy as jnp
import numpy as np
from jax import lax
from jax.experimental import pallas as pl
from jax.experimental.pallas import tpu as pltpu
from jax.sharding import PartitionSpec as P

QUERY_HEADS = 12
KEY_VALUE_HEADS = 2
HEAD_SIZE = 128
GROUP = QUERY_HEADS // KEY_VALUE_HEADS
EPS = 1e-05
ROPE_BASE = 10000.0
NEG = -1e30
F32 = jnp.float32
BF16 = jnp.bfloat16


def dot(left, right, dims):
    return lax.dot_general(left, right, (dims, ((), ())), preferred_element_type=F32)


def norm_factor(rows):
    return lax.rsqrt(jnp.mean(rows * rows, -1, keepdims=True) + EPS)


def norm_back(rows, factor, gain, upstream):
    scaled = upstream * gain
    gain_grad = jnp.sum(upstream * rows * factor, 0)
    inner = jnp.mean(scaled * rows, -1, keepdims=True)
    return factor * scaled - rows * (factor * factor * factor * inner), gain_grad


def layout(starts, parents, places, length):
    labels = jnp.arange(starts.shape[1], dtype=jnp.int32)

    def pick(table, at):
        hot = at[:, :, None] == labels[None, None, :]
        return jnp.sum(jnp.where(hot, table[:, None, :], 0), 2, dtype=jnp.int32)

    segment = jnp.sum((starts[:, None, :] <= places[None, :, None]).astype(jnp.int32), 2) - 1
    above = pick(parents, segment)
    further = pick(parents, above)
    ends = jnp.concatenate(
        [starts[:, 1:], jnp.full((starts.shape[0], 1), length, jnp.int32)], 1
    )
    lengths = ends - starts
    depths = (
        places[None, :]
        - pick(starts, segment)
        + jnp.where(segment != 0, pick(lengths, above), 0)
        + jnp.where(above != 0, pick(lengths, further), 0)
    )
    return segment, above, further, depths


def angles(depths):
    half = HEAD_SIZE // 2
    frequency = ROPE_BASE ** (-2.0 * jnp.arange(half, dtype=F32) / HEAD_SIZE)
    turning = depths.astype(F32)[..., None] * frequency
    return jnp.cos(turning), jnp.sin(turning)


def rotate(heads, cosine, sine):
    half = HEAD_SIZE // 2
    front, back = heads[..., :half], heads[..., half:]
    return jnp.concatenate([front * cosine - back * sine, back * cosine + front * sine], -1)


def general_shards(
    tokens,
    cotangent,
    seg_start,
    seg_parent,
    routes,
    attn_gain,
    w_query,
    w_key,
    w_value,
    w_output,
    moe_gain,
    w_router,
    w_gate,
    w_up,
    w_down,
):
    trees, rows, width = tokens.shape
    expert_count = lax.axis_size("expert")
    tensor_count = lax.axis_size("tensor")
    tensor_at = lax.axis_index("tensor")
    expert_at = lax.axis_index("expert")
    length = rows * expert_count
    heads = w_query.shape[1] // HEAD_SIZE
    kv_head = tensor_at * heads // GROUP
    inv_root = HEAD_SIZE ** (-0.5)
    own_experts = w_gate.shape[0]
    quarter = w_gate.shape[2]
    all_experts = w_router.shape[1]

    def over_dp(array, axis):
        return lax.all_gather(array, "dp", axis=axis, tiled=True)

    w_query = over_dp(w_query, 0)
    w_output = over_dp(w_output, 1)
    gate_t = over_dp(jnp.swapaxes(w_gate, 1, 2), 2)
    up_t = over_dp(jnp.swapaxes(w_up, 1, 2), 2)
    down = over_dp(w_down, 2)
    small = over_dp(
        jnp.concatenate(
            [
                lax.dynamic_slice_in_dim(w_key, kv_head * HEAD_SIZE, HEAD_SIZE, 1),
                lax.dynamic_slice_in_dim(w_value, kv_head * HEAD_SIZE, HEAD_SIZE, 1),
                w_router,
                attn_gain[:, None],
                moe_gain[:, None],
            ],
            1,
        ),
        0,
    )
    w_kv = small[:, : 2 * HEAD_SIZE]
    w_router = small[:, 2 * HEAD_SIZE : 2 * HEAD_SIZE + all_experts]
    attn_gain = small[:, -2].astype(F32)
    moe_gain = small[:, -1].astype(F32)

    all_places = jnp.arange(length, dtype=jnp.int32)
    places = expert_at * rows + jnp.arange(rows, dtype=jnp.int32)
    segment, above, further, depths = layout(seg_start, seg_parent, places, length)
    key_segment = layout(seg_start, seg_parent, all_places, length)[0]
    cosine, sine = angles(depths)
    of_key = key_segment[:, None, :]
    visible = (
        (of_key == segment[:, :, None])
        | (of_key == above[:, :, None])
        | (of_key == further[:, :, None])
    ) & (all_places[None, None, :] <= places[None, :, None])

    residual = tokens.astype(F32).reshape(trees * rows, width)
    factor_one = norm_factor(residual)
    hidden_one = (residual * factor_one * attn_gain).astype(BF16)
    query_pre = dot(hidden_one, w_query, ((1,), (0,))).reshape(trees, rows, heads, HEAD_SIZE)
    kv_pre = dot(hidden_one, w_kv, ((1,), (0,))).reshape(trees, rows, 2 * HEAD_SIZE)
    queries = rotate(query_pre, cosine[:, :, None, :], sine[:, :, None, :]).astype(BF16)
    own_keys = rotate(kv_pre[..., :HEAD_SIZE], cosine, sine).astype(BF16)
    own_kv = jnp.concatenate([own_keys, kv_pre[..., HEAD_SIZE:].astype(BF16)], -1)
    keys_values = lax.all_gather(own_kv, "expert", axis=1, tiled=True)
    keys, values = keys_values[..., :HEAD_SIZE], keys_values[..., HEAD_SIZE:]
    scores = jnp.einsum("bqhd,bkd->bhqk", queries, keys, preferred_element_type=F32) * inv_root
    scores = jnp.where(visible[:, None], scores, NEG)
    row_max = jnp.max(scores, -1, keepdims=True)
    exponent = jnp.exp(scores - row_max)
    probs = exponent / jnp.sum(exponent, -1, keepdims=True)
    probs_low = probs.astype(BF16)
    context = jnp.einsum("bhqk,bkd->bqhd", probs_low, values, preferred_element_type=F32)
    context_low = context.reshape(trees * rows, heads * HEAD_SIZE).astype(BF16)
    attn_out = dot(context_low, w_output, ((1,), (0,))).astype(BF16)
    after_attn = residual + lax.psum(attn_out, "tensor").astype(F32)

    factor_two = norm_factor(after_attn)
    hidden_two = (after_attn * factor_two * moe_gain).astype(BF16)
    logits = dot(hidden_two, w_router, ((1,), (0,)))
    chosen = jnp.any(
        routes.reshape(trees * rows, -1)[:, :, None]
        == jnp.arange(all_experts, dtype=jnp.int32)[None, None, :],
        1,
    )
    masked = jnp.where(chosen, logits, NEG)
    raised = jnp.where(chosen, jnp.exp(masked - jnp.max(masked, -1, keepdims=True)), 0.0)
    mixing = raised / jnp.sum(raised, -1, keepdims=True)

    def over_expert(array):
        full = lax.all_gather(
            array.reshape(trees, rows, array.shape[-1]), "expert", axis=1, tiled=True
        )
        return full.reshape(trees * length, array.shape[-1])

    every_hidden = over_expert(hidden_two)
    every_up = over_expert(cotangent)
    every_mix = lax.dynamic_slice_in_dim(
        over_expert(mixing), expert_at * own_experts, own_experts, 1
    )
    count = trees * length
    pre_gate = dot(every_hidden, gate_t.reshape(-1, width), ((1,), (1,)))
    pre_up = dot(every_hidden, up_t.reshape(-1, width), ((1,), (1,)))
    down_rows = down.reshape(-1, width)
    down_back = dot(every_up, down_rows, ((1,), (1,)))
    wide_mix = jnp.repeat(every_mix, quarter, axis=1)
    activated, pull = jax.vjp(jax.nn.gelu, pre_gate)
    hidden = activated * pre_up
    mixed_hidden = (hidden * wide_mix).astype(BF16)
    moe_part = dot(mixed_hidden, down_rows, ((1,), (0,))).astype(BF16)
    gate_part = jnp.sum((hidden * down_back).reshape(count, own_experts, quarter), -1)
    hidden_grad = wide_mix * down_back
    gate_pre = pull(hidden_grad * pre_up)[0].astype(BF16)
    up_pre = (hidden_grad * activated).astype(BF16)
    two_part = (
        dot(gate_pre, gate_t.reshape(-1, width), ((1,), (0,)))
        + dot(up_pre, up_t.reshape(-1, width), ((1,), (0,)))
    ).astype(BF16)
    d_down = dot(mixed_hidden, every_up, ((0,), (0,)))
    d_gate = dot(gate_pre, every_hidden, ((0,), (0,)))
    d_up = dot(up_pre, every_hidden, ((0,), (0,)))

    def to_owner(array):
        array = array.reshape(trees, length, array.shape[-1])
        part = lax.psum_scatter(array, "expert", scatter_dimension=1, tiled=True)
        return lax.psum(part, "tensor").reshape(trees * rows, -1)

    spread = jnp.arange(all_experts) // own_experts == expert_at
    gate_wide = jnp.where(
        spread[None, :], jnp.tile(gate_part, (1, all_experts // own_experts)), 0.0
    )
    two_grad = to_owner(two_part).astype(F32)
    mix_grad = to_owner(gate_wide)
    mixed_out = (after_attn + to_owner(moe_part).astype(F32)).astype(BF16)

    picked_grad = mixing * (mix_grad - jnp.sum(mixing * mix_grad, -1, keepdims=True))
    logit_grad = picked_grad.astype(BF16)
    two_grad = two_grad + dot(logit_grad, w_router, ((1,), (1,)))
    d_router = dot(hidden_two, logit_grad, ((0,), (0,)))
    norm_two, d_moe_gain = norm_back(after_attn, factor_two, moe_gain, two_grad)
    attn_grad = cotangent.astype(F32).reshape(trees * rows, width) + norm_two
    attn_low = attn_grad.astype(BF16)

    d_output = dot(context_low, attn_low, ((0,), (0,)))
    context_grad = (
        dot(attn_low, w_output, ((1,), (1,)))
        .astype(BF16)
        .reshape(trees, rows, heads, HEAD_SIZE)
    )
    prob_grad = jnp.einsum("bqhd,bkd->bhqk", context_grad, values, preferred_element_type=F32)
    score_grad = probs * (prob_grad - jnp.sum(probs * prob_grad, -1, keepdims=True))
    score_grad = score_grad.astype(BF16)
    query_grad = (
        jnp.einsum("bhqk,bkd->bqhd", score_grad, keys, preferred_element_type=F32) * inv_root
    )
    key_grad = (
        jnp.einsum("bhqk,bqhd->bkd", score_grad, queries, preferred_element_type=F32) * inv_root
    )
    value_grad = jnp.einsum("bhqk,bqhd->bkd", probs_low, context_grad, preferred_element_type=F32)
    kv_part = jnp.concatenate([key_grad, value_grad], -1).astype(BF16)
    kv_sum = lax.psum_scatter(kv_part, "expert", scatter_dimension=1, tiled=True)
    sharing = GROUP // heads
    own_rows = rows // sharing
    place = tensor_at % sharing
    kv_rows = kv_sum.reshape(trees, sharing, own_rows, 2 * HEAD_SIZE)
    mine = lax.dynamic_index_in_dim(kv_rows, place, 1, False).astype(F32)
    for step in range(1, sharing):
        order = [
            (at, at // sharing * sharing + (at + step) % sharing) for at in range(tensor_count)
        ]
        away = lax.dynamic_index_in_dim(kv_rows, (place + step) % sharing, 1, False)
        mine = mine + lax.ppermute(away, "tensor", order).astype(F32)

    def own(array):
        return lax.dynamic_slice_in_dim(array, place * own_rows, own_rows, 1)

    key_low = rotate(mine[..., :HEAD_SIZE], own(cosine), -own(sine)).astype(BF16)
    kv_low = jnp.concatenate([key_low, mine[..., HEAD_SIZE:].astype(BF16)], -1)
    kv_low = kv_low.reshape(trees * own_rows, 2 * HEAD_SIZE)
    hidden_own = own(hidden_one.reshape(trees, rows, width)).reshape(trees * own_rows, width)
    d_kv = dot(hidden_own, kv_low, ((0,), (0,)))
    kv_back = dot(kv_low, w_kv, ((1,), (1,))).reshape(trees, own_rows, width)
    query_low = rotate(query_grad, cosine[:, :, None, :], -sine[:, :, None, :])
    query_low = query_low.astype(BF16).reshape(trees * rows, heads * HEAD_SIZE)
    d_query = dot(hidden_one, query_low, ((0,), (0,)))
    one_part = dot(query_low, w_query, ((1,), (1,))).reshape(trees, rows, width)
    one_part = lax.dynamic_update_slice_in_dim(
        one_part, own(one_part) + kv_back, place * own_rows, 1
    ).reshape(trees * rows, width)
    one_grad = lax.psum(one_part.astype(BF16), "tensor").astype(F32)
    norm_one, d_attn_gain = norm_back(residual, factor_one, attn_gain, one_grad)
    d_tokens = (attn_grad + norm_one).reshape(trees, rows, width)

    def scatter_dp(array, axis):
        return lax.psum_scatter(array, "dp", scatter_dimension=axis, tiled=True)

    def scatter_expert(array, axis):
        return lax.psum_scatter(array, "expert", scatter_dimension=axis, tiled=True)

    def experts_home(array):
        return scatter_dp(array.astype(BF16), 1).astype(F32).reshape(own_experts, quarter, -1)

    d_gate, d_up, d_down = experts_home(d_gate), experts_home(d_up), experts_home(d_down)
    d_query = scatter_expert(scatter_dp(d_query.astype(BF16), 0), 0).astype(F32)
    d_output = scatter_expert(scatter_dp(d_output.astype(BF16), 1), 1).astype(F32)
    flat = jnp.concatenate([d_attn_gain[:, None], d_moe_gain[:, None], d_router], 1)
    flat = scatter_expert(scatter_dp(flat, 0), 0)
    of_head = (jnp.arange(KEY_VALUE_HEADS) == kv_head).astype(F32)[None, None, :, None]
    d_kv = scatter_expert(scatter_dp(d_kv, 0), 0).reshape(-1, 2, 1, HEAD_SIZE) * of_head
    d_kv = d_kv.reshape(-1, 2 * KEY_VALUE_HEADS * HEAD_SIZE)
    d_kv = lax.psum_scatter(d_kv, "tensor", scatter_dimension=0, tiled=True)
    return (
        mixed_out.reshape(trees, rows, width),
        d_tokens,
        flat[:, 0],
        d_query,
        d_kv[:, : KEY_VALUE_HEADS * HEAD_SIZE],
        d_kv[:, KEY_VALUE_HEADS * HEAD_SIZE :],
        d_output,
        flat[:, 1],
        flat[:, 2:],
        jnp.swapaxes(d_gate, 1, 2),
        jnp.swapaxes(d_up, 1, 2),
        d_down,
    )


MESH = pl.DeviceIdType.MESH
NT = (((1,), (1,)), ((), ()))
NN = (((1,), (0,)), ((), ()))
TN = (((0,), (0,)), ((), ()))
CHUNKS = 4


def mm(left, right, dims=NN):
    return lax.dot_general(left, right, dims, preferred_element_type=F32)


class Place:
    def __init__(self):
        self.z = lax.axis_index("dp")
        self.x = lax.axis_index("expert")
        self.t = lax.axis_index("tensor")
        self.y = self.t // 2
        self.c = self.t % 2

    def at_z(self, z):
        return (z, self.x, self.t)

    def x_peer(self):
        return (self.z, 1 - self.x, self.t)

    def y_peer(self):
        return (self.z, self.x, (self.t + 2) % 4)

    def core_peer(self):
        return (self.z, self.x, self.t + 1 - 2 * self.c)


def remote(src, dst, sems, at, device):
    return pltpu.make_async_remote_copy(
        src_ref=src,
        dst_ref=dst,
        send_sem=sems.at[0, at],
        recv_sem=sems.at[1, at],
        device_id=device,
        device_id_type=MESH,
    )


def greet(devices):
    barrier = pltpu.get_barrier_semaphore()
    for device in devices:
        pl.semaphore_signal(barrier, inc=1, device_id=device, device_id_type=MESH)
    pl.semaphore_wait(barrier, len(devices))


def tree_tables(starts, parents, tree, first, rows, length, frequency):
    count = starts.shape[1]
    place = first + lax.broadcasted_iota(jnp.int32, (rows, HEAD_SIZE), 0)
    start = [starts[tree, k] for k in range(count)]
    parent = [parents[tree, k] for k in range(count)]
    size = [(start[k + 1] if k + 1 < count else length) - start[k] for k in range(count)]

    def pick(table, at):
        total = jnp.zeros_like(at)
        for k in range(count):
            total = total + jnp.where(at == k, table[k], 0)
        return total

    def segment_of(at):
        total = jnp.zeros_like(at)
        for k in range(1, count):
            total = total + jnp.where(at >= start[k], 1, 0)
        return total

    segment = segment_of(place)
    above = pick(parent, segment)
    further = pick(parent, above)
    depth = (
        place
        - pick(start, segment)
        + jnp.where(segment != 0, pick(size, above), 0)
        + jnp.where(above != 0, pick(size, further), 0)
    )
    turning = depth.astype(F32) * frequency
    lane = lax.broadcasted_iota(jnp.int32, (rows, HEAD_SIZE), 1)
    cosine = jnp.cos(turning)
    sine = jnp.sin(turning)
    sine = jnp.where(lane < HEAD_SIZE // 2, -sine, sine)
    key_place = lax.broadcasted_iota(jnp.int32, (8, length), 1)
    key_segment = jnp.broadcast_to(segment_of(key_place)[:1], (rows, length))
    key_place = jnp.broadcast_to(key_place[:1], (rows, length))
    wide = length // HEAD_SIZE

    def widen(array):
        return jnp.concatenate([array] * wide, 1)

    visible = (
        (key_segment == widen(segment))
        | (key_segment == widen(above))
        | (key_segment == widen(further))
    ) & (key_place <= widen(place))
    return jnp.where(visible, 1.0, 0.0), cosine, sine


def turn(head, cosine, sine):
    return head * cosine + pltpu.roll(head, HEAD_SIZE // 2, 1) * sine


def attend_kernel(
    starts,
    parents,
    frequency,
    tokens,
    cotangent,
    routes,
    w_query,
    w_key,
    w_value,
    w_output,
    small,
    hid_one,
    wqkv,
    wout,
    smalls,
    queries,
    keys,
    values,
    probs,
    context,
    tables,
    after,
    hid_two,
    ups,
    mixes,
    mask,
    part,
    core_in,
    y_out,
    y_in,
    local_sem,
    small_sem,
    up_sem,
    dn_sem,
    side_sem,
    up_sem2,
    dn_sem2,
    side_sem2,
    kv_sem,
    cot_x_sem,
    cot_c_sem,
    cot_f_sem,
    core_sem,
    y_sem,
    hx_sem,
    hc_sem,
    hf_sem,
    mix_sem,
):
    me = Place()
    z, x, y, c = me.z, me.x, me.y, me.c
    deep = wqkv.shape[0]
    trees, rows, width = tokens.shape
    length = keys.shape[1]
    shard = wqkv.shape[1]
    half = shard // 2
    heads = queries.shape[1]
    step = rows // CHUNKS
    inv_root = HEAD_SIZE ** (-0.5)

    local = [
        pltpu.make_async_copy(w_query, wqkv.at[z, :, pl.ds(0, heads * HEAD_SIZE)], local_sem.at[0]),
        pltpu.make_async_copy(
            w_key.at[:, pl.ds(pl.multiple_of(y * HEAD_SIZE, HEAD_SIZE), HEAD_SIZE)],
            wqkv.at[z, :, pl.ds(heads * HEAD_SIZE, HEAD_SIZE)],
            local_sem.at[1],
        ),
        pltpu.make_async_copy(
            w_value.at[:, pl.ds(pl.multiple_of(y * HEAD_SIZE, HEAD_SIZE), HEAD_SIZE)],
            wqkv.at[z, :, pl.ds((heads + 1) * HEAD_SIZE, HEAD_SIZE)],
            local_sem.at[2],
        ),
        pltpu.make_async_copy(w_output, wout.at[z], local_sem.at[3]),
        pltpu.make_async_copy(small, smalls.at[z], local_sem.at[4]),
        pltpu.make_async_copy(cotangent.at[0], ups.at[0, x], local_sem.at[5]),
        pltpu.make_async_copy(cotangent.at[1], ups.at[1, x], local_sem.at[6]),
    ]
    for copy in local:
        copy.start()
    others = [me.at_z((z + k) % deep) for k in range(1, deep)]
    greet(others + [me.x_peer(), me.y_peer(), me.core_peer()])
    for copy in local:
        copy.wait()

    small_out = [
        remote(small, smalls.at[z], small_sem, k - 1, me.at_z((z + k) % deep))
        for k in range(1, deep)
    ]
    for copy in small_out:
        copy.start()

    def relay(buffer, ups_sem, dns_sem, sides_sem):
        def piece(source, by):
            return buffer.at[source, pl.ds(pl.multiple_of(by * half, half), half)]

        def hop_up(source, at):
            return remote(piece(source, x), piece(source, x), ups_sem, at, me.at_z(jnp.minimum(z + 1, deep - 1)))

        def hop_dn(source, at):
            return remote(piece(source, x), piece(source, x), dns_sem, at, me.at_z(jnp.maximum(z - 1, 0)))

        def hop_side(source, at):
            return remote(piece(source, x), piece(source, x), sides_sem, at, me.x_peer())

        def begin():
            @pl.when(z < deep - 1)
            def _():
                hop_up(z, 0).start()

            @pl.when(z > 0)
            def _():
                hop_dn(z, 0).start()

        def step_on(s):
            @pl.when(z - 1 - s >= 0)
            def _():
                source = z - 1 - s
                hop_up(source, s).wait_recv()

                @pl.when(z < deep - 1)
                def _():
                    hop_up(source, s + 1).start()

                hop_side(source, s).start()

            @pl.when(z + 1 + s < deep)
            def _():
                source = z + 1 + s
                hop_dn(source, s).wait_recv()

                @pl.when(z > 0)
                def _():
                    hop_dn(source, s + 1).start()

                hop_side(source, deep - 1 + s).start()

        def finish():
            for s in range(deep - 1):
                @pl.when(z - 1 - s >= 0)
                def _():
                    source = z - 1 - s
                    copy = remote(piece(source, x), piece(source, 1 - x), sides_sem, s, me.x_peer())
                    copy.wait_recv()

                @pl.when(z + 1 + s < deep)
                def _():
                    source = z + 1 + s
                    copy = remote(
                        piece(source, x), piece(source, 1 - x), sides_sem, deep - 1 + s, me.x_peer()
                    )
                    copy.wait_recv()

        def drain():
            for s in range(deep):
                @pl.when((z - s >= 0) & (z < deep - 1))
                def _():
                    hop_up(z - s, s).wait_send()

                @pl.when((z + s < deep) & (z > 0))
                def _():
                    hop_dn(z + s, s).wait_send()

            for s in range(deep - 1):
                @pl.when(z - 1 - s >= 0)
                def _():
                    hop_side(z - 1 - s, s).wait_send()

                @pl.when(z + 1 + s < deep)
                def _():
                    hop_side(z + 1 + s, deep - 1 + s).wait_send()

        return begin, step_on, finish, drain

    begin1, step1, finish1, drain1 = relay(wqkv, up_sem, dn_sem, side_sem)
    begin2, step2, finish2, drain2 = relay(wout, up_sem2, dn_sem2, side_sem2)
    begin1()

    for tree in range(trees):
        seen, cosine, sine = tree_tables(
            starts, parents, tree, x * rows, rows, length, frequency[:1, :]
        )
        mask[tree] = seen
        tables[0, tree] = cosine
        tables[1, tree] = sine
    step1(0)
    step1(1)
    for k in range(1, deep):
        source = (z + deep - k) % deep
        remote(small, smalls.at[source], small_sem, k - 1, me.at_z(source)).wait_recv()
    gain_one = jnp.concatenate([smalls[k, :1, :] for k in range(deep)], 1).astype(F32)
    gain_two = jnp.concatenate([smalls[k, 1:2, :] for k in range(deep)], 1).astype(F32)
    router = jnp.concatenate([smalls[k, 8:, :] for k in range(deep)], 1)

    def first_norm(at, carry):
        tree, row = at // CHUNKS, pl.multiple_of(at % CHUNKS * step, step)
        value = tokens[tree, pl.ds(row, step), :].astype(F32)
        factor = lax.rsqrt(jnp.mean(value * value, -1, keepdims=True) + EPS)
        hid_one[tree, pl.ds(row, step), :] = (value * factor * gain_one).astype(BF16)
        return carry

    lax.fori_loop(0, trees * CHUNKS, first_norm, 0)
    step1(2)
    begin2()
    finish1()

    for tree in range(trees):
        total = jnp.zeros((rows, wqkv.shape[2]), F32)
        for k in range(deep):
            total = total + mm(hid_one[tree, :, pl.ds(k * shard, shard)], wqkv[k])
        cosine, sine = tables[0, tree], tables[1, tree]
        for head in range(heads):
            part_q = total[:, head * HEAD_SIZE : (head + 1) * HEAD_SIZE]
            queries[tree, head] = turn(part_q, cosine, sine).astype(BF16)
        part_k = total[:, heads * HEAD_SIZE : (heads + 1) * HEAD_SIZE]
        own = pl.ds(pl.multiple_of(x * rows, rows), rows)
        keys[tree, own, :] = turn(part_k, cosine, sine).astype(BF16)
        values[tree, own, :] = total[:, (heads + 1) * HEAD_SIZE :].astype(BF16)
        for which, array in enumerate((keys, values)):
            remote(
                array.at[tree, own], array.at[tree, own], kv_sem, 2 * tree + which, me.x_peer()
            ).start()
    step2(0)
    away = pl.ds(pl.multiple_of((1 - x) * rows, rows), rows)
    for tree in range(trees):
        for which, array in enumerate((keys, values)):
            remote(
                array.at[tree, away], array.at[tree, away], kv_sem, 2 * tree + which, me.x_peer()
            ).wait_recv()

    def attend(tree):
        def one(head, carry):
            score = mm(queries[tree, head], keys[tree], NT) * inv_root
            score = jnp.where(mask[tree] > 0.5, score, NEG)
            top = jnp.max(score, -1, keepdims=True)
            raised = jnp.exp(score - top)
            prob = raised / jnp.sum(raised, -1, keepdims=True)
            prob = prob.astype(BF16)
            probs[tree, head] = prob
            seen = mm(prob, values[tree])
            context[tree, head] = seen.astype(BF16)
            return carry

        lax.fori_loop(0, heads, one, 0)

    attend(0)
    step2(1)
    attend(1)
    step2(2)
    finish2()

    own_up = remote(cotangent.at[c], ups.at[c, x], cot_x_sem, 0, me.x_peer())
    own_up.start()

    def project(tree, row):
        pieces = []
        for k in range(deep):
            piece = jnp.zeros((step, shard), F32)
            for head in range(heads):
                piece = piece + mm(
                    context[tree, head, pl.ds(row, step), :],
                    wout[k, pl.ds(head * HEAD_SIZE, HEAD_SIZE), :],
                )
            pieces.append(piece)
        return pieces

    def spread(k):
        return pl.ds(k * shard, shard)

    def away_rows(chunk):
        return part.at[pl.ds(chunk * step, step)]

    def core_copy(chunk):
        return remote(
            away_rows(chunk), core_in.at[pl.ds(chunk * step, step)], core_sem, chunk, me.core_peer()
        )

    for chunk in range(CHUNKS):
        for k, piece in enumerate(project(1 - c, chunk * step)):
            part[pl.ds(chunk * step, step), spread(k)] = piece.astype(BF16)
        core_copy(chunk).start()

    def y_copy(chunk):
        at = pl.ds(chunk * step, step)
        return remote(y_out.at[at], y_in.at[at], y_sem, chunk, me.y_peer())

    for chunk in range(CHUNKS):
        pieces = project(c, chunk * step)
        core_copy(chunk).wait_recv()
        for k, piece in enumerate(pieces):
            both = piece.astype(BF16).astype(F32) + core_in[
                pl.ds(chunk * step, step), spread(k)
            ].astype(F32)
            y_out[pl.ds(chunk * step, step), spread(k)] = both.astype(BF16)
        y_copy(chunk).start()

    def two_copy(which, sems, chunk, device):
        at = hid_two.at[c, which, pl.ds(chunk * step, step)]
        return remote(at, at, sems, chunk, device)

    for chunk in range(CHUNKS):
        y_copy(chunk).wait_recv()
        at = pl.ds(chunk * step, step)
        value = tokens[c, at, :].astype(F32) + (y_out[at, :].astype(F32) + y_in[at, :].astype(F32))
        after[at, :] = value
        factor = lax.rsqrt(jnp.mean(value * value, -1, keepdims=True) + EPS)
        hid_two[c, x, at, :] = (value * factor * gain_two).astype(BF16)
        two_copy(x, hx_sem, chunk, me.x_peer()).start()
        two_copy(x, hc_sem, chunk, me.core_peer()).start()

    logits = mm(router, hid_two[c, x], NT)
    expert = lax.broadcasted_iota(jnp.int32, logits.shape, 0)
    chosen = expert < 0
    for k in range(routes.shape[1]):
        chosen = chosen | (expert == routes[c, k : k + 1, :])
    logits = jnp.where(chosen, logits, NEG)
    raised = jnp.where(chosen, jnp.exp(logits - jnp.max(logits, 0, keepdims=True)), 0.0)
    mixes[c, x] = raised / jnp.sum(raised, 0, keepdims=True)
    own_mix = mixes.at[c, x]
    mix_x = remote(own_mix, own_mix, mix_sem, 0, me.x_peer())
    mix_c = remote(own_mix, own_mix, mix_sem, 1, me.core_peer())
    mix_x.start()
    mix_c.start()

    up_away = ups.at[c, 1 - x]
    remote(cotangent.at[c], up_away, cot_x_sem, 0, me.x_peer()).wait_recv()
    up_on = remote(up_away, up_away, cot_f_sem, 0, me.core_peer())
    up_on.start()
    for chunk in range(CHUNKS):
        two_copy(1 - x, hx_sem, chunk, me.x_peer()).wait_recv()
        two_copy(1 - x, hf_sem, chunk, me.core_peer()).start()
    mix_away = mixes.at[c, 1 - x]
    remote(mix_away, mix_away, mix_sem, 0, me.x_peer()).wait_recv()
    mix_on = remote(mix_away, mix_away, mix_sem, 2, me.core_peer())
    mix_on.start()

    up_peer = ups.at[1 - c, 1 - x]
    remote(up_peer, up_peer, cot_f_sem, 0, me.core_peer()).wait_recv()
    for chunk in range(CHUNKS):
        for which, sems in ((x, hc_sem), (1 - x, hf_sem)):
            at = hid_two.at[1 - c, which, pl.ds(chunk * step, step)]
            remote(at, at, sems, chunk, me.core_peer()).wait_recv()
    for which, number in ((x, 1), (1 - x, 2)):
        at = mixes.at[1 - c, which]
        remote(at, at, mix_sem, number, me.core_peer()).wait_recv()

    for copy in small_out + [own_up, up_on, mix_x, mix_c, mix_on]:
        copy.wait_send()
    drain1()
    drain2()
    for tree in range(trees):
        for which, array in enumerate((keys, values)):
            own = pl.ds(pl.multiple_of(x * rows, rows), rows)
            remote(
                array.at[tree, own], array.at[tree, own], kv_sem, 2 * tree + which, me.x_peer()
            ).wait_send()
    for chunk in range(CHUNKS):
        core_copy(chunk).wait_send()
        y_copy(chunk).wait_send()
        two_copy(x, hx_sem, chunk, me.x_peer()).wait_send()
        two_copy(x, hc_sem, chunk, me.core_peer()).wait_send()
        two_copy(1 - x, hf_sem, chunk, me.core_peer()).wait_send()


def sems(count):
    return pltpu.SemaphoreType.DMA((2, count))


def attend_call(seg_start, seg_parent, tokens, cotangent, routes, w_query, w_key, w_value, w_output, small, deep):
    trees, rows, width = tokens.shape
    shard, mine = w_query.shape
    heads = mine // HEAD_SIZE
    length = rows * 2
    experts = small.shape[0] - 8
    half = HEAD_SIZE // 2
    frequency = ROPE_BASE ** (-2.0 * np.arange(half, dtype=np.float32) / np.float32(HEAD_SIZE))
    frequency = jnp.asarray(np.tile(np.concatenate([frequency] * 2)[None], (8, 1)).astype(np.float32))
    vmem = pl.BlockSpec(memory_space=pltpu.VMEM)
    smem = pl.BlockSpec(memory_space=pltpu.SMEM)

    def out(shape, dtype):
        return jax.ShapeDtypeStruct(shape, dtype)

    return pl.pallas_call(
        attend_kernel,
        out_shape=(
            out((trees, rows, width), BF16),
            out((deep, shard, mine + 2 * HEAD_SIZE), BF16),
            out((deep, mine, shard), BF16),
            out((deep,) + small.shape, BF16),
            out((trees, heads, rows, HEAD_SIZE), BF16),
            out((trees, length, HEAD_SIZE), BF16),
            out((trees, length, HEAD_SIZE), BF16),
            out((trees, heads, rows, length), BF16),
            out((trees, heads, rows, HEAD_SIZE), BF16),
            out((2, trees, rows, HEAD_SIZE), F32),
            out((rows, width), F32),
            out((trees, 2, rows, width), BF16),
            out((trees, 2, rows, width), BF16),
            out((trees, 2, experts, rows), F32),
        ),
        in_specs=[smem, smem] + [vmem] * 9,
        out_specs=[vmem] * 14,
        scratch_shapes=[
            pltpu.VMEM((trees, rows, length), F32),
            pltpu.VMEM((rows, width), BF16),
            pltpu.VMEM((rows, width), BF16),
            pltpu.VMEM((rows, width), BF16),
            pltpu.VMEM((rows, width), BF16),
            pltpu.SemaphoreType.DMA((7,)),
            sems(deep - 1),
            sems(deep),
            sems(deep),
            sems(2 * deep - 2),
            sems(deep),
            sems(deep),
            sems(2 * deep - 2),
            sems(2 * trees),
            sems(1),
            sems(1),
            sems(1),
            sems(CHUNKS),
            sems(CHUNKS),
            sems(CHUNKS),
            sems(CHUNKS),
            sems(CHUNKS),
            sems(3),
        ],
        compiler_params=pltpu.CompilerParams(
            collective_id=0, has_side_effects=True, vmem_limit_bytes=60 * 2**20
        ),
        name="attend",
    )(seg_start, seg_parent, frequency, tokens, cotangent, routes, w_query, w_key, w_value, w_output, small)


ROOT_2_PI = math.sqrt(2.0 / math.pi)
CUBIC = 0.044715


def expert_acts(mats, hid, ups, mixes, acts, gates, group, held, x, quarter):
    blocks, rows = mixes.shape[0], mixes.shape[2]
    units = held * quarter
    local = mixes.shape[1] // 2
    base = group * held

    def mat(kind):
        return mats[pl.ds((3 * group + kind) * units, units), :]

    def block(at, carry):
        first = pl.multiple_of(at * rows, rows)
        tokens = pl.ds(first, rows)
        hidden_rows = hid[tokens, :]
        pre_gate = mm(mat(0), hidden_rows, NT)
        pre_up = mm(mat(1), hidden_rows, NT)
        back = mm(mat(2), ups[tokens, :], NT)
        own = jnp.where(x == 0, mixes[at, :local, :], mixes[at, local:, :])
        weight = jnp.concatenate(
            [
                jnp.broadcast_to(own[base + i : base + i + 1, :], (quarter, rows))
                for i in range(held)
            ],
            0,
        )
        square = pre_gate * pre_gate
        bent = jnp.tanh(ROOT_2_PI * pre_gate * (1.0 + CUBIC * square))
        slope = 0.5 * (1.0 + bent)
        active = pre_gate * slope
        rise = slope + 0.5 * pre_gate * (1.0 - bent * bent) * ROOT_2_PI * (
            1.0 + 3.0 * CUBIC * square
        )
        hidden = active * pre_up
        share = hidden * back
        for i in range(held):
            gates[pl.ds(i, 1), tokens] = jnp.sum(
                share[i * quarter : (i + 1) * quarter], 0, keepdims=True
            )
        back = weight * back
        acts[3 * group + 0, :, tokens] = (back * pre_up * rise).astype(BF16)
        acts[3 * group + 1, :, tokens] = (back * active).astype(BF16)
        acts[3 * group + 2, :, tokens] = (weight * hidden).astype(BF16)
        return carry

    lax.fori_loop(0, blocks, block, 0)


class Chain:
    def __init__(self, me, stage, from_dn, from_up, dn_sems, up_sems, tile):
        self.me, self.stage, self.tile = me, stage, tile
        self.from_dn, self.from_up = from_dn, from_up
        self.dn_sems, self.up_sems = dn_sems, up_sems
        self.deep, self.count = stage.shape[0], stage.shape[1]

    def rise(self, target, m):
        up = jnp.minimum(self.me.z + 1, self.deep - 1)
        return remote(
            self.stage.at[target, m],
            self.from_dn.at[target - 1, m],
            self.dn_sems,
            (target - 1) * self.count + m,
            self.me.at_z(up),
        )

    def fall(self, target, m):
        down = jnp.maximum(self.me.z - 1, 0)
        return remote(
            self.stage.at[target, m],
            self.from_up.at[target, m],
            self.up_sems,
            target * self.count + m,
            self.me.at_z(down),
        )

    def add(self, target, m, landed):
        def step(at, carry):
            rows = pl.ds(pl.multiple_of(at * self.tile, self.tile), self.tile)
            total = self.stage[target, m, rows, :].astype(F32) + landed[rows, :].astype(F32)
            self.stage[target, m, rows, :] = total.astype(BF16)
            return carry

        lax.fori_loop(0, self.stage.shape[2] // self.tile, step, 0)

    def begin(self, m):
        for k in range(self.deep - 1):

            @pl.when(self.me.z == 0)
            def _():
                self.rise(self.deep - 1 - k, m).start()

            @pl.when(self.me.z == self.deep - 1)
            def _():
                self.fall(k, m).start()

    def advance(self, m, steps=None):
        z = self.me.z
        for k in range(self.deep - 1) if steps is None else steps:
            far, near = self.deep - 1 - k, k

            @pl.when((z >= 1) & (z < far))
            def _():
                self.rise(far, m).wait_recv()
                self.add(far, m, self.from_dn.at[far - 1, m])
                self.rise(far, m).start()

            @pl.when((z < self.deep - 1) & (z > near))
            def _():
                self.fall(near, m).wait_recv()
                self.add(near, m, self.from_up.at[near, m])
                self.fall(near, m).start()

    def finish(self, m, write):
        z = self.me.z

        @pl.when(z > 0)
        def _():
            self.rise(jnp.maximum(z, 1), m).wait_recv()

        @pl.when(z < self.deep - 1)
        def _():
            self.fall(jnp.minimum(z, self.deep - 2), m).wait_recv()

        below, above = jnp.maximum(z - 1, 0), jnp.minimum(z, self.deep - 2)

        def step(at, carry):
            rows = pl.ds(pl.multiple_of(at * self.tile, self.tile), self.tile)
            own = self.stage[z, m, rows, :].astype(F32)
            lower = self.from_dn[below, m, rows, :].astype(F32)
            upper = self.from_up[above, m, rows, :].astype(F32)
            total = own + jnp.where(z > 0, lower, 0.0) + jnp.where(z < self.deep - 1, upper, 0.0)
            write(rows, total)
            return carry

        lax.fori_loop(0, self.stage.shape[2] // self.tile, step, 0)

    def drain(self, m):
        z = self.me.z
        for k in range(self.deep - 1):
            far, near = self.deep - 1 - k, k

            @pl.when(z < far)
            def _():
                self.rise(far, m).wait_send()

            @pl.when(z > near)
            def _():
                self.fall(near, m).wait_send()


def expert_grads(which, group, acts, rows_of, stage):
    columns = stage.shape[3]

    def shard(k, carry):
        at = pl.ds(pl.multiple_of(k * columns, columns), columns)
        stage[k, which] = mm(acts[3 * group + which], rows_of[:, at]).astype(BF16)
        return carry

    lax.fori_loop(0, stage.shape[0], shard, 0)


def experts_kernel(
    quarter,
    mats,
    hid,
    ups,
    mixes,
    acts,
    gates,
    grads,
    stage,
    from_dn,
    from_up,
    dn_sems,
    up_sems,
):
    me = Place()
    deep = stage.shape[0]
    greet([me.at_z((me.z + k) % deep) for k in range(1, deep)])
    chain = Chain(me, stage, from_dn, from_up, dn_sems, up_sems, 64)
    gates[...] = jnp.zeros_like(gates)
    expert_acts(mats, hid, ups, mixes, acts, gates, 0, 2, me.x, quarter)
    for m in range(3):
        expert_grads(m, 0, acts, ups if m == 2 else hid, stage)
        chain.begin(m)

    for m in range(3):
        chain.advance(m)

    for m in range(3):

        def write(rows, value):
            grads[m, rows, :] = value

        chain.finish(m, write)

    for m in range(3):
        chain.drain(m)


def experts_call(mats, hid, ups, mixes, deep):
    units, width = mats.shape[0] // 3, mats.shape[1]
    tokens = hid.shape[0]
    columns = width // deep
    quarter = units // 2
    vmem = pl.BlockSpec(memory_space=pltpu.VMEM)
    return pl.pallas_call(
        functools.partial(experts_kernel, quarter),
        out_shape=(
            jax.ShapeDtypeStruct((3, units, tokens), BF16),
            jax.ShapeDtypeStruct((8, tokens), F32),
            jax.ShapeDtypeStruct((3, units, columns), F32),
        ),
        in_specs=[vmem] * 4,
        out_specs=[vmem] * 3,
        scratch_shapes=[
            pltpu.VMEM((deep, 3, units, columns), BF16),
            pltpu.VMEM((deep - 1, 3, units, columns), BF16),
            pltpu.VMEM((deep - 1, 3, units, columns), BF16),
            sems((deep - 1) * 3),
            sems((deep - 1) * 3),
        ],
        compiler_params=pltpu.CompilerParams(
            collective_id=1, has_side_effects=True, vmem_limit_bytes=60 * 2**20
        ),
        name="experts",
    )(mats, hid, ups, mixes)


class PlaneSum:
    def __init__(self, me, rows, tile, bufs, landing, sem_set):
        self.me, self.rows, self.tile = me, rows, tile
        self.core_out, self.x_out, self.acc, self.y_out = bufs
        self.core_in, self.x_in, self.y_in = landing
        self.core_sems, self.x_sems, self.y_sems = sem_set
        self.tiles = rows // tile
        self.step = rows // CHUNKS
        self.per_tile = tile // self.step

    def at(self, number, size):
        return pl.ds(pl.multiple_of(number * size, size), size)

    def core_copy(self, number):
        at = self.at(number, self.tile)
        return remote(
            self.core_out.at[at], self.core_in.at[at], self.core_sems, number, self.me.core_peer()
        )

    def x_copy(self, number):
        at = self.at(number, self.step)
        return remote(self.x_out.at[at], self.x_in.at[at], self.x_sems, number, self.me.x_peer())

    def y_copy(self, number):
        at = self.at(number, self.step)
        return remote(self.y_out.at[at], self.y_in.at[at], self.y_sems, number, self.me.y_peer())

    def first(self, tree, x, number):
        return pl.multiple_of((tree * 2 + x) * self.rows + number * self.tile, self.tile)

    def outward(self, make):
        me = self.me

        def one(number, carry):
            x = jnp.where(number < self.tiles, 1 - me.x, me.x)
            value = make(self.first(1 - me.c, x, number % self.tiles))
            self.core_out[self.at(number, self.tile), :] = value.astype(BF16)
            self.core_copy(number).start()
            return carry

        lax.fori_loop(0, 2 * self.tiles, one, 0)

    def across(self, make):
        me = self.me

        def one(number, carry):
            value = make(self.first(me.c, 1 - me.x, number)).astype(BF16).astype(F32)
            self.core_copy(number).wait_recv()
            at = self.at(number, self.tile)
            self.x_out[at, :] = (value + self.core_in[at, :].astype(F32)).astype(BF16)
            for k in range(self.per_tile):
                self.x_copy(number * self.per_tile + k).start()
            return carry

        lax.fori_loop(0, self.tiles, one, 0)

    def inward(self, make):
        me = self.me

        def one(number, carry):
            value = make(self.first(me.c, me.x, number)).astype(BF16).astype(F32)
            self.core_copy(self.tiles + number).wait_recv()
            self.acc[self.at(number, self.tile), :] = value + self.core_in[
                self.at(self.tiles + number, self.tile), :
            ].astype(F32)
            return carry

        lax.fori_loop(0, self.tiles, one, 0)

    def pass_on(self):
        def one(number, carry):
            at = self.at(number, self.step)
            self.x_copy(number).wait_recv()
            self.y_out[at, :] = (self.acc[at, :] + self.x_in[at, :].astype(F32)).astype(BF16)
            self.y_copy(number).start()
            return carry

        lax.fori_loop(0, CHUNKS, one, 0)

    def total(self, number):
        at = self.at(number, self.step)
        self.y_copy(number).wait_recv()
        return self.y_out[at, :].astype(F32) + self.y_in[at, :].astype(F32)

    def drain(self):
        for number in range(2 * self.tiles):
            self.core_copy(number).wait_send()
        for number in range(CHUNKS):
            self.x_copy(number).wait_send()
            self.y_copy(number).wait_send()


def rest_kernel(
    quarter,
    mats_a,
    mats_b,
    acts_a,
    gates_a,
    hid_in,
    ups_in,
    mixes,
    hid_one_in,
    tokens_in,
    wqkv_in,
    wout_in,
    smalls,
    queries_in,
    keys_in,
    values_in,
    probs_in,
    context_in,
    tables_in,
    after_in,
    mixed,
    d_tokens,
    grads,
    d_qo,
    d_kv,
    d_small,
    mats,
    acts,
    hid,
    ups,
    wqkv,
    wout,
    queries,
    keys,
    values,
    probs,
    context,
    tables,
    after,
    gates_b,
    gates_out,
    gates_in,
    core_out,
    x_out,
    acc,
    y_out,
    two_core_in,
    two_x_in,
    two_y_in,
    mo_core_in,
    mo_x_in,
    mo_y_in,
    one_core_in,
    one_y_in,
    agrad,
    alow,
    qlow,
    kv_out,
    kv_in,
    kv_own,
    kvx_out,
    kvx_in,
    kvlow,
    dkv_out,
    dkv_in,
    xs_out,
    xs_in,
    stage,
    from_dn,
    from_up,
    stage2,
    from_dn2,
    from_up2,
    small_own,
    small_core,
    small_x,
    small_z,
    kv_last,
    load_sem,
    gate_sem,
    two_core_sem,
    two_x_sem,
    two_y_sem,
    mo_core_sem,
    mo_x_sem,
    mo_y_sem,
    one_core_sem,
    one_y_sem,
    low_sem,
    kv_sem,
    kvx_sem,
    dkv_sem,
    xs_sem,
    dn_sem,
    up_sem,
    dn_sem2,
    up_sem2,
    out_sem,
    mixed_sem,
    token_sem,
    small_c_sem,
    small_x_sem,
    small_z_sem,
    last_sem,
):
    me = Place()
    z, x, y, c = me.z, me.x, me.y, me.c
    deep, shard = wqkv.shape[0], wqkv.shape[1]
    trees, heads, rows, length = probs.shape
    width = hid.shape[1]
    units = acts.shape[1]
    mine = heads * HEAD_SIZE
    half = shard // 2
    inv_root = HEAD_SIZE ** (-0.5)
    step = rows // CHUNKS
    tile = 128
    own_block = c * 2 + x
    own_rows = pl.ds(pl.multiple_of(own_block * rows, rows), rows)

    def load(source, target, at):
        return pltpu.make_async_copy(source, target, load_sem.at[at])

    loads = [
        load(mats_b, mats.at[pl.ds(3 * units, 3 * units)], 0),
        load(hid_in, hid, 1),
        load(ups_in, ups, 2),
        load(mats_a, mats.at[pl.ds(0, 3 * units)], 3),
        load(acts_a, acts.at[pl.ds(0, 3)], 4),
        load(after_in, after, 5),
        load(wqkv_in, wqkv, 6),
        load(wout_in, wout, 7),
        load(queries_in, queries, 8),
        load(keys_in, keys, 9),
        load(values_in, values, 10),
        load(probs_in, probs, 11),
        load(context_in, context, 12),
        load(tables_in, tables, 13),
    ]
    for copy in loads:
        copy.start()

    lin = x * 4 + me.t

    def plane(number):
        return (z, number // 4, number % 4)

    greet(
        [me.at_z((z + k) % deep) for k in range(1, deep)]
        + [plane((lin + k) % 8) for k in range(1, 8)]
    )
    for copy in loads[:3]:
        copy.wait()

    gates_b[...] = jnp.zeros_like(gates_b)
    expert_acts(mats, hid, ups, mixes, acts, gates_b, 1, 2, x, quarter)
    for copy in loads[3:]:
        copy.wait()

    for block in range(2 * trees):
        at = pl.ds(block * rows, rows)
        gates_out[block] = jnp.concatenate(
            [gates_a[:2, at], gates_b[:2, at], jnp.zeros((4, rows), F32)], 0
        )

    def gate_copy(k):
        there = (lin + k) % 8
        block = (there % 2) * 2 + there // 4
        return remote(gates_out.at[block], gates_in.at[lin], gate_sem, k - 1, plane(there))

    for k in range(1, 8):
        gate_copy(k).start()
    gates_in[lin] = gates_out[own_block]

    def mat(group, kind):
        return mats[pl.ds((3 * group + kind) * units, units), :]

    def two_tile(first):
        at = pl.ds(first, tile)
        total = mm(acts[0, :, at], mat(0, 0), TN)
        total = total + mm(acts[1, :, at], mat(0, 1), TN)
        total = total + mm(acts[3, :, at], mat(1, 0), TN)
        return total + mm(acts[4, :, at], mat(1, 1), TN)

    def mo_tile(first):
        at = pl.ds(first, tile)
        return mm(acts[2, :, at], mat(0, 2), TN) + mm(acts[5, :, at], mat(1, 2), TN)

    two = PlaneSum(
        me,
        rows,
        tile,
        (core_out, x_out, acc, y_out),
        (two_core_in, two_x_in, two_y_in),
        (two_core_sem, two_x_sem, two_y_sem),
    )
    two.outward(two_tile)
    two.across(two_tile)
    two.inward(two_tile)

    chain = Chain(me, stage, from_dn, from_up, dn_sem, up_sem, 64)
    for m in range(3):
        expert_grads(m, 1, acts, ups if m == 2 else hid, stage)
        chain.begin(m)

    for k in range(1, 8):
        source = (lin + 8 - k) % 8
        remote(gates_out.at[0], gates_in.at[source], gate_sem, k - 1, plane(source)).wait_recv()
    sums = []
    for side in range(2):
        total = gates_in[side * 4]
        for k in range(1, 4):
            total = total + gates_in[side * 4 + k]
        sums.append(total[:4])
    mix_grad = jnp.concatenate(sums, 0)
    mix = mixes[own_block]
    picked = mix * (mix_grad - jnp.sum(mix * mix_grad, 0, keepdims=True))
    logit_grad = picked.astype(BF16)
    router = jnp.concatenate([smalls[k, 8:, :] for k in range(deep)], 1)
    gain_one = jnp.concatenate([smalls[k, :1, :] for k in range(deep)], 1).astype(F32)
    gain_two = jnp.concatenate([smalls[k, 1:2, :] for k in range(deep)], 1).astype(F32)
    agrad[...] = mm(logit_grad, router, TN)
    small_own[pl.ds(0, 8), :] = jnp.zeros((8, width), F32)
    small_own[pl.ds(8, 8), :] = mm(logit_grad, hid[own_rows, :])

    for number in range(2 * two.tiles):
        two.core_copy(number).wait_send()
    mo = PlaneSum(
        me,
        rows,
        tile,
        (core_out, hid.at[pl.ds(rows, rows)], acc, hid.at[pl.ds(0, rows)]),
        (mo_core_in, mo_x_in, mo_y_in),
        (mo_core_sem, mo_x_sem, mo_y_sem),
    )
    mo.outward(mo_tile)
    mo.across(mo_tile)
    two.pass_on()
    mo.inward(mo_tile)
    late = [
        load(hid_one_in.at[0], mats.at[pl.ds(0, rows)], 0),
        load(hid_one_in.at[1], mats.at[pl.ds(rows, rows)], 1),
        load(tokens_in.at[c], mats.at[pl.ds(2 * rows, rows)], 2),
    ]
    for copy in late:
        copy.start()

    def low_copy(number):
        at = alow.at[c, pl.ds(pl.multiple_of(number * step, step), step)]
        return remote(at, at, low_sem, number, me.core_peer())

    def second_norm(number, gain_grad):
        at = pl.ds(pl.multiple_of(number * step, step), step)
        upstream = two.total(number) + agrad[at, :]
        value = after[at, :]
        factor = lax.rsqrt(jnp.mean(value * value, -1, keepdims=True) + EPS)
        scaled = upstream * gain_two
        inner = jnp.mean(scaled * value, -1, keepdims=True)
        cot = ups[pl.ds(pl.multiple_of(own_block * rows + number * step, step), step), :]
        total = cot.astype(F32) + (factor * scaled - value * (factor * factor * factor * inner))
        agrad[at, :] = total
        alow[c, at, :] = total.astype(BF16)
        low_copy(number).start()
        return gain_grad + jnp.sum(upstream * value * factor, 0, keepdims=True)

    gain_two_grad = lax.fori_loop(0, CHUNKS, second_norm, jnp.zeros((1, width), F32))
    small_own[pl.ds(1, 1), :] = gain_two_grad
    mo.pass_on()

    def attend_back(tree):
        back = jnp.zeros((rows, mine), F32)
        for k in range(deep):
            back = back + mm(alow[tree, :, pl.ds(k * shard, shard)], wout[k], NT)
        back = back.astype(BF16)
        cosine, sine = tables[0, tree], tables[1, tree]
        key_grad = jnp.zeros((length, HEAD_SIZE), F32)
        value_grad = jnp.zeros((length, HEAD_SIZE), F32)
        for head in range(heads):
            lanes = pl.ds(head * HEAD_SIZE, HEAD_SIZE)
            back_head = back[:, head * HEAD_SIZE : (head + 1) * HEAD_SIZE]
            prob = probs[tree, head]
            value_grad = value_grad + mm(prob, back_head, TN)
            prob = prob.astype(F32)
            share = prob * mm(back_head, values[tree], NT)
            score = (share - prob * jnp.sum(share, -1, keepdims=True)).astype(BF16)
            query_grad = mm(score, keys[tree]) * inv_root
            qlow[tree, :, lanes] = turn(query_grad, cosine, -sine).astype(BF16)
            key_grad = key_grad + mm(score, queries[tree, head], TN)
        return jnp.concatenate([key_grad * inv_root, value_grad], 1)

    kv_own[...] = attend_back(c)
    for number in range(CHUNKS):
        at = alow.at[1 - c, pl.ds(number * step, step)]
        remote(at, at, low_sem, number, me.core_peer()).wait_recv()
    kv_out[...] = attend_back(1 - c).astype(BF16)
    kv_copy = remote(kv_out, kv_in, kv_sem, 0, me.core_peer())
    kv_copy.start()
    chain.advance(0)

    def one_tile(tree, number):
        at = pl.ds(pl.multiple_of(number * step, step), step)
        return [mm(qlow[tree, at, :], wqkv[k, :, pl.ds(0, mine)], NT) for k in range(deep)]

    one_out = core_out.at[pl.ds(0, rows)]
    for number in range(2 * mo.tiles):
        mo.core_copy(number).wait_send()

    def one_copy(number):
        at = pl.ds(pl.multiple_of(number * step, step), step)
        return remote(one_out.at[at], one_core_in.at[at], one_core_sem, number, me.core_peer())

    def one_outward(number, carry):
        at = pl.ds(pl.multiple_of(number * step, step), step)
        for k, piece in enumerate(one_tile(1 - c, number)):
            one_out[at, pl.ds(k * shard, shard)] = piece.astype(BF16)
        one_copy(number).start()
        return carry

    lax.fori_loop(0, CHUNKS, one_outward, 0)

    kv_copy.wait_recv()
    kvx_out[...] = (
        jnp.where(x == 0, kv_own[pl.ds(rows, rows), :], kv_own[pl.ds(0, rows), :])
        + jnp.where(x == 0, kv_in[pl.ds(rows, rows), :], kv_in[pl.ds(0, rows), :]).astype(F32)
    ).astype(BF16)
    kvx_copy = remote(kvx_out, kvx_in, kvx_sem, 0, me.x_peer())
    kvx_copy.start()

    for copy in late:
        copy.wait()

    def hid_one(tree, lanes):
        return mats[pl.ds(pl.multiple_of(tree * rows, rows), rows), lanes]

    def halves(value):
        low, high = value[:half], value[half:]
        return jnp.where(x == 0, low, high), jnp.where(x == 0, high, low)

    ctx = [
        jnp.concatenate([context[tree, head] for head in range(heads)], 1) for tree in range(trees)
    ]

    def xs_copy(part):
        lanes = (pl.ds(0, mine), pl.ds(mine, mine), pl.ds(2 * mine, HEAD_SIZE))[part]
        return remote(xs_out.at[:, :, lanes], xs_in.at[:, :, lanes], xs_sem, part, me.x_peer())

    def shard_lanes(k):
        return pl.ds(pl.multiple_of(k * shard, shard), shard)

    def output_grad(k, carry):
        value = sum(mm(alow[tree, :, shard_lanes(k)], ctx[tree], TN) for tree in range(trees))
        keep, away = halves(value)
        stage2[k, 0, :, pl.ds(mine, mine)] = keep.astype(BF16)
        xs_out[k, :, pl.ds(mine, mine)] = away.astype(BF16)
        return carry

    lax.fori_loop(0, deep, output_grad, 0)
    xs_copy(1).start()

    def query_weight_grad(k, carry):
        value = sum(mm(hid_one(tree, shard_lanes(k)), qlow[tree], TN) for tree in range(trees))
        keep, away = halves(value)
        stage2[k, 0, :, pl.ds(0, mine)] = keep.astype(BF16)
        xs_out[k, :, pl.ds(0, mine)] = away.astype(BF16)
        return carry

    lax.fori_loop(0, deep, query_weight_grad, 0)
    xs_copy(0).start()

    kvx_copy.wait_recv()
    own_kv = (
        jnp.where(x == 0, kv_own[pl.ds(0, rows), :], kv_own[pl.ds(rows, rows), :])
        + jnp.where(x == 0, kv_in[pl.ds(0, rows), :], kv_in[pl.ds(rows, rows), :]).astype(F32)
        + kvx_in[...].astype(F32)
    )
    kvlow[:, pl.ds(0, HEAD_SIZE)] = turn(
        own_kv[:, :HEAD_SIZE], tables[0, c], -tables[1, c]
    ).astype(BF16)
    kvlow[:, pl.ds(HEAD_SIZE, HEAD_SIZE)] = own_kv[:, HEAD_SIZE:].astype(BF16)

    for number in range(CHUNKS):
        two.y_copy(number).wait_send()

    def y_copy(number):
        at = pl.ds(pl.multiple_of(number * step, step), step)
        return remote(y_out.at[at], one_y_in.at[at], one_y_sem, number, me.y_peer())

    def one_inward(number, carry):
        at = pl.ds(pl.multiple_of(number * step, step), step)
        one_copy(number).wait_recv()
        for k, piece in enumerate(one_tile(c, number)):
            lanes = pl.ds(k * shard, shard)
            piece = piece + mm(kvlow[at, :], wqkv[k, :, pl.ds(mine, 2 * HEAD_SIZE)], NT)
            y_out[at, lanes] = (piece + one_core_in[at, lanes].astype(F32)).astype(BF16)
        y_copy(number).start()
        return carry

    lax.fori_loop(0, CHUNKS, one_inward, 0)

    def kv_weight_grad(k, carry):
        value = mm(hid_one(c, shard_lanes(k)), kvlow[...], TN)
        low, high = value[:, :HEAD_SIZE], value[:, HEAD_SIZE:]
        dkv_out[0, k] = jnp.where(c == 0, high, low).astype(BF16)
        dkv_out[1, k] = jnp.where(c == 0, low, high).astype(BF16)
        return carry

    lax.fori_loop(0, deep, kv_weight_grad, 0)
    dkv_copy = remote(dkv_out.at[0], dkv_in, dkv_sem, 0, me.core_peer())
    dkv_copy.start()
    chain.advance(1)
    dkv_copy.wait_recv()

    def kv_weight_sum(k, carry):
        keep, away = halves(dkv_out[1, k].astype(F32) + dkv_in[k].astype(F32))
        stage2[k, 0, :, pl.ds(2 * mine, HEAD_SIZE)] = keep.astype(BF16)
        xs_out[k, :, pl.ds(2 * mine, HEAD_SIZE)] = away.astype(BF16)
        return carry

    lax.fori_loop(0, deep, kv_weight_sum, 0)
    xs_copy(2).start()

    for number in range(CHUNKS):
        two.x_copy(number).wait_send()

    def out_copies(buffer, target, sem_at, peer_sems, number):
        at = pl.ds(pl.multiple_of(number * step, step), step)
        here = pltpu.make_async_copy(buffer.at[at], target.at[c, at], out_sem.at[sem_at + number])
        there = remote(buffer.at[at], target.at[c, at], peer_sems, number, me.core_peer())
        return here, there

    def mix_out(number, carry):
        at = pl.ds(pl.multiple_of(number * step, step), step)
        x_out[at, :] = (after[at, :] + mo.total(number)).astype(BF16)
        for copy in out_copies(x_out, mixed, 0, mixed_sem, number):
            copy.start()
        return carry

    lax.fori_loop(0, CHUNKS, mix_out, 0)

    def first_norm(number, gain_grad):
        at = pl.ds(pl.multiple_of(number * step, step), step)
        y_copy(number).wait_recv()
        upstream = y_out[at, :].astype(F32) + one_y_in[at, :].astype(F32)
        value = mats[pl.ds(pl.multiple_of(2 * rows + number * step, step), step), :].astype(F32)
        factor = lax.rsqrt(jnp.mean(value * value, -1, keepdims=True) + EPS)
        scaled = upstream * gain_one
        inner = jnp.mean(scaled * value, -1, keepdims=True)
        acc[at, :] = agrad[at, :] + (
            factor * scaled - value * (factor * factor * factor * inner)
        )
        for copy in out_copies(acc, d_tokens, CHUNKS, token_sem, number):
            copy.start()
        return gain_grad + jnp.sum(upstream * value * factor, 0, keepdims=True)

    gain_one_grad = lax.fori_loop(0, CHUNKS, first_norm, jnp.zeros((1, width), F32))
    small_own[pl.ds(0, 1), :] = gain_one_grad
    small_c = remote(small_own, small_core, small_c_sem, 0, me.core_peer())
    small_c.start()
    chain.advance(2)

    for part in range(3):
        xs_copy(part).wait_recv()

    def side_sum(k, carry):
        stage2[k, 0] = (stage2[k, 0].astype(F32) + xs_in[k].astype(F32)).astype(BF16)
        return carry

    lax.fori_loop(0, deep, side_sum, 0)
    chain2 = Chain(me, stage2, from_dn2, from_up2, dn_sem2, up_sem2, 64)
    chain2.begin(0)

    small_c.wait_recv()
    small_c.wait_send()
    small_own[...] = small_own[...] + small_core[...]
    small_x_copy = remote(small_own, small_x, small_x_sem, 0, me.x_peer())
    small_x_copy.start()
    chain2.advance(0)
    small_x_copy.wait_recv()
    small_x_copy.wait_send()
    small_own[...] = small_own[...] + small_x[...]

    def small_copy(k):
        there = (z + k) % deep
        return remote(
            small_own.at[:, shard_lanes(there)], small_z.at[z], small_z_sem, k - 1, me.at_z(there)
        )

    for k in range(1, deep):
        small_copy(k).start()
    small_z[z] = small_own[:, shard_lanes(z)]
    for m in range(3):

        def write(at, value):
            grads[m, at, :] = value

        chain.finish(m, write)

    def write2(at, value):
        d_qo[at, :] = value[:, : 2 * mine]
        kv_last[at, :] = value[:, 2 * mine :]

    chain2.finish(0, write2)

    share = half // 4
    columns = pl.ds(pl.multiple_of((c * 2 + y) * HEAD_SIZE, HEAD_SIZE), HEAD_SIZE)

    def last_copy(k):
        there = (me.t + k) % 4
        return remote(
            kv_last.at[pl.ds(pl.multiple_of(there * share, 8), share)],
            d_kv.at[:, columns],
            last_sem,
            k - 1,
            (z, x, there),
        )

    for k in range(1, 4):
        last_copy(k).start()
    d_kv[:, columns] = kv_last[pl.ds(pl.multiple_of(me.t * share, 8), share), :]
    for k in range(1, deep):
        source = (z + deep - k) % deep
        remote(
            small_own.at[:, shard_lanes(0)], small_z.at[source], small_z_sem, k - 1, me.at_z(source)
        ).wait_recv()
    total = small_z[0]
    for k in range(1, deep):
        total = total + small_z[k]
    d_small[...] = total
    for k in range(1, 4):
        source = (me.t + 4 - k) % 4
        there = pl.ds(pl.multiple_of(((source % 2) * 2 + source // 2) * HEAD_SIZE, HEAD_SIZE), HEAD_SIZE)
        remote(
            kv_last.at[pl.ds(0, share)], d_kv.at[:, there], last_sem, k - 1, (z, x, source)
        ).wait_recv()

    for number in range(CHUNKS):
        at = pl.ds(number * step, step)
        remote(
            x_out.at[at], mixed.at[1 - c, at], mixed_sem, number, me.core_peer()
        ).wait_recv()
        remote(
            acc.at[at], d_tokens.at[1 - c, at], token_sem, number, me.core_peer()
        ).wait_recv()
        for buffer, target, first, peer_sems in (
            (x_out, mixed, 0, mixed_sem),
            (acc, d_tokens, CHUNKS, token_sem),
        ):
            here, there = out_copies(buffer, target, first, peer_sems, number)
            here.wait()
            there.wait_send()
        mo.x_copy(number).wait_send()
        mo.y_copy(number).wait_send()
        y_copy(number).wait_send()
        one_copy(number).wait_send()
        low_copy(number).wait_send()
    for k in range(1, 8):
        gate_copy(k).wait_send()
    for k in range(1, deep):
        small_copy(k).wait_send()
    for k in range(1, 4):
        last_copy(k).wait_send()
    for part in range(3):
        xs_copy(part).wait_send()
    for copy in (kv_copy, kvx_copy, dkv_copy):
        copy.wait_send()
    for m in range(3):
        chain.drain(m)
    chain2.drain(0)


def rest_call(mats_a, mats_b, acts_a, gates_a, hid, ups, mixes, made, tokens, deep, quarter):
    hid_one, wqkv, wout, smalls, queries, keys, values, probs, context, tables, after = made
    units, width = mats_a.shape[0] // 3, mats_a.shape[1]
    count = hid.shape[0]
    trees, heads, rows, length = probs.shape
    shard = width // deep
    half = shard // 2
    mine = heads * HEAD_SIZE
    lanes = 2 * mine + HEAD_SIZE
    vmem = pl.BlockSpec(memory_space=pltpu.VMEM)
    anywhere = pl.BlockSpec(memory_space=pl.ANY)

    def like(array):
        return pltpu.VMEM(array.shape, array.dtype)

    def plain(*shape):
        return pltpu.VMEM(shape, BF16)

    def wide(*shape):
        return pltpu.VMEM(shape, F32)

    hbm, on_chip = anywhere, vmem
    return pl.pallas_call(
        functools.partial(rest_kernel, quarter),
        out_shape=(
            jax.ShapeDtypeStruct((trees, rows, width), BF16),
            jax.ShapeDtypeStruct((trees, rows, width), F32),
            jax.ShapeDtypeStruct((3, units, shard), F32),
            jax.ShapeDtypeStruct((half, 2 * mine), F32),
            jax.ShapeDtypeStruct((half // 4, 2 * KEY_VALUE_HEADS * HEAD_SIZE), F32),
            jax.ShapeDtypeStruct((smalls.shape[1], shard), F32),
        ),
        in_specs=[hbm, hbm, hbm, on_chip, hbm, hbm, on_chip, hbm, hbm, hbm, hbm, on_chip]
        + [hbm] * 7,
        out_specs=[hbm, hbm] + [on_chip] * 4,
        scratch_shapes=[
            plain(6 * units, width),
            plain(6, units, count),
            plain(count, width),
            plain(count, width),
            like(wqkv),
            like(wout),
            like(queries),
            like(keys),
            like(values),
            like(probs),
            like(context),
            like(tables),
            like(after),
            wide(8, count),
            wide(2 * trees, 8, rows),
            wide(8, 8, rows),
            plain(2 * rows, width),
            plain(rows, width),
            wide(rows, width),
            plain(rows, width),
            plain(2 * rows, width),
            plain(rows, width),
            plain(rows, width),
            plain(2 * rows, width),
            plain(rows, width),
            plain(rows, width),
            plain(rows, width),
            plain(rows, width),
            wide(rows, width),
            plain(trees, rows, width),
            plain(trees, rows, mine),
            plain(length, 2 * HEAD_SIZE),
            plain(length, 2 * HEAD_SIZE),
            wide(length, 2 * HEAD_SIZE),
            plain(rows, 2 * HEAD_SIZE),
            plain(rows, 2 * HEAD_SIZE),
            plain(rows, 2 * HEAD_SIZE),
            plain(2, deep, shard, HEAD_SIZE),
            plain(deep, shard, HEAD_SIZE),
            plain(deep, half, lanes),
            plain(deep, half, lanes),
            plain(deep, 3, units, shard),
            plain(deep - 1, 3, units, shard),
            plain(deep - 1, 3, units, shard),
            plain(deep, 1, half, lanes),
            plain(deep - 1, 1, half, lanes),
            plain(deep - 1, 1, half, lanes),
            wide(smalls.shape[1], width),
            wide(smalls.shape[1], width),
            wide(smalls.shape[1], width),
            wide(deep, smalls.shape[1], shard),
            wide(half, HEAD_SIZE),
            pltpu.SemaphoreType.DMA((14,)),
            sems(7),
            sems(4),
            sems(CHUNKS),
            sems(CHUNKS),
            sems(4),
            sems(CHUNKS),
            sems(CHUNKS),
            sems(CHUNKS),
            sems(CHUNKS),
            sems(CHUNKS),
            sems(1),
            sems(1),
            sems(1),
            sems(3),
            sems((deep - 1) * 3),
            sems((deep - 1) * 3),
            sems(deep - 1),
            sems(deep - 1),
            pltpu.SemaphoreType.DMA((2 * CHUNKS,)),
            sems(CHUNKS),
            sems(CHUNKS),
            sems(1),
            sems(1),
            sems(deep - 1),
            sems(3),
        ],
        compiler_params=pltpu.CompilerParams(
            collective_id=2, has_side_effects=True, vmem_limit_bytes=64 * 2**20
        ),
        name="rest",
    )(
        mats_a,
        mats_b,
        acts_a,
        gates_a,
        hid,
        ups,
        mixes,
        hid_one,
        tokens,
        wqkv,
        wout,
        smalls,
        queries,
        keys,
        values,
        probs,
        context,
        tables,
        after,
    )


def plane_shards(
    tokens,
    cotangent,
    seg_start,
    seg_parent,
    routes,
    attn_gain,
    w_query,
    w_key,
    w_value,
    w_output,
    moe_gain,
    w_router,
    w_gate,
    w_up,
    w_down,
):
    trees, rows, width = tokens.shape
    deep = lax.axis_size("dp")
    held, quarter = w_gate.shape[0], w_gate.shape[2]
    group = held // 2
    heads = w_query.shape[1] // HEAD_SIZE
    mine = heads * HEAD_SIZE
    gate_t, up_t = jnp.swapaxes(w_gate, 1, 2), jnp.swapaxes(w_up, 1, 2)

    def gathered(first):
        some = slice(first, first + group)
        own = jnp.concatenate([gate_t[some], up_t[some], w_down[some]], 0)
        full = lax.all_gather(own, "dp", axis=2, tiled=True)
        return full.reshape(3 * group * quarter, width)

    mats_a, mats_b = gathered(0), gathered(group)
    small = jnp.concatenate(
        [attn_gain[None], moe_gain[None], jnp.zeros((6, attn_gain.shape[0]), BF16), w_router.T], 0
    )
    made = attend_call(
        seg_start,
        seg_parent,
        tokens,
        cotangent,
        jnp.swapaxes(routes, 1, 2),
        w_query,
        w_key,
        w_value,
        w_output,
        small,
        deep,
    )
    hid, ups, mixes = made[11:]
    count = trees * 2 * rows
    hid, ups = hid.reshape(count, width), ups.reshape(count, width)
    mixes = mixes.reshape(trees * 2, -1, rows)
    acts_a, gates_a, grads_a = experts_call(mats_a, hid, ups, mixes, deep)
    mixed, d_tokens, grads_b, d_qo, d_kv, d_small = rest_call(
        mats_a,
        mats_b,
        acts_a,
        gates_a,
        hid,
        ups,
        mixes,
        made[:11],
        tokens,
        deep,
        quarter,
    )
    both = jnp.concatenate(
        [
            grads_a.reshape(3, group, quarter, width // deep),
            grads_b.reshape(3, group, quarter, width // deep),
        ],
        1,
    )
    part = width // deep // 2
    d_small = lax.dynamic_slice_in_dim(d_small, lax.axis_index("expert") * part, part, 1)
    kv = KEY_VALUE_HEADS * HEAD_SIZE
    return (
        mixed,
        d_tokens,
        d_small[0],
        d_qo[:, :mine],
        d_kv[:, :kv],
        d_kv[:, kv:],
        d_qo[:, mine:].T,
        d_small[1],
        d_small[8:].T,
        jnp.swapaxes(both[0], 1, 2),
        jnp.swapaxes(both[1], 1, 2),
        both[2],
    )


def shards(*arrays):
    sizes = lax.axis_size("expert"), lax.axis_size("tensor"), arrays[0].shape[0]
    if sizes == (2, 4, 2):
        return plane_shards(*arrays)
    return general_shards(*arrays)


def solution(mesh):
    placed = (
        P("dp", "expert", None),
        P("dp", "expert", None),
        P("dp", None),
        P("dp", None),
        P("dp", "expert", None),
        P("dp"),
        P("dp", "tensor"),
        P("dp", None),
        P("dp", None),
        P("tensor", "dp"),
        P("dp"),
        P("dp", None),
        P("expert", "dp", "tensor"),
        P("expert", "dp", "tensor"),
        P("expert", "tensor", "dp"),
    )
    return jax.shard_map(
        shards,
        mesh=mesh,
        in_specs=placed,
        out_specs=(
            P("dp", "expert", None),
            P("dp", "expert", None),
            P(("dp", "expert")),
            P(("dp", "expert"), "tensor"),
            P(("dp", "expert", "tensor"), None),
            P(("dp", "expert", "tensor"), None),
            P("tensor", ("dp", "expert")),
            P(("dp", "expert")),
            P(("dp", "expert"), None),
            P("expert", "dp", "tensor"),
            P("expert", "dp", "tensor"),
            P("expert", "tensor", "dp"),
        ),
        check_vma=False,
    )
```

```python
import functools
import math

import jax
import jax.numpy as jnp
import numpy as np
from jax import lax
from jax.experimental import pallas as pl
from jax.experimental.pallas import tpu as pltpu
from jax.sharding import PartitionSpec as P

QUERY_HEADS = 12
KEY_VALUE_HEADS = 2
HEAD_SIZE = 128
GROUP = QUERY_HEADS // KEY_VALUE_HEADS
EPS = 1e-05
ROPE_BASE = 10000.0
NEG = -1e30
F32 = jnp.float32
BF16 = jnp.bfloat16


def dot(left, right, dims):
    return lax.dot_general(left, right, (dims, ((), ())), preferred_element_type=F32)


def norm_factor(rows):
    return lax.rsqrt(jnp.mean(rows * rows, -1, keepdims=True) + EPS)


def norm_back(rows, factor, gain, upstream):
    scaled = upstream * gain
    gain_grad = jnp.sum(upstream * rows * factor, 0)
    inner = jnp.mean(scaled * rows, -1, keepdims=True)
    return factor * scaled - rows * (factor * factor * factor * inner), gain_grad


def layout(starts, parents, places, length):
    labels = jnp.arange(starts.shape[1], dtype=jnp.int32)

    def pick(table, at):
        hot = at[:, :, None] == labels[None, None, :]
        return jnp.sum(jnp.where(hot, table[:, None, :], 0), 2, dtype=jnp.int32)

    segment = jnp.sum((starts[:, None, :] <= places[None, :, None]).astype(jnp.int32), 2) - 1
    above = pick(parents, segment)
    further = pick(parents, above)
    ends = jnp.concatenate(
        [starts[:, 1:], jnp.full((starts.shape[0], 1), length, jnp.int32)], 1
    )
    lengths = ends - starts
    depths = (
        places[None, :]
        - pick(starts, segment)
        + jnp.where(segment != 0, pick(lengths, above), 0)
        + jnp.where(above != 0, pick(lengths, further), 0)
    )
    return segment, above, further, depths


def angles(depths):
    half = HEAD_SIZE // 2
    frequency = ROPE_BASE ** (-2.0 * jnp.arange(half, dtype=F32) / HEAD_SIZE)
    turning = depths.astype(F32)[..., None] * frequency
    return jnp.cos(turning), jnp.sin(turning)


def rotate(heads, cosine, sine):
    half = HEAD_SIZE // 2
    front, back = heads[..., :half], heads[..., half:]
    return jnp.concatenate([front * cosine - back * sine, back * cosine + front * sine], -1)


def general_shards(
    tokens,
    cotangent,
    seg_start,
    seg_parent,
    routes,
    attn_gain,
    w_query,
    w_key,
    w_value,
    w_output,
    moe_gain,
    w_router,
    w_gate,
    w_up,
    w_down,
):
    trees, rows, width = tokens.shape
    expert_count = lax.axis_size("expert")
    tensor_count = lax.axis_size("tensor")
    tensor_at = lax.axis_index("tensor")
    expert_at = lax.axis_index("expert")
    length = rows * expert_count
    heads = w_query.shape[1] // HEAD_SIZE
    kv_head = tensor_at * heads // GROUP
    inv_root = HEAD_SIZE ** (-0.5)
    own_experts = w_gate.shape[0]
    quarter = w_gate.shape[2]
    all_experts = w_router.shape[1]

    def over_dp(array, axis):
        return lax.all_gather(array, "dp", axis=axis, tiled=True)

    w_query = over_dp(w_query, 0)
    w_output = over_dp(w_output, 1)
    gate_t = over_dp(jnp.swapaxes(w_gate, 1, 2), 2)
    up_t = over_dp(jnp.swapaxes(w_up, 1, 2), 2)
    down = over_dp(w_down, 2)
    small = over_dp(
        jnp.concatenate(
            [
                lax.dynamic_slice_in_dim(w_key, kv_head * HEAD_SIZE, HEAD_SIZE, 1),
                lax.dynamic_slice_in_dim(w_value, kv_head * HEAD_SIZE, HEAD_SIZE, 1),
                w_router,
                attn_gain[:, None],
                moe_gain[:, None],
            ],
            1,
        ),
        0,
    )
    w_kv = small[:, : 2 * HEAD_SIZE]
    w_router = small[:, 2 * HEAD_SIZE : 2 * HEAD_SIZE + all_experts]
    attn_gain = small[:, -2].astype(F32)
    moe_gain = small[:, -1].astype(F32)

    all_places = jnp.arange(length, dtype=jnp.int32)
    places = expert_at * rows + jnp.arange(rows, dtype=jnp.int32)
    segment, above, further, depths = layout(seg_start, seg_parent, places, length)
    key_segment = layout(seg_start, seg_parent, all_places, length)[0]
    cosine, sine = angles(depths)
    of_key = key_segment[:, None, :]
    visible = (
        (of_key == segment[:, :, None])
        | (of_key == above[:, :, None])
        | (of_key == further[:, :, None])
    ) & (all_places[None, None, :] <= places[None, :, None])

    residual = tokens.astype(F32).reshape(trees * rows, width)
    factor_one = norm_factor(residual)
    hidden_one = (residual * factor_one * attn_gain).astype(BF16)
    query_pre = dot(hidden_one, w_query, ((1,), (0,))).reshape(trees, rows, heads, HEAD_SIZE)
    kv_pre = dot(hidden_one, w_kv, ((1,), (0,))).reshape(trees, rows, 2 * HEAD_SIZE)
    queries = rotate(query_pre, cosine[:, :, None, :], sine[:, :, None, :]).astype(BF16)
    own_keys = rotate(kv_pre[..., :HEAD_SIZE], cosine, sine).astype(BF16)
    own_kv = jnp.concatenate([own_keys, kv_pre[..., HEAD_SIZE:].astype(BF16)], -1)
    keys_values = lax.all_gather(own_kv, "expert", axis=1, tiled=True)
    keys, values = keys_values[..., :HEAD_SIZE], keys_values[..., HEAD_SIZE:]
    scores = jnp.einsum("bqhd,bkd->bhqk", queries, keys, preferred_element_type=F32) * inv_root
    scores = jnp.where(visible[:, None], scores, NEG)
    row_max = jnp.max(scores, -1, keepdims=True)
    exponent = jnp.exp(scores - row_max)
    probs = exponent / jnp.sum(exponent, -1, keepdims=True)
    probs_low = probs.astype(BF16)
    context = jnp.einsum("bhqk,bkd->bqhd", probs_low, values, preferred_element_type=F32)
    context_low = context.reshape(trees * rows, heads * HEAD_SIZE).astype(BF16)
    attn_out = dot(context_low, w_output, ((1,), (0,))).astype(BF16)
    after_attn = residual + lax.psum(attn_out, "tensor").astype(F32)

    factor_two = norm_factor(after_attn)
    hidden_two = (after_attn * factor_two * moe_gain).astype(BF16)
    logits = dot(hidden_two, w_router, ((1,), (0,)))
    chosen = jnp.any(
        routes.reshape(trees * rows, -1)[:, :, None]
        == jnp.arange(all_experts, dtype=jnp.int32)[None, None, :],
        1,
    )
    masked = jnp.where(chosen, logits, NEG)
    raised = jnp.where(chosen, jnp.exp(masked - jnp.max(masked, -1, keepdims=True)), 0.0)
    mixing = raised / jnp.sum(raised, -1, keepdims=True)

    def over_expert(array):
        full = lax.all_gather(
            array.reshape(trees, rows, array.shape[-1]), "expert", axis=1, tiled=True
        )
        return full.reshape(trees * length, array.shape[-1])

    every_hidden = over_expert(hidden_two)
    every_up = over_expert(cotangent)
    every_mix = lax.dynamic_slice_in_dim(
        over_expert(mixing), expert_at * own_experts, own_experts, 1
    )
    count = trees * length
    pre_gate = dot(every_hidden, gate_t.reshape(-1, width), ((1,), (1,)))
    pre_up = dot(every_hidden, up_t.reshape(-1, width), ((1,), (1,)))
    down_rows = down.reshape(-1, width)
    down_back = dot(every_up, down_rows, ((1,), (1,)))
    wide_mix = jnp.repeat(every_mix, quarter, axis=1)
    activated, pull = jax.vjp(jax.nn.gelu, pre_gate)
    hidden = activated * pre_up
    mixed_hidden = (hidden * wide_mix).astype(BF16)
    moe_part = dot(mixed_hidden, down_rows, ((1,), (0,))).astype(BF16)
    gate_part = jnp.sum((hidden * down_back).reshape(count, own_experts, quarter), -1)
    hidden_grad = wide_mix * down_back
    gate_pre = pull(hidden_grad * pre_up)[0].astype(BF16)
    up_pre = (hidden_grad * activated).astype(BF16)
    two_part = (
        dot(gate_pre, gate_t.reshape(-1, width), ((1,), (0,)))
        + dot(up_pre, up_t.reshape(-1, width), ((1,), (0,)))
    ).astype(BF16)
    d_down = dot(mixed_hidden, every_up, ((0,), (0,)))
    d_gate = dot(gate_pre, every_hidden, ((0,), (0,)))
    d_up = dot(up_pre, every_hidden, ((0,), (0,)))

    def to_owner(array):
        array = array.reshape(trees, length, array.shape[-1])
        part = lax.psum_scatter(array, "expert", scatter_dimension=1, tiled=True)
        return lax.psum(part, "tensor").reshape(trees * rows, -1)

    spread = jnp.arange(all_experts) // own_experts == expert_at
    gate_wide = jnp.where(
        spread[None, :], jnp.tile(gate_part, (1, all_experts // own_experts)), 0.0
    )
    two_grad = to_owner(two_part).astype(F32)
    mix_grad = to_owner(gate_wide)
    mixed_out = (after_attn + to_owner(moe_part).astype(F32)).astype(BF16)

    picked_grad = mixing * (mix_grad - jnp.sum(mixing * mix_grad, -1, keepdims=True))
    logit_grad = picked_grad.astype(BF16)
    two_grad = two_grad + dot(logit_grad, w_router, ((1,), (1,)))
    d_router = dot(hidden_two, logit_grad, ((0,), (0,)))
    norm_two, d_moe_gain = norm_back(after_attn, factor_two, moe_gain, two_grad)
    attn_grad = cotangent.astype(F32).reshape(trees * rows, width) + norm_two
    attn_low = attn_grad.astype(BF16)

    d_output = dot(context_low, attn_low, ((0,), (0,)))
    context_grad = (
        dot(attn_low, w_output, ((1,), (1,)))
        .astype(BF16)
        .reshape(trees, rows, heads, HEAD_SIZE)
    )
    prob_grad = jnp.einsum("bqhd,bkd->bhqk", context_grad, values, preferred_element_type=F32)
    score_grad = probs * (prob_grad - jnp.sum(probs * prob_grad, -1, keepdims=True))
    score_grad = score_grad.astype(BF16)
    query_grad = (
        jnp.einsum("bhqk,bkd->bqhd", score_grad, keys, preferred_element_type=F32) * inv_root
    )
    key_grad = (
        jnp.einsum("bhqk,bqhd->bkd", score_grad, queries, preferred_element_type=F32) * inv_root
    )
    value_grad = jnp.einsum("bhqk,bqhd->bkd", probs_low, context_grad, preferred_element_type=F32)
    kv_part = jnp.concatenate([key_grad, value_grad], -1).astype(BF16)
    kv_sum = lax.psum_scatter(kv_part, "expert", scatter_dimension=1, tiled=True)
    sharing = GROUP // heads
    own_rows = rows // sharing
    place = tensor_at % sharing
    kv_rows = kv_sum.reshape(trees, sharing, own_rows, 2 * HEAD_SIZE)
    mine = lax.dynamic_index_in_dim(kv_rows, place, 1, False).astype(F32)
    for step in range(1, sharing):
        order = [
            (at, at // sharing * sharing + (at + step) % sharing) for at in range(tensor_count)
        ]
        away = lax.dynamic_index_in_dim(kv_rows, (place + step) % sharing, 1, False)
        mine = mine + lax.ppermute(away, "tensor", order).astype(F32)

    def own(array):
        return lax.dynamic_slice_in_dim(array, place * own_rows, own_rows, 1)

    key_low = rotate(mine[..., :HEAD_SIZE], own(cosine), -own(sine)).astype(BF16)
    kv_low = jnp.concatenate([key_low, mine[..., HEAD_SIZE:].astype(BF16)], -1)
    kv_low = kv_low.reshape(trees * own_rows, 2 * HEAD_SIZE)
    hidden_own = own(hidden_one.reshape(trees, rows, width)).reshape(trees * own_rows, width)
    d_kv = dot(hidden_own, kv_low, ((0,), (0,)))
    kv_back = dot(kv_low, w_kv, ((1,), (1,))).reshape(trees, own_rows, width)
    query_low = rotate(query_grad, cosine[:, :, None, :], -sine[:, :, None, :])
    query_low = query_low.astype(BF16).reshape(trees * rows, heads * HEAD_SIZE)
    d_query = dot(hidden_one, query_low, ((0,), (0,)))
    one_part = dot(query_low, w_query, ((1,), (1,))).reshape(trees, rows, width)
    one_part = lax.dynamic_update_slice_in_dim(
        one_part, own(one_part) + kv_back, place * own_rows, 1
    ).reshape(trees * rows, width)
    one_grad = lax.psum(one_part.astype(BF16), "tensor").astype(F32)
    norm_one, d_attn_gain = norm_back(residual, factor_one, attn_gain, one_grad)
    d_tokens = (attn_grad + norm_one).reshape(trees, rows, width)

    def scatter_dp(array, axis):
        return lax.psum_scatter(array, "dp", scatter_dimension=axis, tiled=True)

    def scatter_expert(array, axis):
        return lax.psum_scatter(array, "expert", scatter_dimension=axis, tiled=True)

    def experts_home(array):
        return scatter_dp(array.astype(BF16), 1).astype(F32).reshape(own_experts, quarter, -1)

    d_gate, d_up, d_down = experts_home(d_gate), experts_home(d_up), experts_home(d_down)
    d_query = scatter_expert(scatter_dp(d_query.astype(BF16), 0), 0).astype(F32)
    d_output = scatter_expert(scatter_dp(d_output.astype(BF16), 1), 1).astype(F32)
    flat = jnp.concatenate([d_attn_gain[:, None], d_moe_gain[:, None], d_router], 1)
    flat = scatter_expert(scatter_dp(flat, 0), 0)
    of_head = (jnp.arange(KEY_VALUE_HEADS) == kv_head).astype(F32)[None, None, :, None]
    d_kv = scatter_expert(scatter_dp(d_kv, 0), 0).reshape(-1, 2, 1, HEAD_SIZE) * of_head
    d_kv = d_kv.reshape(-1, 2 * KEY_VALUE_HEADS * HEAD_SIZE)
    d_kv = lax.psum_scatter(d_kv, "tensor", scatter_dimension=0, tiled=True)
    return (
        mixed_out.reshape(trees, rows, width),
        d_tokens,
        flat[:, 0],
        d_query,
        d_kv[:, : KEY_VALUE_HEADS * HEAD_SIZE],
        d_kv[:, KEY_VALUE_HEADS * HEAD_SIZE :],
        d_output,
        flat[:, 1],
        flat[:, 2:],
        jnp.swapaxes(d_gate, 1, 2),
        jnp.swapaxes(d_up, 1, 2),
        d_down,
    )


MESH = pl.DeviceIdType.MESH
NT = (((1,), (1,)), ((), ()))
NN = (((1,), (0,)), ((), ()))
TN = (((0,), (0,)), ((), ()))
CHUNKS = 4
TILE = 128
KINDS = 3
ROOT_2_PI = math.sqrt(2.0 / math.pi)
CUBIC = 0.044715


def mm(left, right, dims=NN):
    return lax.dot_general(left, right, dims, preferred_element_type=F32)


def rows_at(number, size):
    return pl.ds(pl.multiple_of(number * size, size), size)


class Place:
    def __init__(self):
        self.z = lax.axis_index("dp")
        self.x = lax.axis_index("expert")
        self.t = lax.axis_index("tensor")
        self.y = self.t // 2
        self.c = self.t % 2

    def at_z(self, z):
        return (z, self.x, self.t)

    def x_peer(self):
        return (self.z, 1 - self.x, self.t)

    def y_peer(self):
        return (self.z, self.x, (self.t + 2) % 4)

    def core_peer(self):
        return (self.z, self.x, self.t + 1 - 2 * self.c)


def remote(src, dst, sems, at, device):
    return pltpu.make_async_remote_copy(
        src_ref=src,
        dst_ref=dst,
        send_sem=sems.at[0, at],
        recv_sem=sems.at[1, at],
        device_id=device,
        device_id_type=MESH,
    )


def signal(sem, device):
    pl.semaphore_signal(sem, inc=1, device_id=device, device_id_type=MESH)


def await_signal(sem):
    pl.semaphore_wait(sem, 1)


def greet(devices):
    barrier = pltpu.get_barrier_semaphore()
    for device in devices:
        pl.semaphore_signal(barrier, inc=1, device_id=device, device_id_type=MESH)
    pl.semaphore_wait(barrier, len(devices))


def tree_tables(starts, parents, tree, first, rows, length, frequency):
    count = starts.shape[1]
    place = first + lax.broadcasted_iota(jnp.int32, (rows, HEAD_SIZE), 0)
    start = [starts[tree, k] for k in range(count)]
    parent = [parents[tree, k] for k in range(count)]
    size = [(start[k + 1] if k + 1 < count else length) - start[k] for k in range(count)]

    def pick(table, at):
        total = jnp.zeros_like(at)
        for k in range(count):
            total = total + jnp.where(at == k, table[k], 0)
        return total

    def segment_of(at):
        total = jnp.zeros_like(at)
        for k in range(1, count):
            total = total + jnp.where(at >= start[k], 1, 0)
        return total

    segment = segment_of(place)
    above = pick(parent, segment)
    further = pick(parent, above)
    depth = (
        place
        - pick(start, segment)
        + jnp.where(segment != 0, pick(size, above), 0)
        + jnp.where(above != 0, pick(size, further), 0)
    )
    turning = depth.astype(F32) * frequency
    lane = lax.broadcasted_iota(jnp.int32, (rows, HEAD_SIZE), 1)
    cosine = jnp.cos(turning)
    sine = jnp.sin(turning)
    sine = jnp.where(lane < HEAD_SIZE // 2, -sine, sine)
    key_place = lax.broadcasted_iota(jnp.int32, (8, length), 1)
    key_segment = jnp.broadcast_to(segment_of(key_place)[:1], (rows, length))
    key_place = jnp.broadcast_to(key_place[:1], (rows, length))
    wide = length // HEAD_SIZE

    def widen(array):
        return jnp.concatenate([array] * wide, 1)

    visible = (
        (key_segment == widen(segment))
        | (key_segment == widen(above))
        | (key_segment == widen(further))
    ) & (key_place <= widen(place))
    return jnp.where(visible, 1.0, 0.0), cosine, sine


def turn(head, cosine, sine):
    return head * cosine + pltpu.roll(head, HEAD_SIZE // 2, 1) * sine


class Relay:
    def __init__(self, me, deep, piece, up_sems, dn_sems, side_sems=None):
        self.me, self.deep, self.piece = me, deep, piece
        self.up_sems, self.dn_sems, self.side_sems = up_sems, dn_sems, side_sems

    def up(self, source, part, hop):
        above = self.me.at_z(jnp.minimum(self.me.z + 1, self.deep - 1))
        at = self.piece(source, part, self.me.x)
        return remote(at, at, self.up_sems, part * self.deep + hop, above)

    def dn(self, source, part, hop):
        below = self.me.at_z(jnp.maximum(self.me.z - 1, 0))
        at = self.piece(source, part, self.me.x)
        return remote(at, at, self.dn_sems, part * self.deep + hop, below)

    def side(self, source, part, hop, x):
        at = self.piece(source, part, x)
        return remote(at, at, self.side_sems, part * 2 * self.deep + hop, self.me.x_peer())

    def begin(self, part, ends=None):
        z, last = self.me.z, self.deep - 1
        at_end = (z == 0) | (z == last)
        now = z >= 0 if ends is None else at_end if ends else jnp.logical_not(at_end)

        @pl.when((z < last) & now)
        def _():
            self.up(z, part, 0).start()

        @pl.when((z > 0) & now)
        def _():
            self.dn(z, part, 0).start()

    def pass_on(self, part, hop):
        z, deep = self.me.z, self.deep
        sides = self.side_sems is not None
        upward = (z - 1 - hop >= 0) & (z < deep - 1)
        downward = (z + 1 + hop < deep) & (z > 0)
        if sides:

            @pl.when(z - 1 - hop >= 0)
            def _():
                self.up(z - 1 - hop, part, hop).wait_recv()
                self.side(z - 1 - hop, part, hop, self.me.x).start()

            @pl.when(z + 1 + hop < deep)
            def _():
                self.dn(z + 1 + hop, part, hop).wait_recv()
                self.side(z + 1 + hop, part, deep + hop, self.me.x).start()

        @pl.when(upward)
        def _():
            if not sides:
                self.up(z - 1 - hop, part, hop).wait_recv()
            self.up(z - 1 - hop, part, hop + 1).start()

        @pl.when(downward)
        def _():
            if not sides:
                self.dn(z + 1 + hop, part, hop).wait_recv()
            self.dn(z + 1 + hop, part, hop + 1).start()

    def finish(self, part):
        z, deep = self.me.z, self.deep
        for hop in range(deep - 1):
            if self.side_sems is not None:

                @pl.when(z - 1 - hop >= 0)
                def _():
                    self.side(z - 1 - hop, part, hop, 1 - self.me.x).wait_recv()

                @pl.when(z + 1 + hop < deep)
                def _():
                    self.side(z + 1 + hop, part, deep + hop, 1 - self.me.x).wait_recv()

            else:

                @pl.when(z == deep - 1)
                def _():
                    self.up(z - 1 - hop, part, hop).wait_recv()

                @pl.when(z == 0)
                def _():
                    self.dn(z + 1 + hop, part, hop).wait_recv()

    def drain(self, part):
        z, deep = self.me.z, self.deep
        for hop in range(deep):

            @pl.when((z - hop >= 0) & (z < deep - 1))
            def _():
                self.up(z - hop, part, hop).wait_send()

            @pl.when((z + hop < deep) & (z > 0))
            def _():
                self.dn(z + hop, part, hop).wait_send()

        if self.side_sems is not None:
            for hop in range(deep - 1):

                @pl.when(z - 1 - hop >= 0)
                def _():
                    self.side(z - 1 - hop, part, hop, self.me.x).wait_send()

                @pl.when(z + 1 + hop < deep)
                def _():
                    self.side(z + 1 + hop, part, deep + hop, self.me.x).wait_send()


class PlaneSum:
    def __init__(self, me, rows, make, bufs, landing, sem_set):
        self.me, self.rows, self.make = me, rows, make
        self.core_out, self.x_out, self.acc, self.y_out = bufs
        self.core_in, self.x_in, self.y_in = landing
        self.core_sems, self.x_sems, self.y_sems = sem_set
        self.tiles = rows // TILE
        self.step = rows // CHUNKS
        self.per_tile = TILE // self.step

    def core_copy(self, number):
        at = rows_at(number, TILE)
        return remote(
            self.core_out.at[at], self.core_in.at[at], self.core_sems, number, self.me.core_peer()
        )

    def x_copy(self, number):
        at = rows_at(number, self.step)
        return remote(self.x_out.at[at], self.x_in.at[at], self.x_sems, number, self.me.x_peer())

    def y_copy(self, number):
        at = rows_at(number, self.step)
        return remote(self.y_out.at[at], self.y_in.at[at], self.y_sems, number, self.me.y_peer())

    def tile(self, tree, x, number):
        first = pl.multiple_of((tree * 2 + x) * self.rows + number * TILE, TILE)
        return self.make(first)

    def outward(self, side):
        me = self.me
        x = me.x if side else 1 - me.x

        def one(number, carry):
            value = self.tile(1 - me.c, x, number)
            slot = side * self.tiles + number
            self.core_out[rows_at(slot, TILE), :] = value.astype(BF16)
            self.core_copy(slot).start()
            return carry

        lax.fori_loop(0, self.tiles, one, 0)

    def across(self):
        me = self.me

        def one(number, carry):
            value = self.tile(me.c, 1 - me.x, number).astype(BF16).astype(F32)
            self.core_copy(number).wait_recv()
            at = rows_at(number, TILE)
            self.x_out[at, :] = (value + self.core_in[at, :].astype(F32)).astype(BF16)
            for k in range(self.per_tile):
                self.x_copy(number * self.per_tile + k).start()
            return carry

        lax.fori_loop(0, self.tiles, one, 0)

    def inward(self):
        me = self.me

        def one(number, carry):
            value = self.tile(me.c, me.x, number).astype(BF16).astype(F32)
            slot = self.tiles + number
            self.core_copy(slot).wait_recv()
            self.acc[rows_at(number, TILE), :] = value + self.core_in[
                rows_at(slot, TILE), :
            ].astype(F32)
            return carry

        lax.fori_loop(0, self.tiles, one, 0)

    def pass_on(self, first, last):
        def one(number, carry):
            at = rows_at(number, self.step)
            self.x_copy(number).wait_recv()
            self.y_out[at, :] = (self.acc[at, :] + self.x_in[at, :].astype(F32)).astype(BF16)
            self.y_copy(number).start()
            return carry

        lax.fori_loop(first, last, one, 0)

    def total(self, number):
        at = rows_at(number, self.step)
        self.y_copy(number).wait_recv()
        return self.y_out[at, :].astype(F32) + self.y_in[at, :].astype(F32)

    def core_sent(self):
        for number in range(2 * self.tiles):
            self.core_copy(number).wait_send()

    def x_sent(self):
        for number in range(CHUNKS):
            self.x_copy(number).wait_send()

    def y_sent(self):
        for number in range(CHUNKS):
            self.y_copy(number).wait_send()


class Fold:
    def __init__(self, me, groups, bufs, sem_set, tile):
        self.me, self.groups, self.tile = me, groups, tile
        self.own, self.stage, self.land = bufs
        self.send_sems, self.recv_sems, self.free = sem_set
        self.sets, self.count, self.rows = self.stage.shape[0], self.own.shape[1], self.own.shape[2]
        z = me.z
        self.end = jnp.where(z < 2, 0, 3)
        self.mid = jnp.where(z < 2, 1, 2)
        self.is_end = z == self.end
        self.is_mid = z == self.mid
        self.targets = (3 - self.end, 3 - self.mid, jnp.where(self.is_end, self.mid, self.end))

    def place(self, target):
        return (target + 3 - self.me.z) % 4

    def free_at(self, group, which, m):
        return self.free.at[((group % self.sets) * 3 + which) * self.count + m]

    def copy(self, group, which, m, slot=None):
        at = group % self.sets
        target = self.targets[which]
        there = jnp.where(self.is_end, which, (3, 3, 2)[which]) if slot is None else slot
        return pltpu.make_async_remote_copy(
            src_ref=self.stage.at[at, self.place(target), m],
            dst_ref=self.land.at[at, there, m],
            send_sem=self.send_sems.at[(at * 3 + which) * self.count + m],
            recv_sem=self.recv_sems.at[(at * 4 + there) * self.count + m],
            device_id=self.me.at_z(jnp.where(self.is_end, self.mid, target)),
            device_id_type=MESH,
        )

    def send(self, group, which, m):
        if group >= self.sets:
            await_signal(self.free_at(group, which, m))
        self.copy(group, which, m).start()

    def used(self, group, which, m, sender):
        if group + self.sets < self.groups:
            signal(self.free_at(group, which, m), self.me.at_z(sender))

    def begin(self, group, m, hold):
        @pl.when(self.is_end)
        def _():
            for which in range(3):
                self.send(group, which, m)

        if not hold:

            @pl.when(self.is_mid)
            def _():
                self.send(group, 2, m)

    def advance(self, group, m, hold):
        at = group % self.sets

        @pl.when(self.is_mid)
        def _():
            for which in (0, 1):
                self.copy(group, which, m, which).wait_recv()
                term = self.stage.at[at, self.place(self.targets[which]), m]
                landed = self.land.at[at, which, m]

                def step(number, carry):
                    rows = rows_at(number, self.tile)
                    total = term[rows, :].astype(F32) + landed[rows, :].astype(F32)
                    term[rows, :] = total.astype(BF16)
                    return carry

                lax.fori_loop(0, self.rows // self.tile, step, 0)
                self.used(group, which, m, self.end)
                if which == 1 or not hold:
                    self.send(group, which, m)

    def let_go(self, group, m):
        @pl.when(self.is_mid)
        def _():
            self.send(group, 2, m)
            self.send(group, 0, m)

    def finish(self, group, m, write):
        at = group % self.sets
        for slot in (2, 3):
            self.copy(group, 2, m, slot).wait_recv()
        own = self.own.at[group, m]
        near, far = self.land.at[at, 2, m], self.land.at[at, 3, m]

        def step(number, carry):
            rows = rows_at(number, self.tile)
            total = own[rows, :].astype(F32) + near[rows, :].astype(F32)
            write(rows, total + far[rows, :].astype(F32))
            return carry

        lax.fori_loop(0, self.rows // self.tile, step, 0)

        @pl.when(self.is_end)
        def _():
            self.used(group, 2, m, self.mid)
            self.used(group, 0, m, 3 - self.mid)

        @pl.when(self.is_mid)
        def _():
            self.used(group, 2, m, self.end)
            self.used(group, 1, m, 3 - self.mid)

    def drain(self, group, m):
        for which in range(3):
            self.copy(group, which, m).wait_send()


def layer_kernel(
    starts,
    parents,
    frequency,
    routes,
    small,
    tokens_in,
    cotangent_in,
    w_query,
    w_key,
    w_value,
    w_output,
    gate_in,
    up_in,
    down_in,
    mixed,
    d_tokens,
    d_gate,
    d_up,
    d_down,
    d_qo,
    d_kv,
    d_small,
    mats,
    acts,
    hid,
    ups,
    wqkv,
    wout,
    smalls,
    queries,
    keys,
    values,
    probs,
    context,
    tables,
    after,
    mixes,
    gates,
    gates_out,
    gates_in,
    core_out,
    x_out,
    acc,
    y_out,
    two_core_in,
    two_x_in,
    two_y_in,
    mo_core_in,
    mo_x_in,
    mo_y_in,
    agrad,
    alow,
    qlow,
    kv_out,
    kv_in,
    kv_own,
    kvx_out,
    kvx_in,
    kvlow,
    dkv_out,
    dkv_in,
    xs_in,
    own,
    stage,
    land,
    bounce,
    own_o,
    stage_o,
    land_o,
    own_q,
    stage_q,
    land_q,
    small_own,
    small_core,
    small_x,
    small_z,
    kv_last,
    load_sem,
    small_sem,
    up1_sem,
    dn1_sem,
    side1_sem,
    up2_sem,
    dn2_sem,
    side2_sem,
    up3_sem,
    dn3_sem,
    kv_sem,
    cot_sem,
    core_sem,
    y_sem,
    hx_sem,
    hc_sem,
    hf_sem,
    mix_sem,
    gate_sem,
    two_core_sem,
    two_x_sem,
    two_y_sem,
    mo_core_sem,
    mo_x_sem,
    mo_y_sem,
    one_core_sem,
    one_y_sem,
    low_sem,
    kvg_sem,
    xs_sem,
    fold_send,
    fold_recv,
    fold_free,
    fold_send_o,
    fold_recv_o,
    fold_send_q,
    fold_recv_q,
    out_sem,
    mixed_sem,
    token_sem,
    grad_sem,
    small_c_sem,
    small_x_sem,
    small_z_sem,
    last_sem,
):
    me = Place()
    z, x, y, c = me.z, me.x, me.y, me.c
    deep, shard = wqkv.shape[0], wqkv.shape[1]
    trees, heads, rows, length = probs.shape
    width = hid.shape[1]
    groups = gates.shape[0]
    units = mats.shape[1] // groups
    mine = heads * HEAD_SIZE
    half = shard // 2
    step = rows // CHUNKS
    inv_root = HEAD_SIZE ** (-0.5)
    own_block = c * 2 + x
    is_end = (z == 0) | (z == deep - 1)

    def block_rows(tree, side):
        return rows_at(tree * 2 + side, rows)

    def shard_lanes(k):
        return rows_at(k, shard)

    def load(source, target, at):
        return pltpu.make_async_copy(source, target, load_sem.at[at])

    head_lanes = rows_at(y, HEAD_SIZE)
    loads = [
        load(w_query, wqkv.at[z, :, pl.ds(0, mine)], 0),
        load(w_key.at[:, head_lanes], wqkv.at[z, :, pl.ds(mine, HEAD_SIZE)], 1),
        load(w_value.at[:, head_lanes], wqkv.at[z, :, pl.ds(mine + HEAD_SIZE, HEAD_SIZE)], 2),
        load(small, smalls.at[z], 3),
        load(w_output, wout.at[z], 4),
        load(tokens_in, alow, 5),
        load(cotangent_in.at[0], ups.at[block_rows(0, x)], 6),
        load(cotangent_in.at[1], ups.at[block_rows(1, x)], 7),
        load(gate_in, mats.at[0, :, shard_lanes(z)], 8),
        load(up_in, mats.at[1, :, shard_lanes(z)], 9),
        load(down_in, mats.at[2, :, shard_lanes(z)], 10),
    ]
    for copy in loads:
        copy.start()
    lin = x * 4 + me.t

    def plane(number):
        return (z, number // 4, number % 4)

    greet(
        [me.at_z((z + k) % deep) for k in range(1, deep)]
        + [plane((lin + k) % 8) for k in range(1, 8)]
    )
    for copy in loads[:4]:
        copy.wait()

    def halved(buffer):
        def piece(source, part, by):
            return buffer.at[source, rows_at(by, half)]

        return piece

    def expert_piece(source, part, by):
        return mats.at[:, pl.ds(part * units, units), shard_lanes(source)]

    take_qkv = Relay(me, deep, halved(wqkv), up1_sem, dn1_sem, side1_sem)
    take_out = Relay(me, deep, halved(wout), up2_sem, dn2_sem, side2_sem)
    take = Relay(me, deep, expert_piece, up3_sem, dn3_sem)

    def small_out(k):
        there = (z + k) % deep
        return remote(smalls.at[z], smalls.at[z], small_sem, k - 1, me.at_z(there))

    take_qkv.begin(0)
    for k in range(1, deep):
        small_out(k).start()

    def mask(tree):
        return agrad[:, pl.ds(tree * length, length)]

    for tree in range(trees):
        seen, cosine, sine = tree_tables(
            starts, parents, tree, x * rows, rows, length, frequency[:1, :]
        )
        agrad[:, pl.ds(tree * length, length)] = seen
        tables[0, tree] = cosine
        tables[1, tree] = sine
    take_qkv.pass_on(0, 0)
    for copy in loads[4:]:
        copy.wait()
    take_out.begin(0)
    for k in range(1, deep):
        source = (z + deep - k) % deep
        remote(
            smalls.at[source], smalls.at[source], small_sem, k - 1, me.at_z(source)
        ).wait_recv()
    gain_one = jnp.concatenate([smalls[k, :1, :] for k in range(deep)], 1).astype(F32)
    gain_two = jnp.concatenate([smalls[k, 1:2, :] for k in range(deep)], 1).astype(F32)
    router = jnp.concatenate([smalls[k, 8:, :] for k in range(deep)], 1)

    def norm_rows(source, target, at):
        value = source[at, :].astype(F32)
        factor = lax.rsqrt(jnp.mean(value * value, -1, keepdims=True) + EPS)
        target[at, :] = (value * factor * gain_one).astype(BF16)

    for tree in range(trees):

        def first_norm(number, carry):
            at = rows_at(number, step)
            norm_rows(alow.at[tree], core_out.at[pl.ds(tree * rows, rows)], at)
            return carry

        lax.fori_loop(0, CHUNKS, first_norm, 0)
    take_qkv.pass_on(0, 1)
    take_out.pass_on(0, 0)
    take.begin(0)
    take_qkv.pass_on(0, 2)
    take_qkv.finish(0)
    take_out.pass_on(0, 1)

    own_place = rows_at(x, rows)
    away_place = rows_at(1 - x, rows)

    def kv_copy(tree, which, place):
        at = (keys, values)[which].at[tree, place]
        return remote(at, at, kv_sem, 2 * tree + which, me.x_peer())

    for tree in range(trees):
        total = jnp.zeros((rows, wqkv.shape[2]), F32)
        for k in range(deep):
            total = total + mm(
                core_out[pl.ds(tree * rows, rows), pl.ds(k * shard, shard)], wqkv[k]
            )
        cosine, sine = tables[0, tree], tables[1, tree]
        for head in range(heads):
            part_q = total[:, head * HEAD_SIZE : (head + 1) * HEAD_SIZE]
            queries[tree, head] = turn(part_q, cosine, sine).astype(BF16)
        part_k = total[:, mine : mine + HEAD_SIZE]
        keys[tree, own_place, :] = turn(part_k, cosine, sine).astype(BF16)
        values[tree, own_place, :] = total[:, mine + HEAD_SIZE :].astype(BF16)
        for which in range(2):
            kv_copy(tree, which, own_place).start()
    take_out.pass_on(0, 2)
    for tree in range(trees):
        for which in range(2):
            kv_copy(tree, which, away_place).wait_recv()

    def attend(tree):
        def one(head, carry):
            score = mm(queries[tree, head], keys[tree], NT) * inv_root
            score = jnp.where(mask(tree) > 0.5, score, NEG)
            top = jnp.max(score, -1, keepdims=True)
            raised = jnp.exp(score - top)
            prob = (raised / jnp.sum(raised, -1, keepdims=True)).astype(BF16)
            probs[tree, head] = prob
            context[tree, head] = mm(prob, values[tree]).astype(BF16)
            return carry

        lax.fori_loop(0, heads, one, 0)

    attend(0)
    take.pass_on(0, 0)
    take.begin(1, False)
    for part in range(1, groups):
        take.begin(part, True)
    attend(1)
    take_out.finish(0)

    own_up, away_up = ups.at[block_rows(c, x)], ups.at[block_rows(c, 1 - x)]
    peer_up = ups.at[block_rows(1 - c, 1 - x)]
    cot_x = remote(own_up, own_up, cot_sem, 0, me.x_peer())
    cot_x.start()

    def project(tree, row):
        pieces = []
        for k in range(deep):
            piece = jnp.zeros((step, shard), F32)
            for head in range(heads):
                piece = piece + mm(
                    context[tree, head, pl.ds(row, step), :],
                    wout[k, pl.ds(head * HEAD_SIZE, HEAD_SIZE), :],
                )
            pieces.append(piece)
        return pieces

    def core_copy(number):
        at = rows_at(number, step)
        return remote(core_out.at[at], mo_core_in.at[at], core_sem, number, me.core_peer())

    def y_copy(number):
        at = rows_at(number, step)
        return remote(y_out.at[at], mo_y_in.at[at], y_sem, number, me.y_peer())

    for chunk in range(CHUNKS):
        at = pl.ds(chunk * step, step)
        for k, piece in enumerate(project(1 - c, chunk * step)):
            core_out[at, pl.ds(k * shard, shard)] = piece.astype(BF16)
        core_copy(chunk).start()
    for chunk in range(CHUNKS):
        at = pl.ds(chunk * step, step)
        pieces = project(c, chunk * step)
        core_copy(chunk).wait_recv()
        for k, piece in enumerate(pieces):
            lanes = pl.ds(k * shard, shard)
            both = piece.astype(BF16).astype(F32) + mo_core_in[at, lanes].astype(F32)
            y_out[at, lanes] = both.astype(BF16)
        y_copy(chunk).start()
    take.pass_on(0, 1)

    def two_rows(tree, side, number):
        first = (tree * 2 + side) * rows + number * step
        return pl.ds(pl.multiple_of(first, step), step)

    def hid_copy(tree, side, sems, number, device):
        at = hid.at[two_rows(tree, side, number)]
        return remote(at, at, sems, number, device)

    def second(number, carry):
        at = rows_at(number, step)
        y_copy(number).wait_recv()
        value = alow[c, at, :].astype(F32) + (y_out[at, :].astype(F32) + mo_y_in[at, :].astype(F32))
        after[at, :] = value
        factor = lax.rsqrt(jnp.mean(value * value, -1, keepdims=True) + EPS)
        hid[two_rows(c, x, number), :] = (value * factor * gain_two).astype(BF16)
        hid_copy(c, x, hx_sem, number, me.x_peer()).start()
        hid_copy(c, x, hc_sem, number, me.core_peer()).start()
        return carry

    lax.fori_loop(0, 2, second, 0)
    take.pass_on(1, 0)
    take.begin(2, False)
    lax.fori_loop(2, CHUNKS, second, 0)

    logits = mm(router, hid[block_rows(c, x), :], NT)
    expert = lax.broadcasted_iota(jnp.int32, logits.shape, 0)
    chosen = expert < 0
    for k in range(routes.shape[1]):
        chosen = chosen | (expert == routes[c, k : k + 1, :])
    logits = jnp.where(chosen, logits, NEG)
    raised = jnp.where(chosen, jnp.exp(logits - jnp.max(logits, 0, keepdims=True)), 0.0)
    mixes[own_block] = raised / jnp.sum(raised, 0, keepdims=True)

    def mix_copy(tree, side, at, device):
        block = mixes.at[tree * 2 + side]
        return remote(block, block, mix_sem, at, device)

    mix_copy(c, x, 0, me.x_peer()).start()
    mix_copy(c, x, 1, me.core_peer()).start()
    cot_x_in = remote(away_up, away_up, cot_sem, 0, me.x_peer())
    cot_x_in.wait_recv()
    cot_on = remote(away_up, away_up, cot_sem, 1, me.core_peer())
    cot_on.start()
    for number in range(CHUNKS):
        hid_copy(c, 1 - x, hx_sem, number, me.x_peer()).wait_recv()
        hid_copy(c, 1 - x, hf_sem, number, me.core_peer()).start()
    mix_copy(c, 1 - x, 0, me.x_peer()).wait_recv()
    mix_copy(c, 1 - x, 2, me.core_peer()).start()
    remote(peer_up, peer_up, cot_sem, 1, me.core_peer()).wait_recv()
    for number in range(CHUNKS):
        hid_copy(1 - c, x, hc_sem, number, me.core_peer()).wait_recv()
        hid_copy(1 - c, 1 - x, hf_sem, number, me.core_peer()).wait_recv()
    mix_copy(1 - c, x, 1, me.core_peer()).wait_recv()
    mix_copy(1 - c, 1 - x, 2, me.core_peer()).wait_recv()
    take.pass_on(1, 1)
    take.finish(0)

    def expert_block(group, block):
        tokens = rows_at(block, rows)
        some = pl.ds(group * units, units)
        pre_gate = mm(mats[0, some, :], hid[tokens, :], NT)
        pre_up = mm(mats[1, some, :], hid[tokens, :], NT)
        back = mm(mats[2, some, :], ups[tokens, :], NT)
        first, second_half = mixes[block, group : group + 1, :], mixes[
            block, groups + group : groups + group + 1, :
        ]
        weight = jnp.broadcast_to(jnp.where(x == 0, first, second_half), (units, rows))
        square = pre_gate * pre_gate
        bent = jnp.tanh(ROOT_2_PI * pre_gate * (1.0 + CUBIC * square))
        slope = 0.5 * (1.0 + bent)
        active = pre_gate * slope
        rise = slope + 0.5 * pre_gate * (1.0 - bent * bent) * ROOT_2_PI * (
            1.0 + 3.0 * CUBIC * square
        )
        hidden = active * pre_up
        gates[pl.ds(group, 1), tokens] = jnp.sum(hidden * back, 0, keepdims=True)
        back = weight * back
        acts[0, some, tokens] = (back * pre_up * rise).astype(BF16)
        acts[1, some, tokens] = (back * active).astype(BF16)
        acts[2, some, tokens] = (weight * hidden).astype(BF16)

    fold = Fold(me, groups, (own, stage, land), (fold_send, fold_recv, fold_free), 64)
    held_back = 2

    def expert_grad(group, m):
        source = ups if m == 2 else hid
        some = acts.at[m, pl.ds(group * units, units)]

        def one(k, carry):
            value = mm(some[...], source[:, shard_lanes(k)]).astype(BF16)

            @pl.when(k == z)
            def _():
                own[group, m] = value

            @pl.when(k != z)
            def _():
                stage[group % fold.sets, fold.place(k), m] = value

            return carry

        lax.fori_loop(0, deep, one, 0)
        fold.begin(group, m, group < held_back)

    def expert_group(group):
        def one(block, carry):
            expert_block(group, block)
            return carry

        lax.fori_loop(0, 2 * trees, one, 0)
        for m in range(KINDS):
            expert_grad(group, m)

    expert_outs = (d_gate, d_up, d_down)

    def grad_out(group, m):
        return pltpu.make_async_copy(
            bounce.at[m], expert_outs[m].at[pl.ds(group * units, units)], grad_sem.at[m]
        )

    def finish_group(group, ends):
        @pl.when(is_end if ends else jnp.logical_not(is_end))
        def _():
            for m in range(KINDS):
                if group > 0:
                    grad_out(group - 1, m).wait()

                def write(at, value):
                    bounce[m, at, :] = value

                fold.finish(group, m, write)
                grad_out(group, m).start()

    def advance(group):
        for m in range(KINDS):
            fold.advance(group, m, group < held_back)

    def drain(group):
        for m in range(KINDS):
            fold.drain(group, m)

    take.pass_on(2, 0)
    take.begin(3, False)
    expert_group(0)
    take.pass_on(2, 1)
    take.pass_on(3, 0)
    take.finish(1)
    expert_group(1)
    take.pass_on(3, 1)
    advance(0)
    take.finish(2)
    expert_group(2)
    finish_group(0, False)
    advance(1)
    for group in range(held_back):
        for m in range(KINDS):
            fold.let_go(group, m)
    take.finish(3)

    def two_make(first):
        at = pl.ds(first, TILE)
        return mm(acts[0, :, at], mats[0], TN) + mm(acts[1, :, at], mats[1], TN)

    def mo_make(first):
        return mm(acts[2, :, pl.ds(first, TILE)], mats[2], TN)

    two = PlaneSum(
        me,
        rows,
        two_make,
        (core_out, x_out, acc, y_out),
        (two_core_in, two_x_in, two_y_in),
        (two_core_sem, two_x_sem, two_y_sem),
    )
    mo = PlaneSum(
        me,
        rows,
        mo_make,
        (core_out, hid.at[pl.ds(rows, rows)], acc, hid.at[pl.ds(0, rows)]),
        (mo_core_in, mo_x_in, mo_y_in),
        (mo_core_sem, mo_x_sem, mo_y_sem),
    )
    last = groups - 1
    for number in range(CHUNKS):
        core_copy(number).wait_send()
        y_copy(number).wait_send()
    expert_block(last, (1 - c) * 2 + 1 - x)
    two.outward(0)
    expert_block(last, (1 - c) * 2 + x)
    two.outward(1)
    expert_block(last, c * 2 + 1 - x)
    two.across()
    expert_block(last, own_block)

    for block in range(2 * trees):
        gates_out[block, pl.ds(0, groups), :] = gates[:, pl.ds(block * rows, rows)]

    def gate_copy(k):
        there = (lin + k) % 8
        block = (there % 2) * 2 + there // 4
        return remote(gates_out.at[block], gates_in.at[lin], gate_sem, k - 1, plane(there))

    for k in range(1, 8):
        gate_copy(k).start()
    gates_in[lin] = gates_out[own_block]
    two.inward()
    finish_group(1, False)
    drain(0)
    expert_grad(last, 0)
    two.pass_on(0, 1)
    expert_grad(last, 1)
    two.pass_on(1, 2)
    expert_grad(last, 2)
    two.pass_on(2, 3)

    for k in range(1, 8):
        source = (lin + 8 - k) % 8
        remote(gates_out.at[0], gates_in.at[source], gate_sem, k - 1, plane(source)).wait_recv()
    sums = []
    for side in range(2):
        total = gates_in[side * 4]
        for k in range(1, 4):
            total = total + gates_in[side * 4 + k]
        sums.append(total[:groups])
    mix_grad = jnp.concatenate(sums, 0)
    mix = mixes[own_block]
    picked = mix * (mix_grad - jnp.sum(mix * mix_grad, 0, keepdims=True))
    logit_grad = picked.astype(BF16)
    agrad[...] = mm(logit_grad, router, TN)
    small_own[pl.ds(0, 8), :] = jnp.zeros((8, width), F32)
    small_own[pl.ds(8, 8), :] = mm(logit_grad, hid[block_rows(c, x), :])

    for number in range(CHUNKS):
        hid_copy(c, x, hx_sem, number, me.x_peer()).wait_send()
        hid_copy(c, x, hc_sem, number, me.core_peer()).wait_send()
        hid_copy(c, 1 - x, hf_sem, number, me.core_peer()).wait_send()
    two.core_sent()
    mo.outward(0)
    mo.outward(1)
    two.pass_on(3, 4)
    mo.across()
    mo.inward()

    for part in range(groups):
        take.drain(part)
    spare = mats.at[0]
    late = [
        load(tokens_in.at[0], spare.at[pl.ds(0, rows)], 0),
        load(tokens_in.at[1], spare.at[pl.ds(rows, rows)], 1),
    ]
    for copy in late:
        copy.start()
    finish_group(0, True)
    finish_group(1, True)
    advance(2)

    def low_copy(number):
        at = alow.at[c, rows_at(number, step)]
        return remote(at, at, low_sem, number, me.core_peer())

    def second_norm(number, gain_grad):
        at = rows_at(number, step)
        upstream = two.total(number) + agrad[at, :]
        value = after[at, :]
        factor = lax.rsqrt(jnp.mean(value * value, -1, keepdims=True) + EPS)
        scaled = upstream * gain_two
        inner = jnp.mean(scaled * value, -1, keepdims=True)
        cot = ups[two_rows(c, x, number), :]
        total = cot.astype(F32) + (factor * scaled - value * (factor * factor * factor * inner))
        agrad[at, :] = total
        alow[c, at, :] = total.astype(BF16)
        low_copy(number).start()
        return gain_grad + jnp.sum(upstream * value * factor, 0, keepdims=True)

    gain_two_grad = lax.fori_loop(0, CHUNKS, second_norm, jnp.zeros((1, width), F32))
    small_own[pl.ds(1, 1), :] = gain_two_grad

    def attend_back(tree):
        back = jnp.zeros((rows, mine), F32)
        for k in range(deep):
            back = back + mm(alow[tree, :, pl.ds(k * shard, shard)], wout[k], NT)
        back = back.astype(BF16)
        cosine, sine = tables[0, tree], tables[1, tree]
        key_grad = jnp.zeros((length, HEAD_SIZE), F32)
        value_grad = jnp.zeros((length, HEAD_SIZE), F32)
        for head in range(heads):
            lanes = pl.ds(head * HEAD_SIZE, HEAD_SIZE)
            back_head = back[:, head * HEAD_SIZE : (head + 1) * HEAD_SIZE]
            prob = probs[tree, head]
            value_grad = value_grad + mm(prob, back_head, TN)
            prob = prob.astype(F32)
            share = prob * mm(back_head, values[tree], NT)
            score = (share - prob * jnp.sum(share, -1, keepdims=True)).astype(BF16)
            query_grad = mm(score, keys[tree]) * inv_root
            qlow[tree, :, lanes] = turn(query_grad, cosine, -sine).astype(BF16)
            key_grad = key_grad + mm(score, queries[tree, head], TN)
        return jnp.concatenate([key_grad * inv_root, value_grad], 1)

    kv_own[...] = attend_back(c)
    for number in range(CHUNKS):
        at = alow.at[1 - c, pl.ds(number * step, step)]
        remote(at, at, low_sem, number, me.core_peer()).wait_recv()
    kv_out[...] = attend_back(1 - c).astype(BF16)
    kvg_copy = remote(kv_out, kv_in, kvg_sem, 0, me.core_peer())
    kvg_copy.start()

    ctx = [
        jnp.concatenate([context[tree, head] for head in range(heads)], 1) for tree in range(trees)
    ]

    def halves(value):
        low, high = value[:half], value[half:]
        return jnp.where(x == 0, low, high), jnp.where(x == 0, high, low)

    def xs_out(k, lanes):
        return ups.at[pl.ds(k * half, half), lanes]

    xs_lanes = (pl.ds(0, mine), pl.ds(mine, mine), pl.ds(2 * mine, HEAD_SIZE))

    def xs_copy(part):
        lanes = xs_lanes[part]
        return remote(
            ups.at[pl.ds(0, deep * half), lanes], xs_in.at[:, lanes], xs_sem, part, me.x_peer()
        )

    cot_x.wait_send()
    cot_on.wait_send()

    def keep_own(buffer_own, buffer_stage, k, lanes, value):
        @pl.when(k == z)
        def _():
            buffer_own[0, 0, :, lanes] = value.astype(BF16)

        @pl.when(k != z)
        def _():
            buffer_stage[0, fold.place(k), 0, :, lanes] = value.astype(BF16)

    def output_grad(k, carry):
        value = sum(mm(alow[tree, :, shard_lanes(k)], ctx[tree], TN) for tree in range(trees))
        keep, away = halves(value)
        keep_own(own_o, stage_o, k, pl.ds(0, mine), keep)
        ups[rows_at(k, half), xs_lanes[1]] = away.astype(BF16)
        return carry

    lax.fori_loop(0, deep, output_grad, 0)
    xs_copy(1).start()

    def one_tile(tree, at):
        return [mm(qlow[tree, at, :], wqkv[k, :, pl.ds(0, mine)], NT) for k in range(deep)]

    mo.core_sent()

    def one_copy(number):
        at = rows_at(number, step)
        return remote(core_out.at[at], two_core_in.at[at], one_core_sem, number, me.core_peer())

    def one_outward(number, carry):
        at = rows_at(number, step)
        for k, piece in enumerate(one_tile(1 - c, at)):
            core_out[at, pl.ds(k * shard, shard)] = piece.astype(BF16)
        one_copy(number).start()
        return carry

    lax.fori_loop(0, CHUNKS, one_outward, 0)

    kvg_copy.wait_recv()

    def of_side(ref, side):
        low, high = ref[pl.ds(0, rows), :], ref[pl.ds(rows, rows), :]
        return jnp.where(side == 0, low, high).astype(F32)

    kvx_out[...] = (of_side(kv_own, 1 - x) + of_side(kv_in, 1 - x)).astype(BF16)
    kvx_copy = remote(kvx_out, kvx_in, kvg_sem, 1, me.x_peer())
    kvx_copy.start()

    for copy in late:
        copy.wait()
    for tree in range(trees):

        def norm_again(number, carry):
            at = rows_at(number, step)
            norm_rows(
                spare.at[pl.ds(tree * rows, rows)], mats.at[1, pl.ds(tree * rows, rows)], at
            )
            return carry

        lax.fori_loop(0, CHUNKS, norm_again, 0)

    def hid_one(tree, lanes):
        return mats[1, rows_at(tree, rows), lanes]

    def query_weight_grad(k, carry):
        value = sum(mm(hid_one(tree, shard_lanes(k)), qlow[tree], TN) for tree in range(trees))
        keep, away = halves(value)
        keep_own(own_q, stage_q, k, pl.ds(0, mine), keep)
        ups[rows_at(k, half), xs_lanes[0]] = away.astype(BF16)
        return carry

    lax.fori_loop(0, deep, query_weight_grad, 0)
    xs_copy(0).start()
    kvx_copy.wait_recv()
    own_kv = of_side(kv_own, x) + of_side(kv_in, x) + kvx_in[...].astype(F32)
    kvlow[:, pl.ds(0, HEAD_SIZE)] = turn(
        own_kv[:, :HEAD_SIZE], tables[0, c], -tables[1, c]
    ).astype(BF16)
    kvlow[:, pl.ds(HEAD_SIZE, HEAD_SIZE)] = own_kv[:, HEAD_SIZE:].astype(BF16)

    two.y_sent()

    def one_y(number):
        at = rows_at(number, step)
        return remote(y_out.at[at], two_x_in.at[at], one_y_sem, number, me.y_peer())

    def one_inward(number, carry):
        at = rows_at(number, step)
        one_copy(number).wait_recv()
        for k, piece in enumerate(one_tile(c, at)):
            lanes = pl.ds(k * shard, shard)
            piece = piece + mm(kvlow[at, :], wqkv[k, :, pl.ds(mine, 2 * HEAD_SIZE)], NT)
            y_out[at, lanes] = (piece + two_core_in[at, lanes].astype(F32)).astype(BF16)
        one_y(number).start()
        return carry

    lax.fori_loop(0, CHUNKS, one_inward, 0)

    def kv_weight_grad(k, carry):
        value = mm(hid_one(c, shard_lanes(k)), kvlow[...], TN)
        low, high = value[:, :HEAD_SIZE], value[:, HEAD_SIZE:]
        dkv_out[0, k] = jnp.where(c == 0, high, low).astype(BF16)
        dkv_out[1, k] = jnp.where(c == 0, low, high).astype(BF16)
        return carry

    lax.fori_loop(0, deep, kv_weight_grad, 0)
    dkv_copy = remote(dkv_out.at[0], dkv_in, kvg_sem, 2, me.core_peer())
    dkv_copy.start()
    dkv_copy.wait_recv()

    def kv_weight_sum(k, carry):
        keep, away = halves(dkv_out[1, k].astype(F32) + dkv_in[k].astype(F32))
        keep_own(own_q, stage_q, k, pl.ds(mine, HEAD_SIZE), keep)
        ups[rows_at(k, half), xs_lanes[2]] = away.astype(BF16)
        return carry

    lax.fori_loop(0, deep, kv_weight_sum, 0)
    xs_copy(2).start()

    mo.pass_on(0, CHUNKS)
    finish_group(2, False)
    finish_group(2, True)

    fold_o = Fold(me, 1, (own_o, stage_o, land_o), (fold_send_o, fold_recv_o, None), 64)
    fold_q = Fold(me, 1, (own_q, stage_q, land_q), (fold_send_q, fold_recv_q, None), 64)

    def side_sum(buffer_own, buffer_stage, lanes_in, lanes):
        def one(k, carry):
            more = xs_in[rows_at(k, half), lanes_in].astype(F32)

            @pl.when(k == z)
            def _():
                buffer_own[0, 0, :, lanes] = (
                    buffer_own[0, 0, :, lanes].astype(F32) + more
                ).astype(BF16)

            @pl.when(k != z)
            def _():
                buffer_stage[0, fold.place(k), 0, :, lanes] = (
                    buffer_stage[0, fold.place(k), 0, :, lanes].astype(F32) + more
                ).astype(BF16)

            return carry

        lax.fori_loop(0, deep, one, 0)

    xs_copy(1).wait_recv()
    side_sum(own_o, stage_o, xs_lanes[1], pl.ds(0, mine))
    fold_o.begin(0, 0, False)

    def out_copies(buffer, target, first, peer_sems, number):
        at = rows_at(number, step)
        here = pltpu.make_async_copy(buffer.at[at], target.at[c, at], out_sem.at[first + number])
        there = remote(buffer.at[at], target.at[c, at], peer_sems, number, me.core_peer())
        return here, there

    def first_norm_back(number, gain_grad):
        at = rows_at(number, step)
        one_y(number).wait_recv()
        upstream = y_out[at, :].astype(F32) + two_x_in[at, :].astype(F32)
        first = pl.multiple_of(c * rows + number * step, step)
        value = mats[0, pl.ds(first, step), :].astype(F32)
        factor = lax.rsqrt(jnp.mean(value * value, -1, keepdims=True) + EPS)
        scaled = upstream * gain_one
        inner = jnp.mean(scaled * value, -1, keepdims=True)
        acc[at, :] = agrad[at, :] + (
            factor * scaled - value * (factor * factor * factor * inner)
        )
        for copy in out_copies(acc, d_tokens, CHUNKS, token_sem, number):
            copy.start()
        return gain_grad + jnp.sum(upstream * value * factor, 0, keepdims=True)

    gain_one_grad = lax.fori_loop(0, CHUNKS, first_norm_back, jnp.zeros((1, width), F32))
    small_own[pl.ds(0, 1), :] = gain_one_grad
    small_c = remote(small_own, small_core, small_c_sem, 0, me.core_peer())
    small_c.start()
    fold_o.advance(0, 0, False)
    xs_copy(0).wait_recv()
    side_sum(own_q, stage_q, xs_lanes[0], pl.ds(0, mine))
    xs_copy(2).wait_recv()
    side_sum(own_q, stage_q, xs_lanes[2], pl.ds(mine, HEAD_SIZE))
    fold_q.begin(0, 0, False)
    advance(3)

    small_c.wait_recv()
    small_c.wait_send()
    small_own[...] = small_own[...] + small_core[...]
    small_x_copy = remote(small_own, small_x, small_x_sem, 0, me.x_peer())
    small_x_copy.start()

    two.x_sent()

    def mix_out(number, carry):
        at = rows_at(number, step)
        x_out[at, :] = (after[at, :] + mo.total(number)).astype(BF16)
        for copy in out_copies(x_out, mixed, 0, mixed_sem, number):
            copy.start()
        return carry

    lax.fori_loop(0, CHUNKS, mix_out, 0)
    fold_q.advance(0, 0, False)
    small_x_copy.wait_recv()
    small_x_copy.wait_send()
    small_own[...] = small_own[...] + small_x[...]

    def small_copy(k):
        there = (z + k) % deep
        return remote(
            small_own.at[:, shard_lanes(there)], small_z.at[z], small_z_sem, k - 1, me.at_z(there)
        )

    for k in range(1, deep):
        small_copy(k).start()
    small_z[z] = small_own[:, shard_lanes(z)]
    finish_group(3, False)
    finish_group(3, True)

    def write_o(at, value):
        d_qo[at, pl.ds(mine, mine)] = value

    fold_o.finish(0, 0, write_o)

    def write_q(at, value):
        d_qo[at, pl.ds(0, mine)] = value[:, :mine]
        kv_last[at, :] = value[:, mine:]

    fold_q.finish(0, 0, write_q)

    share = half // 4

    def kv_columns(t):
        return rows_at((t % 2) * 2 + t // 2, HEAD_SIZE)

    def share_rows(t):
        return pl.ds(pl.multiple_of(t * share, 8), share)

    def last_copy(k):
        there = (me.t + k) % 4
        return remote(
            kv_last.at[share_rows(there)],
            d_kv.at[:, kv_columns(me.t)],
            last_sem,
            k - 1,
            (z, x, there),
        )

    for k in range(1, 4):
        last_copy(k).start()
    d_kv[:, kv_columns(me.t)] = kv_last[share_rows(me.t), :]
    for k in range(1, deep):
        source = (z + deep - k) % deep
        remote(
            small_own.at[:, shard_lanes(0)], small_z.at[source], small_z_sem, k - 1, me.at_z(source)
        ).wait_recv()
    total = small_z[0]
    for k in range(1, deep):
        total = total + small_z[k]
    d_small[...] = total
    for k in range(1, 4):
        source = (me.t + 4 - k) % 4
        remote(
            kv_last.at[pl.ds(0, share)],
            d_kv.at[:, kv_columns(source)],
            last_sem,
            k - 1,
            (z, x, source),
        ).wait_recv()

    for number in range(CHUNKS):
        at = pl.ds(number * step, step)
        remote(x_out.at[at], mixed.at[1 - c, at], mixed_sem, number, me.core_peer()).wait_recv()
        remote(acc.at[at], d_tokens.at[1 - c, at], token_sem, number, me.core_peer()).wait_recv()
        for buffer, target, first, peer_sems in (
            (x_out, mixed, 0, mixed_sem),
            (acc, d_tokens, CHUNKS, token_sem),
        ):
            here, there = out_copies(buffer, target, first, peer_sems, number)
            here.wait()
            there.wait_send()
        one_y(number).wait_send()
        one_copy(number).wait_send()
        low_copy(number).wait_send()
    mo.x_sent()
    mo.y_sent()
    for m in range(KINDS):
        grad_out(groups - 1, m).wait()
    for k in range(1, 8):
        gate_copy(k).wait_send()
    for k in range(1, deep):
        small_copy(k).wait_send()
        small_out(k).wait_send()
    for k in range(1, 4):
        last_copy(k).wait_send()
    for part in range(3):
        xs_copy(part).wait_send()
    for copy in (kvg_copy, kvx_copy, dkv_copy):
        copy.wait_send()
    for tree in range(trees):
        for which in range(2):
            kv_copy(tree, which, own_place).wait_send()
    mix_copy(c, x, 0, me.x_peer()).wait_send()
    mix_copy(c, x, 1, me.core_peer()).wait_send()
    mix_copy(c, 1 - x, 2, me.core_peer()).wait_send()
    take_qkv.drain(0)
    take_out.drain(0)
    for group in range(1, groups):
        drain(group)
    fold_o.drain(0, 0)
    fold_q.drain(0, 0)


def sems(count):
    return pltpu.SemaphoreType.DMA((2, count))


def layer_call(
    seg_start,
    seg_parent,
    routes,
    small,
    tokens,
    cotangent,
    w_query,
    w_key,
    w_value,
    w_output,
    gate_t,
    up_t,
    w_down,
    deep,
):
    trees, rows, width = tokens.shape
    shard, mine = w_query.shape
    heads = mine // HEAD_SIZE
    length = rows * 2
    held, units = w_down.shape[0], w_down.shape[1]
    total_units = held * units
    experts = small.shape[0] - 8
    blocks = 2 * trees
    half = shard // 2
    count = blocks * rows
    sets = 3
    angle = HEAD_SIZE // 2
    frequency = ROPE_BASE ** (-2.0 * np.arange(angle, dtype=np.float32) / np.float32(HEAD_SIZE))
    frequency = np.tile(np.concatenate([frequency] * 2)[None], (8, 1)).astype(np.float32)
    vmem = pl.BlockSpec(memory_space=pltpu.VMEM)
    smem = pl.BlockSpec(memory_space=pltpu.SMEM)
    hbm = pl.BlockSpec(memory_space=pl.ANY)

    def plain(*shape):
        return pltpu.VMEM(shape, BF16)

    def wide(*shape):
        return pltpu.VMEM(shape, F32)

    def out(*shape, dtype=F32):
        return jax.ShapeDtypeStruct(shape, dtype)

    lanes = 2 * mine + HEAD_SIZE
    last = deep - 1
    return pl.pallas_call(
        layer_kernel,
        out_shape=(
            out(trees, rows, width, dtype=BF16),
            out(trees, rows, width),
            out(total_units, shard),
            out(total_units, shard),
            out(total_units, shard),
            out(half, 2 * mine),
            out(half // 4, 2 * KEY_VALUE_HEADS * HEAD_SIZE),
            out(small.shape[0], shard),
        ),
        in_specs=[smem, smem, vmem, vmem] + [hbm] * 10,
        out_specs=[hbm] * 5 + [vmem] * 3,
        scratch_shapes=[
            plain(KINDS, total_units, width),
            plain(KINDS, total_units, count),
            plain(count, width),
            plain(count, width),
            plain(deep, shard, mine + 2 * HEAD_SIZE),
            plain(deep, mine, shard),
            plain(deep, small.shape[0], shard),
            plain(trees, heads, rows, HEAD_SIZE),
            plain(trees, length, HEAD_SIZE),
            plain(trees, length, HEAD_SIZE),
            plain(trees, heads, rows, length),
            plain(trees, heads, rows, HEAD_SIZE),
            wide(2, trees, rows, HEAD_SIZE),
            wide(rows, width),
            wide(blocks, experts, rows),
            wide(held, count),
            wide(blocks, 8, rows),
            wide(8, 8, rows),
            plain(2 * rows, width),
            plain(rows, width),
            wide(rows, width),
            plain(rows, width),
            plain(2 * rows, width),
            plain(rows, width),
            plain(rows, width),
            plain(2 * rows, width),
            plain(rows, width),
            plain(rows, width),
            wide(rows, width),
            plain(trees, rows, width),
            plain(trees, rows, mine),
            plain(length, 2 * HEAD_SIZE),
            plain(length, 2 * HEAD_SIZE),
            wide(length, 2 * HEAD_SIZE),
            plain(rows, 2 * HEAD_SIZE),
            plain(rows, 2 * HEAD_SIZE),
            plain(rows, 2 * HEAD_SIZE),
            plain(2, deep, shard, HEAD_SIZE),
            plain(deep, shard, HEAD_SIZE),
            plain(deep * half, lanes),
            plain(held, KINDS, units, shard),
            plain(sets, last, KINDS, units, shard),
            plain(sets, deep, KINDS, units, shard),
            wide(KINDS, units, shard),
            plain(1, 1, half, mine),
            plain(1, last, 1, half, mine),
            plain(1, deep, 1, half, mine),
            plain(1, 1, half, mine + HEAD_SIZE),
            plain(1, last, 1, half, mine + HEAD_SIZE),
            plain(1, deep, 1, half, mine + HEAD_SIZE),
            wide(small.shape[0], width),
            wide(small.shape[0], width),
            wide(small.shape[0], width),
            wide(deep, small.shape[0], shard),
            wide(half, HEAD_SIZE),
            pltpu.SemaphoreType.DMA((11,)),
            sems(last),
            sems(deep),
            sems(deep),
            sems(2 * deep),
            sems(deep),
            sems(deep),
            sems(2 * deep),
            sems(held * deep),
            sems(held * deep),
            sems(2 * trees),
            sems(2),
            sems(CHUNKS),
            sems(CHUNKS),
            sems(CHUNKS),
            sems(CHUNKS),
            sems(CHUNKS),
            sems(3),
            sems(7),
            sems(2 * rows // TILE),
            sems(CHUNKS),
            sems(CHUNKS),
            sems(2 * rows // TILE),
            sems(CHUNKS),
            sems(CHUNKS),
            sems(CHUNKS),
            sems(CHUNKS),
            sems(CHUNKS),
            sems(3),
            sems(3),
            pltpu.SemaphoreType.DMA((sets * 3 * KINDS,)),
            pltpu.SemaphoreType.DMA((sets * 4 * KINDS,)),
            pltpu.SemaphoreType.REGULAR((sets * 3 * KINDS,)),
            pltpu.SemaphoreType.DMA((3,)),
            pltpu.SemaphoreType.DMA((4,)),
            pltpu.SemaphoreType.DMA((3,)),
            pltpu.SemaphoreType.DMA((4,)),
            pltpu.SemaphoreType.DMA((2 * CHUNKS,)),
            sems(CHUNKS),
            sems(CHUNKS),
            pltpu.SemaphoreType.DMA((KINDS,)),
            sems(1),
            sems(1),
            sems(last),
            sems(3),
        ],
        compiler_params=pltpu.CompilerParams(
            collective_id=0, has_side_effects=True, vmem_limit_bytes=64 * 2**20
        ),
        name="layer",
    )(
        seg_start,
        seg_parent,
        jnp.asarray(frequency),
        routes,
        small,
        tokens,
        cotangent,
        w_query,
        w_key,
        w_value,
        w_output,
        gate_t.reshape(total_units, -1),
        up_t.reshape(total_units, -1),
        w_down.reshape(total_units, -1),
    )


def plane_shards(
    tokens,
    cotangent,
    seg_start,
    seg_parent,
    routes,
    attn_gain,
    w_query,
    w_key,
    w_value,
    w_output,
    moe_gain,
    w_router,
    w_gate,
    w_up,
    w_down,
):
    width = tokens.shape[2]
    deep = lax.axis_size("dp")
    held, quarter = w_gate.shape[0], w_gate.shape[2]
    mine = w_query.shape[1]
    small = jnp.concatenate(
        [attn_gain[None], moe_gain[None], jnp.zeros((6, attn_gain.shape[0]), BF16), w_router.T], 0
    )
    mixed, d_tokens, d_gate, d_up, d_down, d_qo, d_kv, d_small = layer_call(
        seg_start,
        seg_parent,
        jnp.swapaxes(routes, 1, 2),
        small,
        tokens,
        cotangent,
        w_query,
        w_key,
        w_value,
        w_output,
        jnp.swapaxes(w_gate, 1, 2),
        jnp.swapaxes(w_up, 1, 2),
        w_down,
        deep,
    )
    part = width // deep // 2
    d_small = lax.dynamic_slice_in_dim(d_small, lax.axis_index("expert") * part, part, 1)
    kv = KEY_VALUE_HEADS * HEAD_SIZE

    def experts(array):
        return array.reshape(held, quarter, width // deep)

    return (
        mixed,
        d_tokens,
        d_small[0],
        d_qo[:, :mine],
        d_kv[:, :kv],
        d_kv[:, kv:],
        d_qo[:, mine:].T,
        d_small[1],
        d_small[8:].T,
        jnp.swapaxes(experts(d_gate), 1, 2),
        jnp.swapaxes(experts(d_up), 1, 2),
        experts(d_down),
    )


def shards(*arrays):
    axes = tuple(lax.axis_size(name) for name in ("dp", "expert", "tensor"))
    if axes == (4, 2, 4) and arrays[0].shape[0] == 2:
        return plane_shards(*arrays)
    return general_shards(*arrays)


def solution(mesh):
    placed = (
        P("dp", "expert", None),
        P("dp", "expert", None),
        P("dp", None),
        P("dp", None),
        P("dp", "expert", None),
        P("dp"),
        P("dp", "tensor"),
        P("dp", None),
        P("dp", None),
        P("tensor", "dp"),
        P("dp"),
        P("dp", None),
        P("expert", "dp", "tensor"),
        P("expert", "dp", "tensor"),
        P("expert", "tensor", "dp"),
    )
    return jax.shard_map(
        shards,
        mesh=mesh,
        in_specs=placed,
        out_specs=(
            P("dp", "expert", None),
            P("dp", "expert", None),
            P(("dp", "expert")),
            P(("dp", "expert"), "tensor"),
            P(("dp", "expert", "tensor"), None),
            P(("dp", "expert", "tensor"), None),
            P("tensor", ("dp", "expert")),
            P(("dp", "expert")),
            P(("dp", "expert"), None),
            P("expert", "dp", "tensor"),
            P("expert", "dp", "tensor"),
            P("expert", "tensor", "dp"),
        ),
        check_vma=False,
    )
```

```python
import functools
import math

import jax
import jax.numpy as jnp
import numpy as np
from jax import lax
from jax.experimental import pallas as pl
from jax.experimental.pallas import tpu as pltpu
from jax.sharding import PartitionSpec as P

QUERY_HEADS = 12
KEY_VALUE_HEADS = 2
HEAD_SIZE = 128
GROUP = QUERY_HEADS // KEY_VALUE_HEADS
EPS = 1e-05
ROPE_BASE = 10000.0
NEG = -1e30
F32 = jnp.float32
BF16 = jnp.bfloat16


def dot(left, right, dims):
    return lax.dot_general(left, right, (dims, ((), ())), preferred_element_type=F32)


def norm_factor(rows):
    return lax.rsqrt(jnp.mean(rows * rows, -1, keepdims=True) + EPS)


def norm_back(rows, factor, gain, upstream):
    scaled = upstream * gain
    gain_grad = jnp.sum(upstream * rows * factor, 0)
    inner = jnp.mean(scaled * rows, -1, keepdims=True)
    return factor * scaled - rows * (factor * factor * factor * inner), gain_grad


def layout(starts, parents, places, length):
    labels = jnp.arange(starts.shape[1], dtype=jnp.int32)

    def pick(table, at):
        hot = at[:, :, None] == labels[None, None, :]
        return jnp.sum(jnp.where(hot, table[:, None, :], 0), 2, dtype=jnp.int32)

    segment = jnp.sum((starts[:, None, :] <= places[None, :, None]).astype(jnp.int32), 2) - 1
    above = pick(parents, segment)
    further = pick(parents, above)
    ends = jnp.concatenate(
        [starts[:, 1:], jnp.full((starts.shape[0], 1), length, jnp.int32)], 1
    )
    lengths = ends - starts
    depths = (
        places[None, :]
        - pick(starts, segment)
        + jnp.where(segment != 0, pick(lengths, above), 0)
        + jnp.where(above != 0, pick(lengths, further), 0)
    )
    return segment, above, further, depths


def angles(depths):
    half = HEAD_SIZE // 2
    frequency = ROPE_BASE ** (-2.0 * jnp.arange(half, dtype=F32) / HEAD_SIZE)
    turning = depths.astype(F32)[..., None] * frequency
    return jnp.cos(turning), jnp.sin(turning)


def rotate(heads, cosine, sine):
    half = HEAD_SIZE // 2
    front, back = heads[..., :half], heads[..., half:]
    return jnp.concatenate([front * cosine - back * sine, back * cosine + front * sine], -1)


def general_shards(
    tokens,
    cotangent,
    seg_start,
    seg_parent,
    routes,
    attn_gain,
    w_query,
    w_key,
    w_value,
    w_output,
    moe_gain,
    w_router,
    w_gate,
    w_up,
    w_down,
):
    trees, rows, width = tokens.shape
    expert_count = lax.axis_size("expert")
    tensor_count = lax.axis_size("tensor")
    tensor_at = lax.axis_index("tensor")
    expert_at = lax.axis_index("expert")
    length = rows * expert_count
    heads = w_query.shape[1] // HEAD_SIZE
    kv_head = tensor_at * heads // GROUP
    inv_root = HEAD_SIZE ** (-0.5)
    own_experts = w_gate.shape[0]
    quarter = w_gate.shape[2]
    all_experts = w_router.shape[1]

    def over_dp(array, axis):
        return lax.all_gather(array, "dp", axis=axis, tiled=True)

    w_query = over_dp(w_query, 0)
    w_output = over_dp(w_output, 1)
    gate_t = over_dp(jnp.swapaxes(w_gate, 1, 2), 2)
    up_t = over_dp(jnp.swapaxes(w_up, 1, 2), 2)
    down = over_dp(w_down, 2)
    small = over_dp(
        jnp.concatenate(
            [
                lax.dynamic_slice_in_dim(w_key, kv_head * HEAD_SIZE, HEAD_SIZE, 1),
                lax.dynamic_slice_in_dim(w_value, kv_head * HEAD_SIZE, HEAD_SIZE, 1),
                w_router,
                attn_gain[:, None],
                moe_gain[:, None],
            ],
            1,
        ),
        0,
    )
    w_kv = small[:, : 2 * HEAD_SIZE]
    w_router = small[:, 2 * HEAD_SIZE : 2 * HEAD_SIZE + all_experts]
    attn_gain = small[:, -2].astype(F32)
    moe_gain = small[:, -1].astype(F32)

    all_places = jnp.arange(length, dtype=jnp.int32)
    places = expert_at * rows + jnp.arange(rows, dtype=jnp.int32)
    segment, above, further, depths = layout(seg_start, seg_parent, places, length)
    key_segment = layout(seg_start, seg_parent, all_places, length)[0]
    cosine, sine = angles(depths)
    of_key = key_segment[:, None, :]
    visible = (
        (of_key == segment[:, :, None])
        | (of_key == above[:, :, None])
        | (of_key == further[:, :, None])
    ) & (all_places[None, None, :] <= places[None, :, None])

    residual = tokens.astype(F32).reshape(trees * rows, width)
    factor_one = norm_factor(residual)
    hidden_one = (residual * factor_one * attn_gain).astype(BF16)
    query_pre = dot(hidden_one, w_query, ((1,), (0,))).reshape(trees, rows, heads, HEAD_SIZE)
    kv_pre = dot(hidden_one, w_kv, ((1,), (0,))).reshape(trees, rows, 2 * HEAD_SIZE)
    queries = rotate(query_pre, cosine[:, :, None, :], sine[:, :, None, :]).astype(BF16)
    own_keys = rotate(kv_pre[..., :HEAD_SIZE], cosine, sine).astype(BF16)
    own_kv = jnp.concatenate([own_keys, kv_pre[..., HEAD_SIZE:].astype(BF16)], -1)
    keys_values = lax.all_gather(own_kv, "expert", axis=1, tiled=True)
    keys, values = keys_values[..., :HEAD_SIZE], keys_values[..., HEAD_SIZE:]
    scores = jnp.einsum("bqhd,bkd->bhqk", queries, keys, preferred_element_type=F32) * inv_root
    scores = jnp.where(visible[:, None], scores, NEG)
    row_max = jnp.max(scores, -1, keepdims=True)
    exponent = jnp.exp(scores - row_max)
    probs = exponent / jnp.sum(exponent, -1, keepdims=True)
    probs_low = probs.astype(BF16)
    context = jnp.einsum("bhqk,bkd->bqhd", probs_low, values, preferred_element_type=F32)
    context_low = context.reshape(trees * rows, heads * HEAD_SIZE).astype(BF16)
    attn_out = dot(context_low, w_output, ((1,), (0,))).astype(BF16)
    after_attn = residual + lax.psum(attn_out, "tensor").astype(F32)

    factor_two = norm_factor(after_attn)
    hidden_two = (after_attn * factor_two * moe_gain).astype(BF16)
    logits = dot(hidden_two, w_router, ((1,), (0,)))
    chosen = jnp.any(
        routes.reshape(trees * rows, -1)[:, :, None]
        == jnp.arange(all_experts, dtype=jnp.int32)[None, None, :],
        1,
    )
    masked = jnp.where(chosen, logits, NEG)
    raised = jnp.where(chosen, jnp.exp(masked - jnp.max(masked, -1, keepdims=True)), 0.0)
    mixing = raised / jnp.sum(raised, -1, keepdims=True)

    def over_expert(array):
        full = lax.all_gather(
            array.reshape(trees, rows, array.shape[-1]), "expert", axis=1, tiled=True
        )
        return full.reshape(trees * length, array.shape[-1])

    every_hidden = over_expert(hidden_two)
    every_up = over_expert(cotangent)
    every_mix = lax.dynamic_slice_in_dim(
        over_expert(mixing), expert_at * own_experts, own_experts, 1
    )
    count = trees * length
    pre_gate = dot(every_hidden, gate_t.reshape(-1, width), ((1,), (1,)))
    pre_up = dot(every_hidden, up_t.reshape(-1, width), ((1,), (1,)))
    down_rows = down.reshape(-1, width)
    down_back = dot(every_up, down_rows, ((1,), (1,)))
    wide_mix = jnp.repeat(every_mix, quarter, axis=1)
    activated, pull = jax.vjp(jax.nn.gelu, pre_gate)
    hidden = activated * pre_up
    mixed_hidden = (hidden * wide_mix).astype(BF16)
    moe_part = dot(mixed_hidden, down_rows, ((1,), (0,))).astype(BF16)
    gate_part = jnp.sum((hidden * down_back).reshape(count, own_experts, quarter), -1)
    hidden_grad = wide_mix * down_back
    gate_pre = pull(hidden_grad * pre_up)[0].astype(BF16)
    up_pre = (hidden_grad * activated).astype(BF16)
    two_part = (
        dot(gate_pre, gate_t.reshape(-1, width), ((1,), (0,)))
        + dot(up_pre, up_t.reshape(-1, width), ((1,), (0,)))
    ).astype(BF16)
    d_down = dot(mixed_hidden, every_up, ((0,), (0,)))
    d_gate = dot(gate_pre, every_hidden, ((0,), (0,)))
    d_up = dot(up_pre, every_hidden, ((0,), (0,)))

    def to_owner(array):
        array = array.reshape(trees, length, array.shape[-1])
        part = lax.psum_scatter(array, "expert", scatter_dimension=1, tiled=True)
        return lax.psum(part, "tensor").reshape(trees * rows, -1)

    spread = jnp.arange(all_experts) // own_experts == expert_at
    gate_wide = jnp.where(
        spread[None, :], jnp.tile(gate_part, (1, all_experts // own_experts)), 0.0
    )
    two_grad = to_owner(two_part).astype(F32)
    mix_grad = to_owner(gate_wide)
    mixed_out = (after_attn + to_owner(moe_part).astype(F32)).astype(BF16)

    picked_grad = mixing * (mix_grad - jnp.sum(mixing * mix_grad, -1, keepdims=True))
    logit_grad = picked_grad.astype(BF16)
    two_grad = two_grad + dot(logit_grad, w_router, ((1,), (1,)))
    d_router = dot(hidden_two, logit_grad, ((0,), (0,)))
    norm_two, d_moe_gain = norm_back(after_attn, factor_two, moe_gain, two_grad)
    attn_grad = cotangent.astype(F32).reshape(trees * rows, width) + norm_two
    attn_low = attn_grad.astype(BF16)

    d_output = dot(context_low, attn_low, ((0,), (0,)))
    context_grad = (
        dot(attn_low, w_output, ((1,), (1,)))
        .astype(BF16)
        .reshape(trees, rows, heads, HEAD_SIZE)
    )
    prob_grad = jnp.einsum("bqhd,bkd->bhqk", context_grad, values, preferred_element_type=F32)
    score_grad = probs * (prob_grad - jnp.sum(probs * prob_grad, -1, keepdims=True))
    score_grad = score_grad.astype(BF16)
    query_grad = (
        jnp.einsum("bhqk,bkd->bqhd", score_grad, keys, preferred_element_type=F32) * inv_root
    )
    key_grad = (
        jnp.einsum("bhqk,bqhd->bkd", score_grad, queries, preferred_element_type=F32) * inv_root
    )
    value_grad = jnp.einsum("bhqk,bqhd->bkd", probs_low, context_grad, preferred_element_type=F32)
    kv_part = jnp.concatenate([key_grad, value_grad], -1).astype(BF16)
    kv_sum = lax.psum_scatter(kv_part, "expert", scatter_dimension=1, tiled=True)
    sharing = GROUP // heads
    own_rows = rows // sharing
    place = tensor_at % sharing
    kv_rows = kv_sum.reshape(trees, sharing, own_rows, 2 * HEAD_SIZE)
    mine = lax.dynamic_index_in_dim(kv_rows, place, 1, False).astype(F32)
    for step in range(1, sharing):
        order = [
            (at, at // sharing * sharing + (at + step) % sharing) for at in range(tensor_count)
        ]
        away = lax.dynamic_index_in_dim(kv_rows, (place + step) % sharing, 1, False)
        mine = mine + lax.ppermute(away, "tensor", order).astype(F32)

    def own(array):
        return lax.dynamic_slice_in_dim(array, place * own_rows, own_rows, 1)

    key_low = rotate(mine[..., :HEAD_SIZE], own(cosine), -own(sine)).astype(BF16)
    kv_low = jnp.concatenate([key_low, mine[..., HEAD_SIZE:].astype(BF16)], -1)
    kv_low = kv_low.reshape(trees * own_rows, 2 * HEAD_SIZE)
    hidden_own = own(hidden_one.reshape(trees, rows, width)).reshape(trees * own_rows, width)
    d_kv = dot(hidden_own, kv_low, ((0,), (0,)))
    kv_back = dot(kv_low, w_kv, ((1,), (1,))).reshape(trees, own_rows, width)
    query_low = rotate(query_grad, cosine[:, :, None, :], -sine[:, :, None, :])
    query_low = query_low.astype(BF16).reshape(trees * rows, heads * HEAD_SIZE)
    d_query = dot(hidden_one, query_low, ((0,), (0,)))
    one_part = dot(query_low, w_query, ((1,), (1,))).reshape(trees, rows, width)
    one_part = lax.dynamic_update_slice_in_dim(
        one_part, own(one_part) + kv_back, place * own_rows, 1
    ).reshape(trees * rows, width)
    one_grad = lax.psum(one_part.astype(BF16), "tensor").astype(F32)
    norm_one, d_attn_gain = norm_back(residual, factor_one, attn_gain, one_grad)
    d_tokens = (attn_grad + norm_one).reshape(trees, rows, width)

    def scatter_dp(array, axis):
        return lax.psum_scatter(array, "dp", scatter_dimension=axis, tiled=True)

    def scatter_expert(array, axis):
        return lax.psum_scatter(array, "expert", scatter_dimension=axis, tiled=True)

    def experts_home(array):
        return scatter_dp(array.astype(BF16), 1).astype(F32).reshape(own_experts, quarter, -1)

    d_gate, d_up, d_down = experts_home(d_gate), experts_home(d_up), experts_home(d_down)
    d_query = scatter_expert(scatter_dp(d_query.astype(BF16), 0), 0).astype(F32)
    d_output = scatter_expert(scatter_dp(d_output.astype(BF16), 1), 1).astype(F32)
    flat = jnp.concatenate([d_attn_gain[:, None], d_moe_gain[:, None], d_router], 1)
    flat = scatter_expert(scatter_dp(flat, 0), 0)
    of_head = (jnp.arange(KEY_VALUE_HEADS) == kv_head).astype(F32)[None, None, :, None]
    d_kv = scatter_expert(scatter_dp(d_kv, 0), 0).reshape(-1, 2, 1, HEAD_SIZE) * of_head
    d_kv = d_kv.reshape(-1, 2 * KEY_VALUE_HEADS * HEAD_SIZE)
    d_kv = lax.psum_scatter(d_kv, "tensor", scatter_dimension=0, tiled=True)
    return (
        mixed_out.reshape(trees, rows, width),
        d_tokens,
        flat[:, 0],
        d_query,
        d_kv[:, : KEY_VALUE_HEADS * HEAD_SIZE],
        d_kv[:, KEY_VALUE_HEADS * HEAD_SIZE :],
        d_output,
        flat[:, 1],
        flat[:, 2:],
        jnp.swapaxes(d_gate, 1, 2),
        jnp.swapaxes(d_up, 1, 2),
        d_down,
    )


MESH = pl.DeviceIdType.MESH
NT = (((1,), (1,)), ((), ()))
NN = (((1,), (0,)), ((), ()))
TN = (((0,), (0,)), ((), ()))
CHUNKS = 4
TILE = 128
KINDS = 3
ROOT_2_PI = math.sqrt(2.0 / math.pi)
CUBIC = 0.044715


def mm(left, right, dims=NN):
    return lax.dot_general(left, right, dims, preferred_element_type=F32)


def rows_at(number, size):
    return pl.ds(pl.multiple_of(number * size, size), size)


class Place:
    def __init__(self):
        self.z = lax.axis_index("dp")
        self.x = lax.axis_index("expert")
        self.t = lax.axis_index("tensor")
        self.y = self.t // 2
        self.c = self.t % 2

    def at_z(self, z):
        return (z, self.x, self.t)

    def x_peer(self):
        return (self.z, 1 - self.x, self.t)

    def y_peer(self):
        return (self.z, self.x, (self.t + 2) % 4)

    def core_peer(self):
        return (self.z, self.x, self.t + 1 - 2 * self.c)


def remote(src, dst, sems, at, device):
    return pltpu.make_async_remote_copy(
        src_ref=src,
        dst_ref=dst,
        send_sem=sems.at[0, at],
        recv_sem=sems.at[1, at],
        device_id=device,
        device_id_type=MESH,
    )


def signal(sem, device):
    pl.semaphore_signal(sem, inc=1, device_id=device, device_id_type=MESH)


def await_signal(sem):
    pl.semaphore_wait(sem, 1)


def greet(devices):
    barrier = pltpu.get_barrier_semaphore()
    for device in devices:
        pl.semaphore_signal(barrier, inc=1, device_id=device, device_id_type=MESH)
    pl.semaphore_wait(barrier, len(devices))


def tree_tables(starts, parents, tree, first, rows, length, frequency):
    count = starts.shape[1]
    place = first + lax.broadcasted_iota(jnp.int32, (rows, HEAD_SIZE), 0)
    start = [starts[tree, k] for k in range(count)]
    parent = [parents[tree, k] for k in range(count)]
    size = [(start[k + 1] if k + 1 < count else length) - start[k] for k in range(count)]

    def pick(table, at):
        total = jnp.zeros_like(at)
        for k in range(count):
            total = total + jnp.where(at == k, table[k], 0)
        return total

    def segment_of(at):
        total = jnp.zeros_like(at)
        for k in range(1, count):
            total = total + jnp.where(at >= start[k], 1, 0)
        return total

    segment = segment_of(place)
    above = pick(parent, segment)
    further = pick(parent, above)
    depth = (
        place
        - pick(start, segment)
        + jnp.where(segment != 0, pick(size, above), 0)
        + jnp.where(above != 0, pick(size, further), 0)
    )
    turning = depth.astype(F32) * frequency
    lane = lax.broadcasted_iota(jnp.int32, (rows, HEAD_SIZE), 1)
    cosine = jnp.cos(turning)
    sine = jnp.sin(turning)
    sine = jnp.where(lane < HEAD_SIZE // 2, -sine, sine)
    key_place = lax.broadcasted_iota(jnp.int32, (8, length), 1)
    key_segment = jnp.broadcast_to(segment_of(key_place)[:1], (rows, length))
    key_place = jnp.broadcast_to(key_place[:1], (rows, length))
    wide = length // HEAD_SIZE

    def widen(array):
        return jnp.concatenate([array] * wide, 1)

    visible = (
        (key_segment == widen(segment))
        | (key_segment == widen(above))
        | (key_segment == widen(further))
    ) & (key_place <= widen(place))
    return jnp.where(visible, 1.0, 0.0), cosine, sine


def turn(head, cosine, sine):
    return head * cosine + pltpu.roll(head, HEAD_SIZE // 2, 1) * sine


class Relay:
    def __init__(self, me, deep, piece, up_sems, dn_sems, side_sems=None):
        self.me, self.deep, self.piece = me, deep, piece
        self.up_sems, self.dn_sems, self.side_sems = up_sems, dn_sems, side_sems

    def up(self, source, part, hop):
        above = self.me.at_z(jnp.minimum(self.me.z + 1, self.deep - 1))
        at = self.piece(source, part, self.me.x)
        return remote(at, at, self.up_sems, part * self.deep + hop, above)

    def dn(self, source, part, hop):
        below = self.me.at_z(jnp.maximum(self.me.z - 1, 0))
        at = self.piece(source, part, self.me.x)
        return remote(at, at, self.dn_sems, part * self.deep + hop, below)

    def side(self, source, part, hop, x):
        at = self.piece(source, part, x)
        return remote(at, at, self.side_sems, part * 2 * self.deep + hop, self.me.x_peer())

    def begin(self, part, ends=None):
        z, last = self.me.z, self.deep - 1
        at_end = (z == 0) | (z == last)
        now = z >= 0 if ends is None else at_end if ends else jnp.logical_not(at_end)

        @pl.when((z < last) & now)
        def _():
            self.up(z, part, 0).start()

        @pl.when((z > 0) & now)
        def _():
            self.dn(z, part, 0).start()

    def pass_on(self, part, hop):
        z, deep = self.me.z, self.deep
        sides = self.side_sems is not None
        upward = (z - 1 - hop >= 0) & (z < deep - 1)
        downward = (z + 1 + hop < deep) & (z > 0)
        if sides:

            @pl.when(z - 1 - hop >= 0)
            def _():
                self.up(z - 1 - hop, part, hop).wait_recv()
                self.side(z - 1 - hop, part, hop, self.me.x).start()

            @pl.when(z + 1 + hop < deep)
            def _():
                self.dn(z + 1 + hop, part, hop).wait_recv()
                self.side(z + 1 + hop, part, deep + hop, self.me.x).start()

        @pl.when(upward)
        def _():
            if not sides:
                self.up(z - 1 - hop, part, hop).wait_recv()
            self.up(z - 1 - hop, part, hop + 1).start()

        @pl.when(downward)
        def _():
            if not sides:
                self.dn(z + 1 + hop, part, hop).wait_recv()
            self.dn(z + 1 + hop, part, hop + 1).start()

    def finish(self, part):
        z, deep = self.me.z, self.deep
        for hop in range(deep - 1):
            if self.side_sems is not None:

                @pl.when(z - 1 - hop >= 0)
                def _():
                    self.side(z - 1 - hop, part, hop, 1 - self.me.x).wait_recv()

                @pl.when(z + 1 + hop < deep)
                def _():
                    self.side(z + 1 + hop, part, deep + hop, 1 - self.me.x).wait_recv()

            else:

                @pl.when(z == deep - 1)
                def _():
                    self.up(z - 1 - hop, part, hop).wait_recv()

                @pl.when(z == 0)
                def _():
                    self.dn(z + 1 + hop, part, hop).wait_recv()

    def drain(self, part):
        z, deep = self.me.z, self.deep
        for hop in range(deep):

            @pl.when((z - hop >= 0) & (z < deep - 1))
            def _():
                self.up(z - hop, part, hop).wait_send()

            @pl.when((z + hop < deep) & (z > 0))
            def _():
                self.dn(z + hop, part, hop).wait_send()

        if self.side_sems is not None:
            for hop in range(deep - 1):

                @pl.when(z - 1 - hop >= 0)
                def _():
                    self.side(z - 1 - hop, part, hop, self.me.x).wait_send()

                @pl.when(z + 1 + hop < deep)
                def _():
                    self.side(z + 1 + hop, part, deep + hop, self.me.x).wait_send()


class PlaneSum:
    def __init__(self, me, rows, make, bufs, landing, sem_set):
        self.me, self.rows, self.make = me, rows, make
        self.core_out, self.x_out, self.acc, self.y_out = bufs
        self.core_in, self.x_in, self.y_in = landing
        self.core_sems, self.x_sems, self.y_sems = sem_set
        self.tiles = rows // TILE
        self.step = rows // CHUNKS
        self.per_tile = TILE // self.step

    def core_copy(self, number):
        at = rows_at(number, TILE)
        return remote(
            self.core_out.at[at], self.core_in.at[at], self.core_sems, number, self.me.core_peer()
        )

    def x_copy(self, number):
        at = rows_at(number, self.step)
        return remote(self.x_out.at[at], self.x_in.at[at], self.x_sems, number, self.me.x_peer())

    def y_copy(self, number):
        at = rows_at(number, self.step)
        return remote(self.y_out.at[at], self.y_in.at[at], self.y_sems, number, self.me.y_peer())

    def tile(self, tree, x, number):
        first = pl.multiple_of((tree * 2 + x) * self.rows + number * TILE, TILE)
        return self.make(first)

    def outward(self, side):
        me = self.me
        x = me.x if side else 1 - me.x

        def one(number, carry):
            value = self.tile(1 - me.c, x, number)
            slot = side * self.tiles + number
            self.core_out[rows_at(slot, TILE), :] = value.astype(BF16)
            self.core_copy(slot).start()
            return carry

        lax.fori_loop(0, self.tiles, one, 0)

    def across(self):
        me = self.me

        def one(number, carry):
            value = self.tile(me.c, 1 - me.x, number).astype(BF16).astype(F32)
            self.core_copy(number).wait_recv()
            at = rows_at(number, TILE)
            self.x_out[at, :] = (value + self.core_in[at, :].astype(F32)).astype(BF16)
            for k in range(self.per_tile):
                self.x_copy(number * self.per_tile + k).start()
            return carry

        lax.fori_loop(0, self.tiles, one, 0)

    def inward(self):
        me = self.me

        def one(number, carry):
            value = self.tile(me.c, me.x, number).astype(BF16).astype(F32)
            slot = self.tiles + number
            self.core_copy(slot).wait_recv()
            self.acc[rows_at(number, TILE), :] = value + self.core_in[
                rows_at(slot, TILE), :
            ].astype(F32)
            return carry

        lax.fori_loop(0, self.tiles, one, 0)

    def pass_on(self, first, last):
        def one(number, carry):
            at = rows_at(number, self.step)
            self.x_copy(number).wait_recv()
            self.y_out[at, :] = (self.acc[at, :] + self.x_in[at, :].astype(F32)).astype(BF16)
            self.y_copy(number).start()
            return carry

        lax.fori_loop(first, last, one, 0)

    def total(self, number):
        at = rows_at(number, self.step)
        self.y_copy(number).wait_recv()
        return self.y_out[at, :].astype(F32) + self.y_in[at, :].astype(F32)

    def core_sent(self):
        for number in range(2 * self.tiles):
            self.core_copy(number).wait_send()

    def x_sent(self):
        for number in range(CHUNKS):
            self.x_copy(number).wait_send()

    def y_sent(self):
        for number in range(CHUNKS):
            self.y_copy(number).wait_send()


class Fold:
    def __init__(self, me, groups, bufs, sem_set, tile, merge):
        self.me, self.groups, self.tile, self.merge = me, groups, tile, merge
        self.own, self.stage, self.land = bufs
        self.send_sems, self.recv_sems, self.free = sem_set
        self.sets, self.count, self.rows = self.stage.shape[0], self.own.shape[1], self.own.shape[2]
        self.slots = self.land.shape[1]
        z = me.z
        self.end = jnp.where(z < 2, 0, 3)
        self.mid = jnp.where(z < 2, 1, 2)
        self.far_mid = 3 - self.mid
        self.is_end = z == self.end
        self.is_mid = z == self.mid
        self.targets = (3 - self.end, self.far_mid, jnp.where(self.is_end, self.mid, self.end))

    def place(self, target):
        return (target + 3 - self.me.z) % 4

    def free_at(self, group, which, m):
        return self.free.at[((group % self.sets) * 3 + which) * self.count + m]

    def copy(self, group, which, m, slot=None):
        at = group % self.sets
        target = self.targets[which]
        from_mid = (4 if self.merge else 3, 3, 2)[which]
        there = jnp.where(self.is_end, which, from_mid) if slot is None else slot
        direct = self.far_mid if which == 0 and self.merge else target
        return pltpu.make_async_remote_copy(
            src_ref=self.stage.at[at, self.place(target), m],
            dst_ref=self.land.at[at, there, m],
            send_sem=self.send_sems.at[(at * 3 + which) * self.count + m],
            recv_sem=self.recv_sems.at[(at * self.slots + there) * self.count + m],
            device_id=self.me.at_z(jnp.where(self.is_end, self.mid, direct)),
            device_id_type=MESH,
        )

    def send(self, group, which, m):
        if group >= self.sets:
            await_signal(self.free_at(group, which, m))
        self.copy(group, which, m).start()

    def used(self, group, which, m, sender):
        if group + self.sets < self.groups:
            signal(self.free_at(group, which, m), self.me.at_z(sender))

    def add(self, group, which, m, slot):
        at = group % self.sets
        self.copy(group, which, m, slot).wait_recv()
        term = self.stage.at[at, self.place(self.targets[which]), m]
        landed = self.land.at[at, slot, m]

        def step(number, carry):
            rows = rows_at(number, self.tile)
            total = term[rows, :].astype(F32) + landed[rows, :].astype(F32)
            term[rows, :] = total.astype(BF16)
            return carry

        lax.fori_loop(0, self.rows // self.tile, step, 0)

    def begin(self, group, m):
        @pl.when(self.is_end)
        def _():
            for which in range(3):
                self.send(group, which, m)

        if not self.merge:

            @pl.when(self.is_mid)
            def _():
                self.send(group, 2, m)

    def advance(self, group, m):
        @pl.when(self.is_mid)
        def _():
            for which in (0, 1):
                self.add(group, which, m, which)
                self.used(group, which, m, self.end)
                self.send(group, which, m)

    def let_go(self, group, m):
        @pl.when(self.is_mid)
        def _():
            self.add(group, 2, m, 4)
            self.used(group, 0, m, self.far_mid)
            self.send(group, 2, m)

    def finish(self, group, m, write):
        at = group % self.sets
        own = self.own.at[group, m]
        near, far = self.land.at[at, 2, m], self.land.at[at, 3, m]
        self.copy(group, 2, m, 2).wait_recv()

        def run(pieces):
            def step(number, carry):
                rows = rows_at(number, self.tile)
                total = own[rows, :].astype(F32)
                for piece in pieces:
                    total = total + piece[rows, :].astype(F32)
                write(rows, total)
                return carry

            lax.fori_loop(0, self.rows // self.tile, step, 0)

        if self.merge:

            @pl.when(self.is_end)
            def _():
                run([near])
                self.used(group, 2, m, self.mid)

            @pl.when(self.is_mid)
            def _():
                self.copy(group, 1, m, 3).wait_recv()
                run([near, far])
                self.used(group, 2, m, self.end)
                self.used(group, 1, m, self.far_mid)

        else:
            self.copy(group, 1, m, 3).wait_recv()
            run([near, far])

    def drain(self, group, m):
        for which in range(3):
            self.copy(group, which, m).wait_send()


def place_kernel(*refs):
    count = (len(refs) - 2) // 3
    sources, targets, middles = refs[:count], refs[count : 2 * count], refs[2 * count : -2]
    loads, stores = [], []
    for source, target, middle in zip(sources, targets, middles):
        size = source.shape[0] // 2
        for part in range(2):
            at = pl.ds(part * size, size)
            number = len(loads)
            loads.append(pltpu.make_async_copy(source.at[at], middle.at[at], refs[-2].at[number]))
            stores.append(pltpu.make_async_copy(middle.at[at], target.at[at], refs[-1].at[number]))
    for load in loads:
        load.start()
    for load, store in zip(loads, stores):
        load.wait()
        store.start()
    for store in stores:
        store.wait()


def place_call(arrays):
    hbm = pl.BlockSpec(memory_space=pl.ANY)
    done = pltpu.SemaphoreType.DMA((2 * len(arrays),))
    return pl.pallas_call(
        place_kernel,
        out_shape=tuple(jax.ShapeDtypeStruct(a.shape, a.dtype) for a in arrays),
        in_specs=[hbm] * len(arrays),
        out_specs=[hbm] * len(arrays),
        scratch_shapes=[pltpu.VMEM(a.shape, a.dtype) for a in arrays] + [done, done],
        compiler_params=pltpu.CompilerParams(vmem_limit_bytes=60 * 2**20),
        name="place",
    )(*arrays)


def layer_kernel(
    starts,
    parents,
    frequency,
    routes,
    small,
    tokens_in,
    cotangent_in,
    w_query,
    w_key,
    w_value,
    w_output,
    gate_in,
    up_in,
    down_in,
    mixed,
    d_tokens,
    d_gate,
    d_up,
    d_down,
    d_query,
    d_output,
    d_key,
    d_value,
    d_small,
    mats,
    acts,
    hid,
    ups,
    wqkv,
    wout,
    smalls,
    queries,
    keys,
    values,
    probs,
    context,
    tables,
    after,
    mixes,
    gates,
    gates_out,
    gates_in,
    core_out,
    x_out,
    acc,
    y_out,
    two_core_in,
    two_x_in,
    two_y_in,
    mo_core_in,
    mo_x_in,
    mo_y_in,
    agrad,
    alow,
    qlow,
    kv_out,
    kv_in,
    kv_own,
    kvx_out,
    kvx_in,
    kvlow,
    dkv_out,
    dkv_in,
    xs_in,
    own,
    stage,
    land,
    bounce,
    own_o,
    stage_o,
    land_o,
    own_q,
    stage_q,
    land_q,
    small_own,
    small_in,
    small_z,
    kv_last,
    kv_land,
    load_sem,
    small_sem,
    up1_sem,
    dn1_sem,
    side1_sem,
    up2_sem,
    dn2_sem,
    side2_sem,
    up3_sem,
    dn3_sem,
    kv_sem,
    cot_sem,
    core_sem,
    y_sem,
    hx_sem,
    hc_sem,
    hf_sem,
    mix_sem,
    gate_sem,
    two_core_sem,
    two_x_sem,
    two_y_sem,
    mo_core_sem,
    mo_x_sem,
    mo_y_sem,
    one_core_sem,
    one_y_sem,
    low_sem,
    kvg_sem,
    xs_sem,
    fold_send,
    fold_recv,
    fold_free,
    fold_send_o,
    fold_recv_o,
    fold_send_q,
    fold_recv_q,
    out_sem,
    mixed_sem,
    token_sem,
    grad_sem,
    small_in_sem,
    small_z_sem,
    last_sem,
):
    me = Place()
    z, x, y, c = me.z, me.x, me.y, me.c
    deep, shard = wqkv.shape[0], wqkv.shape[1]
    trees, heads, rows, length = probs.shape
    width = hid.shape[1]
    groups = gates.shape[0]
    units = mats.shape[1] // groups
    mine = heads * HEAD_SIZE
    half = shard // 2
    step = rows // CHUNKS
    inv_root = HEAD_SIZE ** (-0.5)
    own_block = c * 2 + x
    is_end = (z == 0) | (z == deep - 1)

    def block_rows(tree, side):
        return rows_at(tree * 2 + side, rows)

    def shard_lanes(k):
        return rows_at(k, shard)

    def load(source, target, at):
        return pltpu.make_async_copy(source, target, load_sem.at[at])

    head_lanes = rows_at(y, HEAD_SIZE)
    loads = [
        load(w_query, wqkv.at[z, :, pl.ds(0, mine)], 0),
        load(w_key.at[:, head_lanes], wqkv.at[z, :, pl.ds(mine, HEAD_SIZE)], 1),
        load(w_value.at[:, head_lanes], wqkv.at[z, :, pl.ds(mine + HEAD_SIZE, HEAD_SIZE)], 2),
        load(small, smalls.at[z], 3),
        load(w_output, wout.at[z], 4),
        load(tokens_in, alow, 5),
        load(cotangent_in.at[0], ups.at[block_rows(0, x)], 6),
        load(cotangent_in.at[1], ups.at[block_rows(1, x)], 7),
        load(gate_in, mats.at[0, :, shard_lanes(z)], 8),
        load(up_in, mats.at[1, :, shard_lanes(z)], 9),
        load(down_in, mats.at[2, :, shard_lanes(z)], 10),
    ]
    for copy in loads:
        copy.start()
    lin = x * 4 + me.t

    def plane(number):
        return (z, number // 4, number % 4)

    greet(
        [me.at_z((z + k) % deep) for k in range(1, deep)]
        + [plane((lin + k) % 8) for k in range(1, 8)]
    )
    for copy in loads[:4]:
        copy.wait()

    def halved(buffer):
        def piece(source, part, by):
            return buffer.at[source, rows_at(by, half)]

        return piece

    def expert_piece(source, part, by):
        return mats.at[:, pl.ds(part * units, units), shard_lanes(source)]

    take_qkv = Relay(me, deep, halved(wqkv), up1_sem, dn1_sem, side1_sem)
    take_out = Relay(me, deep, halved(wout), up2_sem, dn2_sem, side2_sem)
    take = Relay(me, deep, expert_piece, up3_sem, dn3_sem)

    def small_out(k):
        there = (z + k) % deep
        return remote(smalls.at[z], smalls.at[z], small_sem, k - 1, me.at_z(there))

    take_qkv.begin(0)
    for k in range(1, deep):
        small_out(k).start()

    for tree in range(trees):
        seen, cosine, sine = tree_tables(
            starts, parents, tree, x * rows, rows, length, frequency[:1, :]
        )
        agrad[:, pl.ds(tree * length, length)] = seen
        tables[0, tree] = cosine
        tables[1, tree] = sine
    take_qkv.pass_on(0, 0)
    for copy in loads[4:]:
        copy.wait()
    take_out.begin(0)
    for k in range(1, deep):
        source = (z + deep - k) % deep
        remote(
            smalls.at[source], smalls.at[source], small_sem, k - 1, me.at_z(source)
        ).wait_recv()
    gain_one = jnp.concatenate([smalls[k, :1, :] for k in range(deep)], 1).astype(F32)
    gain_two = jnp.concatenate([smalls[k, 1:2, :] for k in range(deep)], 1).astype(F32)
    router = jnp.concatenate([smalls[k, 8:, :] for k in range(deep)], 1)

    def norm_rows(source, target, at):
        value = source[at, :].astype(F32)
        factor = lax.rsqrt(jnp.mean(value * value, -1, keepdims=True) + EPS)
        target[at, :] = (value * factor * gain_one).astype(BF16)

    for tree in range(trees):

        def first_norm(number, carry):
            at = rows_at(number, step)
            norm_rows(alow.at[tree], core_out.at[pl.ds(tree * rows, rows)], at)
            return carry

        lax.fori_loop(0, CHUNKS, first_norm, 0)
    take_qkv.pass_on(0, 1)
    take_out.pass_on(0, 0)
    take.begin(0)
    take_qkv.pass_on(0, 2)
    take_qkv.finish(0)
    take_out.pass_on(0, 1)

    own_place = rows_at(x, rows)
    away_place = rows_at(1 - x, rows)

    def kv_copy(tree, which, place, on):
        at = (keys, values)[which].at[tree, place]
        return remote(at, at, kv_sem, 2 * on + which, me.core_peer() if on else me.x_peer())

    def project_in(tree):
        total = jnp.zeros((rows, wqkv.shape[2]), F32)
        for k in range(deep):
            total = total + mm(core_out[rows_at(tree, rows), pl.ds(k * shard, shard)], wqkv[k])
        cosine, sine = tables[0, tree], tables[1, tree]
        for head in range(heads):
            part_q = total[:, head * HEAD_SIZE : (head + 1) * HEAD_SIZE]
            queries[tree, head] = turn(part_q, cosine, sine).astype(BF16)
        part_k = total[:, mine : mine + HEAD_SIZE]
        keys[tree, own_place, :] = turn(part_k, cosine, sine).astype(BF16)
        values[tree, own_place, :] = total[:, mine + HEAD_SIZE :].astype(BF16)

    project_in(c)
    for which in range(2):
        kv_copy(c, which, own_place, 0).start()
    project_in(1 - c)
    take_out.pass_on(0, 2)
    for which in range(2):
        kv_copy(c, which, away_place, 0).wait_recv()
        kv_copy(c, which, away_place, 1).start()

    def attend(tree):
        mask = agrad.at[:, rows_at(tree, length)]

        def one(head, carry):
            score = mm(queries[tree, head], keys[tree], NT) * inv_root
            score = jnp.where(mask[...] > 0.5, score, NEG)
            top = jnp.max(score, -1, keepdims=True)
            raised = jnp.exp(score - top)
            prob = (raised / jnp.sum(raised, -1, keepdims=True)).astype(BF16)
            probs[tree, head] = prob
            context[tree, head] = mm(prob, values[tree]).astype(BF16)
            return carry

        lax.fori_loop(0, heads, one, 0)

    attend(c)
    take.pass_on(0, 0)
    take.begin(1, False)
    for part in range(1, groups):
        take.begin(part, True)
    for which in range(2):
        kv_copy(1 - c, which, away_place, 1).wait_recv()
    attend(1 - c)
    take_out.finish(0)

    own_up, away_up = ups.at[block_rows(c, x)], ups.at[block_rows(c, 1 - x)]
    peer_up = ups.at[block_rows(1 - c, 1 - x)]
    cot_x = remote(own_up, own_up, cot_sem, 0, me.x_peer())
    cot_x.start()

    def project(tree, row):
        pieces = []
        for k in range(deep):
            piece = jnp.zeros((step, shard), F32)
            for head in range(heads):
                piece = piece + mm(
                    context[tree, head, pl.ds(row, step), :],
                    wout[k, pl.ds(head * HEAD_SIZE, HEAD_SIZE), :],
                )
            pieces.append(piece)
        return pieces

    def core_copy(number):
        at = rows_at(number, step)
        return remote(core_out.at[at], mo_core_in.at[at], core_sem, number, me.core_peer())

    def y_copy(number):
        at = rows_at(number, step)
        return remote(y_out.at[at], mo_y_in.at[at], y_sem, number, me.y_peer())

    for chunk in range(CHUNKS):
        at = pl.ds(chunk * step, step)
        for k, piece in enumerate(project(1 - c, chunk * step)):
            core_out[at, pl.ds(k * shard, shard)] = piece.astype(BF16)
        core_copy(chunk).start()
    for chunk in range(CHUNKS):
        at = pl.ds(chunk * step, step)
        pieces = project(c, chunk * step)
        core_copy(chunk).wait_recv()
        for k, piece in enumerate(pieces):
            lanes = pl.ds(k * shard, shard)
            both = piece.astype(BF16).astype(F32) + mo_core_in[at, lanes].astype(F32)
            y_out[at, lanes] = both.astype(BF16)
        y_copy(chunk).start()
    take.pass_on(0, 1)

    def two_rows(tree, side, number):
        first = (tree * 2 + side) * rows + number * step
        return pl.ds(pl.multiple_of(first, step), step)

    def hid_copy(tree, side, sems, number, device):
        at = hid.at[two_rows(tree, side, number)]
        return remote(at, at, sems, number, device)

    def second(number, carry):
        at = rows_at(number, step)
        y_copy(number).wait_recv()
        value = alow[c, at, :].astype(F32) + (y_out[at, :].astype(F32) + mo_y_in[at, :].astype(F32))
        after[at, :] = value
        factor = lax.rsqrt(jnp.mean(value * value, -1, keepdims=True) + EPS)
        hid[two_rows(c, x, number), :] = (value * factor * gain_two).astype(BF16)
        hid_copy(c, x, hx_sem, number, me.x_peer()).start()
        hid_copy(c, x, hc_sem, number, me.core_peer()).start()
        return carry

    lax.fori_loop(0, 2, second, 0)
    take.pass_on(1, 0)
    take.begin(2, False)
    lax.fori_loop(2, CHUNKS, second, 0)

    logits = mm(router, hid[block_rows(c, x), :], NT)
    expert = lax.broadcasted_iota(jnp.int32, logits.shape, 0)
    chosen = expert < 0
    for k in range(routes.shape[1]):
        chosen = chosen | (expert == routes[c, k : k + 1, :])
    logits = jnp.where(chosen, logits, NEG)
    raised = jnp.where(chosen, jnp.exp(logits - jnp.max(logits, 0, keepdims=True)), 0.0)
    mixes[own_block] = raised / jnp.sum(raised, 0, keepdims=True)

    def mix_copy(tree, side, at, device):
        block = mixes.at[tree * 2 + side]
        return remote(block, block, mix_sem, at, device)

    mix_copy(c, x, 0, me.x_peer()).start()
    mix_copy(c, x, 1, me.core_peer()).start()
    cot_x_in = remote(away_up, away_up, cot_sem, 0, me.x_peer())
    cot_x_in.wait_recv()
    cot_on = remote(away_up, away_up, cot_sem, 1, me.core_peer())
    cot_on.start()
    for number in range(CHUNKS):
        hid_copy(c, 1 - x, hx_sem, number, me.x_peer()).wait_recv()
        hid_copy(c, 1 - x, hf_sem, number, me.core_peer()).start()
    mix_copy(c, 1 - x, 0, me.x_peer()).wait_recv()
    mix_copy(c, 1 - x, 2, me.core_peer()).start()
    remote(peer_up, peer_up, cot_sem, 1, me.core_peer()).wait_recv()
    for number in range(CHUNKS):
        hid_copy(1 - c, x, hc_sem, number, me.core_peer()).wait_recv()
        hid_copy(1 - c, 1 - x, hf_sem, number, me.core_peer()).wait_recv()
    mix_copy(1 - c, x, 1, me.core_peer()).wait_recv()
    mix_copy(1 - c, 1 - x, 2, me.core_peer()).wait_recv()
    take.pass_on(1, 1)
    take.finish(0)

    def expert_block(group, block):
        tokens = rows_at(block, rows)
        some = pl.ds(group * units, units)
        pre_gate = mm(mats[0, some, :], hid[tokens, :], NT)
        pre_up = mm(mats[1, some, :], hid[tokens, :], NT)
        back = mm(mats[2, some, :], ups[tokens, :], NT)
        first, second_half = mixes[block, group : group + 1, :], mixes[
            block, groups + group : groups + group + 1, :
        ]
        weight = jnp.broadcast_to(jnp.where(x == 0, first, second_half), (units, rows))
        square = pre_gate * pre_gate
        bent = jnp.tanh(ROOT_2_PI * pre_gate * (1.0 + CUBIC * square))
        slope = 0.5 * (1.0 + bent)
        active = pre_gate * slope
        rise = slope + 0.5 * pre_gate * (1.0 - bent * bent) * ROOT_2_PI * (
            1.0 + 3.0 * CUBIC * square
        )
        hidden = active * pre_up
        gates[pl.ds(group, 1), tokens] = jnp.sum(hidden * back, 0, keepdims=True)
        back = weight * back
        acts[0, some, tokens] = (back * pre_up * rise).astype(BF16)
        acts[1, some, tokens] = (back * active).astype(BF16)
        acts[2, some, tokens] = (weight * hidden).astype(BF16)

    fold = Fold(me, groups, (own, stage, land), (fold_send, fold_recv, fold_free), 64, True)

    def expert_grad(group, m):
        source = ups if m == 2 else hid
        some = acts.at[m, pl.ds(group * units, units)]

        def one(k, carry):
            value = mm(some[...], source[:, shard_lanes(k)]).astype(BF16)

            @pl.when(k == z)
            def _():
                own[group, m] = value

            @pl.when(k != z)
            def _():
                stage[group % fold.sets, fold.place(k), m] = value

            return carry

        lax.fori_loop(0, deep, one, 0)
        fold.begin(group, m)

    def expert_group(group):
        def one(block, carry):
            expert_block(group, block)
            return carry

        lax.fori_loop(0, 2 * trees, one, 0)
        for m in range(KINDS):
            expert_grad(group, m)

    expert_outs = (d_gate, d_up, d_down)

    def grad_out(group, m):
        return pltpu.make_async_copy(
            bounce.at[m], expert_outs[m].at[pl.ds(group * units, units)], grad_sem.at[m]
        )

    def finish_group(group, ends):
        @pl.when(is_end if ends else jnp.logical_not(is_end))
        def _():
            for m in range(KINDS):
                if group > 0:
                    grad_out(group - 1, m).wait()

                def write(at, value):
                    bounce[m, at, :] = value

                fold.finish(group, m, write)
                grad_out(group, m).start()

    def advance(group):
        for m in range(KINDS):
            fold.advance(group, m)

    def let_go(group):
        for m in range(KINDS):
            fold.let_go(group, m)

    def drain(group):
        for m in range(KINDS):
            fold.drain(group, m)

    take.pass_on(2, 0)
    take.begin(3, False)
    expert_group(0)
    take.pass_on(2, 1)
    take.pass_on(3, 0)
    take.finish(1)
    expert_group(1)
    take.pass_on(3, 1)
    advance(0)
    take.finish(2)
    expert_group(2)
    finish_group(0, False)
    advance(1)
    let_go(0)
    take.finish(3)

    def two_make(first):
        at = pl.ds(first, TILE)
        return mm(acts[0, :, at], mats[0], TN) + mm(acts[1, :, at], mats[1], TN)

    def mo_make(first):
        return mm(acts[2, :, pl.ds(first, TILE)], mats[2], TN)

    two = PlaneSum(
        me,
        rows,
        two_make,
        (core_out, x_out, acc, y_out),
        (two_core_in, two_x_in, two_y_in),
        (two_core_sem, two_x_sem, two_y_sem),
    )
    mo = PlaneSum(
        me,
        rows,
        mo_make,
        (core_out, hid.at[pl.ds(rows, rows)], acc, hid.at[pl.ds(0, rows)]),
        (mo_core_in, mo_x_in, mo_y_in),
        (mo_core_sem, mo_x_sem, mo_y_sem),
    )
    last = groups - 1
    for number in range(CHUNKS):
        core_copy(number).wait_send()
        y_copy(number).wait_send()
    expert_block(last, (1 - c) * 2 + 1 - x)
    two.outward(0)
    expert_block(last, (1 - c) * 2 + x)
    two.outward(1)
    expert_block(last, c * 2 + 1 - x)
    two.across()
    expert_block(last, own_block)

    for block in range(2 * trees):
        gates_out[block, pl.ds(0, groups), :] = gates[:, pl.ds(block * rows, rows)]

    def gate_copy(k):
        there = (lin + k) % 8
        block = (there % 2) * 2 + there // 4
        return remote(gates_out.at[block], gates_in.at[lin], gate_sem, k - 1, plane(there))

    for k in range(1, 8):
        gate_copy(k).start()
    gates_in[lin] = gates_out[own_block]
    two.inward()
    finish_group(1, False)
    let_go(1)
    drain(0)
    expert_grad(last, 0)
    two.pass_on(0, 1)
    expert_grad(last, 1)
    two.pass_on(1, 2)
    expert_grad(last, 2)
    two.pass_on(2, 3)

    for k in range(1, 8):
        source = (lin + 8 - k) % 8
        remote(gates_out.at[0], gates_in.at[source], gate_sem, k - 1, plane(source)).wait_recv()
    sums = []
    for side in range(2):
        total = gates_in[side * 4]
        for k in range(1, 4):
            total = total + gates_in[side * 4 + k]
        sums.append(total[:groups])
    mix_grad = jnp.concatenate(sums, 0)
    mix = mixes[own_block]
    picked = mix * (mix_grad - jnp.sum(mix * mix_grad, 0, keepdims=True))
    logit_grad = picked.astype(BF16)
    agrad[...] = mm(logit_grad, router, TN)
    small_own[pl.ds(0, 8), :] = jnp.zeros((8, width), F32)
    small_own[pl.ds(8, 8), :] = mm(logit_grad, hid[block_rows(c, x), :])

    for number in range(CHUNKS):
        hid_copy(c, x, hx_sem, number, me.x_peer()).wait_send()
        hid_copy(c, x, hc_sem, number, me.core_peer()).wait_send()
        hid_copy(c, 1 - x, hf_sem, number, me.core_peer()).wait_send()
    two.core_sent()
    mo.outward(0)
    mo.outward(1)
    two.pass_on(3, 4)
    mo.across()
    mo.inward()

    for part in range(groups):
        take.drain(part)
    spare = mats.at[0]
    late = [
        load(tokens_in.at[0], spare.at[pl.ds(0, rows)], 0),
        load(tokens_in.at[1], spare.at[pl.ds(rows, rows)], 1),
    ]
    for copy in late:
        copy.start()

    def low_copy(number):
        at = alow.at[c, rows_at(number, step)]
        return remote(at, at, low_sem, number, me.core_peer())

    def second_norm(number, gain_grad):
        at = rows_at(number, step)
        upstream = two.total(number) + agrad[at, :]
        value = after[at, :]
        factor = lax.rsqrt(jnp.mean(value * value, -1, keepdims=True) + EPS)
        scaled = upstream * gain_two
        inner = jnp.mean(scaled * value, -1, keepdims=True)
        cot = ups[two_rows(c, x, number), :]
        total = cot.astype(F32) + (factor * scaled - value * (factor * factor * factor * inner))
        agrad[at, :] = total
        alow[c, at, :] = total.astype(BF16)
        low_copy(number).start()
        return gain_grad + jnp.sum(upstream * value * factor, 0, keepdims=True)

    gain_two_grad = lax.fori_loop(0, CHUNKS, second_norm, jnp.zeros((1, width), F32))
    small_own[pl.ds(1, 1), :] = gain_two_grad

    def attend_back(tree):
        back = jnp.zeros((rows, mine), F32)
        for k in range(deep):
            back = back + mm(alow[tree, :, pl.ds(k * shard, shard)], wout[k], NT)
        back = back.astype(BF16)
        cosine, sine = tables[0, tree], tables[1, tree]
        key_grad = jnp.zeros((length, HEAD_SIZE), F32)
        value_grad = jnp.zeros((length, HEAD_SIZE), F32)
        for head in range(heads):
            lanes = pl.ds(head * HEAD_SIZE, HEAD_SIZE)
            back_head = back[:, head * HEAD_SIZE : (head + 1) * HEAD_SIZE]
            prob = probs[tree, head]
            value_grad = value_grad + mm(prob, back_head, TN)
            prob = prob.astype(F32)
            share = prob * mm(back_head, values[tree], NT)
            score = (share - prob * jnp.sum(share, -1, keepdims=True)).astype(BF16)
            query_grad = mm(score, keys[tree]) * inv_root
            qlow[tree, :, lanes] = turn(query_grad, cosine, -sine).astype(BF16)
            key_grad = key_grad + mm(score, queries[tree, head], TN)
        return jnp.concatenate([key_grad * inv_root, value_grad], 1)

    for number in range(CHUNKS):
        at = alow.at[1 - c, pl.ds(number * step, step)]
        remote(at, at, low_sem, number, me.core_peer()).wait_recv()
    kv_out[...] = attend_back(1 - c).astype(BF16)
    kvg_copy = remote(kv_out, kv_in, kvg_sem, 0, me.core_peer())
    kvg_copy.start()
    kv_own[...] = attend_back(c)
    advance(2)

    ctx = [
        jnp.concatenate([context[tree, head] for head in range(heads)], 1) for tree in range(trees)
    ]

    def halves(value):
        low, high = value[:half], value[half:]
        return jnp.where(x == 0, low, high), jnp.where(x == 0, high, low)

    def xs_out(k, lanes):
        return ups.at[pl.ds(k * half, half), lanes]

    xs_lanes = (pl.ds(0, mine), pl.ds(mine, mine), pl.ds(2 * mine, HEAD_SIZE))

    def xs_copy(part):
        lanes = xs_lanes[part]
        return remote(
            ups.at[pl.ds(0, deep * half), lanes], xs_in.at[:, lanes], xs_sem, part, me.x_peer()
        )

    cot_x.wait_send()
    cot_on.wait_send()

    def keep_own(buffer_own, buffer_stage, k, lanes, value):
        @pl.when(k == z)
        def _():
            buffer_own[0, 0, :, lanes] = value.astype(BF16)

        @pl.when(k != z)
        def _():
            buffer_stage[0, fold.place(k), 0, :, lanes] = value.astype(BF16)

    def output_grad(k, carry):
        value = sum(mm(alow[tree, :, shard_lanes(k)], ctx[tree], TN) for tree in range(trees))
        keep, away = halves(value)
        keep_own(own_o, stage_o, k, pl.ds(0, mine), keep)
        ups[rows_at(k, half), xs_lanes[1]] = away.astype(BF16)
        return carry

    lax.fori_loop(0, deep, output_grad, 0)
    xs_copy(1).start()

    def one_tile(tree, at):
        return [mm(qlow[tree, at, :], wqkv[k, :, pl.ds(0, mine)], NT) for k in range(deep)]

    mo.core_sent()

    def one_copy(number):
        at = rows_at(number, step)
        return remote(core_out.at[at], two_core_in.at[at], one_core_sem, number, me.core_peer())

    def one_outward(number, carry):
        at = rows_at(number, step)
        for k, piece in enumerate(one_tile(1 - c, at)):
            core_out[at, pl.ds(k * shard, shard)] = piece.astype(BF16)
        one_copy(number).start()
        return carry

    lax.fori_loop(0, CHUNKS, one_outward, 0)

    kvg_copy.wait_recv()

    def of_side(ref, side):
        low, high = ref[pl.ds(0, rows), :], ref[pl.ds(rows, rows), :]
        return jnp.where(side == 0, low, high).astype(F32)

    kvx_out[...] = (of_side(kv_own, 1 - x) + of_side(kv_in, 1 - x)).astype(BF16)
    kvx_copy = remote(kvx_out, kvx_in, kvg_sem, 1, me.x_peer())
    kvx_copy.start()

    for copy in late:
        copy.wait()
    for tree in range(trees):

        def norm_again(number, carry):
            at = rows_at(number, step)
            norm_rows(
                spare.at[pl.ds(tree * rows, rows)], mats.at[1, pl.ds(tree * rows, rows)], at
            )
            return carry

        lax.fori_loop(0, CHUNKS, norm_again, 0)

    def hid_one(tree, lanes):
        return mats[1, rows_at(tree, rows), lanes]

    def query_weight_grad(k, carry):
        value = sum(mm(hid_one(tree, shard_lanes(k)), qlow[tree], TN) for tree in range(trees))
        keep, away = halves(value)
        keep_own(own_q, stage_q, k, pl.ds(0, mine), keep)
        ups[rows_at(k, half), xs_lanes[0]] = away.astype(BF16)
        return carry

    lax.fori_loop(0, deep, query_weight_grad, 0)
    xs_copy(0).start()
    kvx_copy.wait_recv()
    own_kv = of_side(kv_own, x) + of_side(kv_in, x) + kvx_in[...].astype(F32)
    kvlow[:, pl.ds(0, HEAD_SIZE)] = turn(
        own_kv[:, :HEAD_SIZE], tables[0, c], -tables[1, c]
    ).astype(BF16)
    kvlow[:, pl.ds(HEAD_SIZE, HEAD_SIZE)] = own_kv[:, HEAD_SIZE:].astype(BF16)

    two.y_sent()

    def one_y(number):
        at = rows_at(number, step)
        return remote(y_out.at[at], two_x_in.at[at], one_y_sem, number, me.y_peer())

    def one_inward(number, carry):
        at = rows_at(number, step)
        one_copy(number).wait_recv()
        for k, piece in enumerate(one_tile(c, at)):
            lanes = pl.ds(k * shard, shard)
            piece = piece + mm(kvlow[at, :], wqkv[k, :, pl.ds(mine, 2 * HEAD_SIZE)], NT)
            y_out[at, lanes] = (piece + two_core_in[at, lanes].astype(F32)).astype(BF16)
        one_y(number).start()
        return carry

    lax.fori_loop(0, CHUNKS, one_inward, 0)

    def kv_weight_grad(k, carry):
        value = mm(hid_one(c, shard_lanes(k)), kvlow[...], TN)
        low, high = value[:, :HEAD_SIZE], value[:, HEAD_SIZE:]
        dkv_out[0, k] = jnp.where(c == 0, high, low).astype(BF16)
        dkv_out[1, k] = jnp.where(c == 0, low, high).astype(BF16)
        return carry

    lax.fori_loop(0, deep, kv_weight_grad, 0)
    dkv_copy = remote(dkv_out.at[0], dkv_in, kvg_sem, 2, me.core_peer())
    dkv_copy.start()
    dkv_copy.wait_recv()

    def kv_weight_sum(k, carry):
        keep, away = halves(dkv_out[1, k].astype(F32) + dkv_in[k].astype(F32))
        keep_own(own_q, stage_q, k, pl.ds(mine, HEAD_SIZE), keep)
        ups[rows_at(k, half), xs_lanes[2]] = away.astype(BF16)
        return carry

    lax.fori_loop(0, deep, kv_weight_sum, 0)
    xs_copy(2).start()

    mo.pass_on(0, CHUNKS)
    finish_group(0, True)
    finish_group(1, True)
    let_go(2)
    finish_group(2, False)
    advance(3)

    fold_o = Fold(me, 1, (own_o, stage_o, land_o), (fold_send_o, fold_recv_o, None), 64, False)
    fold_q = Fold(me, 1, (own_q, stage_q, land_q), (fold_send_q, fold_recv_q, None), 64, False)

    def side_sum(buffer_own, buffer_stage, lanes_in, lanes):
        def one(k, carry):
            more = xs_in[rows_at(k, half), lanes_in].astype(F32)

            @pl.when(k == z)
            def _():
                buffer_own[0, 0, :, lanes] = (
                    buffer_own[0, 0, :, lanes].astype(F32) + more
                ).astype(BF16)

            @pl.when(k != z)
            def _():
                buffer_stage[0, fold.place(k), 0, :, lanes] = (
                    buffer_stage[0, fold.place(k), 0, :, lanes].astype(F32) + more
                ).astype(BF16)

            return carry

        lax.fori_loop(0, deep, one, 0)

    xs_copy(1).wait_recv()
    side_sum(own_o, stage_o, xs_lanes[1], pl.ds(0, mine))
    fold_o.begin(0, 0)

    def out_copies(buffer, target, first, peer_sems, number):
        at = rows_at(number, step)
        here = pltpu.make_async_copy(buffer.at[at], target.at[c, at], out_sem.at[first + number])
        there = remote(buffer.at[at], target.at[c, at], peer_sems, number, me.core_peer())
        return here, there

    def first_norm_back(number, gain_grad):
        at = rows_at(number, step)
        one_y(number).wait_recv()
        upstream = y_out[at, :].astype(F32) + two_x_in[at, :].astype(F32)
        first = pl.multiple_of(c * rows + number * step, step)
        value = mats[0, pl.ds(first, step), :].astype(F32)
        factor = lax.rsqrt(jnp.mean(value * value, -1, keepdims=True) + EPS)
        scaled = upstream * gain_one
        inner = jnp.mean(scaled * value, -1, keepdims=True)
        acc[at, :] = agrad[at, :] + (
            factor * scaled - value * (factor * factor * factor * inner)
        )
        for copy in out_copies(acc, d_tokens, CHUNKS, token_sem, number):
            copy.start()
        return gain_grad + jnp.sum(upstream * value * factor, 0, keepdims=True)

    gain_one_grad = lax.fori_loop(0, CHUNKS, first_norm_back, jnp.zeros((1, width), F32))
    small_own[pl.ds(0, 1), :] = gain_one_grad
    spot = x * 2 + c

    def spread(k):
        there = (spot + k) % 4
        device = (z, there // 2, 2 * y + there % 2)
        return remote(small_own, small_in.at[spot], small_in_sem, k - 1, device)

    for k in range(1, 4):
        spread(k).start()
    small_in[spot] = small_own[...]
    fold_o.advance(0, 0)
    xs_copy(0).wait_recv()
    side_sum(own_q, stage_q, xs_lanes[0], pl.ds(0, mine))
    xs_copy(2).wait_recv()
    side_sum(own_q, stage_q, xs_lanes[2], pl.ds(mine, HEAD_SIZE))
    fold_q.begin(0, 0)
    let_go(3)
    finish_group(2, True)

    two.x_sent()

    def mix_out(number, carry):
        at = rows_at(number, step)
        x_out[at, :] = (after[at, :] + mo.total(number)).astype(BF16)
        for copy in out_copies(x_out, mixed, 0, mixed_sem, number):
            copy.start()
        return carry

    lax.fori_loop(0, CHUNKS, mix_out, 0)
    fold_q.advance(0, 0)
    for k in range(1, 4):
        source = (spot + 4 - k) % 4
        device = (z, source // 2, 2 * y + source % 2)
        remote(small_own, small_in.at[source], small_in_sem, k - 1, device).wait_recv()
        spread(k).wait_send()
    small_own[...] = (small_in[0] + small_in[1]) + (small_in[2] + small_in[3])

    def small_copy(k):
        there = (z + k) % deep
        return remote(
            small_own.at[:, shard_lanes(there)], small_z.at[z], small_z_sem, k - 1, me.at_z(there)
        )

    for k in range(1, deep):
        small_copy(k).start()
    small_z[z] = small_own[:, shard_lanes(z)]
    finish_group(3, False)
    finish_group(3, True)

    def write_o(at, value):
        d_output[at, :] = value

    fold_o.finish(0, 0, write_o)

    def write_q(at, value):
        d_query[at, :] = value[:, :mine]
        kv_last[at, :] = value[:, mine:]

    fold_q.finish(0, 0, write_q)

    share = half // 4

    def share_rows(t):
        return pl.ds(pl.multiple_of(t * share, 8), share)

    def last_copy(k):
        there = (me.t + k) % 4
        return remote(
            kv_last.at[share_rows(there)], kv_land.at[me.t], last_sem, k - 1, (z, x, there)
        )

    for k in range(1, 4):
        last_copy(k).start()
    kv_land[me.t] = kv_last[share_rows(me.t), :]
    for k in range(1, deep):
        source = (z + deep - k) % deep
        remote(
            small_own.at[:, shard_lanes(0)], small_z.at[source], small_z_sem, k - 1, me.at_z(source)
        ).wait_recv()
    total = small_z[0]
    for k in range(1, deep):
        total = total + small_z[k]
    d_small[...] = jnp.where(x == 0, total[:, :half], total[:, half:])
    for k in range(1, 4):
        source = (me.t + 4 - k) % 4
        remote(
            kv_last.at[pl.ds(0, share)], kv_land.at[source], last_sem, k - 1, (z, x, source)
        ).wait_recv()
    for head in range(KEY_VALUE_HEADS):
        lanes = pl.ds(head * HEAD_SIZE, HEAD_SIZE)
        d_key[:, lanes] = kv_land[2 * head]
        d_value[:, lanes] = kv_land[2 * head + 1]

    for number in range(CHUNKS):
        at = pl.ds(number * step, step)
        remote(x_out.at[at], mixed.at[1 - c, at], mixed_sem, number, me.core_peer()).wait_recv()
        remote(acc.at[at], d_tokens.at[1 - c, at], token_sem, number, me.core_peer()).wait_recv()
        for buffer, target, first, peer_sems in (
            (x_out, mixed, 0, mixed_sem),
            (acc, d_tokens, CHUNKS, token_sem),
        ):
            here, there = out_copies(buffer, target, first, peer_sems, number)
            here.wait()
            there.wait_send()
        one_y(number).wait_send()
        one_copy(number).wait_send()
        low_copy(number).wait_send()
    mo.x_sent()
    mo.y_sent()
    for m in range(KINDS):
        grad_out(groups - 1, m).wait()
    for k in range(1, 8):
        gate_copy(k).wait_send()
    for k in range(1, deep):
        small_copy(k).wait_send()
        small_out(k).wait_send()
    for k in range(1, 4):
        last_copy(k).wait_send()
    for part in range(3):
        xs_copy(part).wait_send()
    for copy in (kvg_copy, kvx_copy, dkv_copy):
        copy.wait_send()
    for which in range(2):
        kv_copy(c, which, own_place, 0).wait_send()
        kv_copy(c, which, away_place, 1).wait_send()
    mix_copy(c, x, 0, me.x_peer()).wait_send()
    mix_copy(c, x, 1, me.core_peer()).wait_send()
    mix_copy(c, 1 - x, 2, me.core_peer()).wait_send()
    take_qkv.drain(0)
    take_out.drain(0)
    for group in range(1, groups):
        drain(group)
    fold_o.drain(0, 0)
    fold_q.drain(0, 0)


def sems(count):
    return pltpu.SemaphoreType.DMA((2, count))


def layer_call(
    seg_start,
    seg_parent,
    routes,
    small,
    tokens,
    cotangent,
    w_query,
    w_key,
    w_value,
    w_output,
    gate_t,
    up_t,
    w_down,
    deep,
):
    trees, rows, width = tokens.shape
    shard, mine = w_query.shape
    heads = mine // HEAD_SIZE
    length = rows * 2
    held, units = w_down.shape[0], w_down.shape[1]
    total_units = held * units
    experts = small.shape[0] - 8
    blocks = 2 * trees
    half = shard // 2
    count = blocks * rows
    sets = 3
    angle = HEAD_SIZE // 2
    frequency = ROPE_BASE ** (-2.0 * np.arange(angle, dtype=np.float32) / np.float32(HEAD_SIZE))
    frequency = np.tile(np.concatenate([frequency] * 2)[None], (8, 1)).astype(np.float32)
    vmem = pl.BlockSpec(memory_space=pltpu.VMEM)
    smem = pl.BlockSpec(memory_space=pltpu.SMEM)
    hbm = pl.BlockSpec(memory_space=pl.ANY)

    def plain(*shape):
        return pltpu.VMEM(shape, BF16)

    def wide(*shape):
        return pltpu.VMEM(shape, F32)

    def out(*shape, dtype=F32):
        return jax.ShapeDtypeStruct(shape, dtype)

    lanes = 2 * mine + HEAD_SIZE
    last = deep - 1
    return pl.pallas_call(
        layer_kernel,
        out_shape=(
            out(trees, rows, width, dtype=BF16),
            out(trees, rows, width),
            out(total_units, shard),
            out(total_units, shard),
            out(total_units, shard),
            out(half, mine),
            out(half, mine),
            out(half // 4, KEY_VALUE_HEADS * HEAD_SIZE),
            out(half // 4, KEY_VALUE_HEADS * HEAD_SIZE),
            out(small.shape[0], half),
        ),
        in_specs=[smem, smem, vmem, vmem] + [hbm] * 10,
        out_specs=[hbm] * 5 + [vmem] * 5,
        scratch_shapes=[
            plain(KINDS, total_units, width),
            plain(KINDS, total_units, count),
            plain(count, width),
            plain(count, width),
            plain(deep, shard, mine + 2 * HEAD_SIZE),
            plain(deep, mine, shard),
            plain(deep, small.shape[0], shard),
            plain(trees, heads, rows, HEAD_SIZE),
            plain(trees, length, HEAD_SIZE),
            plain(trees, length, HEAD_SIZE),
            plain(trees, heads, rows, length),
            plain(trees, heads, rows, HEAD_SIZE),
            wide(2, trees, rows, HEAD_SIZE),
            wide(rows, width),
            wide(blocks, experts, rows),
            wide(held, count),
            wide(blocks, 8, rows),
            wide(8, 8, rows),
            plain(2 * rows, width),
            plain(rows, width),
            wide(rows, width),
            plain(rows, width),
            plain(2 * rows, width),
            plain(rows, width),
            plain(rows, width),
            plain(2 * rows, width),
            plain(rows, width),
            plain(rows, width),
            wide(rows, width),
            plain(trees, rows, width),
            plain(trees, rows, mine),
            plain(length, 2 * HEAD_SIZE),
            plain(length, 2 * HEAD_SIZE),
            wide(length, 2 * HEAD_SIZE),
            plain(rows, 2 * HEAD_SIZE),
            plain(rows, 2 * HEAD_SIZE),
            plain(rows, 2 * HEAD_SIZE),
            plain(2, deep, shard, HEAD_SIZE),
            plain(deep, shard, HEAD_SIZE),
            plain(deep * half, lanes),
            plain(held, KINDS, units, shard),
            plain(sets, last, KINDS, units, shard),
            plain(sets, 5, KINDS, units, shard),
            wide(KINDS, units, shard),
            plain(1, 1, half, mine),
            plain(1, last, 1, half, mine),
            plain(1, deep, 1, half, mine),
            plain(1, 1, half, mine + HEAD_SIZE),
            plain(1, last, 1, half, mine + HEAD_SIZE),
            plain(1, deep, 1, half, mine + HEAD_SIZE),
            wide(small.shape[0], width),
            wide(4, small.shape[0], width),
            wide(deep, small.shape[0], shard),
            wide(half, HEAD_SIZE),
            wide(4, half // 4, HEAD_SIZE),
            pltpu.SemaphoreType.DMA((11,)),
            sems(last),
            sems(deep),
            sems(deep),
            sems(2 * deep),
            sems(deep),
            sems(deep),
            sems(2 * deep),
            sems(held * deep),
            sems(held * deep),
            sems(2 * trees),
            sems(2),
            sems(CHUNKS),
            sems(CHUNKS),
            sems(CHUNKS),
            sems(CHUNKS),
            sems(CHUNKS),
            sems(3),
            sems(7),
            sems(2 * rows // TILE),
            sems(CHUNKS),
            sems(CHUNKS),
            sems(2 * rows // TILE),
            sems(CHUNKS),
            sems(CHUNKS),
            sems(CHUNKS),
            sems(CHUNKS),
            sems(CHUNKS),
            sems(3),
            sems(3),
            pltpu.SemaphoreType.DMA((sets * 3 * KINDS,)),
            pltpu.SemaphoreType.DMA((sets * 5 * KINDS,)),
            pltpu.SemaphoreType.REGULAR((sets * 3 * KINDS,)),
            pltpu.SemaphoreType.DMA((3,)),
            pltpu.SemaphoreType.DMA((4,)),
            pltpu.SemaphoreType.DMA((3,)),
            pltpu.SemaphoreType.DMA((4,)),
            pltpu.SemaphoreType.DMA((2 * CHUNKS,)),
            sems(CHUNKS),
            sems(CHUNKS),
            pltpu.SemaphoreType.DMA((KINDS,)),
            sems(3),
            sems(last),
            sems(3),
        ],
        compiler_params=pltpu.CompilerParams(
            collective_id=0, has_side_effects=True, vmem_limit_bytes=64 * 2**20
        ),
        name="layer",
    )(
        seg_start,
        seg_parent,
        jnp.asarray(frequency),
        routes,
        small,
        tokens,
        cotangent,
        w_query,
        w_key,
        w_value,
        w_output,
        gate_t.reshape(total_units, -1),
        up_t.reshape(total_units, -1),
        w_down.reshape(total_units, -1),
    )


def plane_shards(
    tokens,
    cotangent,
    seg_start,
    seg_parent,
    routes,
    attn_gain,
    w_query,
    w_key,
    w_value,
    w_output,
    moe_gain,
    w_router,
    w_gate,
    w_up,
    w_down,
):
    width = tokens.shape[2]
    deep = lax.axis_size("dp")
    held, quarter = w_gate.shape[0], w_gate.shape[2]
    small = jnp.concatenate(
        [attn_gain[None], moe_gain[None], jnp.zeros((6, attn_gain.shape[0]), BF16), w_router.T], 0
    )
    made = layer_call(
        seg_start,
        seg_parent,
        jnp.swapaxes(routes, 1, 2),
        small,
        tokens,
        cotangent,
        w_query,
        w_key,
        w_value,
        w_output,
        jnp.swapaxes(w_gate, 1, 2),
        jnp.swapaxes(w_up, 1, 2),
        w_down,
        deep,
    )
    placed = place_call(made[:-1])
    mixed, d_tokens, d_gate, d_up, d_down, d_query, d_output, d_key, d_value = placed
    d_small = made[-1]

    def experts(array):
        return array.reshape(held, quarter, width // deep)

    return (
        mixed,
        d_tokens,
        d_small[0],
        d_query,
        d_key,
        d_value,
        d_output.T,
        d_small[1],
        d_small[8:].T,
        jnp.swapaxes(experts(d_gate), 1, 2),
        jnp.swapaxes(experts(d_up), 1, 2),
        experts(d_down),
    )


def shards(*arrays):
    axes = tuple(lax.axis_size(name) for name in ("dp", "expert", "tensor"))
    if axes == (4, 2, 4) and arrays[0].shape[0] == 2:
        return plane_shards(*arrays)
    return general_shards(*arrays)


def solution(mesh):
    placed = (
        P("dp", "expert", None),
        P("dp", "expert", None),
        P("dp", None),
        P("dp", None),
        P("dp", "expert", None),
        P("dp"),
        P("dp", "tensor"),
        P("dp", None),
        P("dp", None),
        P("tensor", "dp"),
        P("dp"),
        P("dp", None),
        P("expert", "dp", "tensor"),
        P("expert", "dp", "tensor"),
        P("expert", "tensor", "dp"),
    )
    return jax.shard_map(
        shards,
        mesh=mesh,
        in_specs=placed,
        out_specs=(
            P("dp", "expert", None),
            P("dp", "expert", None),
            P(("dp", "expert")),
            P(("dp", "expert"), "tensor"),
            P(("dp", "expert", "tensor"), None),
            P(("dp", "expert", "tensor"), None),
            P("tensor", ("dp", "expert")),
            P(("dp", "expert")),
            P(("dp", "expert"), None),
            P("expert", "dp", "tensor"),
            P("expert", "dp", "tensor"),
            P("expert", "tensor", "dp"),
        ),
        check_vma=False,
    )
```

```python
import functools
import math

import jax
import jax.numpy as jnp
import numpy as np
from jax import lax
from jax.experimental import pallas as pl
from jax.experimental.pallas import tpu as pltpu
from jax.sharding import PartitionSpec as P

QUERY_HEADS = 12
KEY_VALUE_HEADS = 2
HEAD_SIZE = 128
GROUP = QUERY_HEADS // KEY_VALUE_HEADS
EPS = 1e-05
ROPE_BASE = 10000.0
NEG = -1e30
F32 = jnp.float32
BF16 = jnp.bfloat16


def dot(left, right, dims):
    return lax.dot_general(left, right, (dims, ((), ())), preferred_element_type=F32)


def norm_factor(rows):
    return lax.rsqrt(jnp.mean(rows * rows, -1, keepdims=True) + EPS)


def norm_back(rows, factor, gain, upstream):
    scaled = upstream * gain
    gain_grad = jnp.sum(upstream * rows * factor, 0)
    inner = jnp.mean(scaled * rows, -1, keepdims=True)
    return factor * scaled - rows * (factor * factor * factor * inner), gain_grad


def layout(starts, parents, places, length):
    labels = jnp.arange(starts.shape[1], dtype=jnp.int32)

    def pick(table, at):
        hot = at[:, :, None] == labels[None, None, :]
        return jnp.sum(jnp.where(hot, table[:, None, :], 0), 2, dtype=jnp.int32)

    segment = jnp.sum((starts[:, None, :] <= places[None, :, None]).astype(jnp.int32), 2) - 1
    above = pick(parents, segment)
    further = pick(parents, above)
    ends = jnp.concatenate(
        [starts[:, 1:], jnp.full((starts.shape[0], 1), length, jnp.int32)], 1
    )
    lengths = ends - starts
    depths = (
        places[None, :]
        - pick(starts, segment)
        + jnp.where(segment != 0, pick(lengths, above), 0)
        + jnp.where(above != 0, pick(lengths, further), 0)
    )
    return segment, above, further, depths


def angles(depths):
    half = HEAD_SIZE // 2
    frequency = ROPE_BASE ** (-2.0 * jnp.arange(half, dtype=F32) / HEAD_SIZE)
    turning = depths.astype(F32)[..., None] * frequency
    return jnp.cos(turning), jnp.sin(turning)


def rotate(heads, cosine, sine):
    half = HEAD_SIZE // 2
    front, back = heads[..., :half], heads[..., half:]
    return jnp.concatenate([front * cosine - back * sine, back * cosine + front * sine], -1)


def general_shards(
    tokens,
    cotangent,
    seg_start,
    seg_parent,
    routes,
    attn_gain,
    w_query,
    w_key,
    w_value,
    w_output,
    moe_gain,
    w_router,
    w_gate,
    w_up,
    w_down,
):
    trees, rows, width = tokens.shape
    expert_count = lax.axis_size("expert")
    tensor_count = lax.axis_size("tensor")
    tensor_at = lax.axis_index("tensor")
    expert_at = lax.axis_index("expert")
    length = rows * expert_count
    heads = w_query.shape[1] // HEAD_SIZE
    kv_head = tensor_at * heads // GROUP
    inv_root = HEAD_SIZE ** (-0.5)
    own_experts = w_gate.shape[0]
    quarter = w_gate.shape[2]
    all_experts = w_router.shape[1]

    def over_dp(array, axis):
        return lax.all_gather(array, "dp", axis=axis, tiled=True)

    w_query = over_dp(w_query, 0)
    w_output = over_dp(w_output, 1)
    gate_t = over_dp(jnp.swapaxes(w_gate, 1, 2), 2)
    up_t = over_dp(jnp.swapaxes(w_up, 1, 2), 2)
    down = over_dp(w_down, 2)
    small = over_dp(
        jnp.concatenate(
            [
                lax.dynamic_slice_in_dim(w_key, kv_head * HEAD_SIZE, HEAD_SIZE, 1),
                lax.dynamic_slice_in_dim(w_value, kv_head * HEAD_SIZE, HEAD_SIZE, 1),
                w_router,
                attn_gain[:, None],
                moe_gain[:, None],
            ],
            1,
        ),
        0,
    )
    w_kv = small[:, : 2 * HEAD_SIZE]
    w_router = small[:, 2 * HEAD_SIZE : 2 * HEAD_SIZE + all_experts]
    attn_gain = small[:, -2].astype(F32)
    moe_gain = small[:, -1].astype(F32)

    all_places = jnp.arange(length, dtype=jnp.int32)
    places = expert_at * rows + jnp.arange(rows, dtype=jnp.int32)
    segment, above, further, depths = layout(seg_start, seg_parent, places, length)
    key_segment = layout(seg_start, seg_parent, all_places, length)[0]
    cosine, sine = angles(depths)
    of_key = key_segment[:, None, :]
    visible = (
        (of_key == segment[:, :, None])
        | (of_key == above[:, :, None])
        | (of_key == further[:, :, None])
    ) & (all_places[None, None, :] <= places[None, :, None])

    residual = tokens.astype(F32).reshape(trees * rows, width)
    factor_one = norm_factor(residual)
    hidden_one = (residual * factor_one * attn_gain).astype(BF16)
    query_pre = dot(hidden_one, w_query, ((1,), (0,))).reshape(trees, rows, heads, HEAD_SIZE)
    kv_pre = dot(hidden_one, w_kv, ((1,), (0,))).reshape(trees, rows, 2 * HEAD_SIZE)
    queries = rotate(query_pre, cosine[:, :, None, :], sine[:, :, None, :]).astype(BF16)
    own_keys = rotate(kv_pre[..., :HEAD_SIZE], cosine, sine).astype(BF16)
    own_kv = jnp.concatenate([own_keys, kv_pre[..., HEAD_SIZE:].astype(BF16)], -1)
    keys_values = lax.all_gather(own_kv, "expert", axis=1, tiled=True)
    keys, values = keys_values[..., :HEAD_SIZE], keys_values[..., HEAD_SIZE:]
    scores = jnp.einsum("bqhd,bkd->bhqk", queries, keys, preferred_element_type=F32) * inv_root
    scores = jnp.where(visible[:, None], scores, NEG)
    row_max = jnp.max(scores, -1, keepdims=True)
    exponent = jnp.exp(scores - row_max)
    probs = exponent / jnp.sum(exponent, -1, keepdims=True)
    probs_low = probs.astype(BF16)
    context = jnp.einsum("bhqk,bkd->bqhd", probs_low, values, preferred_element_type=F32)
    context_low = context.reshape(trees * rows, heads * HEAD_SIZE).astype(BF16)
    attn_out = dot(context_low, w_output, ((1,), (0,))).astype(BF16)
    after_attn = residual + lax.psum(attn_out, "tensor").astype(F32)

    factor_two = norm_factor(after_attn)
    hidden_two = (after_attn * factor_two * moe_gain).astype(BF16)
    logits = dot(hidden_two, w_router, ((1,), (0,)))
    chosen = jnp.any(
        routes.reshape(trees * rows, -1)[:, :, None]
        == jnp.arange(all_experts, dtype=jnp.int32)[None, None, :],
        1,
    )
    masked = jnp.where(chosen, logits, NEG)
    raised = jnp.where(chosen, jnp.exp(masked - jnp.max(masked, -1, keepdims=True)), 0.0)
    mixing = raised / jnp.sum(raised, -1, keepdims=True)

    def over_expert(array):
        full = lax.all_gather(
            array.reshape(trees, rows, array.shape[-1]), "expert", axis=1, tiled=True
        )
        return full.reshape(trees * length, array.shape[-1])

    every_hidden = over_expert(hidden_two)
    every_up = over_expert(cotangent)
    every_mix = lax.dynamic_slice_in_dim(
        over_expert(mixing), expert_at * own_experts, own_experts, 1
    )
    count = trees * length
    pre_gate = dot(every_hidden, gate_t.reshape(-1, width), ((1,), (1,)))
    pre_up = dot(every_hidden, up_t.reshape(-1, width), ((1,), (1,)))
    down_rows = down.reshape(-1, width)
    down_back = dot(every_up, down_rows, ((1,), (1,)))
    wide_mix = jnp.repeat(every_mix, quarter, axis=1)
    activated, pull = jax.vjp(jax.nn.gelu, pre_gate)
    hidden = activated * pre_up
    mixed_hidden = (hidden * wide_mix).astype(BF16)
    moe_part = dot(mixed_hidden, down_rows, ((1,), (0,))).astype(BF16)
    gate_part = jnp.sum((hidden * down_back).reshape(count, own_experts, quarter), -1)
    hidden_grad = wide_mix * down_back
    gate_pre = pull(hidden_grad * pre_up)[0].astype(BF16)
    up_pre = (hidden_grad * activated).astype(BF16)
    two_part = (
        dot(gate_pre, gate_t.reshape(-1, width), ((1,), (0,)))
        + dot(up_pre, up_t.reshape(-1, width), ((1,), (0,)))
    ).astype(BF16)
    d_down = dot(mixed_hidden, every_up, ((0,), (0,)))
    d_gate = dot(gate_pre, every_hidden, ((0,), (0,)))
    d_up = dot(up_pre, every_hidden, ((0,), (0,)))

    def to_owner(array):
        array = array.reshape(trees, length, array.shape[-1])
        part = lax.psum_scatter(array, "expert", scatter_dimension=1, tiled=True)
        return lax.psum(part, "tensor").reshape(trees * rows, -1)

    spread = jnp.arange(all_experts) // own_experts == expert_at
    gate_wide = jnp.where(
        spread[None, :], jnp.tile(gate_part, (1, all_experts // own_experts)), 0.0
    )
    two_grad = to_owner(two_part).astype(F32)
    mix_grad = to_owner(gate_wide)
    mixed_out = (after_attn + to_owner(moe_part).astype(F32)).astype(BF16)

    picked_grad = mixing * (mix_grad - jnp.sum(mixing * mix_grad, -1, keepdims=True))
    logit_grad = picked_grad.astype(BF16)
    two_grad = two_grad + dot(logit_grad, w_router, ((1,), (1,)))
    d_router = dot(hidden_two, logit_grad, ((0,), (0,)))
    norm_two, d_moe_gain = norm_back(after_attn, factor_two, moe_gain, two_grad)
    attn_grad = cotangent.astype(F32).reshape(trees * rows, width) + norm_two
    attn_low = attn_grad.astype(BF16)

    d_output = dot(context_low, attn_low, ((0,), (0,)))
    context_grad = (
        dot(attn_low, w_output, ((1,), (1,)))
        .astype(BF16)
        .reshape(trees, rows, heads, HEAD_SIZE)
    )
    prob_grad = jnp.einsum("bqhd,bkd->bhqk", context_grad, values, preferred_element_type=F32)
    score_grad = probs * (prob_grad - jnp.sum(probs * prob_grad, -1, keepdims=True))
    score_grad = score_grad.astype(BF16)
    query_grad = (
        jnp.einsum("bhqk,bkd->bqhd", score_grad, keys, preferred_element_type=F32) * inv_root
    )
    key_grad = (
        jnp.einsum("bhqk,bqhd->bkd", score_grad, queries, preferred_element_type=F32) * inv_root
    )
    value_grad = jnp.einsum("bhqk,bqhd->bkd", probs_low, context_grad, preferred_element_type=F32)
    kv_part = jnp.concatenate([key_grad, value_grad], -1).astype(BF16)
    kv_sum = lax.psum_scatter(kv_part, "expert", scatter_dimension=1, tiled=True)
    sharing = GROUP // heads
    own_rows = rows // sharing
    place = tensor_at % sharing
    kv_rows = kv_sum.reshape(trees, sharing, own_rows, 2 * HEAD_SIZE)
    mine = lax.dynamic_index_in_dim(kv_rows, place, 1, False).astype(F32)
    for step in range(1, sharing):
        order = [
            (at, at // sharing * sharing + (at + step) % sharing) for at in range(tensor_count)
        ]
        away = lax.dynamic_index_in_dim(kv_rows, (place + step) % sharing, 1, False)
        mine = mine + lax.ppermute(away, "tensor", order).astype(F32)

    def own(array):
        return lax.dynamic_slice_in_dim(array, place * own_rows, own_rows, 1)

    key_low = rotate(mine[..., :HEAD_SIZE], own(cosine), -own(sine)).astype(BF16)
    kv_low = jnp.concatenate([key_low, mine[..., HEAD_SIZE:].astype(BF16)], -1)
    kv_low = kv_low.reshape(trees * own_rows, 2 * HEAD_SIZE)
    hidden_own = own(hidden_one.reshape(trees, rows, width)).reshape(trees * own_rows, width)
    d_kv = dot(hidden_own, kv_low, ((0,), (0,)))
    kv_back = dot(kv_low, w_kv, ((1,), (1,))).reshape(trees, own_rows, width)
    query_low = rotate(query_grad, cosine[:, :, None, :], -sine[:, :, None, :])
    query_low = query_low.astype(BF16).reshape(trees * rows, heads * HEAD_SIZE)
    d_query = dot(hidden_one, query_low, ((0,), (0,)))
    one_part = dot(query_low, w_query, ((1,), (1,))).reshape(trees, rows, width)
    one_part = lax.dynamic_update_slice_in_dim(
        one_part, own(one_part) + kv_back, place * own_rows, 1
    ).reshape(trees * rows, width)
    one_grad = lax.psum(one_part.astype(BF16), "tensor").astype(F32)
    norm_one, d_attn_gain = norm_back(residual, factor_one, attn_gain, one_grad)
    d_tokens = (attn_grad + norm_one).reshape(trees, rows, width)

    def scatter_dp(array, axis):
        return lax.psum_scatter(array, "dp", scatter_dimension=axis, tiled=True)

    def scatter_expert(array, axis):
        return lax.psum_scatter(array, "expert", scatter_dimension=axis, tiled=True)

    def experts_home(array):
        return scatter_dp(array.astype(BF16), 1).astype(F32).reshape(own_experts, quarter, -1)

    d_gate, d_up, d_down = experts_home(d_gate), experts_home(d_up), experts_home(d_down)
    d_query = scatter_expert(scatter_dp(d_query.astype(BF16), 0), 0).astype(F32)
    d_output = scatter_expert(scatter_dp(d_output.astype(BF16), 1), 1).astype(F32)
    flat = jnp.concatenate([d_attn_gain[:, None], d_moe_gain[:, None], d_router], 1)
    flat = scatter_expert(scatter_dp(flat, 0), 0)
    of_head = (jnp.arange(KEY_VALUE_HEADS) == kv_head).astype(F32)[None, None, :, None]
    d_kv = scatter_expert(scatter_dp(d_kv, 0), 0).reshape(-1, 2, 1, HEAD_SIZE) * of_head
    d_kv = d_kv.reshape(-1, 2 * KEY_VALUE_HEADS * HEAD_SIZE)
    d_kv = lax.psum_scatter(d_kv, "tensor", scatter_dimension=0, tiled=True)
    return (
        mixed_out.reshape(trees, rows, width),
        d_tokens,
        flat[:, 0],
        d_query,
        d_kv[:, : KEY_VALUE_HEADS * HEAD_SIZE],
        d_kv[:, KEY_VALUE_HEADS * HEAD_SIZE :],
        d_output,
        flat[:, 1],
        flat[:, 2:],
        jnp.swapaxes(d_gate, 1, 2),
        jnp.swapaxes(d_up, 1, 2),
        d_down,
    )


MESH = pl.DeviceIdType.MESH
NT = (((1,), (1,)), ((), ()))
NN = (((1,), (0,)), ((), ()))
TN = (((0,), (0,)), ((), ()))
CHUNKS = 4
TILE = 128
KINDS = 3
ROOT_2_PI = math.sqrt(2.0 / math.pi)
CUBIC = 0.044715


def mm(left, right, dims=NN):
    return lax.dot_general(left, right, dims, preferred_element_type=F32)


def rows_at(number, size):
    return pl.ds(pl.multiple_of(number * size, size), size)


class Place:
    def __init__(self):
        self.z = lax.axis_index("dp")
        self.x = lax.axis_index("expert")
        self.t = lax.axis_index("tensor")
        self.y = self.t // 2
        self.c = self.t % 2

    def at_z(self, z):
        return (z, self.x, self.t)

    def x_peer(self):
        return (self.z, 1 - self.x, self.t)

    def y_peer(self):
        return (self.z, self.x, (self.t + 2) % 4)

    def core_peer(self):
        return (self.z, self.x, self.t + 1 - 2 * self.c)


def remote(src, dst, sems, at, device):
    return pltpu.make_async_remote_copy(
        src_ref=src,
        dst_ref=dst,
        send_sem=sems.at[0, at],
        recv_sem=sems.at[1, at],
        device_id=device,
        device_id_type=MESH,
    )


def signal(sem, device):
    pl.semaphore_signal(sem, inc=1, device_id=device, device_id_type=MESH)


def await_signal(sem):
    pl.semaphore_wait(sem, 1)


def greet(devices):
    barrier = pltpu.get_barrier_semaphore()
    for device in devices:
        pl.semaphore_signal(barrier, inc=1, device_id=device, device_id_type=MESH)
    pl.semaphore_wait(barrier, len(devices))


def tree_tables(starts, parents, tree, first, rows, length, frequency):
    count = starts.shape[1]
    place = first + lax.broadcasted_iota(jnp.int32, (rows, HEAD_SIZE), 0)
    start = [starts[tree, k] for k in range(count)]
    parent = [parents[tree, k] for k in range(count)]
    size = [(start[k + 1] if k + 1 < count else length) - start[k] for k in range(count)]

    def pick(table, at):
        total = jnp.zeros_like(at)
        for k in range(count):
            total = total + jnp.where(at == k, table[k], 0)
        return total

    def segment_of(at):
        total = jnp.zeros_like(at)
        for k in range(1, count):
            total = total + jnp.where(at >= start[k], 1, 0)
        return total

    segment = segment_of(place)
    above = pick(parent, segment)
    further = pick(parent, above)
    depth = (
        place
        - pick(start, segment)
        + jnp.where(segment != 0, pick(size, above), 0)
        + jnp.where(above != 0, pick(size, further), 0)
    )
    turning = depth.astype(F32) * frequency
    lane = lax.broadcasted_iota(jnp.int32, (rows, HEAD_SIZE), 1)
    cosine = jnp.cos(turning)
    sine = jnp.sin(turning)
    sine = jnp.where(lane < HEAD_SIZE // 2, -sine, sine)
    key_place = lax.broadcasted_iota(jnp.int32, (8, length), 1)
    key_segment = jnp.broadcast_to(segment_of(key_place)[:1], (rows, length))
    key_place = jnp.broadcast_to(key_place[:1], (rows, length))
    wide = length // HEAD_SIZE

    def widen(array):
        return jnp.concatenate([array] * wide, 1)

    visible = (
        (key_segment == widen(segment))
        | (key_segment == widen(above))
        | (key_segment == widen(further))
    ) & (key_place <= widen(place))
    return jnp.where(visible, 1.0, 0.0), cosine, sine


def turn(head, cosine, sine):
    return head * cosine + pltpu.roll(head, HEAD_SIZE // 2, 1) * sine


class Relay:
    def __init__(self, me, deep, piece, up_sems, dn_sems, side_sems=None):
        self.me, self.deep, self.piece = me, deep, piece
        self.up_sems, self.dn_sems, self.side_sems = up_sems, dn_sems, side_sems

    def up(self, source, part, hop):
        above = self.me.at_z(jnp.minimum(self.me.z + 1, self.deep - 1))
        at = self.piece(source, part, self.me.x)
        return remote(at, at, self.up_sems, part * self.deep + hop, above)

    def dn(self, source, part, hop):
        below = self.me.at_z(jnp.maximum(self.me.z - 1, 0))
        at = self.piece(source, part, self.me.x)
        return remote(at, at, self.dn_sems, part * self.deep + hop, below)

    def side(self, source, part, hop, x):
        at = self.piece(source, part, x)
        return remote(at, at, self.side_sems, part * 2 * self.deep + hop, self.me.x_peer())

    def begin(self, part, ends=None):
        z, last = self.me.z, self.deep - 1
        at_end = (z == 0) | (z == last)
        now = z >= 0 if ends is None else at_end if ends else jnp.logical_not(at_end)

        @pl.when((z < last) & now)
        def _():
            self.up(z, part, 0).start()

        @pl.when((z > 0) & now)
        def _():
            self.dn(z, part, 0).start()

    def pass_on(self, part, hop):
        z, deep = self.me.z, self.deep
        sides = self.side_sems is not None
        upward = (z - 1 - hop >= 0) & (z < deep - 1)
        downward = (z + 1 + hop < deep) & (z > 0)
        if sides:

            @pl.when(z - 1 - hop >= 0)
            def _():
                self.up(z - 1 - hop, part, hop).wait_recv()
                self.side(z - 1 - hop, part, hop, self.me.x).start()

            @pl.when(z + 1 + hop < deep)
            def _():
                self.dn(z + 1 + hop, part, hop).wait_recv()
                self.side(z + 1 + hop, part, deep + hop, self.me.x).start()

        @pl.when(upward)
        def _():
            if not sides:
                self.up(z - 1 - hop, part, hop).wait_recv()
            self.up(z - 1 - hop, part, hop + 1).start()

        @pl.when(downward)
        def _():
            if not sides:
                self.dn(z + 1 + hop, part, hop).wait_recv()
            self.dn(z + 1 + hop, part, hop + 1).start()

    def finish(self, part):
        z, deep = self.me.z, self.deep
        for hop in range(deep - 1):
            if self.side_sems is not None:

                @pl.when(z - 1 - hop >= 0)
                def _():
                    self.side(z - 1 - hop, part, hop, 1 - self.me.x).wait_recv()

                @pl.when(z + 1 + hop < deep)
                def _():
                    self.side(z + 1 + hop, part, deep + hop, 1 - self.me.x).wait_recv()

            else:

                @pl.when(z == deep - 1)
                def _():
                    self.up(z - 1 - hop, part, hop).wait_recv()

                @pl.when(z == 0)
                def _():
                    self.dn(z + 1 + hop, part, hop).wait_recv()

    def drain(self, part):
        z, deep = self.me.z, self.deep
        for hop in range(deep):

            @pl.when((z - hop >= 0) & (z < deep - 1))
            def _():
                self.up(z - hop, part, hop).wait_send()

            @pl.when((z + hop < deep) & (z > 0))
            def _():
                self.dn(z + hop, part, hop).wait_send()

        if self.side_sems is not None:
            for hop in range(deep - 1):

                @pl.when(z - 1 - hop >= 0)
                def _():
                    self.side(z - 1 - hop, part, hop, self.me.x).wait_send()

                @pl.when(z + 1 + hop < deep)
                def _():
                    self.side(z + 1 + hop, part, deep + hop, self.me.x).wait_send()


class PlaneSum:
    def __init__(self, me, rows, make, bufs, landing, sem_set, ahead=None):
        self.me, self.rows, self.make, self.ahead = me, rows, make, ahead
        self.core_out, self.x_out, self.acc, self.y_out = bufs
        self.core_in, self.x_in, self.y_in = landing
        self.core_sems, self.x_sems, self.y_sems = sem_set
        self.tiles = rows // TILE
        self.step = rows // CHUNKS
        self.per_tile = TILE // self.step

    def core_copy(self, number):
        at = rows_at(number, TILE)
        return remote(
            self.core_out.at[at], self.core_in.at[at], self.core_sems, number, self.me.core_peer()
        )

    def x_copy(self, number):
        at = rows_at(number, self.step)
        return remote(self.x_out.at[at], self.x_in.at[at], self.x_sems, number, self.me.x_peer())

    def y_copy(self, number):
        at = rows_at(number, self.step)
        return remote(self.y_out.at[at], self.y_in.at[at], self.y_sems, number, self.me.y_peer())

    def first(self, tree, x, number):
        return pl.multiple_of((tree * 2 + x) * self.rows + number * TILE, TILE)

    def tile(self, tree, x, number, buffer, at):
        value = self.make(self.first(tree, x, number))
        if self.ahead is not None:
            value = value + buffer[at, :].astype(F32)
        return value.astype(BF16)

    def prepare(self):
        me = self.me

        def other(number, carry):
            x = jnp.where(number < self.tiles, 1 - me.x, me.x)
            value = self.ahead(self.first(1 - me.c, x, number % self.tiles))
            self.core_out[rows_at(number, TILE), :] = value.astype(BF16)
            return carry

        def same(number, carry):
            at = rows_at(number, TILE)
            self.x_out[at, :] = self.ahead(self.first(me.c, 1 - me.x, number)).astype(BF16)
            self.acc[at, :] = self.ahead(self.first(me.c, me.x, number))
            return carry

        lax.fori_loop(0, 2 * self.tiles, other, 0)
        lax.fori_loop(0, self.tiles, same, 0)

    def outward(self, side):
        me = self.me
        x = me.x if side else 1 - me.x

        def one(number, carry):
            slot = side * self.tiles + number
            at = rows_at(slot, TILE)
            self.core_out[at, :] = self.tile(1 - me.c, x, number, self.core_out, at)
            self.core_copy(slot).start()
            return carry

        lax.fori_loop(0, self.tiles, one, 0)

    def across(self):
        me = self.me

        def one(number, carry):
            at = rows_at(number, TILE)
            value = self.tile(me.c, 1 - me.x, number, self.x_out, at).astype(F32)
            self.core_copy(number).wait_recv()
            self.x_out[at, :] = (value + self.core_in[at, :].astype(F32)).astype(BF16)
            for k in range(self.per_tile):
                self.x_copy(number * self.per_tile + k).start()
            return carry

        lax.fori_loop(0, self.tiles, one, 0)

    def inward(self):
        me = self.me

        def one(number, carry):
            at = rows_at(number, TILE)
            value = self.tile(me.c, me.x, number, self.acc, at).astype(F32)
            slot = self.tiles + number
            self.core_copy(slot).wait_recv()
            self.acc[at, :] = value + self.core_in[rows_at(slot, TILE), :].astype(F32)
            return carry

        lax.fori_loop(0, self.tiles, one, 0)

    def pass_on(self, first, last):
        def one(number, carry):
            at = rows_at(number, self.step)
            self.x_copy(number).wait_recv()
            self.y_out[at, :] = (self.acc[at, :] + self.x_in[at, :].astype(F32)).astype(BF16)
            self.y_copy(number).start()
            return carry

        lax.fori_loop(first, last, one, 0)

    def total(self, number):
        at = rows_at(number, self.step)
        self.y_copy(number).wait_recv()
        return self.y_out[at, :].astype(F32) + self.y_in[at, :].astype(F32)

    def core_sent(self):
        for number in range(2 * self.tiles):
            self.core_copy(number).wait_send()

    def x_sent(self):
        for number in range(CHUNKS):
            self.x_copy(number).wait_send()

    def y_sent(self):
        for number in range(CHUNKS):
            self.y_copy(number).wait_send()


class Fold:
    def __init__(self, me, groups, bufs, sem_set, tile, merge):
        self.me, self.groups, self.tile, self.merge = me, groups, tile, merge
        self.own, self.stage, self.land = bufs
        self.send_sems, self.recv_sems, self.free = sem_set
        self.sets, self.count, self.rows = self.stage.shape[0], self.own.shape[1], self.own.shape[2]
        self.slots = self.land.shape[1]
        z = me.z
        self.end = jnp.where(z < 2, 0, 3)
        self.mid = jnp.where(z < 2, 1, 2)
        self.far_mid = 3 - self.mid
        self.is_end = z == self.end
        self.is_mid = z == self.mid
        self.targets = (3 - self.end, self.far_mid, jnp.where(self.is_end, self.mid, self.end))

    def place(self, target):
        return (target + 3 - self.me.z) % 4

    def free_at(self, group, which, m):
        return self.free.at[((group % self.sets) * 3 + which) * self.count + m]

    def copy(self, group, which, m, slot=None):
        at = group % self.sets
        target = self.targets[which]
        from_mid = (4 if self.merge else 3, 3, 2)[which]
        there = jnp.where(self.is_end, which, from_mid) if slot is None else slot
        direct = self.far_mid if which == 0 and self.merge else target
        return pltpu.make_async_remote_copy(
            src_ref=self.stage.at[at, self.place(target), m],
            dst_ref=self.land.at[at, there, m],
            send_sem=self.send_sems.at[(at * 3 + which) * self.count + m],
            recv_sem=self.recv_sems.at[(at * self.slots + there) * self.count + m],
            device_id=self.me.at_z(jnp.where(self.is_end, self.mid, direct)),
            device_id_type=MESH,
        )

    def send(self, group, which, m):
        if group >= self.sets:
            await_signal(self.free_at(group, which, m))
        self.copy(group, which, m).start()

    def used(self, group, which, m, sender):
        if group + self.sets < self.groups:
            signal(self.free_at(group, which, m), self.me.at_z(sender))

    def add(self, group, which, m, slot):
        at = group % self.sets
        self.copy(group, which, m, slot).wait_recv()
        term = self.stage.at[at, self.place(self.targets[which]), m]
        landed = self.land.at[at, slot, m]

        def step(number, carry):
            rows = rows_at(number, self.tile)
            total = term[rows, :].astype(F32) + landed[rows, :].astype(F32)
            term[rows, :] = total.astype(BF16)
            return carry

        lax.fori_loop(0, self.rows // self.tile, step, 0)

    def begin(self, group, m):
        @pl.when(self.is_end)
        def _():
            for which in range(3):
                self.send(group, which, m)

        if not self.merge:

            @pl.when(self.is_mid)
            def _():
                self.send(group, 2, m)

    def advance(self, group, m):
        @pl.when(self.is_mid)
        def _():
            for which in (0, 1):
                self.add(group, which, m, which)
                self.used(group, which, m, self.end)
                self.send(group, which, m)

    def let_go(self, group, m):
        @pl.when(self.is_mid)
        def _():
            self.add(group, 2, m, 4)
            self.used(group, 0, m, self.far_mid)
            self.send(group, 2, m)

    def finish(self, group, m, write):
        at = group % self.sets
        own = self.own.at[group, m]
        near, far = self.land.at[at, 2, m], self.land.at[at, 3, m]
        self.copy(group, 2, m, 2).wait_recv()

        def run(pieces):
            def step(number, carry):
                rows = rows_at(number, self.tile)
                total = own[rows, :].astype(F32)
                for piece in pieces:
                    total = total + piece[rows, :].astype(F32)
                write(rows, total)
                return carry

            lax.fori_loop(0, self.rows // self.tile, step, 0)

        if self.merge:

            @pl.when(self.is_end)
            def _():
                run([near])
                self.used(group, 2, m, self.mid)

            @pl.when(self.is_mid)
            def _():
                self.copy(group, 1, m, 3).wait_recv()
                run([near, far])
                self.used(group, 2, m, self.end)
                self.used(group, 1, m, self.far_mid)

        else:
            self.copy(group, 1, m, 3).wait_recv()
            run([near, far])

    def drain(self, group, m):
        for which in range(3):
            self.copy(group, which, m).wait_send()


def place_kernel(*refs):
    count = (len(refs) - 2) // 3
    sources, targets, middles = refs[:count], refs[count : 2 * count], refs[2 * count : -2]
    loads, stores = [], []
    for source, target, middle in zip(sources, targets, middles):
        size = source.shape[0] // 2
        for part in range(2):
            at = pl.ds(part * size, size)
            number = len(loads)
            loads.append(pltpu.make_async_copy(source.at[at], middle.at[at], refs[-2].at[number]))
            stores.append(pltpu.make_async_copy(middle.at[at], target.at[at], refs[-1].at[number]))
    for load in loads:
        load.start()
    for load, store in zip(loads, stores):
        load.wait()
        store.start()
    for store in stores:
        store.wait()


def place_call(arrays):
    hbm = pl.BlockSpec(memory_space=pl.ANY)
    done = pltpu.SemaphoreType.DMA((2 * len(arrays),))
    return pl.pallas_call(
        place_kernel,
        out_shape=tuple(jax.ShapeDtypeStruct(a.shape, a.dtype) for a in arrays),
        in_specs=[hbm] * len(arrays),
        out_specs=[hbm] * len(arrays),
        scratch_shapes=[pltpu.VMEM(a.shape, a.dtype) for a in arrays] + [done, done],
        compiler_params=pltpu.CompilerParams(vmem_limit_bytes=60 * 2**20),
        name="place",
    )(*arrays)


def layer_kernel(
    starts,
    parents,
    frequency,
    routes,
    small,
    tokens_in,
    cotangent_in,
    w_query,
    w_key,
    w_value,
    w_output,
    gate_in,
    up_in,
    down_in,
    mixed,
    d_tokens,
    d_gate,
    d_up,
    d_down,
    d_query,
    d_output,
    d_key,
    d_value,
    d_small,
    mats,
    acts,
    hid,
    ups,
    wqkv,
    wout,
    smalls,
    queries,
    keys,
    values,
    probs,
    context,
    tables,
    after,
    mixes,
    gates,
    gates_out,
    gates_in,
    core_out,
    x_out,
    acc,
    y_out,
    two_core_in,
    two_x_in,
    two_y_in,
    mo_core_in,
    mo_x_in,
    mo_y_in,
    agrad,
    alow,
    qlow,
    kv_out,
    kv_in,
    kv_own,
    kvx_out,
    kvx_in,
    kvlow,
    kvlow_x,
    qlow_x,
    hidx,
    alx,
    ctx_x,
    dkv_out,
    dkv_in,
    own,
    stage,
    land,
    bounce,
    own_o,
    stage_o,
    land_o,
    own_q,
    stage_q,
    land_q,
    small_own,
    small_in,
    small_z,
    kv_last,
    kv_land,
    load_sem,
    small_sem,
    up1_sem,
    dn1_sem,
    side1_sem,
    up2_sem,
    dn2_sem,
    side2_sem,
    up3_sem,
    dn3_sem,
    kv_sem,
    cot_sem,
    core_sem,
    y_sem,
    hx_sem,
    hc_sem,
    hf_sem,
    mix_sem,
    gate_sem,
    two_core_sem,
    two_x_sem,
    two_y_sem,
    mo_core_sem,
    mo_x_sem,
    mo_y_sem,
    one_core_sem,
    one_y_sem,
    low_sem,
    kvg_sem,
    qx_sem,
    hidx_sem,
    alx_sem,
    ctx_sem,
    fold_send,
    fold_recv,
    fold_free,
    fold_send_o,
    fold_recv_o,
    fold_send_q,
    fold_recv_q,
    out_sem,
    mixed_sem,
    token_sem,
    grad_sem,
    small_in_sem,
    small_z_sem,
    last_sem,
):
    me = Place()
    z, x, y, c = me.z, me.x, me.y, me.c
    deep, shard = wqkv.shape[0], wqkv.shape[1]
    trees, heads, rows, length = probs.shape
    width = hid.shape[1]
    groups = gates.shape[0]
    units = mats.shape[1] // groups
    mine = heads * HEAD_SIZE
    half = shard // 2
    step = rows // CHUNKS
    inv_root = HEAD_SIZE ** (-0.5)
    own_block = c * 2 + x
    is_end = (z == 0) | (z == deep - 1)

    def block_rows(tree, side):
        return rows_at(tree * 2 + side, rows)

    def shard_lanes(k):
        return rows_at(k, shard)

    def load(source, target, at):
        return pltpu.make_async_copy(source, target, load_sem.at[at])

    head_lanes = rows_at(y, HEAD_SIZE)
    loads = [
        load(w_query, wqkv.at[z, :, pl.ds(0, mine)], 0),
        load(w_key.at[:, head_lanes], wqkv.at[z, :, pl.ds(mine, HEAD_SIZE)], 1),
        load(w_value.at[:, head_lanes], wqkv.at[z, :, pl.ds(mine + HEAD_SIZE, HEAD_SIZE)], 2),
        load(small, smalls.at[z], 3),
        load(w_output, wout.at[z], 4),
        load(tokens_in, alow, 5),
        load(cotangent_in.at[0], ups.at[block_rows(0, x)], 6),
        load(cotangent_in.at[1], ups.at[block_rows(1, x)], 7),
        load(gate_in, mats.at[0, :, shard_lanes(z)], 8),
        load(up_in, mats.at[1, :, shard_lanes(z)], 9),
        load(down_in, mats.at[2, :, shard_lanes(z)], 10),
    ]
    for copy in loads:
        copy.start()
    lin = x * 4 + me.t

    def plane(number):
        return (z, number // 4, number % 4)

    greet(
        [me.at_z((z + k) % deep) for k in range(1, deep)]
        + [plane((lin + k) % 8) for k in range(1, 8)]
    )
    for copy in loads[:4]:
        copy.wait()

    def halved(buffer):
        def piece(source, part, by):
            return buffer.at[source, rows_at(by, half)]

        return piece

    def expert_piece(source, part, by):
        return mats.at[:, pl.ds(part * units, units), shard_lanes(source)]

    take_qkv = Relay(me, deep, halved(wqkv), up1_sem, dn1_sem, side1_sem)
    take_out = Relay(me, deep, halved(wout), up2_sem, dn2_sem, side2_sem)
    take = Relay(me, deep, expert_piece, up3_sem, dn3_sem)

    def small_out(k):
        there = (z + k) % deep
        return remote(smalls.at[z], smalls.at[z], small_sem, k - 1, me.at_z(there))

    take_qkv.begin(0)
    for k in range(1, deep):
        small_out(k).start()

    for tree in range(trees):
        seen, cosine, sine = tree_tables(
            starts, parents, tree, x * rows, rows, length, frequency[:1, :]
        )
        agrad[:, pl.ds(tree * length, length)] = seen
        tables[0, tree] = cosine
        tables[1, tree] = sine
    take_qkv.pass_on(0, 0)
    for copy in loads[4:]:
        copy.wait()
    take_out.begin(0)
    for k in range(1, deep):
        source = (z + deep - k) % deep
        remote(
            smalls.at[source], smalls.at[source], small_sem, k - 1, me.at_z(source)
        ).wait_recv()
    gain_one = jnp.concatenate([smalls[k, :1, :] for k in range(deep)], 1).astype(F32)
    gain_two = jnp.concatenate([smalls[k, 1:2, :] for k in range(deep)], 1).astype(F32)
    router = jnp.concatenate([smalls[k, 8:, :] for k in range(deep)], 1)

    def norm_rows(source, target, at):
        value = source[at, :].astype(F32)
        factor = lax.rsqrt(jnp.mean(value * value, -1, keepdims=True) + EPS)
        target[at, :] = (value * factor * gain_one).astype(BF16)

    for tree in range(trees):

        def first_norm(number, carry):
            at = rows_at(number, step)
            norm_rows(alow.at[tree], core_out.at[pl.ds(tree * rows, rows)], at)
            return carry

        lax.fori_loop(0, CHUNKS, first_norm, 0)
    take_qkv.pass_on(0, 1)
    take_out.pass_on(0, 0)
    take.begin(0)
    take_qkv.pass_on(0, 2)
    take_qkv.finish(0)
    take_out.pass_on(0, 1)

    own_place = rows_at(x, rows)
    away_place = rows_at(1 - x, rows)

    def kv_copy(tree, which, place, on):
        at = (keys, values)[which].at[tree, place]
        return remote(at, at, kv_sem, 2 * on + which, me.core_peer() if on else me.x_peer())

    def project_in(tree):
        total = jnp.zeros((rows, wqkv.shape[2]), F32)
        for k in range(deep):
            total = total + mm(core_out[rows_at(tree, rows), pl.ds(k * shard, shard)], wqkv[k])
        cosine, sine = tables[0, tree], tables[1, tree]
        for head in range(heads):
            part_q = total[:, head * HEAD_SIZE : (head + 1) * HEAD_SIZE]
            queries[tree, head] = turn(part_q, cosine, sine).astype(BF16)
        part_k = total[:, mine : mine + HEAD_SIZE]
        keys[tree, own_place, :] = turn(part_k, cosine, sine).astype(BF16)
        values[tree, own_place, :] = total[:, mine + HEAD_SIZE :].astype(BF16)

    project_in(c)
    for which in range(2):
        kv_copy(c, which, own_place, 0).start()
    project_in(1 - c)
    take_out.pass_on(0, 2)

    own_up, away_up = ups.at[block_rows(c, x)], ups.at[block_rows(c, 1 - x)]
    peer_up = ups.at[block_rows(1 - c, 1 - x)]
    cot_x = remote(own_up, own_up, cot_sem, 0, me.x_peer())
    cot_x.start()
    for which in range(2):
        kv_copy(c, which, away_place, 0).wait_recv()
        kv_copy(c, which, away_place, 1).start()

    def attend(tree):
        mask = agrad.at[:, rows_at(tree, length)]

        def one(head, carry):
            score = mm(queries[tree, head], keys[tree], NT) * inv_root
            score = jnp.where(mask[...] > 0.5, score, NEG)
            top = jnp.max(score, -1, keepdims=True)
            raised = jnp.exp(score - top)
            prob = (raised / jnp.sum(raised, -1, keepdims=True)).astype(BF16)
            probs[tree, head] = prob
            context[tree, head] = mm(prob, values[tree]).astype(BF16)
            return carry

        lax.fori_loop(0, heads, one, 0)

    attend(c)
    take.pass_on(0, 0)
    take.begin(1, False)
    for part in range(1, groups):
        take.begin(part, True)
    for which in range(2):
        kv_copy(1 - c, which, away_place, 1).wait_recv()
    attend(1 - c)
    take_out.finish(0)

    def project(tree, row):
        pieces = []
        for k in range(deep):
            piece = jnp.zeros((step, shard), F32)
            for head in range(heads):
                piece = piece + mm(
                    context[tree, head, pl.ds(row, step), :],
                    wout[k, pl.ds(head * HEAD_SIZE, HEAD_SIZE), :],
                )
            pieces.append(piece)
        return pieces

    def core_copy(number):
        at = rows_at(number, step)
        return remote(core_out.at[at], mo_core_in.at[at], core_sem, number, me.core_peer())

    def y_copy(number):
        at = rows_at(number, step)
        return remote(y_out.at[at], mo_y_in.at[at], y_sem, number, me.y_peer())

    for chunk in range(CHUNKS):
        at = pl.ds(chunk * step, step)
        for k, piece in enumerate(project(1 - c, chunk * step)):
            core_out[at, pl.ds(k * shard, shard)] = piece.astype(BF16)
        core_copy(chunk).start()
    for chunk in range(CHUNKS):
        at = pl.ds(chunk * step, step)
        pieces = project(c, chunk * step)
        core_copy(chunk).wait_recv()
        for k, piece in enumerate(pieces):
            lanes = pl.ds(k * shard, shard)
            both = piece.astype(BF16).astype(F32) + mo_core_in[at, lanes].astype(F32)
            y_out[at, lanes] = both.astype(BF16)
        y_copy(chunk).start()
    take.pass_on(0, 1)

    def two_rows(tree, side, number):
        first = (tree * 2 + side) * rows + number * step
        return pl.ds(pl.multiple_of(first, step), step)

    def hid_copy(tree, side, sems, number, device):
        at = hid.at[two_rows(tree, side, number)]
        return remote(at, at, sems, number, device)

    def second(number, carry):
        at = rows_at(number, step)
        y_copy(number).wait_recv()
        value = alow[c, at, :].astype(F32) + (y_out[at, :].astype(F32) + mo_y_in[at, :].astype(F32))
        after[at, :] = value
        factor = lax.rsqrt(jnp.mean(value * value, -1, keepdims=True) + EPS)
        hid[two_rows(c, x, number), :] = (value * factor * gain_two).astype(BF16)
        hid_copy(c, x, hx_sem, number, me.x_peer()).start()
        hid_copy(c, x, hc_sem, number, me.core_peer()).start()
        return carry

    lax.fori_loop(0, 2, second, 0)
    take.pass_on(1, 0)
    take.begin(2, False)
    lax.fori_loop(2, CHUNKS, second, 0)

    logits = mm(router, hid[block_rows(c, x), :], NT)
    expert = lax.broadcasted_iota(jnp.int32, logits.shape, 0)
    chosen = expert < 0
    for k in range(routes.shape[1]):
        chosen = chosen | (expert == routes[c, k : k + 1, :])
    logits = jnp.where(chosen, logits, NEG)
    raised = jnp.where(chosen, jnp.exp(logits - jnp.max(logits, 0, keepdims=True)), 0.0)
    mixes[own_block] = raised / jnp.sum(raised, 0, keepdims=True)

    def mix_copy(tree, side, at, device):
        block = mixes.at[tree * 2 + side]
        return remote(block, block, mix_sem, at, device)

    mix_copy(c, x, 0, me.x_peer()).start()
    mix_copy(c, x, 1, me.core_peer()).start()
    cot_x_in = remote(away_up, away_up, cot_sem, 0, me.x_peer())
    cot_x_in.wait_recv()
    cot_on = remote(away_up, away_up, cot_sem, 1, me.core_peer())
    cot_on.start()
    for number in range(CHUNKS):
        hid_copy(c, 1 - x, hx_sem, number, me.x_peer()).wait_recv()
        hid_copy(c, 1 - x, hf_sem, number, me.core_peer()).start()
    mix_copy(c, 1 - x, 0, me.x_peer()).wait_recv()
    mix_copy(c, 1 - x, 2, me.core_peer()).start()
    remote(peer_up, peer_up, cot_sem, 1, me.core_peer()).wait_recv()
    for number in range(CHUNKS):
        hid_copy(1 - c, x, hc_sem, number, me.core_peer()).wait_recv()
        hid_copy(1 - c, 1 - x, hf_sem, number, me.core_peer()).wait_recv()
    mix_copy(1 - c, x, 1, me.core_peer()).wait_recv()
    mix_copy(1 - c, 1 - x, 2, me.core_peer()).wait_recv()
    take.pass_on(1, 1)

    def half_lanes(k, side):
        first = k * shard + side * HEAD_SIZE
        return pl.ds(pl.multiple_of(first, HEAD_SIZE), 2 * HEAD_SIZE)

    def cross(source, landing, tree, k, on, sems):
        at = landing.at[tree, k]
        if on:
            return remote(at, at, sems, deep + k, me.core_peer())
        return remote(source.at[:, half_lanes(k, 1 - x)], at, sems, k, me.x_peer())

    def hidx_copy(tree, k, on):
        return cross(x_out, hidx, tree, k, on, hidx_sem)

    def alx_copy(tree, k, on):
        return cross(alow.at[tree], alx, tree, k, on, alx_sem)

    def again(number, carry):
        norm_rows(alow.at[c], x_out, rows_at(number, step))
        return carry

    lax.fori_loop(0, CHUNKS, again, 0)
    for k in range(deep):
        hidx_copy(c, k, 0).start()
    ctx_copy = remote(context, ctx_x, ctx_sem, 0, me.x_peer())
    ctx_copy.start()
    take.finish(0)

    def expert_block(group, block):
        tokens = rows_at(block, rows)
        some = pl.ds(group * units, units)
        pre_gate = mm(mats[0, some, :], hid[tokens, :], NT)
        pre_up = mm(mats[1, some, :], hid[tokens, :], NT)
        back = mm(mats[2, some, :], ups[tokens, :], NT)
        first, second_half = mixes[block, group : group + 1, :], mixes[
            block, groups + group : groups + group + 1, :
        ]
        weight = jnp.broadcast_to(jnp.where(x == 0, first, second_half), (units, rows))
        square = pre_gate * pre_gate
        bent = jnp.tanh(ROOT_2_PI * pre_gate * (1.0 + CUBIC * square))
        slope = 0.5 * (1.0 + bent)
        active = pre_gate * slope
        rise = slope + 0.5 * pre_gate * (1.0 - bent * bent) * ROOT_2_PI * (
            1.0 + 3.0 * CUBIC * square
        )
        hidden = active * pre_up
        gates[pl.ds(group, 1), tokens] = jnp.sum(hidden * back, 0, keepdims=True)
        back = weight * back
        acts[0, some, tokens] = (back * pre_up * rise).astype(BF16)
        acts[1, some, tokens] = (back * active).astype(BF16)
        acts[2, some, tokens] = (weight * hidden).astype(BF16)

    fold = Fold(me, groups, (own, stage, land), (fold_send, fold_recv, fold_free), 64, True)

    def expert_grad(group, m):
        source = ups if m == 2 else hid
        some = acts.at[m, pl.ds(group * units, units)]

        def one(k, carry):
            value = mm(some[...], source[:, shard_lanes(k)]).astype(BF16)

            @pl.when(k == z)
            def _():
                own[group, m] = value

            @pl.when(k != z)
            def _():
                stage[group % fold.sets, fold.place(k), m] = value

            return carry

        lax.fori_loop(0, deep, one, 0)
        fold.begin(group, m)

    def expert_group(group):
        def one(block, carry):
            expert_block(group, block)
            return carry

        lax.fori_loop(0, 2 * trees, one, 0)
        for m in range(KINDS):
            expert_grad(group, m)

    expert_outs = (d_gate, d_up, d_down)

    def grad_out(group, m):
        return pltpu.make_async_copy(
            bounce.at[m], expert_outs[m].at[pl.ds(group * units, units)], grad_sem.at[m]
        )

    def finish_group(group, ends):
        @pl.when(is_end if ends else jnp.logical_not(is_end))
        def _():
            for m in range(KINDS):
                if group > 0:
                    grad_out(group - 1, m).wait()

                def write(at, value):
                    bounce[m, at, :] = value

                fold.finish(group, m, write)
                grad_out(group, m).start()

    def advance(group, kinds=range(KINDS)):
        for m in kinds:
            fold.advance(group, m)

    def let_go(group):
        for m in range(KINDS):
            fold.let_go(group, m)

    def drain(group):
        for m in range(KINDS):
            fold.drain(group, m)

    take.pass_on(2, 0)
    take.begin(3, False)
    expert_group(0)
    take.pass_on(2, 1)
    take.pass_on(3, 0)
    take.finish(1)
    expert_group(1)
    take.pass_on(3, 1)
    for k in range(deep):
        hidx_copy(c, k, 0).wait_recv()
        hidx_copy(c, k, 1).start()
    advance(0)
    take.finish(2)
    expert_group(2)
    finish_group(0, False)
    last = groups - 1

    def two_units(first, some):
        at = pl.ds(first, TILE)
        total = mm(acts[0, some, at], mats[0, some, :], TN)
        return total + mm(acts[1, some, at], mats[1, some, :], TN)

    def two_ahead(first):
        return two_units(first, pl.ds(0, last * units))

    def two_make(first):
        return two_units(first, pl.ds(last * units, units))

    def mo_make(first):
        return mm(acts[2, :, pl.ds(first, TILE)], mats[2], TN)

    two = PlaneSum(
        me,
        rows,
        two_make,
        (core_out, x_out, acc, y_out),
        (two_core_in, two_x_in, two_y_in),
        (two_core_sem, two_x_sem, two_y_sem),
        two_ahead,
    )
    mo = PlaneSum(
        me,
        rows,
        mo_make,
        (core_out, hid.at[pl.ds(rows, rows)], acc, hid.at[pl.ds(0, rows)]),
        (mo_core_in, mo_x_in, mo_y_in),
        (mo_core_sem, mo_x_sem, mo_y_sem),
    )
    for number in range(CHUNKS):
        core_copy(number).wait_send()
        y_copy(number).wait_send()
    for k in range(deep):
        hidx_copy(c, k, 0).wait_send()
    two.prepare()
    advance(1)
    let_go(0)
    take.finish(3)
    expert_block(last, (1 - c) * 2 + 1 - x)
    two.outward(0)
    expert_block(last, (1 - c) * 2 + x)
    two.outward(1)
    expert_block(last, c * 2 + 1 - x)
    two.across()
    expert_block(last, own_block)

    for block in range(2 * trees):
        gates_out[block, pl.ds(0, groups), :] = gates[:, pl.ds(block * rows, rows)]

    def gate_copy(k):
        there = (lin + k) % 8
        block = (there % 2) * 2 + there // 4
        return remote(gates_out.at[block], gates_in.at[lin], gate_sem, k - 1, plane(there))

    for k in range(1, 8):
        gate_copy(k).start()
    gates_in[lin] = gates_out[own_block]
    two.inward()
    drain(0)
    expert_grad(last, 0)
    two.pass_on(0, 1)
    expert_grad(last, 1)
    two.pass_on(1, 2)
    expert_grad(last, 2)
    two.pass_on(2, 3)
    advance(2, [0])

    for k in range(1, 8):
        source = (lin + 8 - k) % 8
        remote(gates_out.at[0], gates_in.at[source], gate_sem, k - 1, plane(source)).wait_recv()
    sums = []
    for side in range(2):
        total = gates_in[side * 4]
        for k in range(1, 4):
            total = total + gates_in[side * 4 + k]
        sums.append(total[:groups])
    mix_grad = jnp.concatenate(sums, 0)
    mix = mixes[own_block]
    picked = mix * (mix_grad - jnp.sum(mix * mix_grad, 0, keepdims=True))
    logit_grad = picked.astype(BF16)
    agrad[...] = mm(logit_grad, router, TN)
    small_own[pl.ds(0, 8), :] = jnp.zeros((8, width), F32)
    small_own[pl.ds(8, 8), :] = mm(logit_grad, hid[block_rows(c, x), :])

    for number in range(CHUNKS):
        hid_copy(c, x, hx_sem, number, me.x_peer()).wait_send()
        hid_copy(c, x, hc_sem, number, me.core_peer()).wait_send()
        hid_copy(c, 1 - x, hf_sem, number, me.core_peer()).wait_send()
    two.pass_on(3, 4)
    two.core_sent()
    mo.outward(0)
    mo.outward(1)
    advance(2, [1])

    def low_copy(number):
        at = alow.at[c, rows_at(number, step)]
        return remote(at, at, low_sem, number, me.core_peer())

    def second_norm(number, gain_grad):
        at = rows_at(number, step)
        upstream = two.total(number) + agrad[at, :]
        value = after[at, :]
        factor = lax.rsqrt(jnp.mean(value * value, -1, keepdims=True) + EPS)
        scaled = upstream * gain_two
        inner = jnp.mean(scaled * value, -1, keepdims=True)
        cot = ups[two_rows(c, x, number), :]
        total = cot.astype(F32) + (factor * scaled - value * (factor * factor * factor * inner))
        agrad[at, :] = total
        alow[c, at, :] = total.astype(BF16)
        low_copy(number).start()
        return gain_grad + jnp.sum(upstream * value * factor, 0, keepdims=True)

    gain_two_grad = lax.fori_loop(0, CHUNKS, second_norm, jnp.zeros((1, width), F32))
    small_own[pl.ds(1, 1), :] = gain_two_grad
    for k in range(deep):
        alx_copy(c, k, 0).start()

    def attend_back(tree):
        back = jnp.zeros((rows, mine), F32)
        for k in range(deep):
            back = back + mm(alow[tree, :, pl.ds(k * shard, shard)], wout[k], NT)
        back = back.astype(BF16)
        cosine, sine = tables[0, tree], tables[1, tree]
        key_grad = jnp.zeros((length, HEAD_SIZE), F32)
        value_grad = jnp.zeros((length, HEAD_SIZE), F32)
        for head in range(heads):
            lanes = pl.ds(head * HEAD_SIZE, HEAD_SIZE)
            back_head = back[:, head * HEAD_SIZE : (head + 1) * HEAD_SIZE]
            prob = probs[tree, head]
            value_grad = value_grad + mm(prob, back_head, TN)
            prob = prob.astype(F32)
            share = prob * mm(back_head, values[tree], NT)
            score = (share - prob * jnp.sum(share, -1, keepdims=True)).astype(BF16)
            query_grad = mm(score, keys[tree]) * inv_root
            qlow[tree, :, lanes] = turn(query_grad, cosine, -sine).astype(BF16)
            key_grad = key_grad + mm(score, queries[tree, head], TN)
        return jnp.concatenate([key_grad * inv_root, value_grad], 1)

    for number in range(CHUNKS):
        at = alow.at[1 - c, pl.ds(number * step, step)]
        remote(at, at, low_sem, number, me.core_peer()).wait_recv()
    kv_out[...] = attend_back(1 - c).astype(BF16)
    kvg_copy = remote(kv_out, kv_in, kvg_sem, 0, me.core_peer())
    kvg_copy.start()
    kv_own[...] = attend_back(c)

    def of_side(ref, side):
        low, high = ref[pl.ds(0, rows), :], ref[pl.ds(rows, rows), :]
        return jnp.where(side == 0, low, high).astype(F32)

    kvg_copy.wait_recv()
    kvx_out[...] = (of_side(kv_own, 1 - x) + of_side(kv_in, 1 - x)).astype(BF16)
    kvx_copy = remote(kvx_out, kvx_in, kvg_sem, 1, me.x_peer())
    kvx_copy.start()
    qx_copy = remote(qlow, qlow_x, qx_sem, 0, me.x_peer())
    qx_copy.start()
    advance(2, [2])

    def one_tile(tree, at):
        return [mm(qlow[tree, at, :], wqkv[k, :, pl.ds(0, mine)], NT) for k in range(deep)]

    mo.core_sent()

    def one_copy(number):
        at = rows_at(number, step)
        return remote(core_out.at[at], two_core_in.at[at], one_core_sem, number, me.core_peer())

    def one_outward(number, carry):
        at = rows_at(number, step)
        for k, piece in enumerate(one_tile(1 - c, at)):
            core_out[at, pl.ds(k * shard, shard)] = piece.astype(BF16)
        one_copy(number).start()
        return carry

    lax.fori_loop(0, CHUNKS, one_outward, 0)
    for k in range(deep):
        alx_copy(c, k, 0).wait_recv()
        alx_copy(c, k, 1).start()
    let_go(1)
    kvx_copy.wait_recv()
    own_kv = of_side(kv_own, x) + of_side(kv_in, x) + kvx_in[...].astype(F32)
    kvlow[:, pl.ds(0, HEAD_SIZE)] = turn(
        own_kv[:, :HEAD_SIZE], tables[0, c], -tables[1, c]
    ).astype(BF16)
    kvlow[:, pl.ds(HEAD_SIZE, HEAD_SIZE)] = own_kv[:, HEAD_SIZE:].astype(BF16)
    kvl_copy = remote(kvlow, kvlow_x, kvg_sem, 2, me.x_peer())
    kvl_copy.start()

    two.y_sent()

    def one_y(number):
        at = rows_at(number, step)
        return remote(y_out.at[at], two_x_in.at[at], one_y_sem, number, me.y_peer())

    def one_inward(number, carry):
        at = rows_at(number, step)
        one_copy(number).wait_recv()
        for k, piece in enumerate(one_tile(c, at)):
            lanes = pl.ds(k * shard, shard)
            piece = piece + mm(kvlow[at, :], wqkv[k, :, pl.ds(mine, 2 * HEAD_SIZE)], NT)
            y_out[at, lanes] = (piece + two_core_in[at, lanes].astype(F32)).astype(BF16)
        one_y(number).start()
        return carry

    lax.fori_loop(0, CHUNKS, one_inward, 0)

    mo.across()
    mo.inward()
    for part in range(groups):
        take.drain(part)
    spare = mats.at[0]
    late = [
        load(tokens_in.at[0], spare.at[pl.ds(0, rows)], 0),
        load(tokens_in.at[1], spare.at[pl.ds(rows, rows)], 1),
    ]
    for copy in late:
        copy.start()

    def chosen_half(value):
        return jnp.where(x == 0, value[:half], value[2 * HEAD_SIZE - half :])

    def keep_own(buffer_own, buffer_stage, k, lanes, value):
        @pl.when(k == z)
        def _():
            buffer_own[0, 0, :, lanes] = value.astype(BF16)

        @pl.when(k != z)
        def _():
            buffer_stage[0, fold.place(k), 0, :, lanes] = value.astype(BF16)

    def heads_of(array, tree):
        return jnp.concatenate([array[tree, head] for head in range(heads)], 1)

    fold_o = Fold(me, 1, (own_o, stage_o, land_o), (fold_send_o, fold_recv_o, None), 64, False)
    fold_q = Fold(me, 1, (own_q, stage_q, land_q), (fold_send_q, fold_recv_q, None), 64, False)
    for k in range(deep):
        alx_copy(1 - c, k, 1).wait_recv()
    remote(context, ctx_x, ctx_sem, 0, me.x_peer()).wait_recv()

    def output_grad(k, carry):
        value = jnp.zeros((2 * HEAD_SIZE, mine), F32)
        for tree in range(trees):
            value = value + mm(alow[tree, :, half_lanes(k, x)], heads_of(context, tree), TN)
            value = value + mm(alx[tree, k], heads_of(ctx_x, tree), TN)
        keep_own(own_o, stage_o, k, pl.ds(0, mine), chosen_half(value))
        return carry

    lax.fori_loop(0, deep, output_grad, 0)
    fold_o.begin(0, 0)
    advance(3, [0])

    for copy in late:
        copy.wait()
    for tree in range(trees):

        def norm_again(number, carry):
            at = rows_at(number, step)
            norm_rows(
                spare.at[pl.ds(tree * rows, rows)], mats.at[1, pl.ds(tree * rows, rows)], at
            )
            return carry

        lax.fori_loop(0, CHUNKS, norm_again, 0)

    def hid_one(tree, k):
        return mats[1, rows_at(tree, rows), half_lanes(k, x)]

    for k in range(deep):
        hidx_copy(1 - c, k, 1).wait_recv()
    qx_copy.wait_recv()

    def query_grad(k, carry):
        value = jnp.zeros((2 * HEAD_SIZE, mine), F32)
        for tree in range(trees):
            value = value + mm(hid_one(tree, k), qlow[tree], TN)
            value = value + mm(hidx[tree, k], qlow_x[tree], TN)
        keep_own(own_q, stage_q, k, pl.ds(0, mine), chosen_half(value))
        return carry

    lax.fori_loop(0, deep, query_grad, 0)

    kvl_copy.wait_recv()

    def kv_weight_grad(k, carry):
        value = mm(hid_one(c, k), kvlow[...], TN) + mm(hidx[c, k], kvlow_x[...], TN)
        value = chosen_half(value)
        low, high = value[:, :HEAD_SIZE], value[:, HEAD_SIZE:]
        dkv_out[0, k] = jnp.where(c == 0, high, low).astype(BF16)
        dkv_out[1, k] = jnp.where(c == 0, low, high).astype(BF16)
        return carry

    lax.fori_loop(0, deep, kv_weight_grad, 0)
    dkv_copy = remote(dkv_out.at[0], dkv_in, kvg_sem, 3, me.core_peer())
    dkv_copy.start()
    dkv_copy.wait_recv()

    def kv_weight_sum(k, carry):
        value = dkv_out[1, k].astype(F32) + dkv_in[k].astype(F32)
        keep_own(own_q, stage_q, k, pl.ds(mine, HEAD_SIZE), value)
        return carry

    lax.fori_loop(0, deep, kv_weight_sum, 0)
    fold_q.begin(0, 0)

    advance(3, [1])
    let_go(2)
    finish_group(0, True)
    finish_group(1, True)
    finish_group(1, False)
    finish_group(2, False)

    def out_copies(buffer, target, first, peer_sems, number):
        at = rows_at(number, step)
        here = pltpu.make_async_copy(buffer.at[at], target.at[c, at], out_sem.at[first + number])
        there = remote(buffer.at[at], target.at[c, at], peer_sems, number, me.core_peer())
        return here, there

    def first_norm_back(number, gain_grad):
        at = rows_at(number, step)
        one_y(number).wait_recv()
        upstream = y_out[at, :].astype(F32) + two_x_in[at, :].astype(F32)
        first = pl.multiple_of(c * rows + number * step, step)
        value = mats[0, pl.ds(first, step), :].astype(F32)
        factor = lax.rsqrt(jnp.mean(value * value, -1, keepdims=True) + EPS)
        scaled = upstream * gain_one
        inner = jnp.mean(scaled * value, -1, keepdims=True)
        agrad[at, :] = agrad[at, :] + (
            factor * scaled - value * (factor * factor * factor * inner)
        )
        for copy in out_copies(agrad, d_tokens, CHUNKS, token_sem, number):
            copy.start()
        return gain_grad + jnp.sum(upstream * value * factor, 0, keepdims=True)

    gain_one_grad = lax.fori_loop(0, CHUNKS, first_norm_back, jnp.zeros((1, width), F32))
    small_own[pl.ds(0, 1), :] = gain_one_grad
    spot = x * 2 + c

    def spread(k):
        there = (spot + k) % 4
        device = (z, there // 2, 2 * y + there % 2)
        return remote(small_own, small_in.at[spot], small_in_sem, k - 1, device)

    for k in range(1, 4):
        spread(k).start()
    small_in[spot] = small_own[...]
    advance(3, [2])
    mo.pass_on(0, CHUNKS)
    fold_o.advance(0, 0)
    let_go(3)
    finish_group(2, True)

    two.x_sent()

    def mix_out(number, carry):
        at = rows_at(number, step)
        x_out[at, :] = (after[at, :] + mo.total(number)).astype(BF16)
        for copy in out_copies(x_out, mixed, 0, mixed_sem, number):
            copy.start()
        return carry

    lax.fori_loop(0, CHUNKS, mix_out, 0)
    fold_q.advance(0, 0)
    for k in range(1, 4):
        source = (spot + 4 - k) % 4
        device = (z, source // 2, 2 * y + source % 2)
        remote(small_own, small_in.at[source], small_in_sem, k - 1, device).wait_recv()
        spread(k).wait_send()
    small_own[...] = (small_in[0] + small_in[1]) + (small_in[2] + small_in[3])

    def small_copy(k):
        there = (z + k) % deep
        return remote(
            small_own.at[:, shard_lanes(there)], small_z.at[z], small_z_sem, k - 1, me.at_z(there)
        )

    for k in range(1, deep):
        small_copy(k).start()
    small_z[z] = small_own[:, shard_lanes(z)]
    finish_group(3, False)
    finish_group(3, True)

    def write_o(at, value):
        d_output[at, :] = value

    fold_o.finish(0, 0, write_o)

    def write_q(at, value):
        d_query[at, :] = value[:, :mine]
        kv_last[at, :] = value[:, mine:]

    fold_q.finish(0, 0, write_q)

    share = half // 4

    def share_rows(t):
        return pl.ds(pl.multiple_of(t * share, 8), share)

    def last_copy(k):
        there = (me.t + k) % 4
        return remote(
            kv_last.at[share_rows(there)], kv_land.at[me.t], last_sem, k - 1, (z, x, there)
        )

    for k in range(1, 4):
        last_copy(k).start()
    kv_land[me.t] = kv_last[share_rows(me.t), :]
    for k in range(1, deep):
        source = (z + deep - k) % deep
        remote(
            small_own.at[:, shard_lanes(0)], small_z.at[source], small_z_sem, k - 1, me.at_z(source)
        ).wait_recv()
    total = small_z[0]
    for k in range(1, deep):
        total = total + small_z[k]
    d_small[...] = jnp.where(x == 0, total[:, :half], total[:, half:])
    for k in range(1, 4):
        source = (me.t + 4 - k) % 4
        remote(
            kv_last.at[pl.ds(0, share)], kv_land.at[source], last_sem, k - 1, (z, x, source)
        ).wait_recv()
    for head in range(KEY_VALUE_HEADS):
        lanes = pl.ds(head * HEAD_SIZE, HEAD_SIZE)
        d_key[:, lanes] = kv_land[2 * head]
        d_value[:, lanes] = kv_land[2 * head + 1]

    for number in range(CHUNKS):
        at = pl.ds(number * step, step)
        remote(x_out.at[at], mixed.at[1 - c, at], mixed_sem, number, me.core_peer()).wait_recv()
        remote(agrad.at[at], d_tokens.at[1 - c, at], token_sem, number, me.core_peer()).wait_recv()
        for buffer, target, first, peer_sems in (
            (x_out, mixed, 0, mixed_sem),
            (agrad, d_tokens, CHUNKS, token_sem),
        ):
            here, there = out_copies(buffer, target, first, peer_sems, number)
            here.wait()
            there.wait_send()
        one_y(number).wait_send()
        one_copy(number).wait_send()
        low_copy(number).wait_send()
    mo.x_sent()
    mo.y_sent()
    for m in range(KINDS):
        grad_out(groups - 1, m).wait()
    for k in range(1, 8):
        gate_copy(k).wait_send()
    for k in range(1, deep):
        small_copy(k).wait_send()
        small_out(k).wait_send()
    for k in range(1, 4):
        last_copy(k).wait_send()
    for k in range(deep):
        hidx_copy(c, k, 1).wait_send()
        alx_copy(c, k, 0).wait_send()
        alx_copy(c, k, 1).wait_send()
    for copy in (kvg_copy, kvx_copy, kvl_copy, dkv_copy, qx_copy, ctx_copy, cot_x, cot_on):
        copy.wait_send()
    for which in range(2):
        kv_copy(c, which, own_place, 0).wait_send()
        kv_copy(c, which, away_place, 1).wait_send()
    mix_copy(c, x, 0, me.x_peer()).wait_send()
    mix_copy(c, x, 1, me.core_peer()).wait_send()
    mix_copy(c, 1 - x, 2, me.core_peer()).wait_send()
    take_qkv.drain(0)
    take_out.drain(0)
    for group in range(1, groups):
        drain(group)
    fold_o.drain(0, 0)
    fold_q.drain(0, 0)


def sems(count):
    return pltpu.SemaphoreType.DMA((2, count))


def layer_call(
    seg_start,
    seg_parent,
    routes,
    small,
    tokens,
    cotangent,
    w_query,
    w_key,
    w_value,
    w_output,
    gate_t,
    up_t,
    w_down,
    deep,
):
    trees, rows, width = tokens.shape
    shard, mine = w_query.shape
    heads = mine // HEAD_SIZE
    length = rows * 2
    held, units = w_down.shape[0], w_down.shape[1]
    total_units = held * units
    experts = small.shape[0] - 8
    blocks = 2 * trees
    half = shard // 2
    count = blocks * rows
    sets = 3
    angle = HEAD_SIZE // 2
    frequency = ROPE_BASE ** (-2.0 * np.arange(angle, dtype=np.float32) / np.float32(HEAD_SIZE))
    frequency = np.tile(np.concatenate([frequency] * 2)[None], (8, 1)).astype(np.float32)
    vmem = pl.BlockSpec(memory_space=pltpu.VMEM)
    smem = pl.BlockSpec(memory_space=pltpu.SMEM)
    hbm = pl.BlockSpec(memory_space=pl.ANY)

    def plain(*shape):
        return pltpu.VMEM(shape, BF16)

    def wide(*shape):
        return pltpu.VMEM(shape, F32)

    def out(*shape, dtype=F32):
        return jax.ShapeDtypeStruct(shape, dtype)

    last = deep - 1
    return pl.pallas_call(
        layer_kernel,
        out_shape=(
            out(trees, rows, width, dtype=BF16),
            out(trees, rows, width),
            out(total_units, shard),
            out(total_units, shard),
            out(total_units, shard),
            out(half, mine),
            out(half, mine),
            out(half // 4, KEY_VALUE_HEADS * HEAD_SIZE),
            out(half // 4, KEY_VALUE_HEADS * HEAD_SIZE),
            out(small.shape[0], half),
        ),
        in_specs=[smem, smem, vmem, vmem] + [hbm] * 10,
        out_specs=[hbm] * 5 + [vmem] * 5,
        scratch_shapes=[
            plain(KINDS, total_units, width),
            plain(KINDS, total_units, count),
            plain(count, width),
            plain(count, width),
            plain(deep, shard, mine + 2 * HEAD_SIZE),
            plain(deep, mine, shard),
            plain(deep, small.shape[0], shard),
            plain(trees, heads, rows, HEAD_SIZE),
            plain(trees, length, HEAD_SIZE),
            plain(trees, length, HEAD_SIZE),
            plain(trees, heads, rows, length),
            plain(trees, heads, rows, HEAD_SIZE),
            wide(2, trees, rows, HEAD_SIZE),
            wide(rows, width),
            wide(blocks, experts, rows),
            wide(held, count),
            wide(blocks, 8, rows),
            wide(8, 8, rows),
            plain(2 * rows, width),
            plain(rows, width),
            wide(rows, width),
            plain(rows, width),
            plain(2 * rows, width),
            plain(rows, width),
            plain(rows, width),
            plain(2 * rows, width),
            plain(rows, width),
            plain(rows, width),
            wide(rows, width),
            plain(trees, rows, width),
            plain(trees, rows, mine),
            plain(length, 2 * HEAD_SIZE),
            plain(length, 2 * HEAD_SIZE),
            wide(length, 2 * HEAD_SIZE),
            plain(rows, 2 * HEAD_SIZE),
            plain(rows, 2 * HEAD_SIZE),
            plain(rows, 2 * HEAD_SIZE),
            plain(rows, 2 * HEAD_SIZE),
            plain(trees, rows, mine),
            plain(trees, deep, rows, 2 * HEAD_SIZE),
            plain(trees, deep, rows, 2 * HEAD_SIZE),
            plain(trees, heads, rows, HEAD_SIZE),
            plain(2, deep, half, HEAD_SIZE),
            plain(deep, half, HEAD_SIZE),
            plain(held, KINDS, units, shard),
            plain(sets, last, KINDS, units, shard),
            plain(sets, 5, KINDS, units, shard),
            wide(KINDS, units, shard),
            plain(1, 1, half, mine),
            plain(1, last, 1, half, mine),
            plain(1, deep, 1, half, mine),
            plain(1, 1, half, mine + HEAD_SIZE),
            plain(1, last, 1, half, mine + HEAD_SIZE),
            plain(1, deep, 1, half, mine + HEAD_SIZE),
            wide(small.shape[0], width),
            wide(4, small.shape[0], width),
            wide(deep, small.shape[0], shard),
            wide(half, HEAD_SIZE),
            wide(4, half // 4, HEAD_SIZE),
            pltpu.SemaphoreType.DMA((11,)),
            sems(last),
            sems(deep),
            sems(deep),
            sems(2 * deep),
            sems(deep),
            sems(deep),
            sems(2 * deep),
            sems(held * deep),
            sems(held * deep),
            sems(2 * trees),
            sems(2),
            sems(CHUNKS),
            sems(CHUNKS),
            sems(CHUNKS),
            sems(CHUNKS),
            sems(CHUNKS),
            sems(3),
            sems(7),
            sems(2 * rows // TILE),
            sems(CHUNKS),
            sems(CHUNKS),
            sems(2 * rows // TILE),
            sems(CHUNKS),
            sems(CHUNKS),
            sems(CHUNKS),
            sems(CHUNKS),
            sems(CHUNKS),
            sems(4),
            sems(1),
            sems(2 * deep),
            sems(2 * deep),
            sems(1),
            pltpu.SemaphoreType.DMA((sets * 3 * KINDS,)),
            pltpu.SemaphoreType.DMA((sets * 5 * KINDS,)),
            pltpu.SemaphoreType.REGULAR((sets * 3 * KINDS,)),
            pltpu.SemaphoreType.DMA((3,)),
            pltpu.SemaphoreType.DMA((4,)),
            pltpu.SemaphoreType.DMA((3,)),
            pltpu.SemaphoreType.DMA((4,)),
            pltpu.SemaphoreType.DMA((2 * CHUNKS,)),
            sems(CHUNKS),
            sems(CHUNKS),
            pltpu.SemaphoreType.DMA((KINDS,)),
            sems(3),
            sems(last),
            sems(3),
        ],
        compiler_params=pltpu.CompilerParams(
            collective_id=0, has_side_effects=True, vmem_limit_bytes=64 * 2**20
        ),
        name="layer",
    )(
        seg_start,
        seg_parent,
        jnp.asarray(frequency),
        routes,
        small,
        tokens,
        cotangent,
        w_query,
        w_key,
        w_value,
        w_output,
        gate_t.reshape(total_units, -1),
        up_t.reshape(total_units, -1),
        w_down.reshape(total_units, -1),
    )


def plane_shards(
    tokens,
    cotangent,
    seg_start,
    seg_parent,
    routes,
    attn_gain,
    w_query,
    w_key,
    w_value,
    w_output,
    moe_gain,
    w_router,
    w_gate,
    w_up,
    w_down,
):
    width = tokens.shape[2]
    deep = lax.axis_size("dp")
    held, quarter = w_gate.shape[0], w_gate.shape[2]
    small = jnp.concatenate(
        [attn_gain[None], moe_gain[None], jnp.zeros((6, attn_gain.shape[0]), BF16), w_router.T], 0
    )
    made = layer_call(
        seg_start,
        seg_parent,
        jnp.swapaxes(routes, 1, 2),
        small,
        tokens,
        cotangent,
        w_query,
        w_key,
        w_value,
        w_output,
        jnp.swapaxes(w_gate, 1, 2),
        jnp.swapaxes(w_up, 1, 2),
        w_down,
        deep,
    )
    placed = place_call(made[:-1])
    mixed, d_tokens, d_gate, d_up, d_down, d_query, d_output, d_key, d_value = placed
    d_small = made[-1]

    def experts(array):
        return array.reshape(held, quarter, width // deep)

    return (
        mixed,
        d_tokens,
        d_small[0],
        d_query,
        d_key,
        d_value,
        d_output.T,
        d_small[1],
        d_small[8:].T,
        jnp.swapaxes(experts(d_gate), 1, 2),
        jnp.swapaxes(experts(d_up), 1, 2),
        experts(d_down),
    )


def shards(*arrays):
    axes = tuple(lax.axis_size(name) for name in ("dp", "expert", "tensor"))
    if axes == (4, 2, 4) and arrays[0].shape[0] == 2:
        return plane_shards(*arrays)
    return general_shards(*arrays)


def solution(mesh):
    placed = (
        P("dp", "expert", None),
        P("dp", "expert", None),
        P("dp", None),
        P("dp", None),
        P("dp", "expert", None),
        P("dp"),
        P("dp", "tensor"),
        P("dp", None),
        P("dp", None),
        P("tensor", "dp"),
        P("dp"),
        P("dp", None),
        P("expert", "dp", "tensor"),
        P("expert", "dp", "tensor"),
        P("expert", "tensor", "dp"),
    )
    return jax.shard_map(
        shards,
        mesh=mesh,
        in_specs=placed,
        out_specs=(
            P("dp", "expert", None),
            P("dp", "expert", None),
            P(("dp", "expert")),
            P(("dp", "expert"), "tensor"),
            P(("dp", "expert", "tensor"), None),
            P(("dp", "expert", "tensor"), None),
            P("tensor", ("dp", "expert")),
            P(("dp", "expert")),
            P(("dp", "expert"), None),
            P("expert", "dp", "tensor"),
            P("expert", "dp", "tensor"),
            P("expert", "tensor", "dp"),
        ),
        check_vma=False,
    )
```

```python
import functools
import math

import jax
import jax.numpy as jnp
import numpy as np
from jax import lax
from jax.experimental import pallas as pl
from jax.experimental.pallas import tpu as pltpu
from jax.sharding import PartitionSpec as P

QUERY_HEADS = 12
KEY_VALUE_HEADS = 2
HEAD_SIZE = 128
GROUP = QUERY_HEADS // KEY_VALUE_HEADS
EPS = 1e-05
ROPE_BASE = 10000.0
NEG = -1e30
F32 = jnp.float32
BF16 = jnp.bfloat16


def dot(left, right, dims):
    return lax.dot_general(left, right, (dims, ((), ())), preferred_element_type=F32)


def norm_factor(rows):
    return lax.rsqrt(jnp.mean(rows * rows, -1, keepdims=True) + EPS)


def norm_back(rows, factor, gain, upstream):
    scaled = upstream * gain
    gain_grad = jnp.sum(upstream * rows * factor, 0)
    inner = jnp.mean(scaled * rows, -1, keepdims=True)
    return factor * scaled - rows * (factor * factor * factor * inner), gain_grad


def layout(starts, parents, places, length):
    labels = jnp.arange(starts.shape[1], dtype=jnp.int32)

    def pick(table, at):
        hot = at[:, :, None] == labels[None, None, :]
        return jnp.sum(jnp.where(hot, table[:, None, :], 0), 2, dtype=jnp.int32)

    segment = jnp.sum((starts[:, None, :] <= places[None, :, None]).astype(jnp.int32), 2) - 1
    above = pick(parents, segment)
    further = pick(parents, above)
    ends = jnp.concatenate(
        [starts[:, 1:], jnp.full((starts.shape[0], 1), length, jnp.int32)], 1
    )
    lengths = ends - starts
    depths = (
        places[None, :]
        - pick(starts, segment)
        + jnp.where(segment != 0, pick(lengths, above), 0)
        + jnp.where(above != 0, pick(lengths, further), 0)
    )
    return segment, above, further, depths


def angles(depths):
    half = HEAD_SIZE // 2
    frequency = ROPE_BASE ** (-2.0 * jnp.arange(half, dtype=F32) / HEAD_SIZE)
    turning = depths.astype(F32)[..., None] * frequency
    return jnp.cos(turning), jnp.sin(turning)


def rotate(heads, cosine, sine):
    half = HEAD_SIZE // 2
    front, back = heads[..., :half], heads[..., half:]
    return jnp.concatenate([front * cosine - back * sine, back * cosine + front * sine], -1)


def general_shards(
    tokens,
    cotangent,
    seg_start,
    seg_parent,
    routes,
    attn_gain,
    w_query,
    w_key,
    w_value,
    w_output,
    moe_gain,
    w_router,
    w_gate,
    w_up,
    w_down,
):
    trees, rows, width = tokens.shape
    expert_count = lax.axis_size("expert")
    tensor_count = lax.axis_size("tensor")
    tensor_at = lax.axis_index("tensor")
    expert_at = lax.axis_index("expert")
    length = rows * expert_count
    heads = w_query.shape[1] // HEAD_SIZE
    kv_head = tensor_at * heads // GROUP
    inv_root = HEAD_SIZE ** (-0.5)
    own_experts = w_gate.shape[0]
    quarter = w_gate.shape[2]
    all_experts = w_router.shape[1]

    def over_dp(array, axis):
        return lax.all_gather(array, "dp", axis=axis, tiled=True)

    w_query = over_dp(w_query, 0)
    w_output = over_dp(w_output, 1)
    gate_t = over_dp(jnp.swapaxes(w_gate, 1, 2), 2)
    up_t = over_dp(jnp.swapaxes(w_up, 1, 2), 2)
    down = over_dp(w_down, 2)
    small = over_dp(
        jnp.concatenate(
            [
                lax.dynamic_slice_in_dim(w_key, kv_head * HEAD_SIZE, HEAD_SIZE, 1),
                lax.dynamic_slice_in_dim(w_value, kv_head * HEAD_SIZE, HEAD_SIZE, 1),
                w_router,
                attn_gain[:, None],
                moe_gain[:, None],
            ],
            1,
        ),
        0,
    )
    w_kv = small[:, : 2 * HEAD_SIZE]
    w_router = small[:, 2 * HEAD_SIZE : 2 * HEAD_SIZE + all_experts]
    attn_gain = small[:, -2].astype(F32)
    moe_gain = small[:, -1].astype(F32)

    all_places = jnp.arange(length, dtype=jnp.int32)
    places = expert_at * rows + jnp.arange(rows, dtype=jnp.int32)
    segment, above, further, depths = layout(seg_start, seg_parent, places, length)
    key_segment = layout(seg_start, seg_parent, all_places, length)[0]
    cosine, sine = angles(depths)
    of_key = key_segment[:, None, :]
    visible = (
        (of_key == segment[:, :, None])
        | (of_key == above[:, :, None])
        | (of_key == further[:, :, None])
    ) & (all_places[None, None, :] <= places[None, :, None])

    residual = tokens.astype(F32).reshape(trees * rows, width)
    factor_one = norm_factor(residual)
    hidden_one = (residual * factor_one * attn_gain).astype(BF16)
    query_pre = dot(hidden_one, w_query, ((1,), (0,))).reshape(trees, rows, heads, HEAD_SIZE)
    kv_pre = dot(hidden_one, w_kv, ((1,), (0,))).reshape(trees, rows, 2 * HEAD_SIZE)
    queries = rotate(query_pre, cosine[:, :, None, :], sine[:, :, None, :]).astype(BF16)
    own_keys = rotate(kv_pre[..., :HEAD_SIZE], cosine, sine).astype(BF16)
    own_kv = jnp.concatenate([own_keys, kv_pre[..., HEAD_SIZE:].astype(BF16)], -1)
    keys_values = lax.all_gather(own_kv, "expert", axis=1, tiled=True)
    keys, values = keys_values[..., :HEAD_SIZE], keys_values[..., HEAD_SIZE:]
    scores = jnp.einsum("bqhd,bkd->bhqk", queries, keys, preferred_element_type=F32) * inv_root
    scores = jnp.where(visible[:, None], scores, NEG)
    row_max = jnp.max(scores, -1, keepdims=True)
    exponent = jnp.exp(scores - row_max)
    probs = exponent / jnp.sum(exponent, -1, keepdims=True)
    probs_low = probs.astype(BF16)
    context = jnp.einsum("bhqk,bkd->bqhd", probs_low, values, preferred_element_type=F32)
    context_low = context.reshape(trees * rows, heads * HEAD_SIZE).astype(BF16)
    attn_out = dot(context_low, w_output, ((1,), (0,))).astype(BF16)
    after_attn = residual + lax.psum(attn_out, "tensor").astype(F32)

    factor_two = norm_factor(after_attn)
    hidden_two = (after_attn * factor_two * moe_gain).astype(BF16)
    logits = dot(hidden_two, w_router, ((1,), (0,)))
    chosen = jnp.any(
        routes.reshape(trees * rows, -1)[:, :, None]
        == jnp.arange(all_experts, dtype=jnp.int32)[None, None, :],
        1,
    )
    masked = jnp.where(chosen, logits, NEG)
    raised = jnp.where(chosen, jnp.exp(masked - jnp.max(masked, -1, keepdims=True)), 0.0)
    mixing = raised / jnp.sum(raised, -1, keepdims=True)

    def over_expert(array):
        full = lax.all_gather(
            array.reshape(trees, rows, array.shape[-1]), "expert", axis=1, tiled=True
        )
        return full.reshape(trees * length, array.shape[-1])

    every_hidden = over_expert(hidden_two)
    every_up = over_expert(cotangent)
    every_mix = lax.dynamic_slice_in_dim(
        over_expert(mixing), expert_at * own_experts, own_experts, 1
    )
    count = trees * length
    pre_gate = dot(every_hidden, gate_t.reshape(-1, width), ((1,), (1,)))
    pre_up = dot(every_hidden, up_t.reshape(-1, width), ((1,), (1,)))
    down_rows = down.reshape(-1, width)
    down_back = dot(every_up, down_rows, ((1,), (1,)))
    wide_mix = jnp.repeat(every_mix, quarter, axis=1)
    activated, pull = jax.vjp(jax.nn.gelu, pre_gate)
    hidden = activated * pre_up
    mixed_hidden = (hidden * wide_mix).astype(BF16)
    moe_part = dot(mixed_hidden, down_rows, ((1,), (0,))).astype(BF16)
    gate_part = jnp.sum((hidden * down_back).reshape(count, own_experts, quarter), -1)
    hidden_grad = wide_mix * down_back
    gate_pre = pull(hidden_grad * pre_up)[0].astype(BF16)
    up_pre = (hidden_grad * activated).astype(BF16)
    two_part = (
        dot(gate_pre, gate_t.reshape(-1, width), ((1,), (0,)))
        + dot(up_pre, up_t.reshape(-1, width), ((1,), (0,)))
    ).astype(BF16)
    d_down = dot(mixed_hidden, every_up, ((0,), (0,)))
    d_gate = dot(gate_pre, every_hidden, ((0,), (0,)))
    d_up = dot(up_pre, every_hidden, ((0,), (0,)))

    def to_owner(array):
        array = array.reshape(trees, length, array.shape[-1])
        part = lax.psum_scatter(array, "expert", scatter_dimension=1, tiled=True)
        return lax.psum(part, "tensor").reshape(trees * rows, -1)

    spread = jnp.arange(all_experts) // own_experts == expert_at
    gate_wide = jnp.where(
        spread[None, :], jnp.tile(gate_part, (1, all_experts // own_experts)), 0.0
    )
    two_grad = to_owner(two_part).astype(F32)
    mix_grad = to_owner(gate_wide)
    mixed_out = (after_attn + to_owner(moe_part).astype(F32)).astype(BF16)

    picked_grad = mixing * (mix_grad - jnp.sum(mixing * mix_grad, -1, keepdims=True))
    logit_grad = picked_grad.astype(BF16)
    two_grad = two_grad + dot(logit_grad, w_router, ((1,), (1,)))
    d_router = dot(hidden_two, logit_grad, ((0,), (0,)))
    norm_two, d_moe_gain = norm_back(after_attn, factor_two, moe_gain, two_grad)
    attn_grad = cotangent.astype(F32).reshape(trees * rows, width) + norm_two
    attn_low = attn_grad.astype(BF16)

    d_output = dot(context_low, attn_low, ((0,), (0,)))
    context_grad = (
        dot(attn_low, w_output, ((1,), (1,)))
        .astype(BF16)
        .reshape(trees, rows, heads, HEAD_SIZE)
    )
    prob_grad = jnp.einsum("bqhd,bkd->bhqk", context_grad, values, preferred_element_type=F32)
    score_grad = probs * (prob_grad - jnp.sum(probs * prob_grad, -1, keepdims=True))
    score_grad = score_grad.astype(BF16)
    query_grad = (
        jnp.einsum("bhqk,bkd->bqhd", score_grad, keys, preferred_element_type=F32) * inv_root
    )
    key_grad = (
        jnp.einsum("bhqk,bqhd->bkd", score_grad, queries, preferred_element_type=F32) * inv_root
    )
    value_grad = jnp.einsum("bhqk,bqhd->bkd", probs_low, context_grad, preferred_element_type=F32)
    kv_part = jnp.concatenate([key_grad, value_grad], -1).astype(BF16)
    kv_sum = lax.psum_scatter(kv_part, "expert", scatter_dimension=1, tiled=True)
    sharing = GROUP // heads
    own_rows = rows // sharing
    place = tensor_at % sharing
    kv_rows = kv_sum.reshape(trees, sharing, own_rows, 2 * HEAD_SIZE)
    mine = lax.dynamic_index_in_dim(kv_rows, place, 1, False).astype(F32)
    for step in range(1, sharing):
        order = [
            (at, at // sharing * sharing + (at + step) % sharing) for at in range(tensor_count)
        ]
        away = lax.dynamic_index_in_dim(kv_rows, (place + step) % sharing, 1, False)
        mine = mine + lax.ppermute(away, "tensor", order).astype(F32)

    def own(array):
        return lax.dynamic_slice_in_dim(array, place * own_rows, own_rows, 1)

    key_low = rotate(mine[..., :HEAD_SIZE], own(cosine), -own(sine)).astype(BF16)
    kv_low = jnp.concatenate([key_low, mine[..., HEAD_SIZE:].astype(BF16)], -1)
    kv_low = kv_low.reshape(trees * own_rows, 2 * HEAD_SIZE)
    hidden_own = own(hidden_one.reshape(trees, rows, width)).reshape(trees * own_rows, width)
    d_kv = dot(hidden_own, kv_low, ((0,), (0,)))
    kv_back = dot(kv_low, w_kv, ((1,), (1,))).reshape(trees, own_rows, width)
    query_low = rotate(query_grad, cosine[:, :, None, :], -sine[:, :, None, :])
    query_low = query_low.astype(BF16).reshape(trees * rows, heads * HEAD_SIZE)
    d_query = dot(hidden_one, query_low, ((0,), (0,)))
    one_part = dot(query_low, w_query, ((1,), (1,))).reshape(trees, rows, width)
    one_part = lax.dynamic_update_slice_in_dim(
        one_part, own(one_part) + kv_back, place * own_rows, 1
    ).reshape(trees * rows, width)
    one_grad = lax.psum(one_part.astype(BF16), "tensor").astype(F32)
    norm_one, d_attn_gain = norm_back(residual, factor_one, attn_gain, one_grad)
    d_tokens = (attn_grad + norm_one).reshape(trees, rows, width)

    def scatter_dp(array, axis):
        return lax.psum_scatter(array, "dp", scatter_dimension=axis, tiled=True)

    def scatter_expert(array, axis):
        return lax.psum_scatter(array, "expert", scatter_dimension=axis, tiled=True)

    def experts_home(array):
        return scatter_dp(array.astype(BF16), 1).astype(F32).reshape(own_experts, quarter, -1)

    d_gate, d_up, d_down = experts_home(d_gate), experts_home(d_up), experts_home(d_down)
    d_query = scatter_expert(scatter_dp(d_query.astype(BF16), 0), 0).astype(F32)
    d_output = scatter_expert(scatter_dp(d_output.astype(BF16), 1), 1).astype(F32)
    flat = jnp.concatenate([d_attn_gain[:, None], d_moe_gain[:, None], d_router], 1)
    flat = scatter_expert(scatter_dp(flat, 0), 0)
    of_head = (jnp.arange(KEY_VALUE_HEADS) == kv_head).astype(F32)[None, None, :, None]
    d_kv = scatter_expert(scatter_dp(d_kv, 0), 0).reshape(-1, 2, 1, HEAD_SIZE) * of_head
    d_kv = d_kv.reshape(-1, 2 * KEY_VALUE_HEADS * HEAD_SIZE)
    d_kv = lax.psum_scatter(d_kv, "tensor", scatter_dimension=0, tiled=True)
    return (
        mixed_out.reshape(trees, rows, width),
        d_tokens,
        flat[:, 0],
        d_query,
        d_kv[:, : KEY_VALUE_HEADS * HEAD_SIZE],
        d_kv[:, KEY_VALUE_HEADS * HEAD_SIZE :],
        d_output,
        flat[:, 1],
        flat[:, 2:],
        jnp.swapaxes(d_gate, 1, 2),
        jnp.swapaxes(d_up, 1, 2),
        d_down,
    )


MESH = pl.DeviceIdType.MESH
NT = (((1,), (1,)), ((), ()))
NN = (((1,), (0,)), ((), ()))
TN = (((0,), (0,)), ((), ()))
CHUNKS = 4
TILE = 128
KINDS = 3
ROOT_2_PI = math.sqrt(2.0 / math.pi)
CUBIC = 0.044715


def mm(left, right, dims=NN):
    return lax.dot_general(left, right, dims, preferred_element_type=F32)


def rows_at(number, size):
    return pl.ds(pl.multiple_of(number * size, size), size)


class Place:
    def __init__(self):
        self.z = lax.axis_index("dp")
        self.x = lax.axis_index("expert")
        self.t = lax.axis_index("tensor")
        self.y = self.t // 2
        self.c = self.t % 2

    def at_z(self, z):
        return (z, self.x, self.t)

    def x_peer(self):
        return (self.z, 1 - self.x, self.t)

    def y_peer(self):
        return (self.z, self.x, (self.t + 2) % 4)

    def core_peer(self):
        return (self.z, self.x, self.t + 1 - 2 * self.c)


def remote(src, dst, sems, at, device):
    return pltpu.make_async_remote_copy(
        src_ref=src,
        dst_ref=dst,
        send_sem=sems.at[0, at],
        recv_sem=sems.at[1, at],
        device_id=device,
        device_id_type=MESH,
    )


def signal(sem, device):
    pl.semaphore_signal(sem, inc=1, device_id=device, device_id_type=MESH)


def await_signal(sem):
    pl.semaphore_wait(sem, 1)


def greet(devices):
    barrier = pltpu.get_barrier_semaphore()
    for device in devices:
        pl.semaphore_signal(barrier, inc=1, device_id=device, device_id_type=MESH)
    pl.semaphore_wait(barrier, len(devices))


def tree_tables(starts, parents, tree, first, rows, length, frequency):
    count = starts.shape[1]
    place = first + lax.broadcasted_iota(jnp.int32, (rows, HEAD_SIZE), 0)
    start = [starts[tree, k] for k in range(count)]
    parent = [parents[tree, k] for k in range(count)]
    size = [(start[k + 1] if k + 1 < count else length) - start[k] for k in range(count)]

    def pick(table, at):
        total = jnp.zeros_like(at)
        for k in range(count):
            total = total + jnp.where(at == k, table[k], 0)
        return total

    def segment_of(at):
        total = jnp.zeros_like(at)
        for k in range(1, count):
            total = total + jnp.where(at >= start[k], 1, 0)
        return total

    segment = segment_of(place)
    above = pick(parent, segment)
    further = pick(parent, above)
    depth = (
        place
        - pick(start, segment)
        + jnp.where(segment != 0, pick(size, above), 0)
        + jnp.where(above != 0, pick(size, further), 0)
    )
    turning = depth.astype(F32) * frequency
    lane = lax.broadcasted_iota(jnp.int32, (rows, HEAD_SIZE), 1)
    cosine = jnp.cos(turning)
    sine = jnp.sin(turning)
    sine = jnp.where(lane < HEAD_SIZE // 2, -sine, sine)
    key_place = lax.broadcasted_iota(jnp.int32, (8, length), 1)
    key_segment = jnp.broadcast_to(segment_of(key_place)[:1], (rows, length))
    key_place = jnp.broadcast_to(key_place[:1], (rows, length))
    wide = length // HEAD_SIZE

    def widen(array):
        return jnp.concatenate([array] * wide, 1)

    visible = (
        (key_segment == widen(segment))
        | (key_segment == widen(above))
        | (key_segment == widen(further))
    ) & (key_place <= widen(place))
    return jnp.where(visible, 1.0, 0.0), cosine, sine


def turn(head, cosine, sine):
    return head * cosine + pltpu.roll(head, HEAD_SIZE // 2, 1) * sine


class Relay:
    def __init__(self, me, deep, piece, up_sems, dn_sems, side_sems=None):
        self.me, self.deep, self.piece = me, deep, piece
        self.up_sems, self.dn_sems, self.side_sems = up_sems, dn_sems, side_sems

    def up(self, source, part, hop):
        above = self.me.at_z(jnp.minimum(self.me.z + 1, self.deep - 1))
        at = self.piece(source, part, self.me.x)
        return remote(at, at, self.up_sems, part * self.deep + hop, above)

    def dn(self, source, part, hop):
        below = self.me.at_z(jnp.maximum(self.me.z - 1, 0))
        at = self.piece(source, part, self.me.x)
        return remote(at, at, self.dn_sems, part * self.deep + hop, below)

    def side(self, source, part, hop, x):
        at = self.piece(source, part, x)
        return remote(at, at, self.side_sems, part * 2 * self.deep + hop, self.me.x_peer())

    def begin(self, part, ends=None):
        z, last = self.me.z, self.deep - 1
        at_end = (z == 0) | (z == last)
        now = z >= 0 if ends is None else at_end if ends else jnp.logical_not(at_end)

        @pl.when((z < last) & now)
        def _():
            self.up(z, part, 0).start()

        @pl.when((z > 0) & now)
        def _():
            self.dn(z, part, 0).start()

    def pass_on(self, part, hop):
        z, deep = self.me.z, self.deep
        sides = self.side_sems is not None
        upward = (z - 1 - hop >= 0) & (z < deep - 1)
        downward = (z + 1 + hop < deep) & (z > 0)
        if sides:

            @pl.when(z - 1 - hop >= 0)
            def _():
                self.up(z - 1 - hop, part, hop).wait_recv()
                self.side(z - 1 - hop, part, hop, self.me.x).start()

            @pl.when(z + 1 + hop < deep)
            def _():
                self.dn(z + 1 + hop, part, hop).wait_recv()
                self.side(z + 1 + hop, part, deep + hop, self.me.x).start()

        @pl.when(upward)
        def _():
            if not sides:
                self.up(z - 1 - hop, part, hop).wait_recv()
            self.up(z - 1 - hop, part, hop + 1).start()

        @pl.when(downward)
        def _():
            if not sides:
                self.dn(z + 1 + hop, part, hop).wait_recv()
            self.dn(z + 1 + hop, part, hop + 1).start()

    def finish(self, part):
        z, deep = self.me.z, self.deep
        for hop in range(deep - 1):
            if self.side_sems is not None:

                @pl.when(z - 1 - hop >= 0)
                def _():
                    self.side(z - 1 - hop, part, hop, 1 - self.me.x).wait_recv()

                @pl.when(z + 1 + hop < deep)
                def _():
                    self.side(z + 1 + hop, part, deep + hop, 1 - self.me.x).wait_recv()

            else:

                @pl.when(z == deep - 1)
                def _():
                    self.up(z - 1 - hop, part, hop).wait_recv()

                @pl.when(z == 0)
                def _():
                    self.dn(z + 1 + hop, part, hop).wait_recv()

    def drain(self, part):
        z, deep = self.me.z, self.deep
        for hop in range(deep):

            @pl.when((z - hop >= 0) & (z < deep - 1))
            def _():
                self.up(z - hop, part, hop).wait_send()

            @pl.when((z + hop < deep) & (z > 0))
            def _():
                self.dn(z + hop, part, hop).wait_send()

        if self.side_sems is not None:
            for hop in range(deep - 1):

                @pl.when(z - 1 - hop >= 0)
                def _():
                    self.side(z - 1 - hop, part, hop, self.me.x).wait_send()

                @pl.when(z + 1 + hop < deep)
                def _():
                    self.side(z + 1 + hop, part, deep + hop, self.me.x).wait_send()


class PlaneSum:
    def __init__(self, me, rows, make, bufs, landing, sem_set, ahead=None):
        self.me, self.rows, self.make, self.ahead = me, rows, make, ahead
        self.core_out, self.x_out, self.acc, self.y_out = bufs
        self.core_in, self.x_in, self.y_in = landing
        self.core_sems, self.x_sems, self.y_sems = sem_set
        self.tiles = rows // TILE
        self.step = rows // CHUNKS
        self.per_tile = TILE // self.step

    def core_copy(self, number):
        at = rows_at(number, TILE)
        return remote(
            self.core_out.at[at], self.core_in.at[at], self.core_sems, number, self.me.core_peer()
        )

    def x_copy(self, number):
        at = rows_at(number, self.step)
        return remote(self.x_out.at[at], self.x_in.at[at], self.x_sems, number, self.me.x_peer())

    def y_copy(self, number):
        at = rows_at(number, self.step)
        return remote(self.y_out.at[at], self.y_in.at[at], self.y_sems, number, self.me.y_peer())

    def first(self, tree, x, number):
        return pl.multiple_of((tree * 2 + x) * self.rows + number * TILE, TILE)

    def tile(self, tree, x, number, buffer, at):
        value = self.make(self.first(tree, x, number))
        if self.ahead is not None:
            value = value + buffer[at, :].astype(F32)
        return value.astype(BF16)

    def prepare(self):
        me = self.me

        def other(number, carry):
            x = jnp.where(number < self.tiles, 1 - me.x, me.x)
            value = self.ahead(self.first(1 - me.c, x, number % self.tiles))
            self.core_out[rows_at(number, TILE), :] = value.astype(BF16)
            return carry

        def same(number, carry):
            at = rows_at(number, TILE)
            self.x_out[at, :] = self.ahead(self.first(me.c, 1 - me.x, number)).astype(BF16)
            self.acc[at, :] = self.ahead(self.first(me.c, me.x, number))
            return carry

        lax.fori_loop(0, 2 * self.tiles, other, 0)
        lax.fori_loop(0, self.tiles, same, 0)

    def outward(self, side):
        me = self.me
        x = me.x if side else 1 - me.x

        def one(number, carry):
            slot = side * self.tiles + number
            at = rows_at(slot, TILE)
            self.core_out[at, :] = self.tile(1 - me.c, x, number, self.core_out, at)
            self.core_copy(slot).start()
            return carry

        lax.fori_loop(0, self.tiles, one, 0)

    def across(self, first=0, last=None):
        me = self.me

        def one(number, carry):
            at = rows_at(number, TILE)
            value = self.tile(me.c, 1 - me.x, number, self.x_out, at).astype(F32)
            self.core_copy(number).wait_recv()
            self.x_out[at, :] = (value + self.core_in[at, :].astype(F32)).astype(BF16)
            for k in range(self.per_tile):
                self.x_copy(number * self.per_tile + k).start()
            return carry

        lax.fori_loop(first, self.tiles if last is None else last, one, 0)

    def inward(self):
        me = self.me

        def one(number, carry):
            at = rows_at(number, TILE)
            value = self.tile(me.c, me.x, number, self.acc, at).astype(F32)
            slot = self.tiles + number
            self.core_copy(slot).wait_recv()
            self.acc[at, :] = value + self.core_in[rows_at(slot, TILE), :].astype(F32)
            return carry

        lax.fori_loop(0, self.tiles, one, 0)

    def pass_on(self, first, last):
        def one(number, carry):
            at = rows_at(number, self.step)
            self.x_copy(number).wait_recv()
            self.y_out[at, :] = (self.acc[at, :] + self.x_in[at, :].astype(F32)).astype(BF16)
            self.y_copy(number).start()
            return carry

        lax.fori_loop(first, last, one, 0)

    def total(self, number):
        at = rows_at(number, self.step)
        self.y_copy(number).wait_recv()
        return self.y_out[at, :].astype(F32) + self.y_in[at, :].astype(F32)

    def core_sent(self):
        for number in range(2 * self.tiles):
            self.core_copy(number).wait_send()

    def x_sent(self):
        for number in range(CHUNKS):
            self.x_copy(number).wait_send()

    def y_sent(self):
        for number in range(CHUNKS):
            self.y_copy(number).wait_send()


class Fold:
    def __init__(self, me, groups, bufs, sem_set, tile, merge):
        self.me, self.groups, self.tile, self.merge = me, groups, tile, merge
        self.own, self.stage, self.land = bufs
        self.send_sems, self.recv_sems, self.free = sem_set
        self.sets, self.count, self.rows = self.stage.shape[0], self.own.shape[1], self.own.shape[2]
        self.slots = self.land.shape[1]
        z = me.z
        self.end = jnp.where(z < 2, 0, 3)
        self.mid = jnp.where(z < 2, 1, 2)
        self.far_mid = 3 - self.mid
        self.is_end = z == self.end
        self.is_mid = z == self.mid
        self.targets = (3 - self.end, self.far_mid, jnp.where(self.is_end, self.mid, self.end))

    def place(self, target):
        return (target + 3 - self.me.z) % 4

    def free_at(self, group, which, m):
        return self.free.at[((group % self.sets) * 3 + which) * self.count + m]

    def copy(self, group, which, m, slot=None):
        at = group % self.sets
        target = self.targets[which]
        from_mid = (4 if self.merge else 3, 3, 2)[which]
        there = jnp.where(self.is_end, which, from_mid) if slot is None else slot
        direct = self.far_mid if which == 0 and self.merge else target
        return pltpu.make_async_remote_copy(
            src_ref=self.stage.at[at, self.place(target), m],
            dst_ref=self.land.at[at, there, m],
            send_sem=self.send_sems.at[(at * 3 + which) * self.count + m],
            recv_sem=self.recv_sems.at[(at * self.slots + there) * self.count + m],
            device_id=self.me.at_z(jnp.where(self.is_end, self.mid, direct)),
            device_id_type=MESH,
        )

    def send(self, group, which, m):
        if group >= self.sets:
            await_signal(self.free_at(group, which, m))
        self.copy(group, which, m).start()

    def used(self, group, which, m, sender):
        if group + self.sets < self.groups:
            signal(self.free_at(group, which, m), self.me.at_z(sender))

    def add(self, group, which, m, slot):
        at = group % self.sets
        self.copy(group, which, m, slot).wait_recv()
        term = self.stage.at[at, self.place(self.targets[which]), m]
        landed = self.land.at[at, slot, m]

        def step(number, carry):
            rows = rows_at(number, self.tile)
            total = term[rows, :].astype(F32) + landed[rows, :].astype(F32)
            term[rows, :] = total.astype(BF16)
            return carry

        lax.fori_loop(0, self.rows // self.tile, step, 0)

    def begin(self, group, m):
        @pl.when(self.is_end)
        def _():
            for which in range(3):
                self.send(group, which, m)

        if not self.merge:

            @pl.when(self.is_mid)
            def _():
                self.send(group, 2, m)

    def advance(self, group, m):
        @pl.when(self.is_mid)
        def _():
            for which in (0, 1):
                self.add(group, which, m, which)
                self.used(group, which, m, self.end)
                self.send(group, which, m)

    def let_go(self, group, m):
        @pl.when(self.is_mid)
        def _():
            self.add(group, 2, m, 4)
            self.used(group, 0, m, self.far_mid)
            self.send(group, 2, m)

    def finish(self, group, m, write):
        at = group % self.sets
        own = self.own.at[group, m]
        near, far = self.land.at[at, 2, m], self.land.at[at, 3, m]
        self.copy(group, 2, m, 2).wait_recv()

        def run(pieces):
            def step(number, carry):
                rows = rows_at(number, self.tile)
                total = own[rows, :].astype(F32)
                for piece in pieces:
                    total = total + piece[rows, :].astype(F32)
                write(rows, total)
                return carry

            lax.fori_loop(0, self.rows // self.tile, step, 0)

        if self.merge:

            @pl.when(self.is_end)
            def _():
                run([near])
                self.used(group, 2, m, self.mid)

            @pl.when(self.is_mid)
            def _():
                self.copy(group, 1, m, 3).wait_recv()
                run([near, far])
                self.used(group, 2, m, self.end)
                self.used(group, 1, m, self.far_mid)

        else:
            self.copy(group, 1, m, 3).wait_recv()
            run([near, far])

    def drain(self, group, m):
        for which in range(3):
            self.copy(group, which, m).wait_send()


def place_kernel(*refs):
    count = (len(refs) - 2) // 3
    sources, targets, middles = refs[:count], refs[count : 2 * count], refs[2 * count : -2]
    loads, stores = [], []
    for source, target, middle in zip(sources, targets, middles):
        size = source.shape[0] // 2
        for part in range(2):
            at = pl.ds(part * size, size)
            number = len(loads)
            loads.append(pltpu.make_async_copy(source.at[at], middle.at[at], refs[-2].at[number]))
            stores.append(pltpu.make_async_copy(middle.at[at], target.at[at], refs[-1].at[number]))
    for load in loads:
        load.start()
    for load, store in zip(loads, stores):
        load.wait()
        store.start()
    for store in stores:
        store.wait()


def place_call(arrays):
    hbm = pl.BlockSpec(memory_space=pl.ANY)
    done = pltpu.SemaphoreType.DMA((2 * len(arrays),))
    return pl.pallas_call(
        place_kernel,
        out_shape=tuple(jax.ShapeDtypeStruct(a.shape, a.dtype) for a in arrays),
        in_specs=[hbm] * len(arrays),
        out_specs=[hbm] * len(arrays),
        scratch_shapes=[pltpu.VMEM(a.shape, a.dtype) for a in arrays] + [done, done],
        compiler_params=pltpu.CompilerParams(vmem_limit_bytes=60 * 2**20),
        name="place",
    )(*arrays)


def layer_kernel(
    starts,
    parents,
    frequency,
    routes,
    gain_one_in,
    gain_two_in,
    router_in,
    tokens_in,
    cotangent_in,
    w_query,
    w_key,
    w_value,
    w_output,
    gate_in,
    up_in,
    down_in,
    mixed,
    d_tokens,
    d_gate,
    d_up,
    d_down,
    d_query,
    d_output,
    d_key,
    d_value,
    d_small,
    mats,
    acts,
    hid,
    ups,
    wqkv,
    wout,
    smalls,
    queries,
    keys,
    values,
    probs,
    context,
    tables,
    after,
    mixes,
    gates,
    gates_out,
    gates_in,
    core_out,
    x_out,
    acc,
    y_out,
    two_core_in,
    two_x_in,
    two_y_in,
    mo_core_in,
    mo_x_in,
    mo_y_in,
    agrad,
    alow,
    qlow,
    kv_out,
    kv_in,
    kv_own,
    kvx_out,
    kvx_in,
    kvlow,
    kvlow_x,
    qlow_x,
    hidx,
    alx,
    ctx_x,
    dkv_out,
    dkv_in,
    own,
    stage,
    land,
    bounce,
    own_o,
    stage_o,
    land_o,
    own_q,
    stage_q,
    land_q,
    small_own,
    small_in,
    small_z,
    kv_last,
    kv_land,
    load_sem,
    small_sem,
    up1_sem,
    dn1_sem,
    side1_sem,
    up2_sem,
    dn2_sem,
    side2_sem,
    trade_sem,
    up3_sem,
    dn3_sem,
    kv_sem,
    cot_sem,
    core_sem,
    y_sem,
    hx_sem,
    hc_sem,
    hf_sem,
    mix_sem,
    gate_sem,
    two_core_sem,
    two_x_sem,
    two_y_sem,
    mo_core_sem,
    mo_x_sem,
    mo_y_sem,
    one_core_sem,
    one_y_sem,
    low_sem,
    kvg_sem,
    qx_sem,
    hidx_sem,
    alx_sem,
    ctx_sem,
    fold_send,
    fold_recv,
    fold_free,
    fold_send_o,
    fold_recv_o,
    fold_send_q,
    fold_recv_q,
    out_sem,
    mixed_sem,
    token_sem,
    grad_sem,
    small_in_sem,
    small_z_sem,
    last_sem,
):
    me = Place()
    z, x, y, c = me.z, me.x, me.y, me.c
    deep, shard = wqkv.shape[0], wqkv.shape[1]
    trees, heads, rows, length = probs.shape
    width = hid.shape[1]
    groups = gates.shape[0]
    units = mats.shape[1] // groups
    mine = heads * HEAD_SIZE
    half = shard // 2
    step = rows // CHUNKS
    inv_root = HEAD_SIZE ** (-0.5)
    own_block = c * 2 + x
    is_end = (z == 0) | (z == deep - 1)

    def block_rows(tree, side):
        return rows_at(tree * 2 + side, rows)

    def shard_lanes(k):
        return rows_at(k, shard)

    def load(source, target, at):
        return pltpu.make_async_copy(source, target, load_sem.at[at])

    head_lanes = rows_at(y, HEAD_SIZE)
    first_lanes, second_lanes = pl.ds(mine, HEAD_SIZE), pl.ds(mine + HEAD_SIZE, HEAD_SIZE)
    loads = [
        load(w_query, wqkv.at[z, :, pl.ds(0, mine)], 0),
        load(w_output, wout.at[z], 4),
        load(tokens_in, alow, 5),
        load(cotangent_in.at[0], ups.at[block_rows(0, x)], 6),
        load(cotangent_in.at[1], ups.at[block_rows(1, x)], 7),
        load(gate_in, mats.at[0, :, shard_lanes(z)], 8),
        load(up_in, mats.at[1, :, shard_lanes(z)], 9),
        load(down_in, mats.at[2, :, shard_lanes(z)], 10),
    ]

    for core, source in enumerate((w_key, w_value)):

        @pl.when(c == core)
        def _():
            load(source.at[:, head_lanes], wqkv.at[z, :, first_lanes], 1).start()

    row = lax.broadcasted_iota(jnp.int32, (8, shard), 0)
    gains = jnp.where(
        row == 0,
        jnp.broadcast_to(gain_one_in[...].astype(F32), (8, shard)),
        jnp.where(row == 1, jnp.broadcast_to(gain_two_in[...].astype(F32), (8, shard)), 0.0),
    )
    smalls[z] = jnp.concatenate([gains, router_in[...].astype(F32)], 0).astype(BF16)
    for copy in loads:
        copy.start()
    lin = x * 4 + me.t

    def plane(number):
        return (z, number // 4, number % 4)

    greet(
        [me.at_z((z + k) % deep) for k in range(1, deep)]
        + [plane((lin + k) % 8) for k in range(1, 8)]
    )
    loads[0].wait()
    load(w_key.at[:, head_lanes], wqkv.at[z, :, first_lanes], 1).wait()

    def qkv_piece(source, part, by):
        return wqkv.at[source, rows_at(by, half), pl.ds(0, mine + HEAD_SIZE)]

    def out_piece(source, part, by):
        return wout.at[source, rows_at(by, half)]

    def expert_piece(source, part, by):
        return mats.at[:, pl.ds(part * units, units), shard_lanes(source)]

    take_qkv = Relay(me, deep, qkv_piece, up1_sem, dn1_sem, side1_sem)
    take_out = Relay(me, deep, out_piece, up2_sem, dn2_sem, side2_sem)
    take = Relay(me, deep, expert_piece, up3_sem, dn3_sem)

    def small_out(k):
        there = (z + k) % deep
        return remote(smalls.at[z], smalls.at[z], small_sem, k - 1, me.at_z(there))

    take_qkv.begin(0)
    for k in range(1, deep):
        small_out(k).start()

    def make_tables(tree):
        seen, cosine, sine = tree_tables(
            starts, parents, tree, x * rows, rows, length, frequency[:1, :]
        )
        agrad[:, pl.ds(tree * length, length)] = seen
        tables[0, tree] = cosine
        tables[1, tree] = sine

    make_tables(0)
    take_qkv.pass_on(0, 0)
    for copy in loads[1:]:
        copy.wait()
    take_out.begin(0)
    for tree in range(1, trees):
        make_tables(tree)
    take_qkv.pass_on(0, 1)
    take_out.pass_on(0, 0)
    for k in range(1, deep):
        source = (z + deep - k) % deep
        remote(
            smalls.at[source], smalls.at[source], small_sem, k - 1, me.at_z(source)
        ).wait_recv()
    gain_one = jnp.concatenate([smalls[k, :1, :] for k in range(deep)], 1).astype(F32)
    gain_two = jnp.concatenate([smalls[k, 1:2, :] for k in range(deep)], 1).astype(F32)
    router = jnp.concatenate([smalls[k, 8:, :] for k in range(deep)], 1)

    def norm_rows(source, target, at):
        value = source[at, :].astype(F32)
        factor = lax.rsqrt(jnp.mean(value * value, -1, keepdims=True) + EPS)
        target[at, :] = (value * factor * gain_one).astype(BF16)

    for tree in range(trees):

        def first_norm(number, carry):
            at = rows_at(number, step)
            norm_rows(alow.at[tree], core_out.at[pl.ds(tree * rows, rows)], at)
            return carry

        lax.fori_loop(0, CHUNKS, first_norm, 0)
    take_qkv.pass_on(0, 2)
    take_out.pass_on(0, 1)
    take.begin(0)
    take_qkv.finish(0)
    trade = remote(
        wqkv.at[:, :, first_lanes], wqkv.at[:, :, second_lanes], trade_sem, 0, me.core_peer()
    )
    trade.start()
    trade.wait_recv()

    own_place = rows_at(x, rows)
    away_place = rows_at(1 - x, rows)

    def kv_copy(tree, which, place, on):
        at = (keys, values)[which].at[tree, place]
        return remote(at, at, kv_sem, 2 * on + which, me.core_peer() if on else me.x_peer())

    def project_in(tree):
        total = jnp.zeros((rows, wqkv.shape[2]), F32)
        for k in range(deep):
            total = total + mm(core_out[rows_at(tree, rows), pl.ds(k * shard, shard)], wqkv[k])
        cosine, sine = tables[0, tree], tables[1, tree]
        for head in range(heads):
            part_q = total[:, head * HEAD_SIZE : (head + 1) * HEAD_SIZE]
            queries[tree, head] = turn(part_q, cosine, sine).astype(BF16)
        first, second_part = total[:, mine : mine + HEAD_SIZE], total[:, mine + HEAD_SIZE :]
        part_k = jnp.where(c == 0, first, second_part)
        keys[tree, own_place, :] = turn(part_k, cosine, sine).astype(BF16)
        values[tree, own_place, :] = jnp.where(c == 0, second_part, first).astype(BF16)

    project_in(c)
    for which in range(2):
        kv_copy(c, which, own_place, 0).start()
    project_in(1 - c)
    take_out.pass_on(0, 2)

    own_up, away_up = ups.at[block_rows(c, x)], ups.at[block_rows(c, 1 - x)]
    peer_up = ups.at[block_rows(1 - c, 1 - x)]
    cot_x = remote(own_up, own_up, cot_sem, 0, me.x_peer())
    cot_x.start()
    for which in range(2):
        kv_copy(c, which, away_place, 0).wait_recv()
        kv_copy(c, which, away_place, 1).start()

    def attend(tree):
        mask = agrad.at[:, rows_at(tree, length)]

        def one(head, carry):
            score = mm(queries[tree, head], keys[tree], NT) * inv_root
            score = jnp.where(mask[...] > 0.5, score, NEG)
            top = jnp.max(score, -1, keepdims=True)
            raised = jnp.exp(score - top)
            prob = (raised / jnp.sum(raised, -1, keepdims=True)).astype(BF16)
            probs[tree, head] = prob
            context[tree, head] = mm(prob, values[tree]).astype(BF16)
            return carry

        lax.fori_loop(0, heads, one, 0)

    attend(c)
    take.pass_on(0, 0)
    take.begin(1, False)
    for part in range(1, groups):
        take.begin(part, True)
    for which in range(2):
        kv_copy(1 - c, which, away_place, 1).wait_recv()
    attend(1 - c)
    take_out.finish(0)

    def project(tree, row):
        pieces = []
        for k in range(deep):
            piece = jnp.zeros((step, shard), F32)
            for head in range(heads):
                piece = piece + mm(
                    context[tree, head, pl.ds(row, step), :],
                    wout[k, pl.ds(head * HEAD_SIZE, HEAD_SIZE), :],
                )
            pieces.append(piece)
        return pieces

    def core_copy(number):
        at = rows_at(number, step)
        return remote(core_out.at[at], mo_core_in.at[at], core_sem, number, me.core_peer())

    def y_copy(number):
        at = rows_at(number, step)
        return remote(y_out.at[at], mo_y_in.at[at], y_sem, number, me.y_peer())

    for chunk in range(CHUNKS):
        at = pl.ds(chunk * step, step)
        for k, piece in enumerate(project(1 - c, chunk * step)):
            core_out[at, pl.ds(k * shard, shard)] = piece.astype(BF16)
        core_copy(chunk).start()
    for chunk in range(CHUNKS):
        at = pl.ds(chunk * step, step)
        pieces = project(c, chunk * step)
        core_copy(chunk).wait_recv()
        for k, piece in enumerate(pieces):
            lanes = pl.ds(k * shard, shard)
            both = piece.astype(BF16).astype(F32) + mo_core_in[at, lanes].astype(F32)
            y_out[at, lanes] = both.astype(BF16)
        y_copy(chunk).start()
    take.pass_on(0, 1)

    def two_rows(tree, side, number):
        first = (tree * 2 + side) * rows + number * step
        return pl.ds(pl.multiple_of(first, step), step)

    def hid_copy(tree, side, sems, number, device):
        at = hid.at[two_rows(tree, side, number)]
        return remote(at, at, sems, number, device)

    def second(number, carry):
        at = rows_at(number, step)
        y_copy(number).wait_recv()
        value = alow[c, at, :].astype(F32) + (y_out[at, :].astype(F32) + mo_y_in[at, :].astype(F32))
        after[at, :] = value
        factor = lax.rsqrt(jnp.mean(value * value, -1, keepdims=True) + EPS)
        hid[two_rows(c, x, number), :] = (value * factor * gain_two).astype(BF16)
        hid_copy(c, x, hx_sem, number, me.x_peer()).start()
        hid_copy(c, x, hc_sem, number, me.core_peer()).start()
        return carry

    lax.fori_loop(0, 2, second, 0)
    take.pass_on(1, 0)
    take.begin(2, False)
    lax.fori_loop(2, CHUNKS, second, 0)

    logits = mm(router, hid[block_rows(c, x), :], NT)
    expert = lax.broadcasted_iota(jnp.int32, logits.shape, 0)
    chosen = expert < 0
    for k in range(routes.shape[1]):
        chosen = chosen | (expert == routes[c, k : k + 1, :])
    logits = jnp.where(chosen, logits, NEG)
    raised = jnp.where(chosen, jnp.exp(logits - jnp.max(logits, 0, keepdims=True)), 0.0)
    mixes[own_block] = raised / jnp.sum(raised, 0, keepdims=True)

    def mix_copy(tree, side, at, device):
        block = mixes.at[tree * 2 + side]
        return remote(block, block, mix_sem, at, device)

    mix_copy(c, x, 0, me.x_peer()).start()
    mix_copy(c, x, 1, me.core_peer()).start()
    cot_x_in = remote(away_up, away_up, cot_sem, 0, me.x_peer())
    cot_x_in.wait_recv()
    cot_on = remote(away_up, away_up, cot_sem, 1, me.core_peer())
    cot_on.start()
    for number in range(CHUNKS):
        hid_copy(c, 1 - x, hx_sem, number, me.x_peer()).wait_recv()
        hid_copy(c, 1 - x, hf_sem, number, me.core_peer()).start()
    mix_copy(c, 1 - x, 0, me.x_peer()).wait_recv()
    mix_copy(c, 1 - x, 2, me.core_peer()).start()
    remote(peer_up, peer_up, cot_sem, 1, me.core_peer()).wait_recv()
    for number in range(CHUNKS):
        hid_copy(1 - c, x, hc_sem, number, me.core_peer()).wait_recv()
        hid_copy(1 - c, 1 - x, hf_sem, number, me.core_peer()).wait_recv()
    mix_copy(1 - c, x, 1, me.core_peer()).wait_recv()
    mix_copy(1 - c, 1 - x, 2, me.core_peer()).wait_recv()
    take.pass_on(1, 1)

    def half_lanes(k, side):
        first = k * shard + side * HEAD_SIZE
        return pl.ds(pl.multiple_of(first, HEAD_SIZE), 2 * HEAD_SIZE)

    def cross(source, landing, tree, k, on, sems):
        at = landing.at[tree, k]
        if on:
            return remote(at, at, sems, deep + k, me.core_peer())
        return remote(source.at[:, half_lanes(k, 1 - x)], at, sems, k, me.x_peer())

    def hidx_copy(tree, k, on):
        return cross(x_out, hidx, tree, k, on, hidx_sem)

    def alx_out(number, k):
        at = rows_at(number, step)
        return remote(
            alow.at[c, at, half_lanes(k, 1 - x)],
            alx.at[c, k, at],
            alx_sem,
            number * deep + k,
            me.x_peer(),
        )

    def alx_on(tree, k):
        at = alx.at[tree, k]
        return remote(at, at, alx_sem, CHUNKS * deep + k, me.core_peer())

    def again(number, carry):
        norm_rows(alow.at[c], x_out, rows_at(number, step))
        return carry

    lax.fori_loop(0, CHUNKS, again, 0)
    for k in range(deep):
        hidx_copy(c, k, 0).start()
    ctx_copy = remote(context, ctx_x, ctx_sem, 0, me.x_peer())
    ctx_copy.start()
    take.finish(0)

    def expert_block(group, block):
        tokens = rows_at(block, rows)
        some = pl.ds(group * units, units)
        pre_gate = mm(mats[0, some, :], hid[tokens, :], NT)
        pre_up = mm(mats[1, some, :], hid[tokens, :], NT)
        back = mm(mats[2, some, :], ups[tokens, :], NT)
        first, second_half = mixes[block, group : group + 1, :], mixes[
            block, groups + group : groups + group + 1, :
        ]
        weight = jnp.broadcast_to(jnp.where(x == 0, first, second_half), (units, rows))
        square = pre_gate * pre_gate
        bent = jnp.tanh(ROOT_2_PI * pre_gate * (1.0 + CUBIC * square))
        slope = 0.5 * (1.0 + bent)
        active = pre_gate * slope
        rise = slope + 0.5 * pre_gate * (1.0 - bent * bent) * ROOT_2_PI * (
            1.0 + 3.0 * CUBIC * square
        )
        hidden = active * pre_up
        gates[pl.ds(group, 1), tokens] = jnp.sum(hidden * back, 0, keepdims=True)
        back = weight * back
        acts[0, some, tokens] = (back * pre_up * rise).astype(BF16)
        acts[1, some, tokens] = (back * active).astype(BF16)
        acts[2, some, tokens] = (weight * hidden).astype(BF16)

    fold = Fold(me, groups, (own, stage, land), (fold_send, fold_recv, fold_free), 64, True)

    def expert_grad(group, m):
        source = ups if m == 2 else hid
        some = acts.at[m, pl.ds(group * units, units)]

        def one(k, carry):
            value = mm(some[...], source[:, shard_lanes(k)]).astype(BF16)

            @pl.when(k == z)
            def _():
                own[group, m] = value

            @pl.when(k != z)
            def _():
                stage[group % fold.sets, fold.place(k), m] = value

            return carry

        lax.fori_loop(0, deep, one, 0)
        fold.begin(group, m)

    def expert_group(group):
        def one(block, carry):
            expert_block(group, block)
            return carry

        lax.fori_loop(0, 2 * trees, one, 0)
        for m in range(KINDS):
            expert_grad(group, m)

    expert_outs = (d_gate, d_up, d_down)

    def grad_out(group, m):
        return pltpu.make_async_copy(
            bounce.at[m], expert_outs[m].at[pl.ds(group * units, units)], grad_sem.at[m]
        )

    def finish_group(group, ends):
        @pl.when(is_end if ends else jnp.logical_not(is_end))
        def _():
            for m in range(KINDS):
                if group > 0:
                    grad_out(group - 1, m).wait()

                def write(at, value):
                    bounce[m, at, :] = value

                fold.finish(group, m, write)
                grad_out(group, m).start()

    def advance(group, kinds=range(KINDS)):
        for m in kinds:
            fold.advance(group, m)

    def let_go(group):
        for m in range(KINDS):
            fold.let_go(group, m)

    def drain(group):
        for m in range(KINDS):
            fold.drain(group, m)

    take.pass_on(2, 0)
    take.begin(3, False)
    expert_group(0)
    take.pass_on(2, 1)
    take.pass_on(3, 0)
    take.finish(1)
    expert_group(1)
    take.pass_on(3, 1)
    for k in range(deep):
        hidx_copy(c, k, 0).wait_recv()
        hidx_copy(c, k, 1).start()
    advance(0)
    take.finish(2)
    expert_group(2)
    finish_group(0, False)
    last = groups - 1

    def two_units(first, some):
        at = pl.ds(first, TILE)
        total = mm(acts[0, some, at], mats[0, some, :], TN)
        return total + mm(acts[1, some, at], mats[1, some, :], TN)

    def two_ahead(first):
        return two_units(first, pl.ds(0, last * units))

    def two_make(first):
        return two_units(first, pl.ds(last * units, units))

    def mo_make(first):
        return mm(acts[2, :, pl.ds(first, TILE)], mats[2], TN)

    two = PlaneSum(
        me,
        rows,
        two_make,
        (core_out, x_out, acc, y_out),
        (two_core_in, two_x_in, two_y_in),
        (two_core_sem, two_x_sem, two_y_sem),
        two_ahead,
    )
    mo = PlaneSum(
        me,
        rows,
        mo_make,
        (core_out, hid.at[pl.ds(rows, rows)], acc, hid.at[pl.ds(0, rows)]),
        (mo_core_in, mo_x_in, mo_y_in),
        (mo_core_sem, mo_x_sem, mo_y_sem),
    )
    for number in range(CHUNKS):
        core_copy(number).wait_send()
        y_copy(number).wait_send()
    for k in range(deep):
        hidx_copy(c, k, 0).wait_send()
    two.prepare()
    advance(1)
    let_go(0)
    take.finish(3)
    expert_block(last, (1 - c) * 2 + 1 - x)
    two.outward(0)
    expert_block(last, (1 - c) * 2 + x)
    two.outward(1)
    expert_block(last, c * 2 + 1 - x)
    two.across()
    expert_block(last, own_block)

    for block in range(2 * trees):
        gates_out[block, pl.ds(0, groups), :] = gates[:, pl.ds(block * rows, rows)]

    def gate_copy(k):
        there = (lin + k) % 8
        block = (there % 2) * 2 + there // 4
        return remote(gates_out.at[block], gates_in.at[lin], gate_sem, k - 1, plane(there))

    for k in range(1, 8):
        gate_copy(k).start()
    gates_in[lin] = gates_out[own_block]
    two.inward()
    drain(0)
    expert_grad(last, 0)
    two.pass_on(0, 1)
    expert_grad(last, 1)
    two.pass_on(1, 2)
    expert_grad(last, 2)
    two.pass_on(2, 3)
    advance(2, [0])

    for k in range(1, 8):
        source = (lin + 8 - k) % 8
        remote(gates_out.at[0], gates_in.at[source], gate_sem, k - 1, plane(source)).wait_recv()
    sums = []
    for side in range(2):
        total = gates_in[side * 4]
        for k in range(1, 4):
            total = total + gates_in[side * 4 + k]
        sums.append(total[:groups])
    mix_grad = jnp.concatenate(sums, 0)
    mix = mixes[own_block]
    picked = mix * (mix_grad - jnp.sum(mix * mix_grad, 0, keepdims=True))
    logit_grad = picked.astype(BF16)
    agrad[...] = mm(logit_grad, router, TN)
    small_own[pl.ds(0, 8), :] = jnp.zeros((8, width), F32)
    small_own[pl.ds(8, 8), :] = mm(logit_grad, hid[block_rows(c, x), :])

    for number in range(CHUNKS):
        hid_copy(c, x, hx_sem, number, me.x_peer()).wait_send()
        hid_copy(c, x, hc_sem, number, me.core_peer()).wait_send()
        hid_copy(c, 1 - x, hf_sem, number, me.core_peer()).wait_send()
    two.pass_on(3, 4)
    two.core_sent()
    mo.outward(0)
    mo.outward(1)
    advance(2, [1])

    def low_copy(number):
        at = alow.at[c, rows_at(number, step)]
        return remote(at, at, low_sem, number, me.core_peer())

    def second_norm(number, gain_grad):
        at = rows_at(number, step)
        upstream = two.total(number) + agrad[at, :]
        value = after[at, :]
        factor = lax.rsqrt(jnp.mean(value * value, -1, keepdims=True) + EPS)
        scaled = upstream * gain_two
        inner = jnp.mean(scaled * value, -1, keepdims=True)
        cot = ups[two_rows(c, x, number), :]
        total = cot.astype(F32) + (factor * scaled - value * (factor * factor * factor * inner))
        agrad[at, :] = total
        alow[c, at, :] = total.astype(BF16)
        low_copy(number).start()
        for k in range(deep):
            alx_out(number, k).start()
        return gain_grad + jnp.sum(upstream * value * factor, 0, keepdims=True)

    gain_two_grad = lax.fori_loop(0, CHUNKS, second_norm, jnp.zeros((1, width), F32))
    small_own[pl.ds(1, 1), :] = gain_two_grad

    def attend_back(tree):
        back = jnp.zeros((rows, mine), F32)
        for k in range(deep):
            back = back + mm(alow[tree, :, pl.ds(k * shard, shard)], wout[k], NT)
        back = back.astype(BF16)
        cosine, sine = tables[0, tree], tables[1, tree]
        key_grad = jnp.zeros((length, HEAD_SIZE), F32)
        value_grad = jnp.zeros((length, HEAD_SIZE), F32)
        for head in range(heads):
            lanes = pl.ds(head * HEAD_SIZE, HEAD_SIZE)
            back_head = back[:, head * HEAD_SIZE : (head + 1) * HEAD_SIZE]
            prob = probs[tree, head]
            value_grad = value_grad + mm(prob, back_head, TN)
            prob = prob.astype(F32)
            share = prob * mm(back_head, values[tree], NT)
            score = (share - prob * jnp.sum(share, -1, keepdims=True)).astype(BF16)
            query_grad = mm(score, keys[tree]) * inv_root
            qlow[tree, :, lanes] = turn(query_grad, cosine, -sine).astype(BF16)
            key_grad = key_grad + mm(score, queries[tree, head], TN)
        return jnp.concatenate([key_grad * inv_root, value_grad], 1)

    for number in range(CHUNKS):
        at = alow.at[1 - c, pl.ds(number * step, step)]
        remote(at, at, low_sem, number, me.core_peer()).wait_recv()
    kv_out[...] = attend_back(1 - c).astype(BF16)
    kvg_copy = remote(kv_out, kv_in, kvg_sem, 0, me.core_peer())
    kvg_copy.start()

    def qx_copy(tree, number):
        return remote(qlow.at[tree], qlow_x.at[tree], qx_sem, number, me.x_peer())

    qx_copy(1 - c, 0).start()
    kv_own[...] = attend_back(c)

    def of_side(ref, side):
        low, high = ref[pl.ds(0, rows), :], ref[pl.ds(rows, rows), :]
        return jnp.where(side == 0, low, high).astype(F32)

    kvg_copy.wait_recv()
    kvx_out[...] = (of_side(kv_own, 1 - x) + of_side(kv_in, 1 - x)).astype(BF16)
    kvx_copy = remote(kvx_out, kvx_in, kvg_sem, 1, me.x_peer())
    kvx_copy.start()
    qx_copy(c, 1).start()
    advance(2, [2])

    def one_tile(tree, at):
        return [mm(qlow[tree, at, :], wqkv[k, :, pl.ds(0, mine)], NT) for k in range(deep)]

    mo.core_sent()

    def one_copy(number):
        at = rows_at(number, step)
        return remote(core_out.at[at], two_core_in.at[at], one_core_sem, number, me.core_peer())

    def one_outward(number, carry):
        at = rows_at(number, step)
        for k, piece in enumerate(one_tile(1 - c, at)):
            core_out[at, pl.ds(k * shard, shard)] = piece.astype(BF16)
        one_copy(number).start()
        return carry

    lax.fori_loop(0, CHUNKS, one_outward, 0)
    for k in range(deep):
        for number in range(CHUNKS):
            alx_out(number, k).wait_recv()
        alx_on(c, k).start()
    let_go(1)
    kvx_copy.wait_recv()
    own_kv = of_side(kv_own, x) + of_side(kv_in, x) + kvx_in[...].astype(F32)
    key_low = turn(own_kv[:, :HEAD_SIZE], tables[0, c], -tables[1, c])
    value_low = own_kv[:, HEAD_SIZE:]
    kvlow[:, pl.ds(0, HEAD_SIZE)] = jnp.where(c == 0, key_low, value_low).astype(BF16)
    kvlow[:, pl.ds(HEAD_SIZE, HEAD_SIZE)] = jnp.where(c == 0, value_low, key_low).astype(BF16)
    kvl_copy = remote(kvlow, kvlow_x, kvg_sem, 2, me.x_peer())
    kvl_copy.start()

    two.y_sent()

    def one_y(number):
        at = rows_at(number, step)
        return remote(y_out.at[at], two_x_in.at[at], one_y_sem, number, me.y_peer())

    def one_inward(number, carry):
        at = rows_at(number, step)
        one_copy(number).wait_recv()
        for k, piece in enumerate(one_tile(c, at)):
            lanes = pl.ds(k * shard, shard)
            piece = piece + mm(kvlow[at, :], wqkv[k, :, pl.ds(mine, 2 * HEAD_SIZE)], NT)
            y_out[at, lanes] = (piece + two_core_in[at, lanes].astype(F32)).astype(BF16)
        one_y(number).start()
        return carry

    lax.fori_loop(0, CHUNKS, one_inward, 0)

    mo.across()
    mo.inward()
    for part in range(groups):
        take.drain(part)
    spare = mats.at[0]
    late = [
        load(tokens_in.at[0], spare.at[pl.ds(0, rows)], 0),
        load(tokens_in.at[1], spare.at[pl.ds(rows, rows)], 1),
    ]
    for copy in late:
        copy.start()

    def chosen_half(value):
        return jnp.where(x == 0, value[:half], value[2 * HEAD_SIZE - half :])

    def keep_own(buffer_own, buffer_stage, k, lanes, value):
        @pl.when(k == z)
        def _():
            buffer_own[0, 0, :, lanes] = value.astype(BF16)

        @pl.when(k != z)
        def _():
            buffer_stage[0, fold.place(k), 0, :, lanes] = value.astype(BF16)

    def heads_of(array, tree):
        return jnp.concatenate([array[tree, head] for head in range(heads)], 1)

    fold_o = Fold(me, 1, (own_o, stage_o, land_o), (fold_send_o, fold_recv_o, None), 64, False)
    fold_q = Fold(me, 1, (own_q, stage_q, land_q), (fold_send_q, fold_recv_q, None), 64, False)
    for k in range(deep):
        alx_on(1 - c, k).wait_recv()
    remote(context, ctx_x, ctx_sem, 0, me.x_peer()).wait_recv()

    def output_grad(k, carry):
        value = jnp.zeros((2 * HEAD_SIZE, mine), F32)
        for tree in range(trees):
            value = value + mm(alow[tree, :, half_lanes(k, x)], heads_of(context, tree), TN)
            value = value + mm(alx[tree, k], heads_of(ctx_x, tree), TN)
        keep_own(own_o, stage_o, k, pl.ds(0, mine), chosen_half(value))
        return carry

    lax.fori_loop(0, deep, output_grad, 0)
    fold_o.begin(0, 0)
    advance(3, [0])

    for copy in late:
        copy.wait()
    for tree in range(trees):

        def norm_again(number, carry):
            at = rows_at(number, step)
            norm_rows(
                spare.at[pl.ds(tree * rows, rows)], mats.at[1, pl.ds(tree * rows, rows)], at
            )
            return carry

        lax.fori_loop(0, CHUNKS, norm_again, 0)

    def hid_one(tree, k):
        return mats[1, rows_at(tree, rows), half_lanes(k, x)]

    for k in range(deep):
        hidx_copy(1 - c, k, 1).wait_recv()
    qx_copy(1 - c, 0).wait_recv()
    qx_copy(c, 1).wait_recv()

    def query_grad(k, carry):
        value = jnp.zeros((2 * HEAD_SIZE, mine), F32)
        for tree in range(trees):
            value = value + mm(hid_one(tree, k), qlow[tree], TN)
            value = value + mm(hidx[tree, k], qlow_x[tree], TN)
        keep_own(own_q, stage_q, k, pl.ds(0, mine), chosen_half(value))
        return carry

    lax.fori_loop(0, deep, query_grad, 0)

    kvl_copy.wait_recv()

    def kv_weight_grad(k, carry):
        value = mm(hid_one(c, k), kvlow[...], TN) + mm(hidx[c, k], kvlow_x[...], TN)
        value = chosen_half(value)
        low, high = value[:, :HEAD_SIZE], value[:, HEAD_SIZE:]
        dkv_out[0, k] = high.astype(BF16)
        dkv_out[1, k] = low.astype(BF16)
        return carry

    lax.fori_loop(0, deep, kv_weight_grad, 0)
    dkv_copy = remote(dkv_out.at[0], dkv_in, kvg_sem, 3, me.core_peer())
    dkv_copy.start()
    dkv_copy.wait_recv()

    def kv_weight_sum(k, carry):
        value = dkv_out[1, k].astype(F32) + dkv_in[k].astype(F32)
        keep_own(own_q, stage_q, k, pl.ds(mine, HEAD_SIZE), value)
        return carry

    lax.fori_loop(0, deep, kv_weight_sum, 0)
    fold_q.begin(0, 0)

    advance(3, [1])
    let_go(2)
    finish_group(0, True)
    finish_group(1, True)
    finish_group(1, False)
    finish_group(2, False)

    def out_copies(buffer, target, first, peer_sems, number):
        at = rows_at(number, step)
        here = pltpu.make_async_copy(buffer.at[at], target.at[c, at], out_sem.at[first + number])
        there = remote(buffer.at[at], target.at[c, at], peer_sems, number, me.core_peer())
        return here, there

    def first_norm_back(number, gain_grad):
        at = rows_at(number, step)
        one_y(number).wait_recv()
        upstream = y_out[at, :].astype(F32) + two_x_in[at, :].astype(F32)
        first = pl.multiple_of(c * rows + number * step, step)
        value = mats[0, pl.ds(first, step), :].astype(F32)
        factor = lax.rsqrt(jnp.mean(value * value, -1, keepdims=True) + EPS)
        scaled = upstream * gain_one
        inner = jnp.mean(scaled * value, -1, keepdims=True)
        agrad[at, :] = agrad[at, :] + (
            factor * scaled - value * (factor * factor * factor * inner)
        )
        for copy in out_copies(agrad, d_tokens, CHUNKS, token_sem, number):
            copy.start()
        return gain_grad + jnp.sum(upstream * value * factor, 0, keepdims=True)

    gain_one_grad = lax.fori_loop(0, CHUNKS, first_norm_back, jnp.zeros((1, width), F32))
    small_own[pl.ds(0, 1), :] = gain_one_grad
    spot = x * 2 + c

    def spread(k):
        there = (spot + k) % 4
        device = (z, there // 2, 2 * y + there % 2)
        return remote(small_own, small_in.at[spot], small_in_sem, k - 1, device)

    for k in range(1, 4):
        spread(k).start()
    small_in[spot] = small_own[...]
    advance(3, [2])
    mo.pass_on(0, CHUNKS)
    fold_o.advance(0, 0)
    let_go(3)
    finish_group(2, True)

    two.x_sent()

    def mix_out(number, carry):
        at = rows_at(number, step)
        x_out[at, :] = (after[at, :] + mo.total(number)).astype(BF16)
        for copy in out_copies(x_out, mixed, 0, mixed_sem, number):
            copy.start()
        return carry

    lax.fori_loop(0, CHUNKS, mix_out, 0)
    fold_q.advance(0, 0)
    for k in range(1, 4):
        source = (spot + 4 - k) % 4
        device = (z, source // 2, 2 * y + source % 2)
        remote(small_own, small_in.at[source], small_in_sem, k - 1, device).wait_recv()
        spread(k).wait_send()
    small_own[...] = (small_in[0] + small_in[1]) + (small_in[2] + small_in[3])

    def small_copy(k):
        there = (z + k) % deep
        return remote(
            small_own.at[:, shard_lanes(there)], small_z.at[z], small_z_sem, k - 1, me.at_z(there)
        )

    for k in range(1, deep):
        small_copy(k).start()
    small_z[z] = small_own[:, shard_lanes(z)]
    finish_group(3, False)
    finish_group(3, True)

    def write_o(at, value):
        d_output[at, :] = value

    fold_o.finish(0, 0, write_o)

    def write_q(at, value):
        d_query[at, :] = value[:, :mine]
        kv_last[at, :] = value[:, mine:]

    fold_q.finish(0, 0, write_q)

    share = half // 4

    def share_rows(t):
        return pl.ds(pl.multiple_of(t * share, 8), share)

    def last_copy(k):
        there = (me.t + k) % 4
        return remote(
            kv_last.at[share_rows(there)], kv_land.at[me.t], last_sem, k - 1, (z, x, there)
        )

    for k in range(1, 4):
        last_copy(k).start()
    kv_land[me.t] = kv_last[share_rows(me.t), :]
    for k in range(1, deep):
        source = (z + deep - k) % deep
        remote(
            small_own.at[:, shard_lanes(0)], small_z.at[source], small_z_sem, k - 1, me.at_z(source)
        ).wait_recv()
    total = small_z[0]
    for k in range(1, deep):
        total = total + small_z[k]
    d_small[...] = jnp.where(x == 0, total[:, :half], total[:, half:])
    for k in range(1, 4):
        source = (me.t + 4 - k) % 4
        remote(
            kv_last.at[pl.ds(0, share)], kv_land.at[source], last_sem, k - 1, (z, x, source)
        ).wait_recv()
    for head in range(KEY_VALUE_HEADS):
        lanes = pl.ds(head * HEAD_SIZE, HEAD_SIZE)
        d_key[:, lanes] = kv_land[2 * head]
        d_value[:, lanes] = kv_land[2 * head + 1]

    for number in range(CHUNKS):
        at = pl.ds(number * step, step)
        remote(x_out.at[at], mixed.at[1 - c, at], mixed_sem, number, me.core_peer()).wait_recv()
        remote(agrad.at[at], d_tokens.at[1 - c, at], token_sem, number, me.core_peer()).wait_recv()
        for buffer, target, first, peer_sems in (
            (x_out, mixed, 0, mixed_sem),
            (agrad, d_tokens, CHUNKS, token_sem),
        ):
            here, there = out_copies(buffer, target, first, peer_sems, number)
            here.wait()
            there.wait_send()
        one_y(number).wait_send()
        one_copy(number).wait_send()
        low_copy(number).wait_send()
    mo.x_sent()
    mo.y_sent()
    for m in range(KINDS):
        grad_out(groups - 1, m).wait()
    for k in range(1, 8):
        gate_copy(k).wait_send()
    for k in range(1, deep):
        small_copy(k).wait_send()
        small_out(k).wait_send()
    for k in range(1, 4):
        last_copy(k).wait_send()
    for k in range(deep):
        hidx_copy(c, k, 1).wait_send()
        for number in range(CHUNKS):
            alx_out(number, k).wait_send()
        alx_on(c, k).wait_send()
    for copy in (trade, kvg_copy, kvx_copy, kvl_copy, dkv_copy, qx_copy(1 - c, 0), qx_copy(c, 1), ctx_copy, cot_x, cot_on):
        copy.wait_send()
    for which in range(2):
        kv_copy(c, which, own_place, 0).wait_send()
        kv_copy(c, which, away_place, 1).wait_send()
    mix_copy(c, x, 0, me.x_peer()).wait_send()
    mix_copy(c, x, 1, me.core_peer()).wait_send()
    mix_copy(c, 1 - x, 2, me.core_peer()).wait_send()
    take_qkv.drain(0)
    take_out.drain(0)
    for group in range(1, groups):
        drain(group)
    fold_o.drain(0, 0)
    fold_q.drain(0, 0)


def sems(count):
    return pltpu.SemaphoreType.DMA((2, count))


def layer_call(
    seg_start,
    seg_parent,
    routes,
    gain_one,
    gain_two,
    router_t,
    tokens,
    cotangent,
    w_query,
    w_key,
    w_value,
    w_output,
    gate_t,
    up_t,
    w_down,
    deep,
):
    trees, rows, width = tokens.shape
    shard, mine = w_query.shape
    heads = mine // HEAD_SIZE
    length = rows * 2
    held, units = w_down.shape[0], w_down.shape[1]
    total_units = held * units
    experts = router_t.shape[0]
    small_rows = 8 + experts
    blocks = 2 * trees
    half = shard // 2
    count = blocks * rows
    sets = 3
    angle = HEAD_SIZE // 2
    frequency = ROPE_BASE ** (-2.0 * np.arange(angle, dtype=np.float32) / np.float32(HEAD_SIZE))
    frequency = np.tile(np.concatenate([frequency] * 2)[None], (8, 1)).astype(np.float32)
    vmem = pl.BlockSpec(memory_space=pltpu.VMEM)
    smem = pl.BlockSpec(memory_space=pltpu.SMEM)
    hbm = pl.BlockSpec(memory_space=pl.ANY)

    def plain(*shape):
        return pltpu.VMEM(shape, BF16)

    def wide(*shape):
        return pltpu.VMEM(shape, F32)

    def out(*shape, dtype=F32):
        return jax.ShapeDtypeStruct(shape, dtype)

    last = deep - 1
    return pl.pallas_call(
        layer_kernel,
        out_shape=(
            out(trees, rows, width, dtype=BF16),
            out(trees, rows, width),
            out(total_units, shard),
            out(total_units, shard),
            out(total_units, shard),
            out(half, mine),
            out(half, mine),
            out(half // 4, KEY_VALUE_HEADS * HEAD_SIZE),
            out(half // 4, KEY_VALUE_HEADS * HEAD_SIZE),
            out(small_rows, half),
        ),
        in_specs=[smem, smem] + [vmem] * 5 + [hbm] * 9,
        out_specs=[hbm] * 5 + [vmem] * 5,
        scratch_shapes=[
            plain(KINDS, total_units, width),
            plain(KINDS, total_units, count),
            plain(count, width),
            plain(count, width),
            plain(deep, shard, mine + 2 * HEAD_SIZE),
            plain(deep, mine, shard),
            plain(deep, small_rows, shard),
            plain(trees, heads, rows, HEAD_SIZE),
            plain(trees, length, HEAD_SIZE),
            plain(trees, length, HEAD_SIZE),
            plain(trees, heads, rows, length),
            plain(trees, heads, rows, HEAD_SIZE),
            wide(2, trees, rows, HEAD_SIZE),
            wide(rows, width),
            wide(blocks, experts, rows),
            wide(held, count),
            wide(blocks, 8, rows),
            wide(8, 8, rows),
            plain(2 * rows, width),
            plain(rows, width),
            wide(rows, width),
            plain(rows, width),
            plain(2 * rows, width),
            plain(rows, width),
            plain(rows, width),
            plain(2 * rows, width),
            plain(rows, width),
            plain(rows, width),
            wide(rows, width),
            plain(trees, rows, width),
            plain(trees, rows, mine),
            plain(length, 2 * HEAD_SIZE),
            plain(length, 2 * HEAD_SIZE),
            wide(length, 2 * HEAD_SIZE),
            plain(rows, 2 * HEAD_SIZE),
            plain(rows, 2 * HEAD_SIZE),
            plain(rows, 2 * HEAD_SIZE),
            plain(rows, 2 * HEAD_SIZE),
            plain(trees, rows, mine),
            plain(trees, deep, rows, 2 * HEAD_SIZE),
            plain(trees, deep, rows, 2 * HEAD_SIZE),
            plain(trees, heads, rows, HEAD_SIZE),
            plain(2, deep, half, HEAD_SIZE),
            plain(deep, half, HEAD_SIZE),
            plain(held, KINDS, units, shard),
            plain(sets, last, KINDS, units, shard),
            plain(sets, 5, KINDS, units, shard),
            wide(KINDS, units, shard),
            plain(1, 1, half, mine),
            plain(1, last, 1, half, mine),
            plain(1, deep, 1, half, mine),
            plain(1, 1, half, mine + HEAD_SIZE),
            plain(1, last, 1, half, mine + HEAD_SIZE),
            plain(1, deep, 1, half, mine + HEAD_SIZE),
            wide(small_rows, width),
            wide(4, small_rows, width),
            wide(deep, small_rows, shard),
            wide(half, HEAD_SIZE),
            wide(4, half // 4, HEAD_SIZE),
            pltpu.SemaphoreType.DMA((11,)),
            sems(last),
            sems(deep),
            sems(deep),
            sems(2 * deep),
            sems(deep),
            sems(deep),
            sems(2 * deep),
            sems(1),
            sems(held * deep),
            sems(held * deep),
            sems(2 * trees),
            sems(2),
            sems(CHUNKS),
            sems(CHUNKS),
            sems(CHUNKS),
            sems(CHUNKS),
            sems(CHUNKS),
            sems(3),
            sems(7),
            sems(2 * rows // TILE),
            sems(CHUNKS),
            sems(CHUNKS),
            sems(2 * rows // TILE),
            sems(CHUNKS),
            sems(CHUNKS),
            sems(CHUNKS),
            sems(CHUNKS),
            sems(CHUNKS),
            sems(4),
            sems(2),
            sems(2 * deep),
            sems((CHUNKS + 1) * deep),
            sems(1),
            pltpu.SemaphoreType.DMA((sets * 3 * KINDS,)),
            pltpu.SemaphoreType.DMA((sets * 5 * KINDS,)),
            pltpu.SemaphoreType.REGULAR((sets * 3 * KINDS,)),
            pltpu.SemaphoreType.DMA((3,)),
            pltpu.SemaphoreType.DMA((4,)),
            pltpu.SemaphoreType.DMA((3,)),
            pltpu.SemaphoreType.DMA((4,)),
            pltpu.SemaphoreType.DMA((2 * CHUNKS,)),
            sems(CHUNKS),
            sems(CHUNKS),
            pltpu.SemaphoreType.DMA((KINDS,)),
            sems(3),
            sems(last),
            sems(3),
        ],
        compiler_params=pltpu.CompilerParams(
            collective_id=0, has_side_effects=True, vmem_limit_bytes=64 * 2**20
        ),
        name="layer",
    )(
        seg_start,
        seg_parent,
        jnp.asarray(frequency),
        routes,
        gain_one,
        gain_two,
        router_t,
        tokens,
        cotangent,
        w_query,
        w_key,
        w_value,
        w_output,
        gate_t.reshape(total_units, -1),
        up_t.reshape(total_units, -1),
        w_down.reshape(total_units, -1),
    )


def plane_shards(
    tokens,
    cotangent,
    seg_start,
    seg_parent,
    routes,
    attn_gain,
    w_query,
    w_key,
    w_value,
    w_output,
    moe_gain,
    w_router,
    w_gate,
    w_up,
    w_down,
):
    width = tokens.shape[2]
    deep = lax.axis_size("dp")
    held, quarter = w_gate.shape[0], w_gate.shape[2]
    made = layer_call(
        seg_start,
        seg_parent,
        jnp.swapaxes(routes, 1, 2),
        attn_gain,
        moe_gain,
        w_router.T,
        tokens,
        cotangent,
        w_query,
        w_key,
        w_value,
        w_output,
        jnp.swapaxes(w_gate, 1, 2),
        jnp.swapaxes(w_up, 1, 2),
        w_down,
        deep,
    )
    placed = place_call(made[:-1])
    mixed, d_tokens, d_gate, d_up, d_down, d_query, d_output, d_key, d_value = placed
    d_small = made[-1]

    def experts(array):
        return array.reshape(held, quarter, width // deep)

    return (
        mixed,
        d_tokens,
        d_small[0],
        d_query,
        d_key,
        d_value,
        d_output.T,
        d_small[1],
        d_small[8:].T,
        jnp.swapaxes(experts(d_gate), 1, 2),
        jnp.swapaxes(experts(d_up), 1, 2),
        experts(d_down),
    )


def shards(*arrays):
    axes = tuple(lax.axis_size(name) for name in ("dp", "expert", "tensor"))
    if axes == (4, 2, 4) and arrays[0].shape[0] == 2:
        return plane_shards(*arrays)
    return general_shards(*arrays)


def solution(mesh):
    placed = (
        P("dp", "expert", None),
        P("dp", "expert", None),
        P("dp", None),
        P("dp", None),
        P("dp", "expert", None),
        P("dp"),
        P("dp", "tensor"),
        P("dp", None),
        P("dp", None),
        P("tensor", "dp"),
        P("dp"),
        P("dp", None),
        P("expert", "dp", "tensor"),
        P("expert", "dp", "tensor"),
        P("expert", "tensor", "dp"),
    )
    return jax.shard_map(
        shards,
        mesh=mesh,
        in_specs=placed,
        out_specs=(
            P("dp", "expert", None),
            P("dp", "expert", None),
            P(("dp", "expert")),
            P(("dp", "expert"), "tensor"),
            P(("dp", "expert", "tensor"), None),
            P(("dp", "expert", "tensor"), None),
            P("tensor", ("dp", "expert")),
            P(("dp", "expert")),
            P(("dp", "expert"), None),
            P("expert", "dp", "tensor"),
            P("expert", "dp", "tensor"),
            P("expert", "tensor", "dp"),
        ),
        check_vma=False,
    )
```

```python
import functools
import math

import jax
import jax.numpy as jnp
import numpy as np
from jax import lax
from jax.experimental import pallas as pl
from jax.experimental.pallas import tpu as pltpu
from jax.sharding import PartitionSpec as P

QUERY_HEADS = 12
KEY_VALUE_HEADS = 2
HEAD_SIZE = 128
GROUP = QUERY_HEADS // KEY_VALUE_HEADS
EPS = 1e-05
ROPE_BASE = 10000.0
NEG = -1e30
F32 = jnp.float32
BF16 = jnp.bfloat16


def dot(left, right, dims):
    return lax.dot_general(left, right, (dims, ((), ())), preferred_element_type=F32)


def norm_factor(rows):
    return lax.rsqrt(jnp.mean(rows * rows, -1, keepdims=True) + EPS)


def norm_back(rows, factor, gain, upstream):
    scaled = upstream * gain
    gain_grad = jnp.sum(upstream * rows * factor, 0)
    inner = jnp.mean(scaled * rows, -1, keepdims=True)
    return factor * scaled - rows * (factor * factor * factor * inner), gain_grad


def layout(starts, parents, places, length):
    labels = jnp.arange(starts.shape[1], dtype=jnp.int32)

    def pick(table, at):
        hot = at[:, :, None] == labels[None, None, :]
        return jnp.sum(jnp.where(hot, table[:, None, :], 0), 2, dtype=jnp.int32)

    segment = jnp.sum((starts[:, None, :] <= places[None, :, None]).astype(jnp.int32), 2) - 1
    above = pick(parents, segment)
    further = pick(parents, above)
    ends = jnp.concatenate(
        [starts[:, 1:], jnp.full((starts.shape[0], 1), length, jnp.int32)], 1
    )
    lengths = ends - starts
    depths = (
        places[None, :]
        - pick(starts, segment)
        + jnp.where(segment != 0, pick(lengths, above), 0)
        + jnp.where(above != 0, pick(lengths, further), 0)
    )
    return segment, above, further, depths


def angles(depths):
    half = HEAD_SIZE // 2
    frequency = ROPE_BASE ** (-2.0 * jnp.arange(half, dtype=F32) / HEAD_SIZE)
    turning = depths.astype(F32)[..., None] * frequency
    return jnp.cos(turning), jnp.sin(turning)


def rotate(heads, cosine, sine):
    half = HEAD_SIZE // 2
    front, back = heads[..., :half], heads[..., half:]
    return jnp.concatenate([front * cosine - back * sine, back * cosine + front * sine], -1)


def general_shards(
    tokens,
    cotangent,
    seg_start,
    seg_parent,
    routes,
    attn_gain,
    w_query,
    w_key,
    w_value,
    w_output,
    moe_gain,
    w_router,
    w_gate,
    w_up,
    w_down,
):
    trees, rows, width = tokens.shape
    expert_count = lax.axis_size("expert")
    tensor_count = lax.axis_size("tensor")
    tensor_at = lax.axis_index("tensor")
    expert_at = lax.axis_index("expert")
    length = rows * expert_count
    heads = w_query.shape[1] // HEAD_SIZE
    kv_head = tensor_at * heads // GROUP
    inv_root = HEAD_SIZE ** (-0.5)
    own_experts = w_gate.shape[0]
    quarter = w_gate.shape[2]
    all_experts = w_router.shape[1]

    def over_dp(array, axis):
        return lax.all_gather(array, "dp", axis=axis, tiled=True)

    w_query = over_dp(w_query, 0)
    w_output = over_dp(w_output, 1)
    gate_t = over_dp(jnp.swapaxes(w_gate, 1, 2), 2)
    up_t = over_dp(jnp.swapaxes(w_up, 1, 2), 2)
    down = over_dp(w_down, 2)
    small = over_dp(
        jnp.concatenate(
            [
                lax.dynamic_slice_in_dim(w_key, kv_head * HEAD_SIZE, HEAD_SIZE, 1),
                lax.dynamic_slice_in_dim(w_value, kv_head * HEAD_SIZE, HEAD_SIZE, 1),
                w_router,
                attn_gain[:, None],
                moe_gain[:, None],
            ],
            1,
        ),
        0,
    )
    w_kv = small[:, : 2 * HEAD_SIZE]
    w_router = small[:, 2 * HEAD_SIZE : 2 * HEAD_SIZE + all_experts]
    attn_gain = small[:, -2].astype(F32)
    moe_gain = small[:, -1].astype(F32)

    all_places = jnp.arange(length, dtype=jnp.int32)
    places = expert_at * rows + jnp.arange(rows, dtype=jnp.int32)
    segment, above, further, depths = layout(seg_start, seg_parent, places, length)
    key_segment = layout(seg_start, seg_parent, all_places, length)[0]
    cosine, sine = angles(depths)
    of_key = key_segment[:, None, :]
    visible = (
        (of_key == segment[:, :, None])
        | (of_key == above[:, :, None])
        | (of_key == further[:, :, None])
    ) & (all_places[None, None, :] <= places[None, :, None])

    residual = tokens.astype(F32).reshape(trees * rows, width)
    factor_one = norm_factor(residual)
    hidden_one = (residual * factor_one * attn_gain).astype(BF16)
    query_pre = dot(hidden_one, w_query, ((1,), (0,))).reshape(trees, rows, heads, HEAD_SIZE)
    kv_pre = dot(hidden_one, w_kv, ((1,), (0,))).reshape(trees, rows, 2 * HEAD_SIZE)
    queries = rotate(query_pre, cosine[:, :, None, :], sine[:, :, None, :]).astype(BF16)
    own_keys = rotate(kv_pre[..., :HEAD_SIZE], cosine, sine).astype(BF16)
    own_kv = jnp.concatenate([own_keys, kv_pre[..., HEAD_SIZE:].astype(BF16)], -1)
    keys_values = lax.all_gather(own_kv, "expert", axis=1, tiled=True)
    keys, values = keys_values[..., :HEAD_SIZE], keys_values[..., HEAD_SIZE:]
    scores = jnp.einsum("bqhd,bkd->bhqk", queries, keys, preferred_element_type=F32) * inv_root
    scores = jnp.where(visible[:, None], scores, NEG)
    row_max = jnp.max(scores, -1, keepdims=True)
    exponent = jnp.exp(scores - row_max)
    probs = exponent / jnp.sum(exponent, -1, keepdims=True)
    probs_low = probs.astype(BF16)
    context = jnp.einsum("bhqk,bkd->bqhd", probs_low, values, preferred_element_type=F32)
    context_low = context.reshape(trees * rows, heads * HEAD_SIZE).astype(BF16)
    attn_out = dot(context_low, w_output, ((1,), (0,))).astype(BF16)
    after_attn = residual + lax.psum(attn_out, "tensor").astype(F32)

    factor_two = norm_factor(after_attn)
    hidden_two = (after_attn * factor_two * moe_gain).astype(BF16)
    logits = dot(hidden_two, w_router, ((1,), (0,)))
    chosen = jnp.any(
        routes.reshape(trees * rows, -1)[:, :, None]
        == jnp.arange(all_experts, dtype=jnp.int32)[None, None, :],
        1,
    )
    masked = jnp.where(chosen, logits, NEG)
    raised = jnp.where(chosen, jnp.exp(masked - jnp.max(masked, -1, keepdims=True)), 0.0)
    mixing = raised / jnp.sum(raised, -1, keepdims=True)

    def over_expert(array):
        full = lax.all_gather(
            array.reshape(trees, rows, array.shape[-1]), "expert", axis=1, tiled=True
        )
        return full.reshape(trees * length, array.shape[-1])

    every_hidden = over_expert(hidden_two)
    every_up = over_expert(cotangent)
    every_mix = lax.dynamic_slice_in_dim(
        over_expert(mixing), expert_at * own_experts, own_experts, 1
    )
    count = trees * length
    pre_gate = dot(every_hidden, gate_t.reshape(-1, width), ((1,), (1,)))
    pre_up = dot(every_hidden, up_t.reshape(-1, width), ((1,), (1,)))
    down_rows = down.reshape(-1, width)
    down_back = dot(every_up, down_rows, ((1,), (1,)))
    wide_mix = jnp.repeat(every_mix, quarter, axis=1)
    activated, pull = jax.vjp(jax.nn.gelu, pre_gate)
    hidden = activated * pre_up
    mixed_hidden = (hidden * wide_mix).astype(BF16)
    moe_part = dot(mixed_hidden, down_rows, ((1,), (0,))).astype(BF16)
    gate_part = jnp.sum((hidden * down_back).reshape(count, own_experts, quarter), -1)
    hidden_grad = wide_mix * down_back
    gate_pre = pull(hidden_grad * pre_up)[0].astype(BF16)
    up_pre = (hidden_grad * activated).astype(BF16)
    two_part = (
        dot(gate_pre, gate_t.reshape(-1, width), ((1,), (0,)))
        + dot(up_pre, up_t.reshape(-1, width), ((1,), (0,)))
    ).astype(BF16)
    d_down = dot(mixed_hidden, every_up, ((0,), (0,)))
    d_gate = dot(gate_pre, every_hidden, ((0,), (0,)))
    d_up = dot(up_pre, every_hidden, ((0,), (0,)))

    def to_owner(array):
        array = array.reshape(trees, length, array.shape[-1])
        part = lax.psum_scatter(array, "expert", scatter_dimension=1, tiled=True)
        return lax.psum(part, "tensor").reshape(trees * rows, -1)

    spread = jnp.arange(all_experts) // own_experts == expert_at
    gate_wide = jnp.where(
        spread[None, :], jnp.tile(gate_part, (1, all_experts // own_experts)), 0.0
    )
    two_grad = to_owner(two_part).astype(F32)
    mix_grad = to_owner(gate_wide)
    mixed_out = (after_attn + to_owner(moe_part).astype(F32)).astype(BF16)

    picked_grad = mixing * (mix_grad - jnp.sum(mixing * mix_grad, -1, keepdims=True))
    logit_grad = picked_grad.astype(BF16)
    two_grad = two_grad + dot(logit_grad, w_router, ((1,), (1,)))
    d_router = dot(hidden_two, logit_grad, ((0,), (0,)))
    norm_two, d_moe_gain = norm_back(after_attn, factor_two, moe_gain, two_grad)
    attn_grad = cotangent.astype(F32).reshape(trees * rows, width) + norm_two
    attn_low = attn_grad.astype(BF16)

    d_output = dot(context_low, attn_low, ((0,), (0,)))
    context_grad = (
        dot(attn_low, w_output, ((1,), (1,)))
        .astype(BF16)
        .reshape(trees, rows, heads, HEAD_SIZE)
    )
    prob_grad = jnp.einsum("bqhd,bkd->bhqk", context_grad, values, preferred_element_type=F32)
    score_grad = probs * (prob_grad - jnp.sum(probs * prob_grad, -1, keepdims=True))
    score_grad = score_grad.astype(BF16)
    query_grad = (
        jnp.einsum("bhqk,bkd->bqhd", score_grad, keys, preferred_element_type=F32) * inv_root
    )
    key_grad = (
        jnp.einsum("bhqk,bqhd->bkd", score_grad, queries, preferred_element_type=F32) * inv_root
    )
    value_grad = jnp.einsum("bhqk,bqhd->bkd", probs_low, context_grad, preferred_element_type=F32)
    kv_part = jnp.concatenate([key_grad, value_grad], -1).astype(BF16)
    kv_sum = lax.psum_scatter(kv_part, "expert", scatter_dimension=1, tiled=True)
    sharing = GROUP // heads
    own_rows = rows // sharing
    place = tensor_at % sharing
    kv_rows = kv_sum.reshape(trees, sharing, own_rows, 2 * HEAD_SIZE)
    mine = lax.dynamic_index_in_dim(kv_rows, place, 1, False).astype(F32)
    for step in range(1, sharing):
        order = [
            (at, at // sharing * sharing + (at + step) % sharing) for at in range(tensor_count)
        ]
        away = lax.dynamic_index_in_dim(kv_rows, (place + step) % sharing, 1, False)
        mine = mine + lax.ppermute(away, "tensor", order).astype(F32)

    def own(array):
        return lax.dynamic_slice_in_dim(array, place * own_rows, own_rows, 1)

    key_low = rotate(mine[..., :HEAD_SIZE], own(cosine), -own(sine)).astype(BF16)
    kv_low = jnp.concatenate([key_low, mine[..., HEAD_SIZE:].astype(BF16)], -1)
    kv_low = kv_low.reshape(trees * own_rows, 2 * HEAD_SIZE)
    hidden_own = own(hidden_one.reshape(trees, rows, width)).reshape(trees * own_rows, width)
    d_kv = dot(hidden_own, kv_low, ((0,), (0,)))
    kv_back = dot(kv_low, w_kv, ((1,), (1,))).reshape(trees, own_rows, width)
    query_low = rotate(query_grad, cosine[:, :, None, :], -sine[:, :, None, :])
    query_low = query_low.astype(BF16).reshape(trees * rows, heads * HEAD_SIZE)
    d_query = dot(hidden_one, query_low, ((0,), (0,)))
    one_part = dot(query_low, w_query, ((1,), (1,))).reshape(trees, rows, width)
    one_part = lax.dynamic_update_slice_in_dim(
        one_part, own(one_part) + kv_back, place * own_rows, 1
    ).reshape(trees * rows, width)
    one_grad = lax.psum(one_part.astype(BF16), "tensor").astype(F32)
    norm_one, d_attn_gain = norm_back(residual, factor_one, attn_gain, one_grad)
    d_tokens = (attn_grad + norm_one).reshape(trees, rows, width)

    def scatter_dp(array, axis):
        return lax.psum_scatter(array, "dp", scatter_dimension=axis, tiled=True)

    def scatter_expert(array, axis):
        return lax.psum_scatter(array, "expert", scatter_dimension=axis, tiled=True)

    def experts_home(array):
        return scatter_dp(array.astype(BF16), 1).astype(F32).reshape(own_experts, quarter, -1)

    d_gate, d_up, d_down = experts_home(d_gate), experts_home(d_up), experts_home(d_down)
    d_query = scatter_expert(scatter_dp(d_query.astype(BF16), 0), 0).astype(F32)
    d_output = scatter_expert(scatter_dp(d_output.astype(BF16), 1), 1).astype(F32)
    flat = jnp.concatenate([d_attn_gain[:, None], d_moe_gain[:, None], d_router], 1)
    flat = scatter_expert(scatter_dp(flat, 0), 0)
    of_head = (jnp.arange(KEY_VALUE_HEADS) == kv_head).astype(F32)[None, None, :, None]
    d_kv = scatter_expert(scatter_dp(d_kv, 0), 0).reshape(-1, 2, 1, HEAD_SIZE) * of_head
    d_kv = d_kv.reshape(-1, 2 * KEY_VALUE_HEADS * HEAD_SIZE)
    d_kv = lax.psum_scatter(d_kv, "tensor", scatter_dimension=0, tiled=True)
    return (
        mixed_out.reshape(trees, rows, width),
        d_tokens,
        flat[:, 0],
        d_query,
        d_kv[:, : KEY_VALUE_HEADS * HEAD_SIZE],
        d_kv[:, KEY_VALUE_HEADS * HEAD_SIZE :],
        d_output,
        flat[:, 1],
        flat[:, 2:],
        jnp.swapaxes(d_gate, 1, 2),
        jnp.swapaxes(d_up, 1, 2),
        d_down,
    )


MESH = pl.DeviceIdType.MESH
NT = (((1,), (1,)), ((), ()))
NN = (((1,), (0,)), ((), ()))
TN = (((0,), (0,)), ((), ()))
CHUNKS = 4
TILE = 128
KINDS = 3
ROOT_2_PI = math.sqrt(2.0 / math.pi)
CUBIC = 0.044715


def mm(left, right, dims=NN):
    return lax.dot_general(left, right, dims, preferred_element_type=F32)


def rows_at(number, size):
    return pl.ds(pl.multiple_of(number * size, size), size)


class Place:
    def __init__(self):
        self.z = lax.axis_index("dp")
        self.x = lax.axis_index("expert")
        self.t = lax.axis_index("tensor")
        self.y = self.t // 2
        self.c = self.t % 2

    def at_z(self, z):
        return (z, self.x, self.t)

    def x_peer(self):
        return (self.z, 1 - self.x, self.t)

    def y_peer(self):
        return (self.z, self.x, (self.t + 2) % 4)

    def core_peer(self):
        return (self.z, self.x, self.t + 1 - 2 * self.c)


def remote(src, dst, sems, at, device):
    return pltpu.make_async_remote_copy(
        src_ref=src,
        dst_ref=dst,
        send_sem=sems.at[0, at],
        recv_sem=sems.at[1, at],
        device_id=device,
        device_id_type=MESH,
    )


def signal(sem, device):
    pl.semaphore_signal(sem, inc=1, device_id=device, device_id_type=MESH)


def await_signal(sem):
    pl.semaphore_wait(sem, 1)


def greet(devices):
    barrier = pltpu.get_barrier_semaphore()
    for device in devices:
        pl.semaphore_signal(barrier, inc=1, device_id=device, device_id_type=MESH)
    pl.semaphore_wait(barrier, len(devices))


def tree_tables(starts, parents, tree, first, rows, length, frequency):
    count = starts.shape[1]
    place = first + lax.broadcasted_iota(jnp.int32, (rows, HEAD_SIZE), 0)
    start = [starts[tree, k] for k in range(count)]
    parent = [parents[tree, k] for k in range(count)]
    size = [(start[k + 1] if k + 1 < count else length) - start[k] for k in range(count)]

    def pick(table, at):
        total = jnp.zeros_like(at)
        for k in range(count):
            total = total + jnp.where(at == k, table[k], 0)
        return total

    def segment_of(at):
        total = jnp.zeros_like(at)
        for k in range(1, count):
            total = total + jnp.where(at >= start[k], 1, 0)
        return total

    segment = segment_of(place)
    above = pick(parent, segment)
    further = pick(parent, above)
    depth = (
        place
        - pick(start, segment)
        + jnp.where(segment != 0, pick(size, above), 0)
        + jnp.where(above != 0, pick(size, further), 0)
    )
    turning = depth.astype(F32) * frequency
    lane = lax.broadcasted_iota(jnp.int32, (rows, HEAD_SIZE), 1)
    cosine = jnp.cos(turning)
    sine = jnp.sin(turning)
    sine = jnp.where(lane < HEAD_SIZE // 2, -sine, sine)
    key_place = lax.broadcasted_iota(jnp.int32, (8, length), 1)
    key_segment = jnp.broadcast_to(segment_of(key_place)[:1], (rows, length))
    key_place = jnp.broadcast_to(key_place[:1], (rows, length))
    wide = length // HEAD_SIZE

    def widen(array):
        return jnp.concatenate([array] * wide, 1)

    visible = (
        (key_segment == widen(segment))
        | (key_segment == widen(above))
        | (key_segment == widen(further))
    ) & (key_place <= widen(place))
    return jnp.where(visible, 1.0, 0.0), cosine, sine


def turn(head, cosine, sine):
    return head * cosine + pltpu.roll(head, HEAD_SIZE // 2, 1) * sine


class Relay:
    def __init__(self, me, deep, piece, up_sems, dn_sems, side_sems=None):
        self.me, self.deep, self.piece = me, deep, piece
        self.up_sems, self.dn_sems, self.side_sems = up_sems, dn_sems, side_sems

    def up(self, source, part, hop):
        above = self.me.at_z(jnp.minimum(self.me.z + 1, self.deep - 1))
        at = self.piece(source, part, self.me.x)
        return remote(at, at, self.up_sems, part * self.deep + hop, above)

    def dn(self, source, part, hop):
        below = self.me.at_z(jnp.maximum(self.me.z - 1, 0))
        at = self.piece(source, part, self.me.x)
        return remote(at, at, self.dn_sems, part * self.deep + hop, below)

    def side(self, source, part, hop, x):
        at = self.piece(source, part, x)
        return remote(at, at, self.side_sems, part * 2 * self.deep + hop, self.me.x_peer())

    def begin(self, part, ends=None):
        z, last = self.me.z, self.deep - 1
        at_end = (z == 0) | (z == last)
        now = z >= 0 if ends is None else at_end if ends else jnp.logical_not(at_end)

        @pl.when((z < last) & now)
        def _():
            self.up(z, part, 0).start()

        @pl.when((z > 0) & now)
        def _():
            self.dn(z, part, 0).start()

    def pass_on(self, part, hop):
        z, deep = self.me.z, self.deep
        sides = self.side_sems is not None
        upward = (z - 1 - hop >= 0) & (z < deep - 1)
        downward = (z + 1 + hop < deep) & (z > 0)
        if sides:

            @pl.when(z - 1 - hop >= 0)
            def _():
                self.up(z - 1 - hop, part, hop).wait_recv()
                self.side(z - 1 - hop, part, hop, self.me.x).start()

            @pl.when(z + 1 + hop < deep)
            def _():
                self.dn(z + 1 + hop, part, hop).wait_recv()
                self.side(z + 1 + hop, part, deep + hop, self.me.x).start()

        @pl.when(upward)
        def _():
            if not sides:
                self.up(z - 1 - hop, part, hop).wait_recv()
            self.up(z - 1 - hop, part, hop + 1).start()

        @pl.when(downward)
        def _():
            if not sides:
                self.dn(z + 1 + hop, part, hop).wait_recv()
            self.dn(z + 1 + hop, part, hop + 1).start()

    def finish(self, part):
        z, deep = self.me.z, self.deep
        for hop in range(deep - 1):
            if self.side_sems is not None:

                @pl.when(z - 1 - hop >= 0)
                def _():
                    self.side(z - 1 - hop, part, hop, 1 - self.me.x).wait_recv()

                @pl.when(z + 1 + hop < deep)
                def _():
                    self.side(z + 1 + hop, part, deep + hop, 1 - self.me.x).wait_recv()

            else:

                @pl.when(z == deep - 1)
                def _():
                    self.up(z - 1 - hop, part, hop).wait_recv()

                @pl.when(z == 0)
                def _():
                    self.dn(z + 1 + hop, part, hop).wait_recv()

    def drain(self, part):
        z, deep = self.me.z, self.deep
        for hop in range(deep):

            @pl.when((z - hop >= 0) & (z < deep - 1))
            def _():
                self.up(z - hop, part, hop).wait_send()

            @pl.when((z + hop < deep) & (z > 0))
            def _():
                self.dn(z + hop, part, hop).wait_send()

        if self.side_sems is not None:
            for hop in range(deep - 1):

                @pl.when(z - 1 - hop >= 0)
                def _():
                    self.side(z - 1 - hop, part, hop, self.me.x).wait_send()

                @pl.when(z + 1 + hop < deep)
                def _():
                    self.side(z + 1 + hop, part, deep + hop, self.me.x).wait_send()


class PlaneSum:
    def __init__(self, me, rows, make, bufs, landing, sem_set, ahead=None):
        self.me, self.rows, self.make, self.ahead = me, rows, make, ahead
        self.core_out, self.x_out, self.acc, self.y_out = bufs
        self.core_in, self.x_in, self.y_in = landing
        self.core_sems, self.x_sems, self.y_sems = sem_set
        self.tiles = rows // TILE
        self.step = rows // CHUNKS
        self.per_tile = TILE // self.step

    def core_copy(self, number):
        at = rows_at(number, TILE)
        return remote(
            self.core_out.at[at], self.core_in.at[at], self.core_sems, number, self.me.core_peer()
        )

    def x_copy(self, number):
        at = rows_at(number, self.step)
        return remote(self.x_out.at[at], self.x_in.at[at], self.x_sems, number, self.me.x_peer())

    def y_copy(self, number):
        at = rows_at(number, self.step)
        return remote(self.y_out.at[at], self.y_in.at[at], self.y_sems, number, self.me.y_peer())

    def first(self, tree, x, number):
        return pl.multiple_of((tree * 2 + x) * self.rows + number * TILE, TILE)

    def tile(self, tree, x, number, buffer, at):
        value = self.make(self.first(tree, x, number))
        if self.ahead is not None:
            value = value + buffer[at, :].astype(F32)
        return value.astype(BF16)

    def prepare(self):
        me = self.me

        def other(number, carry):
            x = jnp.where(number < self.tiles, 1 - me.x, me.x)
            value = self.ahead(self.first(1 - me.c, x, number % self.tiles))
            self.core_out[rows_at(number, TILE), :] = value.astype(BF16)
            return carry

        def same(number, carry):
            at = rows_at(number, TILE)
            self.x_out[at, :] = self.ahead(self.first(me.c, 1 - me.x, number)).astype(BF16)
            self.acc[at, :] = self.ahead(self.first(me.c, me.x, number))
            return carry

        lax.fori_loop(0, 2 * self.tiles, other, 0)
        lax.fori_loop(0, self.tiles, same, 0)

    def outward(self, side):
        me = self.me
        x = me.x if side else 1 - me.x

        def one(number, carry):
            slot = side * self.tiles + number
            at = rows_at(slot, TILE)
            self.core_out[at, :] = self.tile(1 - me.c, x, number, self.core_out, at)
            self.core_copy(slot).start()
            return carry

        lax.fori_loop(0, self.tiles, one, 0)

    def across(self, first=0, last=None):
        me = self.me

        def one(number, carry):
            at = rows_at(number, TILE)
            value = self.tile(me.c, 1 - me.x, number, self.x_out, at).astype(F32)
            self.core_copy(number).wait_recv()
            self.x_out[at, :] = (value + self.core_in[at, :].astype(F32)).astype(BF16)
            for k in range(self.per_tile):
                self.x_copy(number * self.per_tile + k).start()
            return carry

        lax.fori_loop(first, self.tiles if last is None else last, one, 0)

    def inward(self):
        me = self.me

        def one(number, carry):
            at = rows_at(number, TILE)
            value = self.tile(me.c, me.x, number, self.acc, at).astype(F32)
            slot = self.tiles + number
            self.core_copy(slot).wait_recv()
            self.acc[at, :] = value + self.core_in[rows_at(slot, TILE), :].astype(F32)
            return carry

        lax.fori_loop(0, self.tiles, one, 0)

    def pass_on(self, first, last):
        def one(number, carry):
            at = rows_at(number, self.step)
            self.x_copy(number).wait_recv()
            self.y_out[at, :] = (self.acc[at, :] + self.x_in[at, :].astype(F32)).astype(BF16)
            self.y_copy(number).start()
            return carry

        lax.fori_loop(first, last, one, 0)

    def total(self, number):
        at = rows_at(number, self.step)
        self.y_copy(number).wait_recv()
        return self.y_out[at, :].astype(F32) + self.y_in[at, :].astype(F32)

    def core_sent(self):
        for number in range(2 * self.tiles):
            self.core_copy(number).wait_send()

    def x_sent(self):
        for number in range(CHUNKS):
            self.x_copy(number).wait_send()

    def y_sent(self):
        for number in range(CHUNKS):
            self.y_copy(number).wait_send()


class Fold:
    def __init__(self, me, groups, bufs, sem_set, tile, merge):
        self.me, self.groups, self.tile, self.merge = me, groups, tile, merge
        self.own, self.stage, self.land = bufs
        self.send_sems, self.recv_sems, self.free = sem_set
        self.sets, self.count, self.rows = self.stage.shape[0], self.own.shape[1], self.own.shape[2]
        self.slots = self.land.shape[1]
        z = me.z
        self.end = jnp.where(z < 2, 0, 3)
        self.mid = jnp.where(z < 2, 1, 2)
        self.far_mid = 3 - self.mid
        self.is_end = z == self.end
        self.is_mid = z == self.mid
        self.targets = (3 - self.end, self.far_mid, jnp.where(self.is_end, self.mid, self.end))

    def place(self, target):
        return (target + 3 - self.me.z) % 4

    def free_at(self, group, which, m):
        return self.free.at[((group % self.sets) * 3 + which) * self.count + m]

    def copy(self, group, which, m, slot=None):
        at = group % self.sets
        target = self.targets[which]
        from_mid = (4 if self.merge else 3, 3, 2)[which]
        there = jnp.where(self.is_end, which, from_mid) if slot is None else slot
        direct = self.far_mid if which == 0 and self.merge else target
        return pltpu.make_async_remote_copy(
            src_ref=self.stage.at[at, self.place(target), m],
            dst_ref=self.land.at[at, there, m],
            send_sem=self.send_sems.at[(at * 3 + which) * self.count + m],
            recv_sem=self.recv_sems.at[(at * self.slots + there) * self.count + m],
            device_id=self.me.at_z(jnp.where(self.is_end, self.mid, direct)),
            device_id_type=MESH,
        )

    def send(self, group, which, m):
        if group >= self.sets:
            await_signal(self.free_at(group, which, m))
        self.copy(group, which, m).start()

    def used(self, group, which, m, sender):
        if group + self.sets < self.groups:
            signal(self.free_at(group, which, m), self.me.at_z(sender))

    def add(self, group, which, m, slot):
        at = group % self.sets
        self.copy(group, which, m, slot).wait_recv()
        term = self.stage.at[at, self.place(self.targets[which]), m]
        landed = self.land.at[at, slot, m]

        def step(number, carry):
            rows = rows_at(number, self.tile)
            total = term[rows, :].astype(F32) + landed[rows, :].astype(F32)
            term[rows, :] = total.astype(BF16)
            return carry

        lax.fori_loop(0, self.rows // self.tile, step, 0)

    def begin(self, group, m):
        @pl.when(self.is_end)
        def _():
            for which in range(3):
                self.send(group, which, m)

        if not self.merge:

            @pl.when(self.is_mid)
            def _():
                self.send(group, 2, m)

    def advance(self, group, m):
        @pl.when(self.is_mid)
        def _():
            for which in (0, 1):
                self.add(group, which, m, which)
                self.used(group, which, m, self.end)
                self.send(group, which, m)

    def let_go(self, group, m):
        @pl.when(self.is_mid)
        def _():
            self.add(group, 2, m, 4)
            self.used(group, 0, m, self.far_mid)
            self.send(group, 2, m)

    def finish(self, group, m, write):
        at = group % self.sets
        own = self.own.at[group, m]
        near, far = self.land.at[at, 2, m], self.land.at[at, 3, m]
        self.copy(group, 2, m, 2).wait_recv()

        def run(pieces):
            def step(number, carry):
                rows = rows_at(number, self.tile)
                total = own[rows, :].astype(F32)
                for piece in pieces:
                    total = total + piece[rows, :].astype(F32)
                write(rows, total)
                return carry

            lax.fori_loop(0, self.rows // self.tile, step, 0)

        if self.merge:

            @pl.when(self.is_end)
            def _():
                run([near])
                self.used(group, 2, m, self.mid)

            @pl.when(self.is_mid)
            def _():
                self.copy(group, 1, m, 3).wait_recv()
                run([near, far])
                self.used(group, 2, m, self.end)
                self.used(group, 1, m, self.far_mid)

        else:
            self.copy(group, 1, m, 3).wait_recv()
            run([near, far])

    def drain(self, group, m):
        for which in range(3):
            self.copy(group, which, m).wait_send()


def place_kernel(*refs):
    count = (len(refs) - 2) // 3
    sources, targets, middles = refs[:count], refs[count : 2 * count], refs[2 * count : -2]
    loads, stores = [], []
    for source, target, middle in zip(sources, targets, middles):
        size = source.shape[0] // 2
        for part in range(2):
            at = pl.ds(part * size, size)
            number = len(loads)
            loads.append(pltpu.make_async_copy(source.at[at], middle.at[at], refs[-2].at[number]))
            stores.append(pltpu.make_async_copy(middle.at[at], target.at[at], refs[-1].at[number]))
    for load in loads:
        load.start()
    for load, store in zip(loads, stores):
        load.wait()
        store.start()
    for store in stores:
        store.wait()


def place_call(arrays):
    hbm = pl.BlockSpec(memory_space=pl.ANY)
    done = pltpu.SemaphoreType.DMA((2 * len(arrays),))
    return pl.pallas_call(
        place_kernel,
        out_shape=tuple(jax.ShapeDtypeStruct(a.shape, a.dtype) for a in arrays),
        in_specs=[hbm] * len(arrays),
        out_specs=[hbm] * len(arrays),
        scratch_shapes=[pltpu.VMEM(a.shape, a.dtype) for a in arrays] + [done, done],
        compiler_params=pltpu.CompilerParams(vmem_limit_bytes=60 * 2**20),
        name="place",
    )(*arrays)


def layer_kernel(
    starts,
    parents,
    frequency,
    routes,
    gain_one_in,
    gain_two_in,
    router_in,
    tokens_in,
    cotangent_in,
    w_query,
    w_key,
    w_value,
    w_output,
    gate_in,
    up_in,
    down_in,
    mixed,
    d_tokens,
    d_gate,
    d_up,
    d_down,
    d_query,
    d_output,
    d_key,
    d_value,
    d_small,
    mats,
    acts,
    hid,
    ups,
    wqkv,
    wout,
    smalls,
    queries,
    keys,
    values,
    probs,
    context,
    tables,
    after,
    mixes,
    gates,
    gates_out,
    gates_in,
    core_out,
    x_out,
    acc,
    y_out,
    two_core_in,
    two_x_in,
    two_y_in,
    mo_core_in,
    mo_x_in,
    mo_y_in,
    agrad,
    alow,
    qlow,
    kv_out,
    kv_in,
    kv_own,
    kvx_out,
    kvx_in,
    kvlow,
    kvlow_x,
    qlow_x,
    hidx,
    alx,
    ctx_x,
    dkv_out,
    dkv_in,
    own,
    stage,
    land,
    bounce,
    own_o,
    stage_o,
    land_o,
    own_q,
    stage_q,
    land_q,
    small_own,
    small_in,
    small_z,
    kv_last,
    kv_land,
    load_sem,
    small_sem,
    up1_sem,
    dn1_sem,
    side1_sem,
    up2_sem,
    dn2_sem,
    side2_sem,
    trade_sem,
    up3_sem,
    dn3_sem,
    kv_sem,
    cot_sem,
    core_sem,
    y_sem,
    hx_sem,
    hc_sem,
    hf_sem,
    mix_sem,
    gate_sem,
    two_core_sem,
    two_x_sem,
    two_y_sem,
    mo_core_sem,
    mo_x_sem,
    mo_y_sem,
    one_core_sem,
    one_y_sem,
    low_sem,
    kvg_sem,
    qx_sem,
    hidx_sem,
    alx_sem,
    ctx_sem,
    fold_send,
    fold_recv,
    fold_free,
    fold_send_o,
    fold_recv_o,
    fold_send_q,
    fold_recv_q,
    out_sem,
    mixed_sem,
    token_sem,
    grad_sem,
    small_in_sem,
    small_z_sem,
    last_sem,
):
    me = Place()
    z, x, y, c = me.z, me.x, me.y, me.c
    deep, shard = wqkv.shape[0], wqkv.shape[1]
    trees, heads, rows, length = probs.shape
    width = hid.shape[1]
    groups = gates.shape[0]
    units = mats.shape[1] // groups
    mine = heads * HEAD_SIZE
    half = shard // 2
    step = rows // CHUNKS
    inv_root = HEAD_SIZE ** (-0.5)
    own_block = c * 2 + x
    is_end = (z == 0) | (z == deep - 1)

    def block_rows(tree, side):
        return rows_at(tree * 2 + side, rows)

    def shard_lanes(k):
        return rows_at(k, shard)

    def load(source, target, at):
        return pltpu.make_async_copy(source, target, load_sem.at[at])

    head_lanes = rows_at(y, HEAD_SIZE)
    first_lanes, second_lanes = pl.ds(mine, HEAD_SIZE), pl.ds(mine + HEAD_SIZE, HEAD_SIZE)
    loads = [
        load(w_query, wqkv.at[z, :, pl.ds(0, mine)], 0),
        load(w_output, wout.at[z], 4),
        load(tokens_in, alow, 5),
        load(cotangent_in.at[0], ups.at[block_rows(0, x)], 6),
        load(cotangent_in.at[1], ups.at[block_rows(1, x)], 7),
        load(gate_in, mats.at[0, :, shard_lanes(z)], 8),
        load(up_in, mats.at[1, :, shard_lanes(z)], 9),
        load(down_in, mats.at[2, :, shard_lanes(z)], 10),
    ]

    for core, source in enumerate((w_key, w_value)):

        @pl.when(c == core)
        def _():
            load(source.at[:, head_lanes], wqkv.at[z, :, first_lanes], 1).start()

    row = lax.broadcasted_iota(jnp.int32, (8, shard), 0)
    gains = jnp.where(
        row == 0,
        jnp.broadcast_to(gain_one_in[...].astype(F32), (8, shard)),
        jnp.where(row == 1, jnp.broadcast_to(gain_two_in[...].astype(F32), (8, shard)), 0.0),
    )
    smalls[z] = jnp.concatenate([gains, router_in[...].astype(F32)], 0).astype(BF16)
    for copy in loads:
        copy.start()
    lin = x * 4 + me.t

    def plane(number):
        return (z, number // 4, number % 4)

    greet(
        [me.at_z((z + k) % deep) for k in range(1, deep)]
        + [plane((lin + k) % 8) for k in range(1, 8)]
    )
    loads[0].wait()
    load(w_key.at[:, head_lanes], wqkv.at[z, :, first_lanes], 1).wait()

    def qkv_piece(source, part, by):
        return wqkv.at[source, rows_at(by, half), pl.ds(0, mine + HEAD_SIZE)]

    def out_piece(source, part, by):
        return wout.at[source, rows_at(by, half)]

    def expert_piece(source, part, by):
        return mats.at[:, pl.ds(part * units, units), shard_lanes(source)]

    take_qkv = Relay(me, deep, qkv_piece, up1_sem, dn1_sem, side1_sem)
    take_out = Relay(me, deep, out_piece, up2_sem, dn2_sem, side2_sem)
    take = Relay(me, deep, expert_piece, up3_sem, dn3_sem)

    def small_out(k):
        there = (z + k) % deep
        return remote(smalls.at[z], smalls.at[z], small_sem, k - 1, me.at_z(there))

    take_qkv.begin(0)
    for k in range(1, deep):
        small_out(k).start()

    def make_tables(tree):
        seen, cosine, sine = tree_tables(
            starts, parents, tree, x * rows, rows, length, frequency[:1, :]
        )
        agrad[:, pl.ds(tree * length, length)] = seen
        tables[0, tree] = cosine
        tables[1, tree] = sine

    make_tables(0)
    take_qkv.pass_on(0, 0)
    for copy in loads[1:]:
        copy.wait()
    take_out.begin(0)
    for tree in range(1, trees):
        make_tables(tree)
    take_qkv.pass_on(0, 1)
    take_out.pass_on(0, 0)
    for k in range(1, deep):
        source = (z + deep - k) % deep
        remote(
            smalls.at[source], smalls.at[source], small_sem, k - 1, me.at_z(source)
        ).wait_recv()
    every_small = jnp.concatenate([smalls[k].astype(F32) for k in range(deep)], 1)
    gain_one, gain_two = every_small[:1], every_small[1:2]
    router = every_small[8:].astype(BF16)

    def norm_rows(source, target, at):
        value = source[at, :].astype(F32)
        factor = lax.rsqrt(jnp.mean(value * value, -1, keepdims=True) + EPS)
        target[at, :] = (value * factor * gain_one).astype(BF16)

    for tree in range(trees):

        def first_norm(number, carry):
            at = rows_at(number, step)
            norm_rows(alow.at[tree], core_out.at[pl.ds(tree * rows, rows)], at)
            return carry

        lax.fori_loop(0, CHUNKS, first_norm, 0)
    take_qkv.pass_on(0, 2)
    take_out.pass_on(0, 1)
    take.begin(0)
    take_qkv.finish(0)
    trade = remote(
        wqkv.at[:, :, first_lanes], wqkv.at[:, :, second_lanes], trade_sem, 0, me.core_peer()
    )
    trade.start()
    trade.wait_recv()

    own_place = rows_at(x, rows)
    away_place = rows_at(1 - x, rows)

    def kv_copy(tree, which, place, on):
        at = (keys, values)[which].at[tree, place]
        return remote(at, at, kv_sem, 2 * on + which, me.core_peer() if on else me.x_peer())

    def project_in(tree):
        total = jnp.zeros((rows, wqkv.shape[2]), F32)
        for k in range(deep):
            total = total + mm(core_out[rows_at(tree, rows), pl.ds(k * shard, shard)], wqkv[k])
        cosine, sine = tables[0, tree], tables[1, tree]
        for head in range(heads):
            part_q = total[:, head * HEAD_SIZE : (head + 1) * HEAD_SIZE]
            queries[tree, head] = turn(part_q, cosine, sine).astype(BF16)
        first, second_part = total[:, mine : mine + HEAD_SIZE], total[:, mine + HEAD_SIZE :]
        part_k = jnp.where(c == 0, first, second_part)
        keys[tree, own_place, :] = turn(part_k, cosine, sine).astype(BF16)
        values[tree, own_place, :] = jnp.where(c == 0, second_part, first).astype(BF16)

    project_in(c)
    for which in range(2):
        kv_copy(c, which, own_place, 0).start()
    project_in(1 - c)
    take_out.pass_on(0, 2)

    own_up, away_up = ups.at[block_rows(c, x)], ups.at[block_rows(c, 1 - x)]
    peer_up = ups.at[block_rows(1 - c, 1 - x)]
    cot_x = remote(own_up, own_up, cot_sem, 0, me.x_peer())
    cot_x.start()
    for which in range(2):
        kv_copy(c, which, away_place, 0).wait_recv()
        kv_copy(c, which, away_place, 1).start()

    def attend(tree):
        mask = agrad.at[:, rows_at(tree, length)]

        def one(head, carry):
            score = mm(queries[tree, head], keys[tree], NT) * inv_root
            score = jnp.where(mask[...] > 0.5, score, NEG)
            top = jnp.max(score, -1, keepdims=True)
            raised = jnp.exp(score - top)
            prob = (raised / jnp.sum(raised, -1, keepdims=True)).astype(BF16)
            probs[tree, head] = prob
            context[tree, head] = mm(prob, values[tree]).astype(BF16)
            return carry

        lax.fori_loop(0, heads, one, 0)

    attend(c)
    take.pass_on(0, 0)
    take.begin(1, False)
    for part in range(1, groups):
        take.begin(part, True)
    for which in range(2):
        kv_copy(1 - c, which, away_place, 1).wait_recv()
    attend(1 - c)
    take_out.finish(0)

    def project(tree, row):
        pieces = []
        for k in range(deep):
            piece = jnp.zeros((step, shard), F32)
            for head in range(heads):
                piece = piece + mm(
                    context[tree, head, pl.ds(row, step), :],
                    wout[k, pl.ds(head * HEAD_SIZE, HEAD_SIZE), :],
                )
            pieces.append(piece)
        return pieces

    def core_copy(number):
        at = rows_at(number, step)
        return remote(core_out.at[at], mo_core_in.at[at], core_sem, number, me.core_peer())

    def y_copy(number):
        at = rows_at(number, step)
        return remote(y_out.at[at], mo_y_in.at[at], y_sem, number, me.y_peer())

    for chunk in range(CHUNKS):
        at = pl.ds(chunk * step, step)
        for k, piece in enumerate(project(1 - c, chunk * step)):
            core_out[at, pl.ds(k * shard, shard)] = piece.astype(BF16)
        core_copy(chunk).start()
    for chunk in range(CHUNKS):
        at = pl.ds(chunk * step, step)
        pieces = project(c, chunk * step)
        core_copy(chunk).wait_recv()
        for k, piece in enumerate(pieces):
            lanes = pl.ds(k * shard, shard)
            both = piece.astype(BF16).astype(F32) + mo_core_in[at, lanes].astype(F32)
            y_out[at, lanes] = both.astype(BF16)
        y_copy(chunk).start()
    take.pass_on(0, 1)

    def two_rows(tree, side, number):
        first = (tree * 2 + side) * rows + number * step
        return pl.ds(pl.multiple_of(first, step), step)

    def hid_copy(tree, side, sems, number, device):
        at = hid.at[two_rows(tree, side, number)]
        return remote(at, at, sems, number, device)

    def second(number, carry):
        at = rows_at(number, step)
        y_copy(number).wait_recv()
        value = alow[c, at, :].astype(F32) + (y_out[at, :].astype(F32) + mo_y_in[at, :].astype(F32))
        after[at, :] = value
        factor = lax.rsqrt(jnp.mean(value * value, -1, keepdims=True) + EPS)
        hid[two_rows(c, x, number), :] = (value * factor * gain_two).astype(BF16)
        hid_copy(c, x, hx_sem, number, me.x_peer()).start()
        hid_copy(c, x, hc_sem, number, me.core_peer()).start()
        return carry

    lax.fori_loop(0, 2, second, 0)
    take.pass_on(1, 0)
    take.begin(2, False)
    lax.fori_loop(2, CHUNKS, second, 0)

    logits = mm(router, hid[block_rows(c, x), :], NT)
    expert = lax.broadcasted_iota(jnp.int32, logits.shape, 0)
    chosen = expert < 0
    for k in range(routes.shape[1]):
        chosen = chosen | (expert == routes[c, k : k + 1, :])
    logits = jnp.where(chosen, logits, NEG)
    raised = jnp.where(chosen, jnp.exp(logits - jnp.max(logits, 0, keepdims=True)), 0.0)
    mixes[own_block] = raised / jnp.sum(raised, 0, keepdims=True)

    def mix_copy(tree, side, at, device):
        block = mixes.at[tree * 2 + side]
        return remote(block, block, mix_sem, at, device)

    mix_copy(c, x, 0, me.x_peer()).start()
    mix_copy(c, x, 1, me.core_peer()).start()
    cot_x_in = remote(away_up, away_up, cot_sem, 0, me.x_peer())
    cot_x_in.wait_recv()
    cot_on = remote(away_up, away_up, cot_sem, 1, me.core_peer())
    cot_on.start()
    for number in range(CHUNKS):
        hid_copy(c, 1 - x, hx_sem, number, me.x_peer()).wait_recv()
        hid_copy(c, 1 - x, hf_sem, number, me.core_peer()).start()
    mix_copy(c, 1 - x, 0, me.x_peer()).wait_recv()
    mix_copy(c, 1 - x, 2, me.core_peer()).start()
    remote(peer_up, peer_up, cot_sem, 1, me.core_peer()).wait_recv()
    for number in range(CHUNKS):
        hid_copy(1 - c, x, hc_sem, number, me.core_peer()).wait_recv()
        hid_copy(1 - c, 1 - x, hf_sem, number, me.core_peer()).wait_recv()
    mix_copy(1 - c, x, 1, me.core_peer()).wait_recv()
    mix_copy(1 - c, 1 - x, 2, me.core_peer()).wait_recv()
    take.pass_on(1, 1)

    def half_lanes(k, side):
        first = k * shard + side * HEAD_SIZE
        return pl.ds(pl.multiple_of(first, HEAD_SIZE), 2 * HEAD_SIZE)

    def cross(source, landing, tree, k, on, sems):
        at = landing.at[tree, k]
        if on:
            return remote(at, at, sems, deep + k, me.core_peer())
        return remote(source.at[:, half_lanes(k, 1 - x)], at, sems, k, me.x_peer())

    def hidx_copy(tree, k, on):
        return cross(x_out, hidx, tree, k, on, hidx_sem)

    def alx_out(number, k):
        at = rows_at(number, step)
        return remote(
            alow.at[c, at, half_lanes(k, 1 - x)],
            alx.at[c, k, at],
            alx_sem,
            number * deep + k,
            me.x_peer(),
        )

    def alx_on(tree, k):
        at = alx.at[tree, k]
        return remote(at, at, alx_sem, CHUNKS * deep + k, me.core_peer())

    def again(number, carry):
        norm_rows(alow.at[c], x_out, rows_at(number, step))
        return carry

    lax.fori_loop(0, CHUNKS, again, 0)
    for k in range(deep):
        hidx_copy(c, k, 0).start()
    ctx_copy = remote(context, ctx_x, ctx_sem, 0, me.x_peer())
    ctx_copy.start()
    take.finish(0)

    def expert_block(group, block):
        tokens = rows_at(block, rows)
        some = pl.ds(group * units, units)
        pre_gate = mm(mats[0, some, :], hid[tokens, :], NT)
        pre_up = mm(mats[1, some, :], hid[tokens, :], NT)
        back = mm(mats[2, some, :], ups[tokens, :], NT)
        first, second_half = mixes[block, group : group + 1, :], mixes[
            block, groups + group : groups + group + 1, :
        ]
        weight = jnp.broadcast_to(jnp.where(x == 0, first, second_half), (units, rows))
        square = pre_gate * pre_gate
        bent = jnp.tanh(ROOT_2_PI * pre_gate * (1.0 + CUBIC * square))
        slope = 0.5 * (1.0 + bent)
        active = pre_gate * slope
        rise = slope + 0.5 * pre_gate * (1.0 - bent * bent) * ROOT_2_PI * (
            1.0 + 3.0 * CUBIC * square
        )
        hidden = active * pre_up
        gates[pl.ds(group, 1), tokens] = jnp.sum(hidden * back, 0, keepdims=True)
        back = weight * back
        acts[0, some, tokens] = (back * pre_up * rise).astype(BF16)
        acts[1, some, tokens] = (back * active).astype(BF16)
        acts[2, some, tokens] = (weight * hidden).astype(BF16)

    fold = Fold(me, groups, (own, stage, land), (fold_send, fold_recv, fold_free), 64, True)

    def expert_grad(group, m):
        source = ups if m == 2 else hid
        some = acts.at[m, pl.ds(group * units, units)]

        def one(k, carry):
            value = mm(some[...], source[:, shard_lanes(k)]).astype(BF16)

            @pl.when(k == z)
            def _():
                own[group, m] = value

            @pl.when(k != z)
            def _():
                stage[group % fold.sets, fold.place(k), m] = value

            return carry

        lax.fori_loop(0, deep, one, 0)
        fold.begin(group, m)

    def expert_group(group):
        def one(block, carry):
            expert_block(group, block)
            return carry

        lax.fori_loop(0, 2 * trees, one, 0)
        for m in range(KINDS):
            expert_grad(group, m)

    expert_outs = (d_gate, d_up, d_down)

    def grad_out(group, m):
        return pltpu.make_async_copy(
            bounce.at[m], expert_outs[m].at[pl.ds(group * units, units)], grad_sem.at[m]
        )

    def finish_group(group, ends):
        @pl.when(is_end if ends else jnp.logical_not(is_end))
        def _():
            for m in range(KINDS):
                if group > 0:
                    grad_out(group - 1, m).wait()

                def write(at, value):
                    bounce[m, at, :] = value

                fold.finish(group, m, write)
                grad_out(group, m).start()

    def advance(group, kinds=range(KINDS)):
        for m in kinds:
            fold.advance(group, m)

    def let_go(group):
        for m in range(KINDS):
            fold.let_go(group, m)

    def drain(group):
        for m in range(KINDS):
            fold.drain(group, m)

    take.pass_on(2, 0)
    take.begin(3, False)
    expert_group(0)
    take.pass_on(2, 1)
    take.pass_on(3, 0)
    take.finish(1)
    expert_group(1)
    take.pass_on(3, 1)
    for k in range(deep):
        hidx_copy(c, k, 0).wait_recv()
        hidx_copy(c, k, 1).start()
    advance(0)
    take.finish(2)
    expert_group(2)
    finish_group(0, False)
    last = groups - 1

    def two_units(first, some):
        at = pl.ds(first, TILE)
        total = mm(acts[0, some, at], mats[0, some, :], TN)
        return total + mm(acts[1, some, at], mats[1, some, :], TN)

    def two_ahead(first):
        return two_units(first, pl.ds(0, last * units))

    def two_make(first):
        return two_units(first, pl.ds(last * units, units))

    def mo_make(first):
        return mm(acts[2, :, pl.ds(first, TILE)], mats[2], TN)

    two = PlaneSum(
        me,
        rows,
        two_make,
        (core_out, x_out, acc, y_out),
        (two_core_in, two_x_in, two_y_in),
        (two_core_sem, two_x_sem, two_y_sem),
        two_ahead,
    )
    mo = PlaneSum(
        me,
        rows,
        mo_make,
        (core_out, hid.at[pl.ds(rows, rows)], acc, hid.at[pl.ds(0, rows)]),
        (mo_core_in, mo_x_in, mo_y_in),
        (mo_core_sem, mo_x_sem, mo_y_sem),
    )
    for number in range(CHUNKS):
        core_copy(number).wait_send()
        y_copy(number).wait_send()
    for k in range(deep):
        hidx_copy(c, k, 0).wait_send()
    two.prepare()
    advance(1)
    let_go(0)
    take.finish(3)
    expert_block(last, (1 - c) * 2 + 1 - x)
    two.outward(0)
    expert_block(last, c * 2 + 1 - x)
    two.across()
    expert_block(last, (1 - c) * 2 + x)
    two.outward(1)
    expert_block(last, own_block)

    for block in range(2 * trees):
        gates_out[block, pl.ds(0, groups), :] = gates[:, pl.ds(block * rows, rows)]

    def gate_copy(k):
        there = (lin + k) % 8
        block = (there % 2) * 2 + there // 4
        return remote(gates_out.at[block], gates_in.at[lin], gate_sem, k - 1, plane(there))

    for k in range(1, 8):
        gate_copy(k).start()
    gates_in[lin] = gates_out[own_block]
    two.inward()
    drain(0)
    expert_grad(last, 0)
    two.pass_on(0, 1)
    expert_grad(last, 1)
    two.pass_on(1, 2)
    expert_grad(last, 2)
    two.pass_on(2, 3)
    advance(2, [0])

    for k in range(1, 8):
        source = (lin + 8 - k) % 8
        remote(gates_out.at[0], gates_in.at[source], gate_sem, k - 1, plane(source)).wait_recv()
    sums = []
    for side in range(2):
        total = gates_in[side * 4]
        for k in range(1, 4):
            total = total + gates_in[side * 4 + k]
        sums.append(total[:groups])
    mix_grad = jnp.concatenate(sums, 0)
    mix = mixes[own_block]
    picked = mix * (mix_grad - jnp.sum(mix * mix_grad, 0, keepdims=True))
    logit_grad = picked.astype(BF16)
    agrad[...] = mm(logit_grad, router, TN)
    small_own[pl.ds(0, 8), :] = jnp.zeros((8, width), F32)
    small_own[pl.ds(8, 8), :] = mm(logit_grad, hid[block_rows(c, x), :])

    for number in range(CHUNKS):
        hid_copy(c, x, hx_sem, number, me.x_peer()).wait_send()
        hid_copy(c, x, hc_sem, number, me.core_peer()).wait_send()
        hid_copy(c, 1 - x, hf_sem, number, me.core_peer()).wait_send()
    two.pass_on(3, 4)
    two.core_sent()
    mo.outward(0)
    mo.outward(1)
    advance(2, [1])

    def low_copy(number):
        at = alow.at[c, rows_at(number, step)]
        return remote(at, at, low_sem, number, me.core_peer())

    def second_norm(number, gain_grad):
        at = rows_at(number, step)
        upstream = two.total(number) + agrad[at, :]
        value = after[at, :]
        factor = lax.rsqrt(jnp.mean(value * value, -1, keepdims=True) + EPS)
        scaled = upstream * gain_two
        inner = jnp.mean(scaled * value, -1, keepdims=True)
        cot = ups[two_rows(c, x, number), :]
        total = cot.astype(F32) + (factor * scaled - value * (factor * factor * factor * inner))
        agrad[at, :] = total
        alow[c, at, :] = total.astype(BF16)
        low_copy(number).start()
        for k in range(deep):
            alx_out(number, k).start()
        return gain_grad + jnp.sum(upstream * value * factor, 0, keepdims=True)

    gain_two_grad = lax.fori_loop(0, CHUNKS, second_norm, jnp.zeros((1, width), F32))
    small_own[pl.ds(1, 1), :] = gain_two_grad

    def attend_back(tree):
        back = jnp.zeros((rows, mine), F32)
        for k in range(deep):
            back = back + mm(alow[tree, :, pl.ds(k * shard, shard)], wout[k], NT)
        back = back.astype(BF16)
        cosine, sine = tables[0, tree], tables[1, tree]
        key_grad = jnp.zeros((length, HEAD_SIZE), F32)
        value_grad = jnp.zeros((length, HEAD_SIZE), F32)
        for head in range(heads):
            lanes = pl.ds(head * HEAD_SIZE, HEAD_SIZE)
            back_head = back[:, head * HEAD_SIZE : (head + 1) * HEAD_SIZE]
            prob = probs[tree, head]
            value_grad = value_grad + mm(prob, back_head, TN)
            prob = prob.astype(F32)
            share = prob * mm(back_head, values[tree], NT)
            score = (share - prob * jnp.sum(share, -1, keepdims=True)).astype(BF16)
            query_grad = mm(score, keys[tree]) * inv_root
            qlow[tree, :, lanes] = turn(query_grad, cosine, -sine).astype(BF16)
            key_grad = key_grad + mm(score, queries[tree, head], TN)
        return jnp.concatenate([key_grad * inv_root, value_grad], 1)

    for number in range(CHUNKS):
        at = alow.at[1 - c, pl.ds(number * step, step)]
        remote(at, at, low_sem, number, me.core_peer()).wait_recv()
    kv_out[...] = attend_back(1 - c).astype(BF16)
    kvg_copy = remote(kv_out, kv_in, kvg_sem, 0, me.core_peer())
    kvg_copy.start()

    def qx_copy(tree, number):
        return remote(qlow.at[tree], qlow_x.at[tree], qx_sem, number, me.x_peer())

    qx_copy(1 - c, 0).start()
    kv_own[...] = attend_back(c)

    def of_side(ref, side):
        low, high = ref[pl.ds(0, rows), :], ref[pl.ds(rows, rows), :]
        return jnp.where(side == 0, low, high).astype(F32)

    kvg_copy.wait_recv()
    kvx_out[...] = (of_side(kv_own, 1 - x) + of_side(kv_in, 1 - x)).astype(BF16)
    kvx_copy = remote(kvx_out, kvx_in, kvg_sem, 1, me.x_peer())
    kvx_copy.start()
    qx_copy(c, 1).start()
    advance(2, [2])

    def one_tile(tree, at):
        return [mm(qlow[tree, at, :], wqkv[k, :, pl.ds(0, mine)], NT) for k in range(deep)]

    mo.core_sent()

    def one_copy(number):
        at = rows_at(number, step)
        return remote(core_out.at[at], two_core_in.at[at], one_core_sem, number, me.core_peer())

    def one_outward(number, carry):
        at = rows_at(number, step)
        for k, piece in enumerate(one_tile(1 - c, at)):
            core_out[at, pl.ds(k * shard, shard)] = piece.astype(BF16)
        one_copy(number).start()
        return carry

    lax.fori_loop(0, CHUNKS, one_outward, 0)
    for k in range(deep):
        for number in range(CHUNKS):
            alx_out(number, k).wait_recv()
        alx_on(c, k).start()
    let_go(1)
    kvx_copy.wait_recv()
    own_kv = of_side(kv_own, x) + of_side(kv_in, x) + kvx_in[...].astype(F32)
    key_low = turn(own_kv[:, :HEAD_SIZE], tables[0, c], -tables[1, c])
    value_low = own_kv[:, HEAD_SIZE:]
    kvlow[:, pl.ds(0, HEAD_SIZE)] = jnp.where(c == 0, key_low, value_low).astype(BF16)
    kvlow[:, pl.ds(HEAD_SIZE, HEAD_SIZE)] = jnp.where(c == 0, value_low, key_low).astype(BF16)
    kvl_copy = remote(kvlow, kvlow_x, kvg_sem, 2, me.x_peer())
    kvl_copy.start()

    two.y_sent()

    def one_y(number):
        at = rows_at(number, step)
        return remote(y_out.at[at], two_x_in.at[at], one_y_sem, number, me.y_peer())

    def one_inward(number, carry):
        at = rows_at(number, step)
        one_copy(number).wait_recv()
        for k, piece in enumerate(one_tile(c, at)):
            lanes = pl.ds(k * shard, shard)
            piece = piece + mm(kvlow[at, :], wqkv[k, :, pl.ds(mine, 2 * HEAD_SIZE)], NT)
            y_out[at, lanes] = (piece + two_core_in[at, lanes].astype(F32)).astype(BF16)
        one_y(number).start()
        return carry

    lax.fori_loop(0, CHUNKS, one_inward, 0)

    mo.across()
    mo.inward()
    for part in range(groups):
        take.drain(part)
    spare = mats.at[0]
    late = [
        load(tokens_in.at[0], spare.at[pl.ds(0, rows)], 0),
        load(tokens_in.at[1], spare.at[pl.ds(rows, rows)], 1),
    ]
    for copy in late:
        copy.start()

    def chosen_half(value):
        return jnp.where(x == 0, value[:half], value[2 * HEAD_SIZE - half :])

    def keep_own(buffer_own, buffer_stage, k, lanes, value):
        @pl.when(k == z)
        def _():
            buffer_own[0, 0, :, lanes] = value.astype(BF16)

        @pl.when(k != z)
        def _():
            buffer_stage[0, fold.place(k), 0, :, lanes] = value.astype(BF16)

    def heads_of(array, tree):
        return jnp.concatenate([array[tree, head] for head in range(heads)], 1)

    fold_o = Fold(me, 1, (own_o, stage_o, land_o), (fold_send_o, fold_recv_o, None), 64, False)
    fold_q = Fold(me, 1, (own_q, stage_q, land_q), (fold_send_q, fold_recv_q, None), 64, False)
    for k in range(deep):
        alx_on(1 - c, k).wait_recv()
    remote(context, ctx_x, ctx_sem, 0, me.x_peer()).wait_recv()

    def output_grad(k, carry):
        value = jnp.zeros((2 * HEAD_SIZE, mine), F32)
        for tree in range(trees):
            value = value + mm(alow[tree, :, half_lanes(k, x)], heads_of(context, tree), TN)
            value = value + mm(alx[tree, k], heads_of(ctx_x, tree), TN)
        keep_own(own_o, stage_o, k, pl.ds(0, mine), chosen_half(value))
        return carry

    lax.fori_loop(0, deep, output_grad, 0)
    fold_o.begin(0, 0)
    advance(3, [0])

    for copy in late:
        copy.wait()
    for tree in range(trees):

        def norm_again(number, carry):
            at = rows_at(number, step)
            norm_rows(
                spare.at[pl.ds(tree * rows, rows)], mats.at[1, pl.ds(tree * rows, rows)], at
            )
            return carry

        lax.fori_loop(0, CHUNKS, norm_again, 0)

    def hid_one(tree, k):
        return mats[1, rows_at(tree, rows), half_lanes(k, x)]

    for k in range(deep):
        hidx_copy(1 - c, k, 1).wait_recv()
    qx_copy(1 - c, 0).wait_recv()
    qx_copy(c, 1).wait_recv()

    def query_grad(k, carry):
        value = jnp.zeros((2 * HEAD_SIZE, mine), F32)
        for tree in range(trees):
            value = value + mm(hid_one(tree, k), qlow[tree], TN)
            value = value + mm(hidx[tree, k], qlow_x[tree], TN)
        keep_own(own_q, stage_q, k, pl.ds(0, mine), chosen_half(value))
        return carry

    lax.fori_loop(0, deep, query_grad, 0)

    kvl_copy.wait_recv()

    def kv_weight_grad(k, carry):
        value = mm(hid_one(c, k), kvlow[...], TN) + mm(hidx[c, k], kvlow_x[...], TN)
        value = chosen_half(value)
        low, high = value[:, :HEAD_SIZE], value[:, HEAD_SIZE:]
        dkv_out[0, k] = high.astype(BF16)
        dkv_out[1, k] = low.astype(BF16)
        return carry

    lax.fori_loop(0, deep, kv_weight_grad, 0)
    dkv_copy = remote(dkv_out.at[0], dkv_in, kvg_sem, 3, me.core_peer())
    dkv_copy.start()
    dkv_copy.wait_recv()

    def kv_weight_sum(k, carry):
        value = dkv_out[1, k].astype(F32) + dkv_in[k].astype(F32)
        keep_own(own_q, stage_q, k, pl.ds(mine, HEAD_SIZE), value)
        return carry

    lax.fori_loop(0, deep, kv_weight_sum, 0)
    fold_q.begin(0, 0)

    advance(3, [1])
    let_go(2)
    finish_group(0, True)
    finish_group(1, True)
    finish_group(1, False)
    finish_group(2, False)

    def out_copies(buffer, target, first, peer_sems, number):
        at = rows_at(number, step)
        here = pltpu.make_async_copy(buffer.at[at], target.at[c, at], out_sem.at[first + number])
        there = remote(buffer.at[at], target.at[c, at], peer_sems, number, me.core_peer())
        return here, there

    def first_norm_back(number, gain_grad):
        at = rows_at(number, step)
        one_y(number).wait_recv()
        upstream = y_out[at, :].astype(F32) + two_x_in[at, :].astype(F32)
        first = pl.multiple_of(c * rows + number * step, step)
        value = mats[0, pl.ds(first, step), :].astype(F32)
        factor = lax.rsqrt(jnp.mean(value * value, -1, keepdims=True) + EPS)
        scaled = upstream * gain_one
        inner = jnp.mean(scaled * value, -1, keepdims=True)
        agrad[at, :] = agrad[at, :] + (
            factor * scaled - value * (factor * factor * factor * inner)
        )
        for copy in out_copies(agrad, d_tokens, CHUNKS, token_sem, number):
            copy.start()
        return gain_grad + jnp.sum(upstream * value * factor, 0, keepdims=True)

    gain_one_grad = lax.fori_loop(0, CHUNKS, first_norm_back, jnp.zeros((1, width), F32))
    small_own[pl.ds(0, 1), :] = gain_one_grad
    spot = x * 2 + c

    def spread(k):
        there = (spot + k) % 4
        device = (z, there // 2, 2 * y + there % 2)
        return remote(small_own, small_in.at[spot], small_in_sem, k - 1, device)

    for k in range(1, 4):
        spread(k).start()
    small_in[spot] = small_own[...]
    advance(3, [2])
    mo.pass_on(0, CHUNKS)
    fold_o.advance(0, 0)
    let_go(3)
    finish_group(2, True)

    two.x_sent()

    def mix_out(number, carry):
        at = rows_at(number, step)
        x_out[at, :] = (after[at, :] + mo.total(number)).astype(BF16)
        for copy in out_copies(x_out, mixed, 0, mixed_sem, number):
            copy.start()
        return carry

    lax.fori_loop(0, CHUNKS, mix_out, 0)
    fold_q.advance(0, 0)
    for k in range(1, 4):
        source = (spot + 4 - k) % 4
        device = (z, source // 2, 2 * y + source % 2)
        remote(small_own, small_in.at[source], small_in_sem, k - 1, device).wait_recv()
        spread(k).wait_send()
    small_own[...] = (small_in[0] + small_in[1]) + (small_in[2] + small_in[3])

    def small_copy(k):
        there = (z + k) % deep
        return remote(
            small_own.at[:, shard_lanes(there)], small_z.at[z], small_z_sem, k - 1, me.at_z(there)
        )

    for k in range(1, deep):
        small_copy(k).start()
    small_z[z] = small_own[:, shard_lanes(z)]
    finish_group(3, False)
    finish_group(3, True)

    def write_o(at, value):
        d_output[at, :] = value

    fold_o.finish(0, 0, write_o)

    def write_q(at, value):
        d_query[at, :] = value[:, :mine]
        kv_last[at, :] = value[:, mine:]

    fold_q.finish(0, 0, write_q)

    share = half // 4

    def share_rows(t):
        return pl.ds(pl.multiple_of(t * share, 8), share)

    def last_copy(k):
        there = (me.t + k) % 4
        return remote(
            kv_last.at[share_rows(there)], kv_land.at[me.t], last_sem, k - 1, (z, x, there)
        )

    for k in range(1, 4):
        last_copy(k).start()
    kv_land[me.t] = kv_last[share_rows(me.t), :]
    for k in range(1, deep):
        source = (z + deep - k) % deep
        remote(
            small_own.at[:, shard_lanes(0)], small_z.at[source], small_z_sem, k - 1, me.at_z(source)
        ).wait_recv()
    total = small_z[0]
    for k in range(1, deep):
        total = total + small_z[k]
    d_small[...] = jnp.where(x == 0, total[:, :half], total[:, half:])
    for k in range(1, 4):
        source = (me.t + 4 - k) % 4
        remote(
            kv_last.at[pl.ds(0, share)], kv_land.at[source], last_sem, k - 1, (z, x, source)
        ).wait_recv()
    for head in range(KEY_VALUE_HEADS):
        lanes = pl.ds(head * HEAD_SIZE, HEAD_SIZE)
        d_key[:, lanes] = kv_land[2 * head]
        d_value[:, lanes] = kv_land[2 * head + 1]

    for number in range(CHUNKS):
        at = pl.ds(number * step, step)
        remote(x_out.at[at], mixed.at[1 - c, at], mixed_sem, number, me.core_peer()).wait_recv()
        remote(agrad.at[at], d_tokens.at[1 - c, at], token_sem, number, me.core_peer()).wait_recv()
        for buffer, target, first, peer_sems in (
            (x_out, mixed, 0, mixed_sem),
            (agrad, d_tokens, CHUNKS, token_sem),
        ):
            here, there = out_copies(buffer, target, first, peer_sems, number)
            here.wait()
            there.wait_send()
        one_y(number).wait_send()
        one_copy(number).wait_send()
        low_copy(number).wait_send()
    mo.x_sent()
    mo.y_sent()
    for m in range(KINDS):
        grad_out(groups - 1, m).wait()
    for k in range(1, 8):
        gate_copy(k).wait_send()
    for k in range(1, deep):
        small_copy(k).wait_send()
        small_out(k).wait_send()
    for k in range(1, 4):
        last_copy(k).wait_send()
    for k in range(deep):
        hidx_copy(c, k, 1).wait_send()
        for number in range(CHUNKS):
            alx_out(number, k).wait_send()
        alx_on(c, k).wait_send()
    for copy in (trade, kvg_copy, kvx_copy, kvl_copy, dkv_copy, qx_copy(1 - c, 0), qx_copy(c, 1), ctx_copy, cot_x, cot_on):
        copy.wait_send()
    for which in range(2):
        kv_copy(c, which, own_place, 0).wait_send()
        kv_copy(c, which, away_place, 1).wait_send()
    mix_copy(c, x, 0, me.x_peer()).wait_send()
    mix_copy(c, x, 1, me.core_peer()).wait_send()
    mix_copy(c, 1 - x, 2, me.core_peer()).wait_send()
    take_qkv.drain(0)
    take_out.drain(0)
    for group in range(1, groups):
        drain(group)
    fold_o.drain(0, 0)
    fold_q.drain(0, 0)


def sems(count):
    return pltpu.SemaphoreType.DMA((2, count))


def layer_call(
    seg_start,
    seg_parent,
    routes,
    gain_one,
    gain_two,
    router_t,
    tokens,
    cotangent,
    w_query,
    w_key,
    w_value,
    w_output,
    gate_t,
    up_t,
    w_down,
    deep,
):
    trees, rows, width = tokens.shape
    shard, mine = w_query.shape
    heads = mine // HEAD_SIZE
    length = rows * 2
    held, units = w_down.shape[0], w_down.shape[1]
    total_units = held * units
    experts = router_t.shape[0]
    small_rows = 8 + experts
    blocks = 2 * trees
    half = shard // 2
    count = blocks * rows
    sets = 3
    angle = HEAD_SIZE // 2
    frequency = ROPE_BASE ** (-2.0 * np.arange(angle, dtype=np.float32) / np.float32(HEAD_SIZE))
    frequency = np.tile(np.concatenate([frequency] * 2)[None], (8, 1)).astype(np.float32)
    vmem = pl.BlockSpec(memory_space=pltpu.VMEM)
    smem = pl.BlockSpec(memory_space=pltpu.SMEM)
    hbm = pl.BlockSpec(memory_space=pl.ANY)

    def plain(*shape):
        return pltpu.VMEM(shape, BF16)

    def wide(*shape):
        return pltpu.VMEM(shape, F32)

    def out(*shape, dtype=F32):
        return jax.ShapeDtypeStruct(shape, dtype)

    last = deep - 1
    return pl.pallas_call(
        layer_kernel,
        out_shape=(
            out(trees, rows, width, dtype=BF16),
            out(trees, rows, width),
            out(total_units, shard),
            out(total_units, shard),
            out(total_units, shard),
            out(half, mine),
            out(half, mine),
            out(half // 4, KEY_VALUE_HEADS * HEAD_SIZE),
            out(half // 4, KEY_VALUE_HEADS * HEAD_SIZE),
            out(small_rows, half),
        ),
        in_specs=[smem, smem] + [vmem] * 5 + [hbm] * 9,
        out_specs=[hbm] * 5 + [vmem] * 5,
        scratch_shapes=[
            plain(KINDS, total_units, width),
            plain(KINDS, total_units, count),
            plain(count, width),
            plain(count, width),
            plain(deep, shard, mine + 2 * HEAD_SIZE),
            plain(deep, mine, shard),
            plain(deep, small_rows, shard),
            plain(trees, heads, rows, HEAD_SIZE),
            plain(trees, length, HEAD_SIZE),
            plain(trees, length, HEAD_SIZE),
            plain(trees, heads, rows, length),
            plain(trees, heads, rows, HEAD_SIZE),
            wide(2, trees, rows, HEAD_SIZE),
            wide(rows, width),
            wide(blocks, experts, rows),
            wide(held, count),
            wide(blocks, 8, rows),
            wide(8, 8, rows),
            plain(2 * rows, width),
            plain(rows, width),
            wide(rows, width),
            plain(rows, width),
            plain(2 * rows, width),
            plain(rows, width),
            plain(rows, width),
            plain(2 * rows, width),
            plain(rows, width),
            plain(rows, width),
            wide(rows, width),
            plain(trees, rows, width),
            plain(trees, rows, mine),
            plain(length, 2 * HEAD_SIZE),
            plain(length, 2 * HEAD_SIZE),
            wide(length, 2 * HEAD_SIZE),
            plain(rows, 2 * HEAD_SIZE),
            plain(rows, 2 * HEAD_SIZE),
            plain(rows, 2 * HEAD_SIZE),
            plain(rows, 2 * HEAD_SIZE),
            plain(trees, rows, mine),
            plain(trees, deep, rows, 2 * HEAD_SIZE),
            plain(trees, deep, rows, 2 * HEAD_SIZE),
            plain(trees, heads, rows, HEAD_SIZE),
            plain(2, deep, half, HEAD_SIZE),
            plain(deep, half, HEAD_SIZE),
            plain(held, KINDS, units, shard),
            plain(sets, last, KINDS, units, shard),
            plain(sets, 5, KINDS, units, shard),
            wide(KINDS, units, shard),
            plain(1, 1, half, mine),
            plain(1, last, 1, half, mine),
            plain(1, deep, 1, half, mine),
            plain(1, 1, half, mine + HEAD_SIZE),
            plain(1, last, 1, half, mine + HEAD_SIZE),
            plain(1, deep, 1, half, mine + HEAD_SIZE),
            wide(small_rows, width),
            wide(4, small_rows, width),
            wide(deep, small_rows, shard),
            wide(half, HEAD_SIZE),
            wide(4, half // 4, HEAD_SIZE),
            pltpu.SemaphoreType.DMA((11,)),
            sems(last),
            sems(deep),
            sems(deep),
            sems(2 * deep),
            sems(deep),
            sems(deep),
            sems(2 * deep),
            sems(1),
            sems(held * deep),
            sems(held * deep),
            sems(2 * trees),
            sems(2),
            sems(CHUNKS),
            sems(CHUNKS),
            sems(CHUNKS),
            sems(CHUNKS),
            sems(CHUNKS),
            sems(3),
            sems(7),
            sems(2 * rows // TILE),
            sems(CHUNKS),
            sems(CHUNKS),
            sems(2 * rows // TILE),
            sems(CHUNKS),
            sems(CHUNKS),
            sems(CHUNKS),
            sems(CHUNKS),
            sems(CHUNKS),
            sems(4),
            sems(2),
            sems(2 * deep),
            sems((CHUNKS + 1) * deep),
            sems(1),
            pltpu.SemaphoreType.DMA((sets * 3 * KINDS,)),
            pltpu.SemaphoreType.DMA((sets * 5 * KINDS,)),
            pltpu.SemaphoreType.REGULAR((sets * 3 * KINDS,)),
            pltpu.SemaphoreType.DMA((3,)),
            pltpu.SemaphoreType.DMA((4,)),
            pltpu.SemaphoreType.DMA((3,)),
            pltpu.SemaphoreType.DMA((4,)),
            pltpu.SemaphoreType.DMA((2 * CHUNKS,)),
            sems(CHUNKS),
            sems(CHUNKS),
            pltpu.SemaphoreType.DMA((KINDS,)),
            sems(3),
            sems(last),
            sems(3),
        ],
        compiler_params=pltpu.CompilerParams(
            collective_id=0, has_side_effects=True, vmem_limit_bytes=64 * 2**20
        ),
        name="layer",
    )(
        seg_start,
        seg_parent,
        jnp.asarray(frequency),
        routes,
        gain_one,
        gain_two,
        router_t,
        tokens,
        cotangent,
        w_query,
        w_key,
        w_value,
        w_output,
        gate_t.reshape(total_units, -1),
        up_t.reshape(total_units, -1),
        w_down.reshape(total_units, -1),
    )


def plane_shards(
    tokens,
    cotangent,
    seg_start,
    seg_parent,
    routes,
    attn_gain,
    w_query,
    w_key,
    w_value,
    w_output,
    moe_gain,
    w_router,
    w_gate,
    w_up,
    w_down,
):
    width = tokens.shape[2]
    deep = lax.axis_size("dp")
    held, quarter = w_gate.shape[0], w_gate.shape[2]
    made = layer_call(
        seg_start,
        seg_parent,
        jnp.swapaxes(routes, 1, 2),
        attn_gain,
        moe_gain,
        w_router.T,
        tokens,
        cotangent,
        w_query,
        w_key,
        w_value,
        w_output,
        jnp.swapaxes(w_gate, 1, 2),
        jnp.swapaxes(w_up, 1, 2),
        w_down,
        deep,
    )
    placed = place_call(made[:-1])
    mixed, d_tokens, d_gate, d_up, d_down, d_query, d_output, d_key, d_value = placed
    d_small = made[-1]

    def experts(array):
        return array.reshape(held, quarter, width // deep)

    return (
        mixed,
        d_tokens,
        d_small[0],
        d_query,
        d_key,
        d_value,
        d_output.T,
        d_small[1],
        d_small[8:].T,
        jnp.swapaxes(experts(d_gate), 1, 2),
        jnp.swapaxes(experts(d_up), 1, 2),
        experts(d_down),
    )


def shards(*arrays):
    axes = tuple(lax.axis_size(name) for name in ("dp", "expert", "tensor"))
    if axes == (4, 2, 4) and arrays[0].shape[0] == 2:
        return plane_shards(*arrays)
    return general_shards(*arrays)


def solution(mesh):
    placed = (
        P("dp", "expert", None),
        P("dp", "expert", None),
        P("dp", None),
        P("dp", None),
        P("dp", "expert", None),
        P("dp"),
        P("dp", "tensor"),
        P("dp", None),
        P("dp", None),
        P("tensor", "dp"),
        P("dp"),
        P("dp", None),
        P("expert", "dp", "tensor"),
        P("expert", "dp", "tensor"),
        P("expert", "tensor", "dp"),
    )
    return jax.shard_map(
        shards,
        mesh=mesh,
        in_specs=placed,
        out_specs=(
            P("dp", "expert", None),
            P("dp", "expert", None),
            P(("dp", "expert")),
            P(("dp", "expert"), "tensor"),
            P(("dp", "expert", "tensor"), None),
            P(("dp", "expert", "tensor"), None),
            P("tensor", ("dp", "expert")),
            P(("dp", "expert")),
            P(("dp", "expert"), None),
            P("expert", "dp", "tensor"),
            P("expert", "dp", "tensor"),
            P("expert", "tensor", "dp"),
        ),
        check_vma=False,
    )
```
